32 devices in a mesh: ctx: 8 (over y, x, core), head: 4 (over z).
Axes of the slice: x: 2, y: 2, z: 4, core: 2. Of those that a mesh axis runs over, the one named last changes fastest.
Arguments:
- queries: bfloat16 [8192, 2048], P(('ctx', 'head')), may hold values from -6 to 6
- keys: bfloat16 [8192, 2048], P(('ctx', 'head')), may hold values from -6 to 6
- values: bfloat16 [8192, 2048], P(('ctx', 'head')), may hold values from -6 to 6
- grad_out: bfloat16 [8192, 2048], P(('ctx', 'head')), may hold values from -6 to 6
- gain: float32 [2048], replicated, may hold values from 0.1 to 1.9
- lengths: int32 [4], replicated, may hold values from 1 to 4096, 8192 in all
- block_mask: int32 [16, 6], P('ctx'), may hold values 0 or 1
Outputs:
- output: bfloat16 [8192, 2048], P(('ctx', 'head'))
- grad_queries: bfloat16 [8192, 2048], P(('ctx', 'head'))
- grad_keys: bfloat16 [8192, 2048], P(('ctx', 'head'))
- grad_values: bfloat16 [8192, 2048], P(('ctx', 'head'))
The draws below stay inside these ranges and needn't reach their ends.
Inputs may be any that keep to these rules, and one draw needn't show every extreme that they name: The lengths of the 4 packed repertoires in order; they sum to 8192.
All inputs are finite; a program needn't handle non-finite values. No bound on the sum of `block_mask` on one device may be relied on, other than what follows from the above.
Results may differ from the reference program's by a relative error of at most 0.0051.
Values may be sent and summed in bfloat16 or wider, within the bound.
No kernel may reach another device: no remote copies, remote signals or barrier semaphores. Data moves between devices by JAX's collectives and lax.ppermute only.
A program may use at most 64 MiB of HBM per device.

```python
import math
import jax
import jax.numpy as jnp
import numpy as np
from jax import lax

HEADS = 16
DH = 128
GROUP = 512
SEQS = 4
TOKENS = 8192


def with_ends(result, own_key, least, top_value):
    shape = result.shape
    spot = [jax.random.randint(jax.random.fold_in(own_key, axis), (), 0, shape[axis]) for axis in range(len(shape))]
    result = result.at[tuple(spot)].set(least)
    longest = shape.index(max(shape))
    spot[longest] = (spot[longest] + 1) % shape[longest]
    return result.at[tuple(spot)].set(top_value)


def block_scale(stream_key, shape, shards, least, high):
    level, own = 1.0, jax.random.fold_in(stream_key, 6)
    for axis_at, shards_of in shards:
        heights = jnp.exp(jax.random.uniform(jax.random.fold_in(own, axis_at), (shards_of,), jnp.float32, least / len(shards), high / len(shards)))
        level = level * jnp.repeat(heights, shape[axis_at] // shards_of).reshape([-1 if axis == axis_at else 1 for axis in range(len(shape))])
    return level


def profile(count, total, most, slope):
    portions = [(1 << 20) // math.isqrt(standing ** slope) + 1 for standing in range(2, count + 1)]
    rest, counts = total - most - (count - 1), [1] * (count - 1)
    while rest > 0:
        movable = [i for i in range(count - 1) if counts[i] < most]
        mass, remaining = sum([portions[i] for i in movable]), rest
        for i in movable:
            addition = min(most - counts[i], max(1, remaining * portions[i] // mass), rest)
            counts[i] = counts[i] + addition
            rest = rest - addition
    return np.array([most] + counts)


def uneven_parts(rng, number_of, total, reach, skew):
    if number_of == 2:
        one = jax.random.randint(rng, (), max(1, total - reach), min(reach, total - 1) + 1)
        return jnp.stack([one, total - one])
    sizes = jnp.asarray(profile(number_of, total, reach, skew), jnp.int32)
    couples = (number_of - 1) // 2
    source_of, receiver = sizes[1:1 + 2 * couples:2], sizes[2:2 + 2 * couples:2]
    margin = jnp.minimum(source_of - 1, reach - receiver)
    shifted = jax.random.randint(jax.random.fold_in(rng, 1), (couples,), 0, 1 << 20) % (margin + 1)
    sizes = sizes.at[1:1 + 2 * couples:2].set(source_of - shifted).at[2:2 + 2 * couples:2].set(receiver + shifted)
    return sizes[jax.random.permutation(jax.random.fold_in(rng, 2), number_of)]


def noise(own_key, shape, deviation, limit, pieces=(), kind=jnp.bfloat16):
    drawn = jax.random.normal(own_key, shape, jnp.float32) * deviation
    if len(pieces) > 0:
        drawn = block_scale(own_key, shape, pieces, -0.22, 0.18) * drawn
    return jnp.clip(drawn, min=-limit, max=limit).astype(kind)


def setup_inputs(seed: int = 0) -> dict:
    seeds = jax.random.split(jax.random.key(seed), 8)
    queries = noise(seeds[0], (TOKENS, HEADS * DH), 1.0, 6.0, ((0, 32),))
    keys = noise(seeds[1], (TOKENS, HEADS * DH), 1.0, 6.0, ((0, 32),))
    values = noise(seeds[2], (TOKENS, HEADS * DH), 1.0, 6.0, ((0, 32),))
    grad_out = noise(seeds[3], (TOKENS, HEADS * DH), 1.0, 6.0, ((0, 32),))
    gain = jnp.clip(1.0 + 0.18 * jax.random.normal(seeds[4], (HEADS * DH,), jnp.float32), 0.1, 1.9)
    lengths = uneven_parts(seeds[5], SEQS, TOKENS, TOKENS // 2, 2).astype(jnp.int32)
    block_mask = with_ends((jax.random.randint(seeds[6], (TOKENS // GROUP, 6), 0, 2) < 1).astype(jnp.int32), jax.random.fold_in(seeds[6], 1), 0, 1)
    return dict(queries=queries, keys=keys, values=values, grad_out=grad_out, gain=gain, lengths=lengths, block_mask=block_mask)


eps_norm = 1e-06
pair_slots = [-1, -1, -1, -1, 0, -1, -1, -1, 1, 2, -1, -1, 3, 4, 5, -1]

def segment_of(position, bounds):
    return lax.optimization_barrier(jnp.sum((position[..., None] >= bounds).astype(jnp.int32), axis=-1))

def group_weights(mask_row, seg_group):
    full_side = seg_group.shape[0]
    quarter = full_side // 4
    select = (lax.broadcasted_iota(jnp.int32, (6, 16), 0) == jnp.array(pair_slots, dtype=jnp.int32)[None, :]).astype(jnp.float32)
    blocks = jnp.dot(mask_row.astype(jnp.float32), select).reshape(4, 4) + jnp.eye(4, dtype=jnp.float32)
    spread = jnp.broadcast_to(blocks[:, None, :, None], (4, quarter, 4, quarter)).reshape(full_side, full_side)
    row_ids = lax.broadcasted_iota(jnp.int32, (full_side, full_side), 0)
    col_ids = lax.broadcasted_iota(jnp.int32, (full_side, full_side), 1)
    causal = (col_ids <= row_ids).astype(jnp.float32)
    shared = (seg_group[:, None] == seg_group[None, :]).astype(jnp.float32)
    return spread * causal * shared

def as_float(source):
    return source.astype(jnp.float32)

def reference(queries, keys, values, grad_out, gain, lengths, block_mask):
    tok_total, full_width = queries.shape
    head_count = full_width // DH
    group_count = tok_total // GROUP

    def blocked(source):
        return source.reshape(group_count, GROUP, head_count, DH)
    bounds = jnp.cumsum(lengths)[:3].astype(jnp.int32)
    positions = lax.iota(jnp.int32, tok_total).reshape(group_count, GROUP)
    seg_ids = segment_of(positions, bounds)
    seg_before = segment_of(positions[:, 0] - 1, bounds)
    seg_after = segment_of(positions[:, -1] + 1, bounds)
    seg_start = seg_ids[:, 0]
    seg_end = seg_ids[:, -1]
    q_blocks = blocked(queries)
    k_blocks = blocked(keys)
    v_blocks = blocked(values)
    highest = lax.Precision.HIGHEST

    def forward_step(kv_carry, inputs):
        q_part, k_part, v_part, mask_row, seg_group, before_seg, end_seg = inputs
        weights = group_weights(mask_row, seg_group)
        before_mask = (seg_group == before_seg).astype(jnp.float32)
        scores = jnp.einsum('thd,shd->hts', as_float(q_part), as_float(k_part)) * weights[None]
        prob_bf = scores.astype(jnp.bfloat16)
        intra_term = jnp.einsum('hts,shd->thd', as_float(prob_bf), as_float(v_part))
        inter_term = jnp.einsum('thi,hij->thj', as_float(q_part), kv_carry, precision=highest)
        raw_part = (intra_term + inter_term * before_mask[:, None, None]).astype(jnp.bfloat16)
        end_mask = (seg_group == end_seg).astype(jnp.float32)
        update = jnp.einsum('thi,thj->hij', as_float(k_part) * end_mask[:, None, None], as_float(v_part))
        carry_on = (end_seg == before_seg).astype(jnp.float32)
        return (carry_on * kv_carry + update, (raw_part, kv_carry))
    zero_state = jnp.zeros((head_count, DH, DH), jnp.float32)
    _, (raw_blocks, kv_states) = lax.scan(forward_step, zero_state, (q_blocks, k_blocks, v_blocks, block_mask, seg_ids, seg_before, seg_end))
    raw = raw_blocks.reshape(tok_total, full_width)
    raw_float = raw.astype(jnp.float32)
    scale_rms = jnp.sqrt(lax.optimization_barrier(jnp.sum(raw_float * raw_float, axis=1)) / full_width + eps_norm)
    normed = raw_float / scale_rms[:, None]
    output = (normed * gain[None, :]).astype(jnp.bfloat16)
    grad_norm = grad_out.astype(jnp.float32) * gain[None, :]
    cross_mean = lax.optimization_barrier(jnp.sum(grad_norm * normed, axis=1)) / full_width
    grad_raw = ((grad_norm - normed * cross_mean[:, None]) / scale_rms[:, None]).astype(jnp.bfloat16)
    d_blocks = blocked(grad_raw)

    def backward_step(grad_carry, inputs):
        q_part, k_part, v_part, d_part, mask_row, seg_group, before_seg, after_seg, start_seg, kv_state = inputs
        weights = group_weights(mask_row, seg_group)
        before_mask = (seg_group == before_seg).astype(jnp.float32)
        after_mask = (seg_group == after_seg).astype(jnp.float32)
        start_mask = (seg_group == start_seg).astype(jnp.float32)
        prob_bf = (jnp.einsum('thd,shd->hts', as_float(q_part), as_float(k_part)) * weights[None]).astype(jnp.bfloat16)
        grad_probs = (jnp.einsum('thd,shd->hts', as_float(d_part), as_float(v_part)) * weights[None]).astype(jnp.bfloat16)
        grad_q = jnp.einsum('hts,shd->thd', as_float(grad_probs), as_float(k_part)) + jnp.einsum('thj,hij->thi', as_float(d_part), kv_state, precision=highest) * before_mask[:, None, None]
        grad_k = jnp.einsum('hts,thd->shd', as_float(grad_probs), as_float(q_part)) + jnp.einsum('shj,hij->shi', as_float(v_part), grad_carry, precision=highest) * after_mask[:, None, None]
        grad_v = jnp.einsum('hts,thd->shd', as_float(prob_bf), as_float(d_part)) + jnp.einsum('shi,hij->shj', as_float(k_part), grad_carry, precision=highest) * after_mask[:, None, None]
        update = jnp.einsum('thi,thj->hij', as_float(q_part) * start_mask[:, None, None], as_float(d_part))
        carry_on = (start_seg == after_seg).astype(jnp.float32)
        outs_part = (grad_q.astype(jnp.bfloat16), grad_k.astype(jnp.bfloat16), grad_v.astype(jnp.bfloat16))
        return (carry_on * grad_carry + update, outs_part)
    _, (grad_qs, grad_ks, grad_vs) = lax.scan(backward_step, zero_state, (q_blocks, k_blocks, v_blocks, d_blocks, block_mask, seg_ids, seg_before, seg_after, seg_start, kv_states), reverse=True)
    return (output, grad_qs.reshape(tok_total, full_width), grad_ks.reshape(tok_total, full_width), grad_vs.reshape(tok_total, full_width))
```

```python
import functools

import jax
import jax.numpy as jnp
from jax import lax
from jax.experimental import pallas as pl
from jax.experimental.pallas import tpu as pltpu
from jax.sharding import PartitionSpec as P

DH = 128
GROUP = 512
BLOCK = 128
UNROLL = 4

eps_norm = 1e-06
BF = jnp.bfloat16
F32 = jnp.float32
AXES = ("ctx", "head")

NN = (((1,), (0,)), ((), ()))
NT = (((1,), (1,)), ((), ()))
TN = (((0,), (0,)), ((), ()))


def dot(a, b, dims):
    return lax.dot_general(a, b, dims, preferred_element_type=F32)


def bounds_of(len_ref):
    bounds, total = [], None
    for k in range(len_ref.shape[0] - 1):
        total = len_ref[k] if total is None else total + len_ref[k]
        bounds.append(total)
    return bounds


def segment(position, bounds):
    result = (position >= bounds[0]).astype(jnp.int32)
    for bound in bounds[1:]:
        result = result + (position >= bound).astype(jnp.int32)
    return result


def same(a, b):
    return (a == b).astype(F32)


class Place:
    def __init__(self, len_ref, rows, mask_ref=None):
        self.rows = rows
        self.blocks = rows // BLOCK
        self.devices = GROUP // rows
        self.bounds = bounds_of(len_ref)
        spot = lax.axis_index("head")
        index = lax.axis_index("ctx") * lax.axis_size("head") + spot
        self.first = index * rows
        self.part = lax.rem(spot, self.devices)
        self.group = lax.div(spot, self.devices)
        self.group_first = self.first - self.part * rows
        self.mask_ref = mask_ref

    def seg(self, position):
        return segment(position, self.bounds)

    def row_segments(self, block=None):
        count, start = (self.rows, 0) if block is None else (BLOCK, block * BLOCK)
        rows = lax.broadcasted_iota(jnp.int32, (count, 1), 0)
        return self.seg(rows + (self.first + start))

    def pair(self, i, j):
        slot = jnp.clip(lax.div(i * (i - 1), 2) + j, 0, self.mask_ref.shape[1] - 1)
        return self.mask_ref[self.group, slot].astype(F32)

    def weights(self):
        rows = self.rows
        t = lax.broadcasted_iota(jnp.int32, (rows, rows), 0)
        s = lax.broadcasted_iota(jnp.int32, (rows, rows), 1)
        keep = (s <= t) & (self.seg(t + self.first) == self.seg(s + self.first))
        result = jnp.where(keep, 1.0, 0.0)
        for i in range(1, self.blocks):
            for j in range(i):
                bit = self.pair(self.part * self.blocks + i, self.part * self.blocks + j)
                inside = (
                    (t >= i * BLOCK)
                    & (t < (i + 1) * BLOCK)
                    & (s >= j * BLOCK)
                    & (s < (j + 1) * BLOCK)
                )
                result = jnp.where(inside, result * bit, result)
        return result

    def before(self, block):
        own = self.part * self.blocks + block
        edge = self.seg(self.first + block * BLOCK - 1)
        carried = same(self.seg(self.group_first - 1), edge)
        peers = []
        for away in range(1, self.devices):
            there = (self.part >= away).astype(F32)
            for j in range(self.blocks):
                other = (self.part - away) * self.blocks + j
                last = self.first - away * self.rows + (j + 1) * BLOCK - 1
                peers.append(self.pair(own, other) * same(self.seg(last), edge) * there)
        reach = self.row_segments(block) == edge
        return carried, peers, reach

    def after(self, block):
        own = self.part * self.blocks + block
        edge = self.seg(self.first + (block + 1) * BLOCK)
        carried = same(self.seg(self.group_first + GROUP), edge)
        peers = []
        for away in range(1, self.devices):
            there = (self.part + away < self.devices).astype(F32)
            for i in range(self.blocks):
                other = (self.part + away) * self.blocks + i
                start = self.first + away * self.rows + i * BLOCK
                peers.append(self.pair(other, own) * same(self.seg(start), edge) * there)
        reach = self.row_segments(block) == edge
        return carried, peers, reach


def mixed(state_ref, peer_refs, factors, blocks, head):
    carried, peers, _ = factors
    total = state_ref[head].astype(F32) * carried
    for at, factor in enumerate(peers):
        total = total + peer_refs[at // blocks][at % blocks, head].astype(F32) * factor
    return total.astype(BF)


def columns(head):
    return pl.ds(pl.multiple_of(head * DH, DH), DH)


def each_head(heads, body, carry=()):
    step = UNROLL if heads % UNROLL == 0 else 1

    def some(turn, carry):
        for k in range(step):
            carry = body(turn * step + k, carry)
        return carry

    return lax.fori_loop(0, heads // step, some, carry)


def rows_of(block):
    return pl.ds(block * BLOCK, BLOCK)


def state_kernel(len_ref, k_ref, v_ref, u_ref, t_ref):
    rows, width = k_ref.shape
    place = Place(len_ref, rows)
    last = place.seg(place.first + rows - 1)
    ends = [place.seg(place.first + (b + 1) * BLOCK - 1) for b in range(place.blocks)]
    masks = [(place.row_segments(b) == ends[b]).astype(BF) for b in range(place.blocks)]
    into = [same(e, last) for e in ends]

    def one(head, carry):
        total = jnp.zeros((DH, DH), F32)
        for b in range(place.blocks):
            k = k_ref[rows_of(b), columns(head)] * masks[b]
            update = dot(k, v_ref[rows_of(b), columns(head)], TN)
            u_ref[b, head] = update.astype(BF)
            total = total + update * into[b]
        t_ref[head] = total.astype(BF)
        return carry

    each_head(width // DH, one)


def inner_kernel(len_ref, mask_ref, q_ref, k_ref, v_ref, raw_ref, weight_ref):
    rows, width = q_ref.shape
    weight_ref[...] = Place(len_ref, rows, mask_ref).weights()

    def one(head, carry):
        at = columns(head)
        probs = (dot(q_ref[:, at], k_ref[:, at], NT) * weight_ref[...]).astype(BF)
        raw_ref[:, at] = dot(probs, v_ref[:, at], NN)
        return carry

    each_head(width // DH, one)


def scan_kernel(len_ref, t_ref, out_ref, *, rows, backward):
    count = t_ref.shape[0]
    devices = GROUP // rows
    bounds = bounds_of(len_ref)

    def one(turn, acc):
        group = count // devices - 1 - turn if backward else turn
        for k in range(devices):
            out_ref[group * devices + k] = acc.astype(BF)
        for k in range(devices):
            index = group * devices + (devices - 1 - k if backward else k)
            first = index * rows
            if backward:
                keep = same(segment(first, bounds), segment(first + rows, bounds))
            else:
                keep = same(segment(first - 1, bounds), segment(first + rows - 1, bounds))
            acc = acc * keep + t_ref[index].astype(F32)
        return acc

    lax.fori_loop(0, count // devices, one, jnp.zeros(t_ref.shape[1:], F32))


def norm_kernel(len_ref, mask_ref, gain_ref, q_ref, raw_ref, grad_ref, kv_ref, *rest, peers):
    peer_refs, (out_ref, d_ref, w_ref, t_ref, held_ref) = rest[:peers], rest[peers:]
    rows, width = q_ref.shape
    heads = width // DH
    place = Place(len_ref, rows, mask_ref)
    starts = [place.seg(place.first + b * BLOCK) for b in range(place.blocks)]
    into = [same(s, starts[0]) for s in starts]
    for b in range(place.blocks):
        factors = place.before(b)
        reach = factors[2].astype(F32)
        begin = (place.row_segments(b) == starts[b]).astype(BF)
        at_rows = rows_of(b)

        def add_up(head, carry):
            squares, cross = carry
            at = columns(head)
            state = mixed(kv_ref, peer_refs, factors, place.blocks, head)
            raw = raw_ref[at_rows, at] + dot(q_ref[at_rows, at], state, NN) * reach
            raw = raw.astype(BF)
            held_ref[at_rows, at] = raw
            raw = raw.astype(F32)
            scaled = grad_ref[at_rows, at].astype(F32) * gain_ref[:, at]
            return squares + raw * raw, cross + scaled * raw

        zero = jnp.zeros((BLOCK, DH), F32)
        squares, cross = each_head(heads, add_up, (zero, zero))
        rms = jnp.sqrt(jnp.sum(squares, axis=1, keepdims=True) / width + eps_norm)
        inverse = 1.0 / rms
        cross = jnp.sum(cross, axis=1, keepdims=True) * inverse / width

        def give(head, carry):
            at = columns(head)
            gain = gain_ref[:, at]
            normed = held_ref[at_rows, at].astype(F32) * inverse
            out_ref[at_rows, at] = (normed * gain).astype(BF)
            scaled = grad_ref[at_rows, at].astype(F32) * gain
            grad = ((scaled - normed * cross) * inverse).astype(BF)
            d_ref[at_rows, at] = grad
            update = dot(q_ref[at_rows, at] * begin, grad, TN)
            w_ref[b, head] = update.astype(BF)
            if b == 0:
                held = update
            else:
                held = t_ref[head].astype(F32) + update * into[b]
            t_ref[head] = held.astype(t_ref.dtype)
            return carry

        each_head(heads, give)


def grads_kernel(len_ref, mask_ref, q_ref, k_ref, v_ref, d_ref, kv_ref, *rest, peers):
    peer_refs, (gq_ref, gk_ref, gv_ref, weight_ref) = rest[:peers], rest[peers:]
    rows, width = q_ref.shape
    place = Place(len_ref, rows, mask_ref)
    weight_ref[...] = place.weights()
    factors = [place.before(b) for b in range(place.blocks)]

    def one(head, carry):
        at = columns(head)
        q, k, v, d = q_ref[:, at], k_ref[:, at], v_ref[:, at], d_ref[:, at]
        probs = (dot(q, k, NT) * weight_ref[...]).astype(BF)
        grad_probs = (dot(d, v, NT) * weight_ref[...]).astype(BF)
        inner = dot(grad_probs, k, NN)
        for b in range(place.blocks):
            state = mixed(kv_ref, peer_refs, factors[b], place.blocks, head)
            outer = dot(d_ref[rows_of(b), at], state, NT) * factors[b][2].astype(F32)
            part = inner[b * BLOCK : (b + 1) * BLOCK] + outer
            gq_ref[rows_of(b), at] = part.astype(BF)
        gk_ref[:, at] = dot(grad_probs, q, TN)
        gv_ref[:, at] = dot(probs, d, TN)
        return carry

    each_head(width // DH, one)


def last_kernel(len_ref, mask_ref, k_ref, v_ref, gk_in, gv_in, gs_ref, *rest, peers):
    peer_refs, (gk_ref, gv_ref) = rest[:peers], rest[peers:]
    rows, width = k_ref.shape
    place = Place(len_ref, rows, mask_ref)
    factors = [place.after(b) for b in range(place.blocks)]

    def one(head, carry):
        at = columns(head)
        for b in range(place.blocks):
            at_rows = rows_of(b)
            state = mixed(gs_ref, peer_refs, factors[b], place.blocks, head)
            reach = factors[b][2].astype(F32)
            gk = gk_in[at_rows, at] + dot(v_ref[at_rows, at], state, NT) * reach
            gv = gv_in[at_rows, at] + dot(k_ref[at_rows, at], state, NN) * reach
            gk_ref[at_rows, at] = gk.astype(BF)
            gv_ref[at_rows, at] = gv.astype(BF)
        return carry

    each_head(width // DH, one)


SMEM = pl.BlockSpec(memory_space=pltpu.SMEM)
VMEM = pl.BlockSpec(memory_space=pltpu.VMEM)


def call(kernel, name, scalars, arrays, outs, scratch=(), flops=0):
    moved = sum(a.size * a.dtype.itemsize for a in arrays)
    moved += sum(o.size * o.dtype.itemsize for o in outs)
    single = len(outs) == 1
    return pl.pallas_call(
        kernel,
        name=name,
        in_specs=[SMEM] * len(scalars) + [VMEM] * len(arrays),
        out_specs=VMEM if single else [VMEM] * len(outs),
        out_shape=outs[0] if single else outs,
        scratch_shapes=scratch,
        compiler_params=pltpu.CompilerParams(vmem_limit_bytes=32 * 1024 * 1024),
        cost_estimate=pl.CostEstimate(flops=flops, bytes_accessed=moved, transcendentals=0),
    )(*scalars, *arrays)


def local(queries, keys, values, grad_out, gain, lengths, block_mask):
    rows, width = queries.shape
    heads = width // DH
    blocks = rows // BLOCK
    devices = GROUP // rows
    head_count = lax.axis_size("head")
    total = lax.axis_size("ctx") * head_count
    shape = jax.ShapeDtypeStruct
    state = shape((heads, DH, DH), BF)
    block_states = shape((blocks, heads, DH, DH), BF)
    tokens = shape((rows, width), BF)
    partial = shape((rows, width), F32)
    square = [pltpu.VMEM((rows, rows), F32)]
    unit = 2 * rows * width * DH
    inner = 2 * rows * rows * width

    def to_peers(states, backward):
        result = []
        for away in range(1, devices):
            pairs = [
                (z, z + away) for z in range(head_count - away) if z % devices + away < devices
            ]
            if backward:
                pairs = [(b, a) for a, b in pairs]
            result.append(lax.ppermute(states, "head", pairs))
        return result

    def scanned(sums, backward):
        slices = sums.reshape(total, heads * DH // total, DH)
        slices = lax.all_to_all(slices, AXES, split_axis=0, concat_axis=0, tiled=True)
        kernel = functools.partial(scan_kernel, rows=rows, backward=backward)
        slices = call(
            kernel, "scan", [lengths], [slices], [shape(slices.shape, BF)]
        )
        slices = lax.all_to_all(slices, AXES, split_axis=0, concat_axis=0, tiled=True)
        return slices.reshape(heads, DH, DH)

    gain_row = gain.reshape(1, width)
    block_kv, sum_kv = call(
        state_kernel, "states", [lengths], [keys, values], [block_states, state], flops=unit
    )
    kv_state = scanned(sum_kv, False)
    peer_kv = to_peers(block_kv, False)
    raw_inner = call(
        inner_kernel,
        "inner",
        [lengths, block_mask],
        [queries, keys, values],
        [partial],
        square,
        flops=2 * inner,
    )
    peers = len(peer_kv)
    output, grad_raw, block_grad, sum_grad = call(
        functools.partial(norm_kernel, peers=peers),
        "norm",
        [lengths, block_mask],
        [gain_row, queries, raw_inner, grad_out, kv_state, *peer_kv],
        [tokens, tokens, block_states, state],
        [pltpu.VMEM((rows, width), BF)],
        flops=2 * unit,
    )
    grad_state = scanned(sum_grad, True)
    peer_grad = to_peers(block_grad, True)
    grad_q, part_k, part_v = call(
        functools.partial(grads_kernel, peers=peers),
        "grads",
        [lengths, block_mask],
        [queries, keys, values, grad_raw, kv_state, *peer_kv],
        [tokens, partial, partial],
        square,
        flops=5 * inner + unit,
    )
    grad_k, grad_v = call(
        functools.partial(last_kernel, peers=peers),
        "last",
        [lengths, block_mask],
        [keys, values, part_k, part_v, grad_state, *peer_grad],
        [tokens, tokens],
        flops=2 * unit,
    )
    return output, grad_q, grad_k, grad_v


def solution(mesh):
    tokens = P(AXES, None)
    return jax.shard_map(
        local,
        mesh=mesh,
        in_specs=(tokens, tokens, tokens, tokens, P(), P(), P("ctx", None)),
        out_specs=(tokens, tokens, tokens, tokens),
        check_vma=False,
    )
```

```python
import functools

import jax
import jax.numpy as jnp
from jax import lax
from jax.experimental import pallas as pl
from jax.experimental.pallas import tpu as pltpu
from jax.sharding import PartitionSpec as P

DH = 128
GROUP = 512
BLOCK = 128
HEADS_AT_ONCE = 4

eps_norm = 1e-06
BF = jnp.bfloat16
F32 = jnp.float32
AXES = ("ctx", "head")

NN = (((1,), (0,)), ((), ()))
NT = (((1,), (1,)), ((), ()))
TN = (((0,), (0,)), ((), ()))


def dot(a, b, dims):
    return lax.dot_general(a, b, dims, preferred_element_type=F32)


def bounds_of(len_ref):
    bounds, total = [], None
    for k in range(len_ref.shape[0] - 1):
        total = len_ref[k] if total is None else total + len_ref[k]
        bounds.append(total)
    return bounds


def segment(position, bounds):
    result = (position >= bounds[0]).astype(jnp.int32)
    for bound in bounds[1:]:
        result = result + (position >= bound).astype(jnp.int32)
    return result


def same(a, b):
    return (a == b).astype(F32)


class Place:
    def __init__(self, len_ref, rows, mask_ref=None):
        self.rows = rows
        self.blocks = rows // BLOCK
        self.devices = GROUP // rows
        self.bounds = bounds_of(len_ref)
        spot = lax.axis_index("head")
        index = lax.axis_index("ctx") * lax.axis_size("head") + spot
        self.first = index * rows
        self.part = lax.rem(spot, self.devices)
        self.group = lax.div(spot, self.devices)
        self.group_first = self.first - self.part * rows
        self.mask_ref = mask_ref

    def seg(self, position):
        return segment(position, self.bounds)

    def start(self, block):
        return self.first + block * BLOCK

    def row_segments(self, block):
        rows = lax.broadcasted_iota(jnp.int32, (BLOCK, 1), 0)
        return self.seg(rows + self.start(block))

    def pair(self, i, j):
        slot = jnp.clip(lax.div(i * (i - 1), 2) + j, 0, self.mask_ref.shape[1] - 1)
        return self.mask_ref[self.group, slot].astype(F32)

    def weights(self):
        rows = self.rows
        t = lax.broadcasted_iota(jnp.int32, (rows, rows), 0)
        s = lax.broadcasted_iota(jnp.int32, (rows, rows), 1)
        keep = (s <= t) & (self.seg(t + self.first) == self.seg(s + self.first))
        result = jnp.where(keep, 1.0, 0.0)
        for i in range(1, self.blocks):
            for j in range(i):
                bit = self.pair(self.part * self.blocks + i, self.part * self.blocks + j)
                inside = (
                    (t >= i * BLOCK)
                    & (t < (i + 1) * BLOCK)
                    & (s >= j * BLOCK)
                    & (s < (j + 1) * BLOCK)
                )
                result = jnp.where(inside, result * bit, result)
        return result

    def to_later(self, away, block):
        there = (self.part + away) * self.blocks + block
        edge = self.seg(self.start(block) + away * self.rows - 1)
        return [
            self.pair(there, self.part * self.blocks + j) * same(self.seg(self.start(j + 1) - 1), edge)
            for j in range(self.blocks)
        ]

    def before(self, block):
        edge = self.seg(self.start(block) - 1)
        carried = same(self.seg(self.group_first - 1), edge)
        peers = [(self.part >= away).astype(F32) for away in range(1, self.devices)]
        return carried, peers, (self.row_segments(block) == edge).astype(F32)

    def after(self, block):
        own = self.part * self.blocks + block
        edge = self.seg(self.start(block + 1))
        carried = same(self.seg(self.group_first + GROUP), edge)
        peers = []
        for i in range(self.blocks):
            for away in range(1, self.devices):
                there = (self.part + away < self.devices).astype(F32)
                other = (self.part + away) * self.blocks + i
                start = self.start(i) + away * self.rows
                peers.append(self.pair(other, own) * same(self.seg(start), edge) * there)
        return carried, peers, (self.row_segments(block) == edge).astype(F32)


def mixed(state_ref, peer_refs, factors, head):
    carried, peers, _ = factors
    total = state_ref[head].astype(F32) * carried
    for ref, factor in zip(peer_refs, peers, strict=True):
        total = total + ref[head].astype(F32) * factor
    return total.astype(BF)


def columns(head):
    return pl.ds(head * DH, DH)


def rows_of(block):
    return pl.ds(block * BLOCK, BLOCK)


def state_kernel(len_ref, mask_ref, k_ref, v_ref, t_ref, *x_refs):
    rows, width = k_ref.shape
    place = Place(len_ref, rows, mask_ref)
    last = place.seg(place.start(place.blocks) - 1)
    ends = [place.seg(place.start(b + 1) - 1) for b in range(place.blocks)]
    masks = [(place.row_segments(b) == ends[b]).astype(BF) for b in range(place.blocks)]
    wanted = [[same(e, last) for e in ends]]
    for b in range(place.blocks):
        for away in range(1, place.devices):
            wanted.append(place.to_later(away, b))
    for head in range(width // DH):
        updates = []
        for b in range(place.blocks):
            k = k_ref[rows_of(b), columns(head)] * masks[b]
            updates.append(dot(k, v_ref[rows_of(b), columns(head)], TN))
        for ref, factors in zip((t_ref, *x_refs), wanted, strict=True):
            total = updates[0] * factors[0]
            for update, factor in zip(updates[1:], factors[1:], strict=True):
                total = total + update * factor
            ref[head] = total.astype(BF)


def inner_kernel(len_ref, mask_ref, q_ref, k_ref, v_ref, raw_ref, weight_ref):
    rows, width = q_ref.shape

    @pl.when(pl.program_id(0) == 0)
    def _():
        weight_ref[...] = Place(len_ref, rows, mask_ref).weights()

    for head in range(width // DH):
        at = columns(head)
        probs = (dot(q_ref[:, at], k_ref[:, at], NT) * weight_ref[...]).astype(BF)
        raw_ref[:, at] = dot(probs, v_ref[:, at], NN)


def scan_kernel(len_ref, t_ref, out_ref, *, rows, backward):
    count = t_ref.shape[0]
    devices = GROUP // rows
    bounds = bounds_of(len_ref)

    def one(turn, acc):
        group = count // devices - 1 - turn if backward else turn
        for k in range(devices):
            out_ref[group * devices + k] = acc.astype(BF)
        for k in range(devices):
            index = group * devices + (devices - 1 - k if backward else k)
            first = index * rows
            if backward:
                keep = same(segment(first, bounds), segment(first + rows, bounds))
            else:
                keep = same(segment(first - 1, bounds), segment(first + rows - 1, bounds))
            acc = acc * keep + t_ref[index].astype(F32)
        return acc

    lax.fori_loop(0, count // devices, one, jnp.zeros(t_ref.shape[1:], F32))


def norm_kernel(len_ref, mask_ref, gain_ref, q_ref, raw_ref, grad_ref, kv_ref, *rest, rows, block, peers):
    peer_refs, rest = rest[:peers], rest[peers:]
    earlier_refs, rest = rest[:block], rest[block:]
    scale_ref, held_out_ref, d_ref, w_ref = rest[:4]
    held_ref, squares_ref, cross_ref = rest[-3:]
    width = q_ref.shape[1]
    heads = width // DH
    chunk = pl.program_id(1)
    chunks = pl.num_programs(1)
    place = Place(len_ref, rows, mask_ref)

    @pl.when(pl.program_id(0) == 0)
    def _():
        factors = place.before(block)
        squares = cross = None
        for head in range(heads):
            at = columns(head)
            state = mixed(kv_ref, peer_refs, factors, head)
            raw = raw_ref[:, at] + dot(q_ref[:, at], state, NN) * factors[2]
            raw = raw.astype(BF)
            held_ref[chunk, :, at] = raw
            held_out_ref[:, at] = raw
            raw = raw.astype(F32)
            scaled = grad_ref[:, at].astype(F32) * gain_ref[:, at]
            squares = raw * raw if head == 0 else squares + raw * raw
            cross = scaled * raw if head == 0 else cross + scaled * raw
        fresh = chunk == 0
        squares = squares + jnp.where(fresh, 0.0, squares_ref[...])
        cross = cross + jnp.where(fresh, 0.0, cross_ref[...])
        squares_ref[...] = squares
        cross_ref[...] = cross

        @pl.when(chunk == chunks - 1)
        def _():
            full = width * chunks
            total = jnp.sum(squares, axis=1, keepdims=True)
            inverse = 1.0 / jnp.sqrt(total / full + eps_norm)
            mean = jnp.sum(cross, axis=1, keepdims=True) * inverse / full
            squares_ref[...] = jnp.broadcast_to(inverse, squares_ref.shape)
            cross_ref[...] = jnp.broadcast_to(mean, cross_ref.shape)
            scale_ref[...] = squares_ref[...]

    @pl.when(pl.program_id(0) == 1)
    def _():
        inverse, mean = squares_ref[...], cross_ref[...]
        own = place.seg(place.start(block))
        begin = (place.row_segments(block) == own).astype(BF)
        into = [same(place.seg(place.start(b)), place.seg(place.first)) for b in range(block + 1)]
        for head in range(heads):
            at = columns(head)
            normed = held_ref[chunk, :, at].astype(F32) * inverse
            scaled = grad_ref[:, at].astype(F32) * gain_ref[:, at]
            grad = ((scaled - normed * mean) * inverse).astype(BF)
            d_ref[:, at] = grad
            update = dot(q_ref[:, at] * begin, grad, TN)
            w_ref[head] = update.astype(BF)
            if len(rest) > 7:
                total = update * into[block]
                for ref, factor in zip(earlier_refs, into[:block], strict=True):
                    total = total + ref[head].astype(F32) * factor
                rest[4][head] = total.astype(BF)


def grads_kernel(len_ref, mask_ref, gain_ref, q_ref, k_ref, v_ref, kv_ref, *rest, blocks, peers):
    ins = 3 * blocks + blocks * peers
    d_refs, raw_refs, scale_refs = rest[:blocks], rest[blocks : 2 * blocks], rest[2 * blocks : 3 * blocks]
    peer_refs = rest[3 * blocks : ins]
    out_ref, gq_ref, gk_ref, gv_ref, weight_ref = rest[ins:]
    rows, width = q_ref.shape
    place = Place(len_ref, rows, mask_ref)

    @pl.when(pl.program_id(0) == 0)
    def _():
        weight_ref[...] = place.weights()

    factors = [place.before(b) for b in range(blocks)]
    for head in range(width // DH):
        at = columns(head)
        q, k, v = q_ref[:, at], k_ref[:, at], v_ref[:, at]
        d = jnp.concatenate([ref[:, at] for ref in d_refs], axis=0)
        probs = (dot(q, k, NT) * weight_ref[...]).astype(BF)
        grad_probs = (dot(d, v, NT) * weight_ref[...]).astype(BF)
        inner = dot(grad_probs, k, NN)
        for b in range(blocks):
            state = mixed(kv_ref, peer_refs[b * peers : (b + 1) * peers], factors[b], head)
            outer = dot(d_refs[b][:, at], state, NT) * factors[b][2]
            part = inner[b * BLOCK : (b + 1) * BLOCK] + outer
            gq_ref[rows_of(b), at] = part.astype(BF)
            normed = raw_refs[b][:, at].astype(F32) * scale_refs[b][...]
            out_ref[rows_of(b), at] = (normed * gain_ref[:, at]).astype(BF)
        gk_ref[:, at] = dot(grad_probs, q, TN)
        gv_ref[:, at] = dot(probs, d, TN)


def last_kernel(len_ref, mask_ref, k_ref, v_ref, gk_in, gv_in, gs_ref, *rest):
    peer_refs, (gk_ref, gv_ref) = rest[:-2], rest[-2:]
    rows, width = k_ref.shape
    place = Place(len_ref, rows, mask_ref)
    factors = [place.after(b) for b in range(place.blocks)]
    for head in range(width // DH):
        at = columns(head)
        for b in range(place.blocks):
            at_rows = rows_of(b)
            state = mixed(gs_ref, peer_refs, factors[b], head)
            reach = factors[b][2]
            gk = gk_in[at_rows, at] + dot(v_ref[at_rows, at], state, NT) * reach
            gv = gv_in[at_rows, at] + dot(k_ref[at_rows, at], state, NN) * reach
            gk_ref[at_rows, at] = gk.astype(BF)
            gv_ref[at_rows, at] = gv.astype(BF)


SMEM = pl.BlockSpec(memory_space=pltpu.SMEM)


def call(kernel, name, grid, scalars, arrays, outs, scratch=(), flops=0):
    moved = sum(a.size * a.dtype.itemsize for a, _ in (*arrays, *outs))
    return pl.pallas_call(
        kernel,
        name=name,
        grid=grid,
        in_specs=[SMEM] * len(scalars) + [spec for _, spec in arrays],
        out_specs=[spec for _, spec in outs],
        out_shape=[shape for shape, _ in outs],
        scratch_shapes=scratch,
        compiler_params=pltpu.CompilerParams(vmem_limit_bytes=48 * 1024 * 1024),
        cost_estimate=pl.CostEstimate(flops=flops, bytes_accessed=moved, transcendentals=0),
    )(*scalars, *[a for a, _ in arrays])


def local(queries, keys, values, grad_out, gain, lengths, block_mask):
    rows, width = queries.shape
    heads = width // DH
    blocks = rows // BLOCK
    devices = GROUP // rows
    peers = devices - 1
    head_count = lax.axis_size("head")
    total = lax.axis_size("ctx") * head_count
    shape = jax.ShapeDtypeStruct
    state = shape((heads, DH, DH), BF)
    tokens = shape((rows, width), BF)
    partial = shape((rows, width), F32)
    block_tokens = shape((BLOCK, width), BF)
    square = [pltpu.VMEM((rows, rows), F32)]
    unit = 2 * rows * width * DH
    inner = 2 * rows * rows * width
    scalars = [lengths, block_mask]
    group_heads = HEADS_AT_ONCE if heads % HEADS_AT_ONCE == 0 else heads
    chunks = heads // group_heads
    span = group_heads * DH

    wide = pl.BlockSpec((rows, span), lambda c: (0, c))
    block_wide = pl.BlockSpec((BLOCK, span), lambda c: (0, c))
    state_part = pl.BlockSpec((group_heads, DH, DH), lambda c: (c, 0, 0))
    gain_part = pl.BlockSpec((1, span), lambda c: (0, c))
    scale_whole = pl.BlockSpec((BLOCK, DH), lambda c: (0, 0))

    def to_peers(states, away, backward):
        pairs = [(z, z + away) for z in range(head_count - away) if z % devices + away < devices]
        if backward:
            pairs = [(b, a) for a, b in pairs]
        return lax.ppermute(states, "head", pairs)

    def scanned(sums, backward):
        height = heads * DH // total
        slices = sums.reshape(total, height, DH)
        slices = lax.all_to_all(slices, AXES, split_axis=0, concat_axis=0, tiled=True)
        part = 16 if height % 16 == 0 else height
        spec = pl.BlockSpec((total, part, DH), lambda c: (0, c, 0))
        (slices,) = call(
            functools.partial(scan_kernel, rows=rows, backward=backward),
            "scan",
            (height // part,),
            [lengths],
            [(slices, spec)],
            [(shape(slices.shape, BF), spec)],
        )
        slices = lax.all_to_all(slices, AXES, split_axis=0, concat_axis=0, tiled=True)
        return slices.reshape(heads, DH, DH)

    gain_row = gain.reshape(1, width)
    sum_kv, *later = call(
        state_kernel,
        "states",
        (chunks,),
        scalars,
        [(keys, wide), (values, wide)],
        [(state, state_part)] * (1 + blocks * peers),
        flops=unit,
    )
    kv_state = scanned(sum_kv, False)
    from_peers = [to_peers(x, 1 + at % peers, False) for at, x in enumerate(later)]
    (raw_inner,) = call(
        inner_kernel,
        "inner",
        (chunks,),
        scalars,
        [(queries, wide), (keys, wide), (values, wide)],
        [(partial, wide)],
        square,
        flops=2 * inner,
    )

    def norm(block, own_peers, earlier):
        first = lambda p, c: c * (1 - p) + (chunks - 1) * p
        second = lambda p, c: c * p
        both_rows = pl.BlockSpec((BLOCK, span), lambda p, c: (block, c))
        first_rows = pl.BlockSpec((BLOCK, span), lambda p, c: (block, first(p, c)))
        first_block = pl.BlockSpec((BLOCK, span), lambda p, c: (0, first(p, c)))
        second_block = pl.BlockSpec((BLOCK, span), lambda p, c: (0, second(p, c)))
        first_state = pl.BlockSpec((group_heads, DH, DH), lambda p, c: (first(p, c), 0, 0))
        second_state = pl.BlockSpec((group_heads, DH, DH), lambda p, c: (second(p, c), 0, 0))
        ends = [(state, second_state)] if block == blocks - 1 and blocks > 1 else []
        return call(
            functools.partial(norm_kernel, rows=rows, block=block, peers=peers),
            "norm",
            (2, chunks),
            scalars,
            [
                (gain_row, pl.BlockSpec((1, span), lambda p, c: (0, c))),
                (queries, both_rows),
                (raw_inner, first_rows),
                (grad_out, both_rows),
                (kv_state, first_state),
                *[(x, first_state) for x in own_peers],
                *[(w, second_state) for w in earlier],
            ],
            [
                (shape((BLOCK, DH), F32), pl.BlockSpec((BLOCK, DH), lambda p, c: (0, 0))),
                (block_tokens, first_block),
                (block_tokens, second_block),
                (state, second_state),
                *ends,
            ],
            [
                pltpu.VMEM((chunks, BLOCK, span), BF),
                pltpu.VMEM((BLOCK, DH), F32),
                pltpu.VMEM((BLOCK, DH), F32),
            ],
            flops=2 * unit // blocks,
        )

    scales, raws, grads, updates, back = [], [], [], [], []
    for b in range(blocks):
        scale, raw, grad, update, *ends = norm(b, from_peers[b * peers : (b + 1) * peers], updates)
        scales.append(scale)
        raws.append(raw)
        grads.append(grad)
        updates.append(update)
        back += [to_peers(update, away, True) for away in range(1, devices)]
    grad_state = scanned(ends[0] if ends else updates[0], True)
    output, grad_q, part_k, part_v = call(
        functools.partial(grads_kernel, blocks=blocks, peers=peers),
        "grads",
        (chunks,),
        scalars,
        [
            (gain_row, gain_part),
            (queries, wide),
            (keys, wide),
            (values, wide),
            (kv_state, state_part),
            *[(d, block_wide) for d in grads],
            *[(r, block_wide) for r in raws],
            *[(s, scale_whole) for s in scales],
            *[(x, state_part) for x in from_peers],
        ],
        [(tokens, wide), (tokens, wide), (partial, wide), (partial, wide)],
        square,
        flops=5 * inner + unit,
    )
    grad_k, grad_v = call(
        last_kernel,
        "last",
        (chunks,),
        scalars,
        [
            (keys, wide),
            (values, wide),
            (part_k, wide),
            (part_v, wide),
            (grad_state, state_part),
            *[(w, state_part) for w in back],
        ],
        [(tokens, wide), (tokens, wide)],
        flops=2 * unit,
    )
    return output, grad_q, grad_k, grad_v


def solution(mesh):
    tokens = P(AXES, None)
    return jax.shard_map(
        local,
        mesh=mesh,
        in_specs=(tokens, tokens, tokens, tokens, P(), P(), P("ctx", None)),
        out_specs=(tokens, tokens, tokens, tokens),
        check_vma=False,
    )
```

```python
import functools

import jax
import jax.numpy as jnp
from jax import lax
from jax.experimental import pallas as pl
from jax.experimental.pallas import tpu as pltpu
from jax.sharding import PartitionSpec as P

DH = 128
GROUP = 512
BLOCK = 128
CHUNKS = 4
VMEM_BYTES = 60 * 1024 * 1024

eps_norm = 1e-06
BF = jnp.bfloat16
F32 = jnp.float32
AXES = ("ctx", "head")

NN = (((1,), (0,)), ((), ()))
NT = (((1,), (1,)), ((), ()))
TN = (((0,), (0,)), ((), ()))


def dot(a, b, dims):
    return lax.dot_general(a, b, dims, preferred_element_type=F32)


def bounds_of(len_ref):
    bounds, total = [], None
    for k in range(len_ref.shape[0] - 1):
        total = len_ref[k] if total is None else total + len_ref[k]
        bounds.append(total)
    return bounds


def segment(position, bounds):
    result = (position >= bounds[0]).astype(jnp.int32)
    for bound in bounds[1:]:
        result = result + (position >= bound).astype(jnp.int32)
    return result


def same(a, b):
    return (a == b).astype(F32)


class Place:
    def __init__(self, len_ref, rows, mask_ref=None):
        self.rows = rows
        self.blocks = rows // BLOCK
        self.devices = GROUP // rows
        self.bounds = bounds_of(len_ref)
        spot = lax.axis_index("head")
        index = lax.axis_index("ctx") * lax.axis_size("head") + spot
        self.first = index * rows
        self.part = lax.rem(spot, self.devices)
        self.group = lax.div(spot, self.devices)
        self.group_first = self.first - self.part * rows
        self.mask_ref = mask_ref

    def seg(self, position):
        return segment(position, self.bounds)

    def start(self, block):
        return self.first + block * BLOCK

    def row_segments(self, block):
        rows = lax.broadcasted_iota(jnp.int32, (BLOCK, 1), 0)
        return self.seg(rows + self.start(block))

    def pair(self, i, j):
        slot = jnp.clip(lax.div(i * (i - 1), 2) + j, 0, self.mask_ref.shape[1] - 1)
        return self.mask_ref[self.group, slot].astype(F32)

    def weights(self):
        rows = self.rows
        t = lax.broadcasted_iota(jnp.int32, (rows, rows), 0)
        s = lax.broadcasted_iota(jnp.int32, (rows, rows), 1)
        keep = (s <= t) & (self.seg(t + self.first) == self.seg(s + self.first))
        result = jnp.where(keep, 1.0, 0.0)
        for i in range(1, self.blocks):
            for j in range(i):
                bit = self.pair(self.part * self.blocks + i, self.part * self.blocks + j)
                inside = (
                    (t >= i * BLOCK)
                    & (t < (i + 1) * BLOCK)
                    & (s >= j * BLOCK)
                    & (s < (j + 1) * BLOCK)
                )
                result = jnp.where(inside, result * bit, result)
        return result

    def to_later(self, away, block):
        there = (self.part + away) * self.blocks + block
        edge = self.seg(self.start(block) + away * self.rows - 1)
        return [
            self.pair(there, self.part * self.blocks + j) * same(self.seg(self.start(j + 1) - 1), edge)
            for j in range(self.blocks)
        ]

    def before(self, block):
        edge = self.seg(self.start(block) - 1)
        carried = same(self.seg(self.group_first - 1), edge)
        peers = [(self.part >= away).astype(F32) for away in range(1, self.devices)]
        return carried, peers, (self.row_segments(block) == edge).astype(F32)

    def after(self, block):
        own = self.part * self.blocks + block
        edge = self.seg(self.start(block + 1))
        carried = same(self.seg(self.group_first + GROUP), edge)
        peers = []
        for i in range(self.blocks):
            for away in range(1, self.devices):
                there = (self.part + away < self.devices).astype(F32)
                other = (self.part + away) * self.blocks + i
                start = self.start(i) + away * self.rows
                peers.append(self.pair(other, own) * same(self.seg(start), edge) * there)
        return carried, peers, (self.row_segments(block) == edge).astype(F32)


def mixed(state_ref, peer_refs, factors, head):
    carried, peers, _ = factors
    total = state_ref[head].astype(F32) * carried
    for ref, factor in zip(peer_refs, peers, strict=True):
        total = total + ref[head].astype(F32) * factor
    return total.astype(BF)


def columns(head):
    return pl.ds(head * DH, DH)


def rows_of(block):
    return pl.ds(block * BLOCK, BLOCK)


def state_body(place_of, ins, outs, scratch, arrive, leave, chunks):
    k_ref, v_ref = ins
    rows, width = k_ref.shape
    place = place_of(rows)
    last = place.seg(place.start(place.blocks) - 1)
    ends = [place.seg(place.start(b + 1) - 1) for b in range(place.blocks)]
    masks = [(place.row_segments(b) == ends[b]).astype(BF) for b in range(place.blocks)]
    wanted = [[same(e, last) for e in ends]]
    for b in range(place.blocks):
        for away in range(1, place.devices):
            wanted.append(place.to_later(away, b))
    for c, heads in enumerate(chunks):
        arrive(c)
        for head in heads:
            updates = []
            for b in range(place.blocks):
                k = k_ref[rows_of(b), columns(head)] * masks[b]
                updates.append(dot(k, v_ref[rows_of(b), columns(head)], TN))
            for ref, factors in zip(outs, wanted, strict=True):
                total = updates[0] * factors[0]
                for update, factor in zip(updates[1:], factors[1:], strict=True):
                    total = total + update * factor
                ref[head] = total.astype(BF)
        leave(c)


def inner_body(place_of, ins, outs, scratch, arrive, leave, chunks):
    q_ref, k_ref, v_ref = ins
    (raw_ref,), (weight_ref,) = outs, scratch
    weight_ref[...] = place_of(q_ref.shape[0]).weights()
    for c, heads in enumerate(chunks):
        arrive(c)
        for head in heads:
            at = columns(head)
            probs = (dot(q_ref[:, at], k_ref[:, at], NT) * weight_ref[...]).astype(BF)
            raw_ref[:, at] = dot(probs, v_ref[:, at], NN)
        leave(c)


def scan_body(place_of, ins, outs, scratch, arrive, leave, chunks, *, rows, backward):
    (t_ref,), (out_ref,) = ins, outs
    count, height, _ = t_ref.shape
    devices = GROUP // rows
    bounds = place_of(rows).bounds
    part = height // len(chunks)

    for c in range(len(chunks)):
        arrive(c)
        at = pl.ds(c * part, part)

        def one(turn, acc):
            group = count // devices - 1 - turn if backward else turn
            for k in range(devices):
                out_ref[group * devices + k, at] = acc.astype(BF)
            for k in range(devices):
                index = group * devices + (devices - 1 - k if backward else k)
                first = index * rows
                if backward:
                    keep = same(segment(first, bounds), segment(first + rows, bounds))
                else:
                    keep = same(segment(first - 1, bounds), segment(first + rows - 1, bounds))
                acc = acc * keep + t_ref[index, at].astype(F32)
            return acc

        lax.fori_loop(0, count // devices, one, jnp.zeros((part, DH), F32))
        leave(c)


def norm_body(place_of, ins, outs, scratch, arrive, leave, chunks, *, rows, block, peers):
    gain_ref, q_ref, raw_ref, grad_ref, kv_ref = ins[:5]
    peer_refs, earlier_refs = ins[5 : 5 + peers], ins[5 + peers :]
    scale_ref, held_ref, d_ref, w_ref, *t_refs = outs
    width = q_ref.shape[1]
    place = place_of(rows)
    factors = place.before(block)
    squares = cross = jnp.zeros((BLOCK, DH), F32)
    for c, heads in enumerate(chunks):
        arrive(c)
        for head in heads:
            at = columns(head)
            state = mixed(kv_ref, peer_refs, factors, head)
            raw = raw_ref[:, at] + dot(q_ref[:, at], state, NN) * factors[2]
            raw = raw.astype(BF)
            held_ref[:, at] = raw
            raw = raw.astype(F32)
            scaled = grad_ref[:, at].astype(F32) * gain_ref[:, at]
            squares = squares + raw * raw
            cross = cross + scaled * raw
        leave(c, [1])
    total = jnp.sum(squares, axis=1, keepdims=True)
    inverse = 1.0 / jnp.sqrt(total / width + eps_norm)
    mean = jnp.sum(cross, axis=1, keepdims=True) * inverse / width
    scale_ref[...] = jnp.broadcast_to(inverse, scale_ref.shape)
    leave(0, [0])
    own = place.seg(place.start(block))
    begin = (place.row_segments(block) == own).astype(BF)
    into = [same(place.seg(place.start(b)), place.seg(place.first)) for b in range(block + 1)]
    for c, heads in enumerate(chunks):
        for head in heads:
            at = columns(head)
            normed = held_ref[:, at].astype(F32) * inverse
            scaled = grad_ref[:, at].astype(F32) * gain_ref[:, at]
            grad = ((scaled - normed * mean) * inverse).astype(BF)
            d_ref[:, at] = grad
            update = dot(q_ref[:, at] * begin, grad, TN)
            w_ref[head] = update.astype(BF)
            for t_ref in t_refs:
                sums = update * into[block]
                for ref, factor in zip(earlier_refs, into[:block], strict=True):
                    sums = sums + ref[head].astype(F32) * factor
                t_ref[head] = sums.astype(BF)
        leave(c, range(2, len(outs)))


def grads_body(place_of, ins, outs, scratch, arrive, leave, chunks, *, peers):
    gain_ref, q_ref, k_ref, v_ref, kv_ref = ins[:5]
    rows, width = q_ref.shape
    place = place_of(rows)
    blocks = place.blocks
    rest = ins[5:]
    d_refs, raw_refs, scale_refs = rest[:blocks], rest[blocks : 2 * blocks], rest[2 * blocks : 3 * blocks]
    peer_refs = rest[3 * blocks :]
    out_ref, gq_ref, gk_ref, gv_ref = outs
    (weight_ref,) = scratch
    weight_ref[...] = place.weights()
    factors = [place.before(b) for b in range(blocks)]
    for c, heads in enumerate(chunks):
        arrive(c)
        for head in heads:
            at = columns(head)
            q, k, v = q_ref[:, at], k_ref[:, at], v_ref[:, at]
            d = jnp.concatenate([ref[:, at] for ref in d_refs], axis=0)
            probs = (dot(q, k, NT) * weight_ref[...]).astype(BF)
            grad_probs = (dot(d, v, NT) * weight_ref[...]).astype(BF)
            inner = dot(grad_probs, k, NN)
            for b in range(blocks):
                state = mixed(kv_ref, peer_refs[b * peers : (b + 1) * peers], factors[b], head)
                outer = dot(d_refs[b][:, at], state, NT) * factors[b][2]
                part = inner[b * BLOCK : (b + 1) * BLOCK] + outer
                gq_ref[rows_of(b), at] = part.astype(BF)
                normed = raw_refs[b][:, at].astype(F32) * scale_refs[b][...]
                out_ref[rows_of(b), at] = (normed * gain_ref[:, at]).astype(BF)
            gk_ref[:, at] = dot(grad_probs, q, TN)
            gv_ref[:, at] = dot(probs, d, TN)
        leave(c)


def last_body(place_of, ins, outs, scratch, arrive, leave, chunks):
    k_ref, v_ref, gk_in, gv_in, gs_ref = ins[:5]
    peer_refs, (gk_ref, gv_ref) = ins[5:], outs
    place = place_of(k_ref.shape[0])
    factors = [place.after(b) for b in range(place.blocks)]
    for c, heads in enumerate(chunks):
        arrive(c)
        for head in heads:
            at = columns(head)
            for b in range(place.blocks):
                at_rows = rows_of(b)
                state = mixed(gs_ref, peer_refs, factors[b], head)
                reach = factors[b][2]
                gk = gk_in[at_rows, at] + dot(v_ref[at_rows, at], state, NT) * reach
                gv = gv_in[at_rows, at] + dot(k_ref[at_rows, at], state, NN) * reach
                gk_ref[at_rows, at] = gk.astype(BF)
                gv_ref[at_rows, at] = gv.astype(BF)
        leave(c)


class Part:
    def __init__(self, array, axis=None, block=None):
        self.array, self.axis, self.block = array, axis, block
        self.shape = array.shape if block is None else (BLOCK, *array.shape[1:])

    def pieces(self, far, near, sems, count):
        far = far if self.block is None else far.at[rows_of(self.block)]
        if self.axis is None:
            return [(far, near, sems.at[0])]
        size = self.shape[self.axis] // count
        result = []
        for c in range(count):
            at = [slice(None)] * len(self.shape)
            at[self.axis] = pl.ds(c * size, size)
            result.append((far.at[tuple(at)], near.at[tuple(at)], sems.at[c]))
        return result


def call(body, name, scalars, ins, outs, heads, chunks, scratch=(), flops=0, after=()):
    sizes = (len(scalars), len(ins), len(after), len(outs), len(ins), len(outs), 2, len(scratch))

    def kernel(*refs):
        split, at = [], 0
        for size in sizes:
            split.append(refs[at : at + size])
            at += size
        settings, far_in, _, far_out, near_in, near_out, (in_sems, out_sems), rest = split
        coming = [
            part.pieces(far, near, in_sems.at[i], chunks)
            for i, (part, far, near) in enumerate(zip(ins, far_in, near_in, strict=True))
        ]
        going = [
            part.pieces(far, near, out_sems.at[i], chunks)
            for i, (part, far, near) in enumerate(zip(outs, far_out, near_out, strict=True))
        ]

        def copies(parts, c, which=None):
            for i, pieces in enumerate(parts):
                if c < len(pieces) and (which is None or i in which):
                    yield pieces[c]

        def arrive(c):
            for far, near, sem in copies(coming, c):
                pltpu.make_async_copy(far, near, sem).wait()

        def leave(c, which=None):
            for far, near, sem in copies(going, c, which):
                pltpu.make_async_copy(near, far, sem).start()

        for c in range(chunks):
            for far, near, sem in copies(coming, c):
                pltpu.make_async_copy(far, near, sem).start()
        each = heads // chunks
        turns = [range(c * each, (c + 1) * each) for c in range(chunks)]
        place_of = lambda rows: Place(settings[0], rows, *settings[1:])
        body(place_of, near_in, near_out, rest, arrive, leave, turns)
        for c in range(chunks):
            for far, near, sem in copies(going, c):
                pltpu.make_async_copy(near, far, sem).wait()

    everything = [p.array for p in (*ins, *outs)]
    anywhere = pl.BlockSpec(memory_space=pl.ANY)
    return pl.pallas_call(
        kernel,
        name=name,
        in_specs=[pl.BlockSpec(memory_space=pltpu.SMEM)] * len(scalars) + [anywhere] * (len(ins) + len(after)),
        out_specs=[anywhere] * len(outs),
        out_shape=[p.array for p in outs],
        scratch_shapes=[
            *[pltpu.VMEM(p.shape, p.array.dtype) for p in (*ins, *outs)],
            pltpu.SemaphoreType.DMA((len(ins), chunks)),
            pltpu.SemaphoreType.DMA((len(outs), chunks)),
            *scratch,
        ],
        compiler_params=pltpu.CompilerParams(vmem_limit_bytes=VMEM_BYTES),
        cost_estimate=pl.CostEstimate(
            flops=flops,
            bytes_accessed=sum(a.size * a.dtype.itemsize for a in everything),
            transcendentals=0,
        ),
    )(*scalars, *[p.array for p in ins], *after)


def local(queries, keys, values, grad_out, gain, lengths, block_mask):
    rows, width = queries.shape
    heads = width // DH
    blocks = rows // BLOCK
    devices = GROUP // rows
    peers = devices - 1
    head_count = lax.axis_size("head")
    total = lax.axis_size("ctx") * head_count
    chunks = CHUNKS if heads % CHUNKS == 0 else 1
    shape = jax.ShapeDtypeStruct
    state = shape((heads, DH, DH), BF)
    tokens = shape((rows, width), BF)
    partial = shape((rows, width), F32)
    block_tokens = shape((BLOCK, width), BF)
    square = [pltpu.VMEM((rows, rows), F32)]
    unit = 2 * rows * width * DH
    inner = 2 * rows * rows * width
    scalars = [lengths, block_mask]

    def wide(array, block=None):
        return Part(array, 1, block)

    def states(array):
        return Part(array, 0)

    def to_peers(array, away, backward):
        pairs = [(z, z + away) for z in range(head_count - away) if z % devices + away < devices]
        if backward:
            pairs = [(b, a) for a, b in pairs]
        return lax.ppermute(array, "head", pairs)

    def scanned(sums, backward, after):
        height = heads * DH // total
        slices = sums.reshape(total, height, DH)
        slices = lax.all_to_all(slices, AXES, split_axis=0, concat_axis=0, tiled=True)
        (slices,) = call(
            functools.partial(scan_body, rows=rows, backward=backward),
            "scan",
            [lengths],
            [Part(slices, 1)],
            [Part(shape(slices.shape, BF), 1)],
            heads,
            2 if height % 32 == 0 else 1,
            after=after,
        )
        slices = lax.all_to_all(slices, AXES, split_axis=0, concat_axis=0, tiled=True)
        return slices.reshape(heads, DH, DH)

    gain_row = Part(gain.reshape(1, width))
    sum_kv, *later = call(
        state_body,
        "states",
        scalars,
        [wide(keys), wide(values)],
        [states(state)] * (1 + blocks * peers),
        heads,
        chunks,
        flops=unit,
    )
    from_peers = [to_peers(x, 1 + at % peers, False) for at, x in enumerate(later)]
    (raw_inner,) = call(
        inner_body,
        "inner",
        scalars,
        [wide(queries), wide(keys), wide(values)],
        [wide(partial)],
        heads,
        chunks,
        square,
        flops=2 * inner,
    )
    kv_state = scanned(sum_kv, False, [raw_inner])

    scales, raws, grads, updates, back = [], [], [], [], []
    for b in range(blocks):
        ends = [states(state)] if b == blocks - 1 and blocks > 1 else []
        scale, raw, grad, update, *sums = call(
            functools.partial(norm_body, rows=rows, block=b, peers=peers),
            "norm",
            scalars,
            [
                gain_row,
                wide(queries, b),
                wide(raw_inner, b),
                wide(grad_out, b),
                states(kv_state),
                *[states(x) for x in from_peers[b * peers : (b + 1) * peers]],
                *[states(w) for w in (updates if ends else [])],
            ],
            [Part(shape((BLOCK, DH), F32)), wide(block_tokens), wide(block_tokens), states(state), *ends],
            heads,
            chunks,
            flops=2 * unit // blocks,
        )
        scales.append(scale)
        raws.append(raw)
        grads.append(grad)
        updates.append(update)
        back += [to_peers(update, away, True) for away in range(1, devices)]
    output, grad_q, part_k, part_v = call(
        functools.partial(grads_body, peers=peers),
        "grads",
        scalars,
        [
            gain_row,
            wide(queries),
            wide(keys),
            wide(values),
            states(kv_state),
            *[wide(d) for d in grads],
            *[wide(r) for r in raws],
            *[Part(s) for s in scales],
            *[states(x) for x in from_peers],
        ],
        [wide(tokens), wide(tokens), wide(partial), wide(partial)],
        heads,
        chunks,
        square,
        flops=5 * inner + unit,
    )
    grad_state = scanned(sums[0] if sums else updates[0], True, [part_v])
    grad_k, grad_v = call(
        last_body,
        "last",
        scalars,
        [
            wide(keys),
            wide(values),
            wide(part_k),
            wide(part_v),
            states(grad_state),
            *[states(w) for w in back],
        ],
        [wide(tokens), wide(tokens)],
        heads,
        chunks,
        flops=2 * unit,
    )
    return output, grad_q, grad_k, grad_v


def solution(mesh):
    tokens = P(AXES, None)
    return jax.shard_map(
        local,
        mesh=mesh,
        in_specs=(tokens, tokens, tokens, tokens, P(), P(), P("ctx", None)),
        out_specs=(tokens, tokens, tokens, tokens),
        check_vma=False,
    )
```

```python
import functools

import jax
import jax.numpy as jnp
from jax import lax
from jax.experimental import pallas as pl
from jax.experimental.pallas import tpu as pltpu
from jax.sharding import PartitionSpec as P

DH = 128
GROUP = 512
BLOCK = 128
CHUNKS = 8
LONG = 40_000_000_000
VMEM_BYTES = 60 * 1024 * 1024

eps_norm = 1e-06
BF = jnp.bfloat16
F32 = jnp.float32
AXES = ("ctx", "head")

NN = (((1,), (0,)), ((), ()))
NT = (((1,), (1,)), ((), ()))
TN = (((0,), (0,)), ((), ()))


def dot(a, b, dims):
    return lax.dot_general(a, b, dims, preferred_element_type=F32)


def bounds_of(len_ref):
    bounds, total = [], None
    for k in range(len_ref.shape[0] - 1):
        total = len_ref[k] if total is None else total + len_ref[k]
        bounds.append(total)
    return bounds


def segment(position, bounds):
    result = (position >= bounds[0]).astype(jnp.int32)
    for bound in bounds[1:]:
        result = result + (position >= bound).astype(jnp.int32)
    return result


def same(a, b):
    return (a == b).astype(F32)


class Place:
    def __init__(self, len_ref, rows, mask_ref=None):
        self.rows = rows
        self.blocks = rows // BLOCK
        self.devices = GROUP // rows
        self.bounds = bounds_of(len_ref)
        spot = lax.axis_index("head")
        index = lax.axis_index("ctx") * lax.axis_size("head") + spot
        self.first = index * rows
        self.part = lax.rem(spot, self.devices)
        self.group = lax.div(spot, self.devices)
        self.group_first = self.first - self.part * rows
        self.mask_ref = mask_ref

    def seg(self, position):
        return segment(position, self.bounds)

    def start(self, block):
        return self.first + block * BLOCK

    def row_segments(self, block):
        rows = lax.broadcasted_iota(jnp.int32, (BLOCK, 1), 0)
        return self.seg(rows + self.start(block))

    def pair(self, i, j):
        slot = jnp.clip(lax.div(i * (i - 1), 2) + j, 0, self.mask_ref.shape[1] - 1)
        return self.mask_ref[self.group, slot].astype(F32)

    def weights(self):
        rows = self.rows
        t = lax.broadcasted_iota(jnp.int32, (rows, rows), 0)
        s = lax.broadcasted_iota(jnp.int32, (rows, rows), 1)
        keep = (s <= t) & (self.seg(t + self.first) == self.seg(s + self.first))
        result = jnp.where(keep, 1.0, 0.0)
        for i in range(1, self.blocks):
            for j in range(i):
                bit = self.pair(self.part * self.blocks + i, self.part * self.blocks + j)
                inside = (
                    (t >= i * BLOCK)
                    & (t < (i + 1) * BLOCK)
                    & (s >= j * BLOCK)
                    & (s < (j + 1) * BLOCK)
                )
                result = jnp.where(inside, result * bit, result)
        return result

    def to_later(self, away, block):
        there = (self.part + away) * self.blocks + block
        edge = self.seg(self.start(block) + away * self.rows - 1)
        return [
            self.pair(there, self.part * self.blocks + j) * same(self.seg(self.start(j + 1) - 1), edge)
            for j in range(self.blocks)
        ]

    def before(self, block):
        edge = self.seg(self.start(block) - 1)
        carried = same(self.seg(self.group_first - 1), edge)
        peers = [(self.part >= away).astype(F32) for away in range(1, self.devices)]
        return carried, peers, (self.row_segments(block) == edge).astype(F32)

    def after(self, block):
        own = self.part * self.blocks + block
        edge = self.seg(self.start(block + 1))
        carried = same(self.seg(self.group_first + GROUP), edge)
        peers = []
        for i in range(self.blocks):
            for away in range(1, self.devices):
                there = (self.part + away < self.devices).astype(F32)
                other = (self.part + away) * self.blocks + i
                start = self.start(i) + away * self.rows
                peers.append(self.pair(other, own) * same(self.seg(start), edge) * there)
        return carried, peers, (self.row_segments(block) == edge).astype(F32)


def mixed(state_ref, peer_refs, factors, head):
    carried, peers, _ = factors
    total = state_ref[head].astype(F32) * carried
    for ref, factor in zip(peer_refs, peers, strict=True):
        total = total + ref[head].astype(F32) * factor
    return total.astype(BF)


def columns(head):
    return pl.ds(head * DH, DH)


def rows_of(block):
    return pl.ds(block * BLOCK, BLOCK)


def state_body(place_of, ins, outs, scratch, arrive, leave, chunks):
    k_ref, v_ref = ins
    rows, width = k_ref.shape
    place = place_of(rows)
    last = place.seg(place.start(place.blocks) - 1)
    ends = [place.seg(place.start(b + 1) - 1) for b in range(place.blocks)]
    masks = [(place.row_segments(b) == ends[b]).astype(BF) for b in range(place.blocks)]
    wanted = [[same(e, last) for e in ends]]
    for b in range(place.blocks):
        for away in range(1, place.devices):
            wanted.append(place.to_later(away, b))
    for c, heads in enumerate(chunks):
        arrive(c)
        for head in heads:
            updates = []
            for b in range(place.blocks):
                k = k_ref[rows_of(b), columns(head)] * masks[b]
                updates.append(dot(k, v_ref[rows_of(b), columns(head)], TN))
            for ref, factors in zip(outs, wanted, strict=True):
                total = updates[0] * factors[0]
                for update, factor in zip(updates[1:], factors[1:], strict=True):
                    total = total + update * factor
                ref[head] = total.astype(BF)
        leave(c)


def inner_body(place_of, ins, outs, scratch, arrive, leave, chunks):
    q_ref, k_ref, v_ref = ins
    (raw_ref,), (weight_ref,) = outs, scratch
    weight_ref[...] = place_of(q_ref.shape[0]).weights()
    for c, heads in enumerate(chunks):
        arrive(c)
        for head in heads:
            at = columns(head)
            probs = (dot(q_ref[:, at], k_ref[:, at], NT) * weight_ref[...]).astype(BF)
            raw_ref[:, at] = dot(probs, v_ref[:, at], NN)
        leave(c)


def scan_body(place_of, ins, outs, scratch, arrive, leave, chunks, *, rows, backward):
    (t_ref,), (out_ref,) = ins, outs
    count, height, _ = t_ref.shape
    devices = GROUP // rows
    bounds = place_of(rows).bounds
    part = height // len(chunks)

    for c in range(len(chunks)):
        arrive(c)
        at = pl.ds(c * part, part)

        def one(turn, acc):
            group = count // devices - 1 - turn if backward else turn
            for k in range(devices):
                out_ref[group * devices + k, at] = acc.astype(BF)
            for k in range(devices):
                index = group * devices + (devices - 1 - k if backward else k)
                first = index * rows
                if backward:
                    keep = same(segment(first, bounds), segment(first + rows, bounds))
                else:
                    keep = same(segment(first - 1, bounds), segment(first + rows - 1, bounds))
                acc = acc * keep + t_ref[index, at].astype(F32)
            return acc

        acc = jnp.zeros((part, DH), F32)
        if count <= 32:
            for turn in range(count // devices):
                acc = one(turn, acc)
        else:
            lax.fori_loop(0, count // devices, one, acc)
        leave(c)


def norm_body(place_of, ins, outs, scratch, arrive, leave, chunks, *, rows, block, peers):
    gain_ref, q_ref, raw_ref, grad_ref, kv_ref = ins[:5]
    peer_refs, earlier_refs = ins[5 : 5 + peers], ins[5 + peers :]
    scale_ref, held_ref, d_ref, w_ref, *t_refs = outs
    width = q_ref.shape[1]
    place = place_of(rows)
    factors = place.before(block)
    squares = cross = jnp.zeros((BLOCK, DH), F32)
    for c, heads in enumerate(chunks):
        arrive(c)
        for head in heads:
            at = columns(head)
            state = mixed(kv_ref, peer_refs, factors, head)
            raw = raw_ref[:, at] + dot(q_ref[:, at], state, NN) * factors[2]
            raw = raw.astype(BF)
            held_ref[:, at] = raw
            raw = raw.astype(F32)
            scaled = grad_ref[:, at].astype(F32) * gain_ref[:, at]
            squares = squares + raw * raw
            cross = cross + scaled * raw
        leave(c, [1])
    total = jnp.sum(squares, axis=1, keepdims=True)
    inverse = 1.0 / jnp.sqrt(total / width + eps_norm)
    mean = jnp.sum(cross, axis=1, keepdims=True) * inverse / width
    scale_ref[...] = jnp.broadcast_to(inverse, scale_ref.shape)
    leave(0, [0])
    own = place.seg(place.start(block))
    begin = (place.row_segments(block) == own).astype(BF)
    into = [same(place.seg(place.start(b)), place.seg(place.first)) for b in range(block + 1)]
    for c, heads in enumerate(chunks):
        for head in heads:
            at = columns(head)
            normed = held_ref[:, at].astype(F32) * inverse
            scaled = grad_ref[:, at].astype(F32) * gain_ref[:, at]
            grad = ((scaled - normed * mean) * inverse).astype(BF)
            d_ref[:, at] = grad
            update = dot(q_ref[:, at] * begin, grad, TN)
            w_ref[head] = update.astype(BF)
            for t_ref in t_refs:
                sums = update * into[block]
                for ref, factor in zip(earlier_refs, into[:block], strict=True):
                    sums = sums + ref[head].astype(F32) * factor
                t_ref[head] = sums.astype(BF)
        leave(c, range(2, len(outs)))


def query_grads_body(place_of, ins, outs, scratch, arrive, leave, chunks, *, peers):
    gain_ref, k_ref, v_ref, kv_ref = ins[:4]
    rows, width = k_ref.shape
    place = place_of(rows)
    blocks = place.blocks
    rest = ins[4:]
    d_refs, raw_refs, scale_refs = rest[:blocks], rest[blocks : 2 * blocks], rest[2 * blocks : 3 * blocks]
    peer_refs = rest[3 * blocks :]
    out_ref, gq_ref = outs
    (weight_ref,) = scratch
    weight_ref[...] = place.weights()
    factors = [place.before(b) for b in range(blocks)]
    for c, heads in enumerate(chunks):
        arrive(c)
        for head in heads:
            at = columns(head)
            d = jnp.concatenate([ref[:, at] for ref in d_refs], axis=0)
            grad_probs = (dot(d, v_ref[:, at], NT) * weight_ref[...]).astype(BF)
            inner = dot(grad_probs, k_ref[:, at], NN)
            for b in range(blocks):
                state = mixed(kv_ref, peer_refs[b * peers : (b + 1) * peers], factors[b], head)
                outer = dot(d_refs[b][:, at], state, NT) * factors[b][2]
                part = inner[b * BLOCK : (b + 1) * BLOCK] + outer
                gq_ref[rows_of(b), at] = part.astype(BF)
                normed = raw_refs[b][:, at].astype(F32) * scale_refs[b][...]
                out_ref[rows_of(b), at] = (normed * gain_ref[:, at]).astype(BF)
        leave(c)


def key_grads_body(place_of, ins, outs, scratch, arrive, leave, chunks):
    q_ref, k_ref, v_ref, *d_refs = ins
    place = place_of(q_ref.shape[0])
    gk_ref, gv_ref = outs
    (weight_ref,) = scratch
    weight_ref[...] = place.weights()
    for c, heads in enumerate(chunks):
        arrive(c)
        for head in heads:
            at = columns(head)
            q, d = q_ref[:, at], jnp.concatenate([ref[:, at] for ref in d_refs], axis=0)
            probs = (dot(q, k_ref[:, at], NT) * weight_ref[...]).astype(BF)
            grad_probs = (dot(d, v_ref[:, at], NT) * weight_ref[...]).astype(BF)
            gk_ref[:, at] = dot(grad_probs, q, TN)
            gv_ref[:, at] = dot(probs, d, TN)
        leave(c)


def last_body(place_of, ins, outs, scratch, arrive, leave, chunks):
    k_ref, v_ref, gk_in, gv_in, gs_ref = ins[:5]
    peer_refs, (gk_ref, gv_ref) = ins[5:], outs
    place = place_of(k_ref.shape[0])
    factors = [place.after(b) for b in range(place.blocks)]
    for c, heads in enumerate(chunks):
        arrive(c)
        for head in heads:
            at = columns(head)
            for b in range(place.blocks):
                at_rows = rows_of(b)
                state = mixed(gs_ref, peer_refs, factors[b], head)
                reach = factors[b][2]
                gk = gk_in[at_rows, at] + dot(v_ref[at_rows, at], state, NT) * reach
                gv = gv_in[at_rows, at] + dot(k_ref[at_rows, at], state, NN) * reach
                gk_ref[at_rows, at] = gk.astype(BF)
                gv_ref[at_rows, at] = gv.astype(BF)
        leave(c)


class Part:
    def __init__(self, array, axis=None, block=None):
        self.array, self.axis, self.block = array, axis, block
        self.shape = array.shape if block is None else (BLOCK, *array.shape[1:])

    def pieces(self, far, near, sems, count):
        far = far if self.block is None else far.at[rows_of(self.block)]
        if self.axis is None:
            return [(far, near, sems.at[0])]
        size = self.shape[self.axis] // count
        result = []
        for c in range(count):
            at = [slice(None)] * len(self.shape)
            at[self.axis] = pl.ds(c * size, size)
            result.append((far.at[tuple(at)], near.at[tuple(at)], sems.at[c]))
        return result


def call(body, name, scalars, ins, outs, heads, chunks, scratch=(), flops=0, after=()):
    sizes = (len(scalars), len(ins), len(after), len(outs), len(ins), len(outs), 2, len(scratch))

    def kernel(*refs):
        split, at = [], 0
        for size in sizes:
            split.append(refs[at : at + size])
            at += size
        settings, far_in, _, far_out, near_in, near_out, (in_sems, out_sems), rest = split
        coming = [
            part.pieces(far, near, in_sems.at[i], chunks)
            for i, (part, far, near) in enumerate(zip(ins, far_in, near_in, strict=True))
        ]
        going = [
            part.pieces(far, near, out_sems.at[i], chunks)
            for i, (part, far, near) in enumerate(zip(outs, far_out, near_out, strict=True))
        ]

        def copies(parts, c, which=None):
            for i, pieces in enumerate(parts):
                if c < len(pieces) and (which is None or i in which):
                    yield pieces[c]

        def arrive(c):
            for far, near, sem in copies(coming, c):
                pltpu.make_async_copy(far, near, sem).wait()

        def leave(c, which=None):
            for far, near, sem in copies(going, c, which):
                pltpu.make_async_copy(near, far, sem).start()

        for c in range(chunks):
            for far, near, sem in copies(coming, c):
                pltpu.make_async_copy(far, near, sem).start()
        each = heads // chunks
        turns = [range(c * each, (c + 1) * each) for c in range(chunks)]
        place_of = lambda rows: Place(settings[0], rows, *settings[1:])
        body(place_of, near_in, near_out, rest, arrive, leave, turns)
        for c in range(chunks):
            for far, near, sem in copies(going, c):
                pltpu.make_async_copy(near, far, sem).wait()

    everything = [p.array for p in (*ins, *outs)]
    anywhere = pl.BlockSpec(memory_space=pl.ANY)
    return pl.pallas_call(
        kernel,
        name=name,
        in_specs=[pl.BlockSpec(memory_space=pltpu.SMEM)] * len(scalars) + [anywhere] * (len(ins) + len(after)),
        out_specs=[anywhere] * len(outs),
        out_shape=[p.array for p in outs],
        scratch_shapes=[
            *[pltpu.VMEM(p.shape, p.array.dtype) for p in (*ins, *outs)],
            pltpu.SemaphoreType.DMA((len(ins), chunks)),
            pltpu.SemaphoreType.DMA((len(outs), chunks)),
            *scratch,
        ],
        compiler_params=pltpu.CompilerParams(vmem_limit_bytes=VMEM_BYTES),
        cost_estimate=pl.CostEstimate(
            flops=flops,
            bytes_accessed=sum(a.size * a.dtype.itemsize for a in everything),
            transcendentals=0,
        ),
    )(*scalars, *[p.array for p in ins], *after)


def local(queries, keys, values, grad_out, gain, lengths, block_mask):
    rows, width = queries.shape
    heads = width // DH
    blocks = rows // BLOCK
    devices = GROUP // rows
    peers = devices - 1
    head_count = lax.axis_size("head")
    total = lax.axis_size("ctx") * head_count
    chunks = CHUNKS if heads % CHUNKS == 0 else 1
    shape = jax.ShapeDtypeStruct
    state = shape((heads, DH, DH), BF)
    tokens = shape((rows, width), BF)
    partial = shape((rows, width), F32)
    block_tokens = shape((BLOCK, width), BF)
    square = [pltpu.VMEM((rows, rows), F32)]
    unit = 2 * rows * width * DH
    inner = 2 * rows * rows * width
    scalars = [lengths, block_mask]

    def wide(array, block=None):
        return Part(array, 1, block)

    def states(array):
        return Part(array, 0)

    def to_peers(array, away, backward):
        pairs = [(z, z + away) for z in range(head_count - away) if z % devices + away < devices]
        if backward:
            pairs = [(b, a) for a, b in pairs]
        return lax.ppermute(array, "head", pairs)

    def exchanged(slices):
        return lax.all_to_all(slices, AXES, split_axis=0, concat_axis=0, tiled=True)

    def scanned(sums, backward, after=()):
        height = heads * DH // total
        slices = exchanged(sums.reshape(total, height, DH))
        (slices,) = call(
            functools.partial(scan_body, rows=rows, backward=backward),
            "scan",
            [lengths],
            [Part(slices, 1)],
            [Part(shape(slices.shape, BF), 1)],
            heads,
            2 if height % 32 == 0 else 1,
            after=after,
        )
        return slices

    gain_row = Part(gain.reshape(1, width))
    sum_kv, *later = call(
        state_body,
        "states",
        scalars,
        [wide(keys), wide(values)],
        [states(state)] * (1 + blocks * peers),
        heads,
        chunks,
        flops=unit,
    )
    from_peers = [to_peers(x, 1 + at % peers, False) for at, x in enumerate(later)]
    slices = scanned(sum_kv, False)
    (raw_inner,) = call(
        inner_body,
        "inner",
        scalars,
        [wide(queries), wide(keys), wide(values)],
        [wide(partial)],
        heads,
        chunks,
        square,
        flops=LONG,
        after=[slices, *from_peers[:peers]],
    )
    kv_state = exchanged(slices).reshape(heads, DH, DH)

    scales, raws, grads, updates, back = [], [], [], [], []
    for b in range(blocks):
        ends = [states(state)] if b == blocks - 1 and blocks > 1 else []
        scale, raw, grad, update, *sums = call(
            functools.partial(norm_body, rows=rows, block=b, peers=peers),
            "norm",
            scalars,
            [
                gain_row,
                wide(queries, b),
                wide(raw_inner, b),
                wide(grad_out, b),
                states(kv_state),
                *[states(x) for x in from_peers[b * peers : (b + 1) * peers]],
                *[states(w) for w in (updates if ends else [])],
            ],
            [Part(shape((BLOCK, DH), F32)), wide(block_tokens), wide(block_tokens), states(state), *ends],
            heads,
            chunks,
            flops=LONG if b > 0 else 2 * unit // blocks,
        )
        scales.append(scale)
        raws.append(raw)
        grads.append(grad)
        updates.append(update)
        back += [to_peers(update, away, True) for away in range(1, devices)]
    output, grad_q = call(
        functools.partial(query_grads_body, peers=peers),
        "query_grads",
        scalars,
        [
            gain_row,
            wide(keys),
            wide(values),
            states(kv_state),
            *[wide(d) for d in grads],
            *[wide(r) for r in raws],
            *[Part(s) for s in scales],
            *[states(x) for x in from_peers],
        ],
        [wide(tokens), wide(tokens)],
        heads,
        chunks,
        square,
        flops=LONG,
        after=back[:peers],
    )
    slices = scanned(sums[0] if sums else updates[0], True, [grad_q])
    part_k, part_v = call(
        key_grads_body,
        "key_grads",
        scalars,
        [wide(queries), wide(keys), wide(values), *[wide(d) for d in grads]],
        [wide(partial), wide(partial)],
        heads,
        chunks,
        square,
        flops=LONG,
        after=[slices, *back[peers:]],
    )
    grad_state = exchanged(slices).reshape(heads, DH, DH)
    grad_k, grad_v = call(
        last_body,
        "last",
        scalars,
        [
            wide(keys),
            wide(values),
            wide(part_k),
            wide(part_v),
            states(grad_state),
            *[states(w) for w in back],
        ],
        [wide(tokens), wide(tokens)],
        heads,
        chunks,
        flops=2 * unit,
    )
    return output, grad_q, grad_k, grad_v


def solution(mesh):
    tokens = P(AXES, None)
    return jax.shard_map(
        local,
        mesh=mesh,
        in_specs=(tokens, tokens, tokens, tokens, P(), P(), P("ctx", None)),
        out_specs=(tokens, tokens, tokens, tokens),
        check_vma=False,
    )
```

```python
import functools

import jax
import jax.numpy as jnp
from jax import lax
from jax.experimental import pallas as pl
from jax.experimental.pallas import tpu as pltpu
from jax.sharding import PartitionSpec as P

DH = 128
GROUP = 512
BLOCK = 128
CHUNKS = 4
LONG = 40_000_000_000
VMEM_BYTES = 60 * 1024 * 1024
SOME_BYTES = 24 * 1024 * 1024

eps_norm = 1e-06
BF = jnp.bfloat16
F32 = jnp.float32
AXES = ("ctx", "head")

NN = (((1,), (0,)), ((), ()))
NT = (((1,), (1,)), ((), ()))
TN = (((0,), (0,)), ((), ()))


def dot(a, b, dims):
    return lax.dot_general(a, b, dims, preferred_element_type=F32)


def bounds_of(len_ref):
    bounds, total = [], None
    for k in range(len_ref.shape[0] - 1):
        total = len_ref[k] if total is None else total + len_ref[k]
        bounds.append(total)
    return bounds


def segment(position, bounds):
    result = (position >= bounds[0]).astype(jnp.int32)
    for bound in bounds[1:]:
        result = result + (position >= bound).astype(jnp.int32)
    return result


def same(a, b):
    return (a == b).astype(F32)


class Place:
    def __init__(self, len_ref, rows, mask_ref=None):
        self.rows = rows
        self.blocks = rows // BLOCK
        self.devices = GROUP // rows
        self.bounds = bounds_of(len_ref)
        spot = lax.axis_index("head")
        index = lax.axis_index("ctx") * lax.axis_size("head") + spot
        self.first = index * rows
        self.part = lax.rem(spot, self.devices)
        self.group = lax.div(spot, self.devices)
        self.group_first = self.first - self.part * rows
        self.mask_ref = mask_ref

    def seg(self, position):
        return segment(position, self.bounds)

    def start(self, block):
        return self.first + block * BLOCK

    def row_segments(self, block):
        rows = lax.broadcasted_iota(jnp.int32, (BLOCK, 1), 0)
        return self.seg(rows + self.start(block))

    def pair(self, i, j):
        slot = jnp.clip(lax.div(i * (i - 1), 2) + j, 0, self.mask_ref.shape[1] - 1)
        return self.mask_ref[self.group, slot].astype(F32)

    def weights(self):
        rows = self.rows
        t = lax.broadcasted_iota(jnp.int32, (rows, rows), 0)
        s = lax.broadcasted_iota(jnp.int32, (rows, rows), 1)
        keep = (s <= t) & (self.seg(t + self.first) == self.seg(s + self.first))
        result = jnp.where(keep, 1.0, 0.0)
        for i in range(1, self.blocks):
            for j in range(i):
                bit = self.pair(self.part * self.blocks + i, self.part * self.blocks + j)
                inside = (
                    (t >= i * BLOCK)
                    & (t < (i + 1) * BLOCK)
                    & (s >= j * BLOCK)
                    & (s < (j + 1) * BLOCK)
                )
                result = jnp.where(inside, result * bit, result)
        return result

    def to_later(self, away, block):
        there = (self.part + away) * self.blocks + block
        edge = self.seg(self.start(block) + away * self.rows - 1)
        return [
            self.pair(there, self.part * self.blocks + j) * same(self.seg(self.start(j + 1) - 1), edge)
            for j in range(self.blocks)
        ]

    def before(self, block):
        edge = self.seg(self.start(block) - 1)
        carried = same(self.seg(self.group_first - 1), edge)
        peers = [(self.part >= away).astype(F32) for away in range(1, self.devices)]
        return carried, peers, (self.row_segments(block) == edge).astype(F32)

    def after(self, block):
        own = self.part * self.blocks + block
        edge = self.seg(self.start(block + 1))
        carried = same(self.seg(self.group_first + GROUP), edge)
        peers = []
        for i in range(self.blocks):
            for away in range(1, self.devices):
                there = (self.part + away < self.devices).astype(F32)
                other = (self.part + away) * self.blocks + i
                start = self.start(i) + away * self.rows
                peers.append(self.pair(other, own) * same(self.seg(start), edge) * there)
        return carried, peers, (self.row_segments(block) == edge).astype(F32)


def mixed(state_ref, peer_refs, factors, head):
    carried, peers, _ = factors
    total = state_ref[head].astype(F32) * carried
    for ref, factor in zip(peer_refs, peers, strict=True):
        total = total + ref[head].astype(F32) * factor
    return total.astype(BF)


def columns(head):
    return pl.ds(head * DH, DH)


def rows_of(block):
    return pl.ds(block * BLOCK, BLOCK)


def state_body(place_of, ins, outs, scratch, arrive, leave, chunks):
    k_ref, v_ref = ins
    rows, width = k_ref.shape
    place = place_of(rows)
    last = place.seg(place.start(place.blocks) - 1)
    ends = [place.seg(place.start(b + 1) - 1) for b in range(place.blocks)]
    masks = [(place.row_segments(b) == ends[b]).astype(BF) for b in range(place.blocks)]
    wanted = [[same(e, last) for e in ends]]
    for b in range(place.blocks):
        for away in range(1, place.devices):
            wanted.append(place.to_later(away, b))
    for c, heads in enumerate(chunks):
        arrive(c)
        for head in heads:
            updates = []
            for b in range(place.blocks):
                k = k_ref[rows_of(b), columns(head)] * masks[b]
                updates.append(dot(k, v_ref[rows_of(b), columns(head)], TN))
            for ref, factors in zip(outs, wanted, strict=True):
                total = updates[0] * factors[0]
                for update, factor in zip(updates[1:], factors[1:], strict=True):
                    total = total + update * factor
                ref[head] = total.astype(BF)
        leave(c)


def inner_body(place_of, ins, outs, scratch, arrive, leave, chunks):
    q_ref, k_ref, v_ref = ins
    (raw_ref,), (weight_ref,) = outs, scratch
    weight_ref[...] = place_of(q_ref.shape[0]).weights()
    for c, heads in enumerate(chunks):
        arrive(c)
        for head in heads:
            at = columns(head)
            probs = (dot(q_ref[:, at], k_ref[:, at], NT) * weight_ref[...]).astype(BF)
            raw_ref[:, at] = dot(probs, v_ref[:, at], NN)
        leave(c)


def scan_body(place_of, ins, outs, scratch, arrive, leave, chunks, *, rows, backward):
    (t_ref,), (out_ref, token_ref) = ins, outs
    token_ref[...] = jnp.zeros_like(token_ref)
    count, height, _ = t_ref.shape
    devices = GROUP // rows
    bounds = place_of(rows).bounds
    part = height // len(chunks)
    for c in range(len(chunks)):
        arrive(c)
        at = pl.ds(c * part, part)

        def one(turn, acc):
            group = count // devices - 1 - turn if backward else turn
            for k in range(devices):
                out_ref[group * devices + k, at] = acc.astype(BF)
            for k in range(devices):
                index = group * devices + (devices - 1 - k if backward else k)
                first = index * rows
                if backward:
                    keep = same(segment(first, bounds), segment(first + rows, bounds))
                else:
                    keep = same(segment(first - 1, bounds), segment(first + rows - 1, bounds))
                acc = acc * keep + t_ref[index, at].astype(F32)
            return acc

        acc = jnp.zeros((part, DH), F32)
        if count <= 32:
            for turn in range(count // devices):
                acc = one(turn, acc)
        else:
            lax.fori_loop(0, count // devices, one, acc)
        leave(c)


def norm_body(place_of, ins, outs, scratch, arrive, leave, chunks, *, rows, block, peers):
    gain_ref, q_ref, raw_ref, grad_ref, kv_ref = ins[:5]
    peer_refs, earlier_refs = ins[5 : 5 + peers], ins[5 + peers :]
    scale_ref, held_ref, d_ref, w_ref, *t_refs = outs
    width = q_ref.shape[1]
    place = place_of(rows)
    factors = place.before(block)
    squares = cross = jnp.zeros((BLOCK, DH), F32)
    for c, heads in enumerate(chunks):
        arrive(c)
        for head in heads:
            at = columns(head)
            state = mixed(kv_ref, peer_refs, factors, head)
            raw = raw_ref[:, at] + dot(q_ref[:, at], state, NN) * factors[2]
            raw = raw.astype(BF)
            held_ref[:, at] = raw
            raw = raw.astype(F32)
            scaled = grad_ref[:, at].astype(F32) * gain_ref[:, at]
            squares = squares + raw * raw
            cross = cross + scaled * raw
        leave(c, [1])
    total = jnp.sum(squares, axis=1, keepdims=True)
    inverse = 1.0 / jnp.sqrt(total / width + eps_norm)
    mean = jnp.sum(cross, axis=1, keepdims=True) * inverse / width
    scale_ref[...] = jnp.broadcast_to(inverse, scale_ref.shape)
    leave(0, [0])
    own = place.seg(place.start(block))
    begin = (place.row_segments(block) == own).astype(BF)
    into = [same(place.seg(place.start(b)), place.seg(place.first)) for b in range(block + 1)]
    for c, heads in enumerate(chunks):
        for head in heads:
            at = columns(head)
            normed = held_ref[:, at].astype(F32) * inverse
            scaled = grad_ref[:, at].astype(F32) * gain_ref[:, at]
            grad = ((scaled - normed * mean) * inverse).astype(BF)
            d_ref[:, at] = grad
            update = dot(q_ref[:, at] * begin, grad, TN)
            w_ref[head] = update.astype(BF)
            for t_ref in t_refs:
                sums = update * into[block]
                for ref, factor in zip(earlier_refs, into[:block], strict=True):
                    sums = sums + ref[head].astype(F32) * factor
                t_ref[head] = sums.astype(BF)
        leave(c, range(2, len(outs)))


def query_grads_body(place_of, ins, outs, scratch, arrive, leave, chunks, *, peers):
    gain_ref, k_ref, v_ref, kv_ref = ins[:4]
    rows, width = k_ref.shape
    place = place_of(rows)
    blocks = place.blocks
    rest = ins[4:]
    d_refs, raw_refs, scale_refs = rest[:blocks], rest[blocks : 2 * blocks], rest[2 * blocks : 3 * blocks]
    peer_refs = rest[3 * blocks :]
    out_ref, gq_ref, token_ref = outs
    (weight_ref,) = scratch
    token_ref[...] = jnp.zeros_like(token_ref)
    weight_ref[...] = place.weights()
    factors = [place.before(b) for b in range(blocks)]
    for c, heads in enumerate(chunks):
        arrive(c)
        for head in heads:
            at = columns(head)
            d = jnp.concatenate([ref[:, at] for ref in d_refs], axis=0)
            grad_probs = (dot(d, v_ref[:, at], NT) * weight_ref[...]).astype(BF)
            inner = dot(grad_probs, k_ref[:, at], NN)
            for b in range(blocks):
                state = mixed(kv_ref, peer_refs[b * peers : (b + 1) * peers], factors[b], head)
                outer = dot(d_refs[b][:, at], state, NT) * factors[b][2]
                part = inner[b * BLOCK : (b + 1) * BLOCK] + outer
                gq_ref[rows_of(b), at] = part.astype(BF)
                normed = raw_refs[b][:, at].astype(F32) * scale_refs[b][...]
                out_ref[rows_of(b), at] = (normed * gain_ref[:, at]).astype(BF)
        leave(c)


def key_grads_body(place_of, ins, outs, scratch, arrive, leave, chunks):
    q_ref, k_ref, v_ref, *d_refs = ins
    place = place_of(q_ref.shape[0])
    gk_ref, gv_ref, k_out, v_out = outs
    (weight_ref,) = scratch
    weight_ref[...] = place.weights()
    for c, heads in enumerate(chunks):
        arrive(c)
        for head in heads:
            at = columns(head)
            q, d = q_ref[:, at], jnp.concatenate([ref[:, at] for ref in d_refs], axis=0)
            probs = (dot(q, k_ref[:, at], NT) * weight_ref[...]).astype(BF)
            grad_probs = (dot(d, v_ref[:, at], NT) * weight_ref[...]).astype(BF)
            gk_ref[:, at] = dot(grad_probs, q, TN)
            gv_ref[:, at] = dot(probs, d, TN)
            k_out[:, at] = k_ref[:, at]
            v_out[:, at] = v_ref[:, at]
        leave(c)


def last_body(place_of, ins, outs, scratch, arrive, leave, chunks):
    k_ref, v_ref, gk_in, gv_in, gs_ref = ins[:5]
    peer_refs, (gk_ref, gv_ref) = ins[5:], outs
    place = place_of(k_ref.shape[0])
    factors = [place.after(b) for b in range(place.blocks)]
    for c, heads in enumerate(chunks):
        arrive(c)
        for head in heads:
            at = columns(head)
            for b in range(place.blocks):
                at_rows = rows_of(b)
                state = mixed(gs_ref, peer_refs, factors[b], head)
                reach = factors[b][2]
                gk = gk_in[at_rows, at] + dot(v_ref[at_rows, at], state, NT) * reach
                gv = gv_in[at_rows, at] + dot(k_ref[at_rows, at], state, NN) * reach
                gk_ref[at_rows, at] = gk.astype(BF)
                gv_ref[at_rows, at] = gv.astype(BF)
        leave(c)


class Part:
    def __init__(self, array, axis=None, block=None, near=False):
        self.array, self.axis, self.block, self.near = array, axis, block, near
        self.shape = array.shape if block is None else (BLOCK, *array.shape[1:])
        self.spec = pl.BlockSpec(memory_space=pltpu.VMEM if near else pltpu.HBM)

    def pieces(self, far, near, sems, count):
        far = far if self.block is None else far.at[rows_of(self.block)]
        if self.axis is None:
            return [(far, near, sems.at[0])]
        size = self.shape[self.axis] // count
        result = []
        for c in range(count):
            at = [slice(None)] * len(self.shape)
            at[self.axis] = pl.ds(c * size, size)
            result.append((far.at[tuple(at)], near.at[tuple(at)], sems.at[c]))
        return result


def call(body, name, scalars, ins, outs, heads, chunks, scratch=(), flops=0, after=(), limit=VMEM_BYTES):
    far = [p for p in (*ins, *outs) if not p.near]
    sizes = (len(scalars), len(ins), len(after), len(outs), len(far), 2, len(scratch))

    def kernel(*refs):
        split, at = [], 0
        for size in sizes:
            split.append(refs[at : at + size])
            at += size
        settings, in_refs, _, out_refs, buffers, (in_sems, out_sems), rest = split
        buffers = iter(buffers)

        def opened(parts, given, sems):
            refs, pieces = [], []
            for i, (part, ref) in enumerate(zip(parts, given, strict=True)):
                refs.append(ref if part.near else next(buffers))
                pieces.append([] if part.near else part.pieces(ref, refs[-1], sems.at[i], chunks))
            return refs, pieces

        near_in, coming = opened(ins, in_refs, in_sems)
        near_out, going = opened(outs, out_refs, out_sems)

        def copies(parts, c, which=None):
            for i, pieces in enumerate(parts):
                if c < len(pieces) and (which is None or i in which):
                    yield pieces[c]

        def arrive(c):
            for far, near, sem in copies(coming, c):
                pltpu.make_async_copy(far, near, sem).wait()

        def leave(c, which=None):
            for far, near, sem in copies(going, c, which):
                pltpu.make_async_copy(near, far, sem).start()

        for c in range(chunks):
            for far, near, sem in copies(coming, c):
                pltpu.make_async_copy(far, near, sem).start()
        each = heads // chunks
        turns = [range(c * each, (c + 1) * each) for c in range(chunks)]
        place_of = lambda rows: Place(settings[0], rows, *settings[1:])
        body(place_of, near_in, near_out, rest, arrive, leave, turns)
        for c in range(chunks):
            for far, near, sem in copies(going, c):
                pltpu.make_async_copy(near, far, sem).wait()

    anywhere = pl.BlockSpec(memory_space=pl.ANY)
    return pl.pallas_call(
        kernel,
        name=name,
        in_specs=[
            *[pl.BlockSpec(memory_space=pltpu.SMEM)] * len(scalars),
            *[p.spec for p in ins],
            *[anywhere] * len(after),
        ],
        out_specs=[p.spec for p in outs],
        out_shape=[p.array for p in outs],
        scratch_shapes=[
            *[pltpu.VMEM(p.shape, p.array.dtype) for p in far],
            pltpu.SemaphoreType.DMA((len(ins), chunks)),
            pltpu.SemaphoreType.DMA((len(outs), chunks)),
            *scratch,
        ],
        compiler_params=pltpu.CompilerParams(vmem_limit_bytes=limit),
        cost_estimate=pl.CostEstimate(
            flops=flops,
            bytes_accessed=sum(p.array.size * p.array.dtype.itemsize for p in (*ins, *outs)),
            transcendentals=0,
        ),
    )(*scalars, *[p.array for p in ins], *after)


def local(queries, keys, values, grad_out, gain, lengths, block_mask):
    rows, width = queries.shape
    heads = width // DH
    blocks = rows // BLOCK
    devices = GROUP // rows
    peers = devices - 1
    head_count = lax.axis_size("head")
    total = lax.axis_size("ctx") * head_count
    chunks = CHUNKS if heads % CHUNKS == 0 else 1
    shape = jax.ShapeDtypeStruct
    state = shape((heads, DH, DH), BF)
    tokens = shape((rows, width), BF)
    partial = shape((rows, width), F32)
    block_tokens = shape((BLOCK, width), BF)
    square = [pltpu.VMEM((rows, rows), F32)]
    unit = 2 * rows * width * DH
    inner = 2 * rows * rows * width
    scalars = [lengths, block_mask]
    token_part = Part(shape((8, DH), F32), near=True)

    def wide(array, block=None):
        return Part(array, 1, block)

    def states(array):
        return Part(array, 0)

    def to_peers(array, away, backward):
        pairs = [(z, z + away) for z in range(head_count - away) if z % devices + away < devices]
        if backward:
            pairs = [(b, a) for a, b in pairs]
        return lax.ppermute(array, "head", pairs)

    def exchanged(slices):
        return lax.all_to_all(slices, AXES, split_axis=0, concat_axis=0, tiled=True)

    def scanned(sums, backward, after=()):
        height = heads * DH // total
        slices = exchanged(sums.reshape(total, height, DH))
        slices, token = call(
            functools.partial(scan_body, rows=rows, backward=backward),
            "scan",
            [lengths],
            [Part(slices, near=True)],
            [Part(shape(slices.shape, BF), 1), token_part],
            heads,
            2 if height % 32 == 0 else 1,
            after=after,
            limit=SOME_BYTES,
        )
        return slices, token

    gain_row = Part(gain.reshape(1, width))
    sum_kv, *later = call(
        state_body,
        "states",
        scalars,
        [wide(keys), wide(values)],
        [states(state)] * (1 + blocks * peers),
        heads,
        chunks,
        flops=unit,
    )
    from_peers = [to_peers(x, 1 + at % peers, False) for at, x in enumerate(later)]
    slices, token = scanned(sum_kv, False)
    (raw_inner,) = call(
        inner_body,
        "inner",
        scalars,
        [wide(queries), wide(keys), wide(values)],
        [wide(partial)],
        heads,
        chunks,
        square,
        flops=LONG,
        after=[token, *from_peers[:peers]],
    )
    kv_state = exchanged(slices).reshape(heads, DH, DH)

    scales, raws, grads, updates, back = [], [], [], [], []
    for b in range(blocks):
        ends = [states(state)] if b == blocks - 1 and blocks > 1 else []
        scale, raw, grad, update, *sums = call(
            functools.partial(norm_body, rows=rows, block=b, peers=peers),
            "norm",
            scalars,
            [
                gain_row,
                wide(queries, b),
                wide(raw_inner, b),
                wide(grad_out, b),
                states(kv_state),
                *[states(x) for x in from_peers[b * peers : (b + 1) * peers]],
                *[states(w) for w in (updates if ends else [])],
            ],
            [Part(shape((BLOCK, DH), F32)), wide(block_tokens), wide(block_tokens), states(state), *ends],
            heads,
            chunks,
            flops=LONG if b > 0 else 2 * unit // blocks,
        )
        scales.append(scale)
        raws.append(raw)
        grads.append(grad)
        updates.append(update)
        back += [to_peers(update, away, True) for away in range(1, devices)]
    output, grad_q, token = call(
        functools.partial(query_grads_body, peers=peers),
        "query_grads",
        scalars,
        [
            gain_row,
            wide(keys),
            wide(values),
            states(kv_state),
            *[wide(d) for d in grads],
            *[wide(r) for r in raws],
            *[Part(s) for s in scales],
            *[states(x) for x in from_peers],
        ],
        [wide(tokens), wide(tokens), token_part],
        heads,
        chunks,
        square,
        flops=LONG,
        after=back[:peers],
    )
    slices, token = scanned(sums[0] if sums else updates[0], True, [token])
    part_k, part_v, near_k, near_v = call(
        key_grads_body,
        "key_grads",
        scalars,
        [wide(queries), wide(keys), wide(values), *[wide(d) for d in grads]],
        [Part(a, near=True) for a in (partial, partial, tokens, tokens)],
        heads,
        chunks,
        square,
        flops=LONG,
        after=[token, *back[peers:]],
        limit=SOME_BYTES,
    )
    grad_state = exchanged(slices).reshape(heads, DH, DH)
    grad_k, grad_v = call(
        last_body,
        "last",
        scalars,
        [
            *[Part(a, near=True) for a in (near_k, near_v, part_k, part_v)],
            Part(grad_state, near=True),
            *[Part(w, near=True) for w in back],
        ],
        [wide(tokens), wide(tokens)],
        heads,
        chunks,
        flops=2 * unit,
        limit=SOME_BYTES,
    )
    return output, grad_q, grad_k, grad_v


def solution(mesh):
    tokens = P(AXES, None)
    return jax.shard_map(
        local,
        mesh=mesh,
        in_specs=(tokens, tokens, tokens, tokens, P(), P(), P("ctx", None)),
        out_specs=(tokens, tokens, tokens, tokens),
        check_vma=False,
    )
```

```python
import functools

import jax
import jax.numpy as jnp
from jax import lax
from jax.experimental import pallas as pl
from jax.experimental.pallas import tpu as pltpu
from jax.sharding import PartitionSpec as P

DH = 128
GROUP = 512
BLOCK = 128
CHUNKS = 4
LONG = 40_000_000_000
VMEM_BYTES = 60 * 1024 * 1024
SOME_BYTES = 24 * 1024 * 1024

eps_norm = 1e-06
BF = jnp.bfloat16
F32 = jnp.float32
AXES = ("ctx", "head")

NN = (((1,), (0,)), ((), ()))
NT = (((1,), (1,)), ((), ()))
TN = (((0,), (0,)), ((), ()))


def dot(a, b, dims):
    return lax.dot_general(a, b, dims, preferred_element_type=F32)


def bounds_of(len_ref):
    bounds, total = [], None
    for k in range(len_ref.shape[0] - 1):
        total = len_ref[k] if total is None else total + len_ref[k]
        bounds.append(total)
    return bounds


def segment(position, bounds):
    result = (position >= bounds[0]).astype(jnp.int32)
    for bound in bounds[1:]:
        result = result + (position >= bound).astype(jnp.int32)
    return result


def same(a, b):
    return (a == b).astype(F32)


class Place:
    def __init__(self, len_ref, rows, mask_ref=None):
        self.rows = rows
        self.blocks = rows // BLOCK
        self.devices = GROUP // rows
        self.bounds = bounds_of(len_ref)
        spot = lax.axis_index("head")
        index = lax.axis_index("ctx") * lax.axis_size("head") + spot
        self.first = index * rows
        self.part = lax.rem(spot, self.devices)
        self.group = lax.div(spot, self.devices)
        self.group_first = self.first - self.part * rows
        self.mask_ref = mask_ref

    def seg(self, position):
        return segment(position, self.bounds)

    def start(self, block):
        return self.first + block * BLOCK

    def row_segments(self, block):
        rows = lax.broadcasted_iota(jnp.int32, (BLOCK, 1), 0)
        return self.seg(rows + self.start(block))

    def pair(self, i, j):
        slot = jnp.clip(lax.div(i * (i - 1), 2) + j, 0, self.mask_ref.shape[1] - 1)
        return self.mask_ref[self.group, slot].astype(F32)

    def weights(self):
        rows = self.rows
        t = lax.broadcasted_iota(jnp.int32, (rows, rows), 0)
        s = lax.broadcasted_iota(jnp.int32, (rows, rows), 1)
        keep = (s <= t) & (self.seg(t + self.first) == self.seg(s + self.first))
        result = jnp.where(keep, 1.0, 0.0)
        for i in range(1, self.blocks):
            for j in range(i):
                bit = self.pair(self.part * self.blocks + i, self.part * self.blocks + j)
                inside = (
                    (t >= i * BLOCK)
                    & (t < (i + 1) * BLOCK)
                    & (s >= j * BLOCK)
                    & (s < (j + 1) * BLOCK)
                )
                result = jnp.where(inside, result * bit, result)
        return result

    def to_later(self, away, block):
        there = (self.part + away) * self.blocks + block
        edge = self.seg(self.start(block) + away * self.rows - 1)
        return [
            self.pair(there, self.part * self.blocks + j) * same(self.seg(self.start(j + 1) - 1), edge)
            for j in range(self.blocks)
        ]

    def before(self, block):
        edge = self.seg(self.start(block) - 1)
        carried = same(self.seg(self.group_first - 1), edge)
        peers = [(self.part >= away).astype(F32) for away in range(1, self.devices)]
        return carried, peers, (self.row_segments(block) == edge).astype(F32)

    def after(self, block):
        own = self.part * self.blocks + block
        edge = self.seg(self.start(block + 1))
        carried = same(self.seg(self.group_first + GROUP), edge)
        peers = []
        for i in range(self.blocks):
            for away in range(1, self.devices):
                there = (self.part + away < self.devices).astype(F32)
                other = (self.part + away) * self.blocks + i
                start = self.start(i) + away * self.rows
                peers.append(self.pair(other, own) * same(self.seg(start), edge) * there)
        return carried, peers, (self.row_segments(block) == edge).astype(F32)


def mixed(refs, factors, head):
    total = refs[0][head].astype(F32) * factors[0]
    for ref, factor in zip(refs[1:], factors[1:], strict=True):
        total = total + ref[head].astype(F32) * factor
    return total.astype(BF)


def columns(head):
    return pl.ds(head * DH, DH)


def rows_of(block):
    return pl.ds(block * BLOCK, BLOCK)


def state_body(place_of, ins, outs, scratch, arrive, leave, chunks):
    k_ref, v_ref = ins
    rows, width = k_ref.shape
    place = place_of(rows)
    last = place.seg(place.start(place.blocks) - 1)
    ends = [place.seg(place.start(b + 1) - 1) for b in range(place.blocks)]
    masks = [(place.row_segments(b) == ends[b]).astype(BF) for b in range(place.blocks)]
    wanted = [[same(e, last) for e in ends]]
    for b in range(place.blocks):
        for away in range(1, place.devices):
            wanted.append(place.to_later(away, b))
    for c, heads in enumerate(chunks):
        arrive(c)
        for head in heads:
            updates = []
            for b in range(place.blocks):
                k = k_ref[rows_of(b), columns(head)] * masks[b]
                updates.append(dot(k, v_ref[rows_of(b), columns(head)], TN))
            for ref, factors in zip(outs, wanted, strict=True):
                total = updates[0] * factors[0]
                for update, factor in zip(updates[1:], factors[1:], strict=True):
                    total = total + update * factor
                ref[head] = total.astype(BF)
        leave(c)


def inner_body(place_of, ins, outs, scratch, arrive, leave, chunks, *, peers):
    q_ref, k_ref, v_ref, *x_refs = ins
    (raw_ref,), (weight_ref,) = outs, scratch
    place = place_of(q_ref.shape[0])
    weight_ref[...] = place.weights()
    factors = [place.before(b) for b in range(place.blocks)]
    for c, heads in enumerate(chunks):
        arrive(c)
        for head in heads:
            at = columns(head)
            probs = (dot(q_ref[:, at], k_ref[:, at], NT) * weight_ref[...]).astype(BF)
            raw = dot(probs, v_ref[:, at], NN)
            for b in range(place.blocks):
                part = raw[b * BLOCK : (b + 1) * BLOCK]
                if peers:
                    state = mixed(x_refs[b * peers : (b + 1) * peers], factors[b][1], head)
                    part = part + dot(q_ref[rows_of(b), at], state, NN) * factors[b][2]
                raw_ref[rows_of(b), at] = part
        leave(c)


def scan_body(place_of, ins, outs, scratch, arrive, leave, chunks, *, rows, backward):
    (t_ref,), (out_ref, token_ref) = ins, outs
    token_ref[...] = jnp.zeros_like(token_ref)
    count, height, _ = t_ref.shape
    devices = GROUP // rows
    bounds = place_of(rows).bounds
    part = height // len(chunks)
    for c in range(len(chunks)):
        arrive(c)
        at = pl.ds(c * part, part)

        def one(turn, acc):
            group = count // devices - 1 - turn if backward else turn
            for k in range(devices):
                out_ref[group * devices + k, at] = acc.astype(BF)
            for k in range(devices):
                index = group * devices + (devices - 1 - k if backward else k)
                first = index * rows
                if backward:
                    keep = same(segment(first, bounds), segment(first + rows, bounds))
                else:
                    keep = same(segment(first - 1, bounds), segment(first + rows - 1, bounds))
                acc = acc * keep + t_ref[index, at].astype(F32)
            return acc

        acc = jnp.zeros((part, DH), F32)
        if count <= 32:
            for turn in range(count // devices):
                acc = one(turn, acc)
        else:
            lax.fori_loop(0, count // devices, one, acc)
        leave(c)


def norm_body(place_of, ins, outs, scratch, arrive, leave, chunks, *, rows, block):
    gain_ref, q_ref, raw_ref, grad_ref, kv_ref, *earlier_refs = ins
    scale_ref, held_ref, d_ref, w_ref, *t_refs = outs
    width = q_ref.shape[1]
    place = place_of(rows)
    carried, _, reach = place.before(block)
    reach = reach * carried
    squares = cross = jnp.zeros((BLOCK, DH), F32)
    for c, heads in enumerate(chunks):
        arrive(c)
        for head in heads:
            at = columns(head)
            raw = raw_ref[:, at] + dot(q_ref[:, at], kv_ref[head], NN) * reach
            raw = raw.astype(BF)
            held_ref[:, at] = raw
            raw = raw.astype(F32)
            scaled = grad_ref[:, at].astype(F32) * gain_ref[:, at]
            squares = squares + raw * raw
            cross = cross + scaled * raw
        leave(c, [1])
    total = jnp.sum(squares, axis=1, keepdims=True)
    inverse = 1.0 / jnp.sqrt(total / width + eps_norm)
    mean = jnp.sum(cross, axis=1, keepdims=True) * inverse / width
    scale_ref[...] = jnp.broadcast_to(inverse, scale_ref.shape)
    leave(0, [0])
    own = place.seg(place.start(block))
    begin = (place.row_segments(block) == own).astype(BF)
    into = [same(place.seg(place.start(b)), place.seg(place.first)) for b in range(block + 1)]
    for c, heads in enumerate(chunks):
        for head in heads:
            at = columns(head)
            normed = held_ref[:, at].astype(F32) * inverse
            scaled = grad_ref[:, at].astype(F32) * gain_ref[:, at]
            grad = ((scaled - normed * mean) * inverse).astype(BF)
            d_ref[:, at] = grad
            update = dot(q_ref[:, at] * begin, grad, TN)
            w_ref[head] = update.astype(BF)
            for t_ref in t_refs:
                sums = update * into[block]
                for ref, factor in zip(earlier_refs, into[:block], strict=True):
                    sums = sums + ref[head].astype(F32) * factor
                t_ref[head] = sums.astype(BF)
        leave(c, range(2, len(outs)))


def query_grads_body(place_of, ins, outs, scratch, arrive, leave, chunks, *, peers):
    gain_ref, k_ref, v_ref, kv_ref = ins[:4]
    rows, width = k_ref.shape
    place = place_of(rows)
    blocks = place.blocks
    rest = ins[4:]
    d_refs, raw_refs, scale_refs = rest[:blocks], rest[blocks : 2 * blocks], rest[2 * blocks : 3 * blocks]
    peer_refs = rest[3 * blocks :]
    out_ref, gq_ref, token_ref = outs
    (weight_ref,) = scratch
    token_ref[...] = jnp.zeros_like(token_ref)
    weight_ref[...] = place.weights()
    factors = [place.before(b) for b in range(blocks)]
    for c, heads in enumerate(chunks):
        arrive(c)
        for head in heads:
            at = columns(head)
            d = jnp.concatenate([ref[:, at] for ref in d_refs], axis=0)
            grad_probs = (dot(d, v_ref[:, at], NT) * weight_ref[...]).astype(BF)
            inner = dot(grad_probs, k_ref[:, at], NN)
            for b in range(blocks):
                carried, there, _ = factors[b]
                state = mixed([kv_ref, *peer_refs[b * peers : (b + 1) * peers]], [carried, *there], head)
                outer = dot(d_refs[b][:, at], state, NT) * factors[b][2]
                part = inner[b * BLOCK : (b + 1) * BLOCK] + outer
                gq_ref[rows_of(b), at] = part.astype(BF)
                normed = raw_refs[b][:, at].astype(F32) * scale_refs[b][...]
                out_ref[rows_of(b), at] = (normed * gain_ref[:, at]).astype(BF)
        leave(c)


def key_grads_body(place_of, ins, outs, scratch, arrive, leave, chunks, *, peers):
    q_ref, k_ref, v_ref, *rest = ins
    place = place_of(q_ref.shape[0])
    blocks = place.blocks
    d_refs, w_refs = rest[:blocks], rest[blocks:]
    gk_ref, gv_ref = outs
    (weight_ref,) = scratch
    weight_ref[...] = place.weights()
    factors = [place.after(b) for b in range(blocks)]
    for c, heads in enumerate(chunks):
        arrive(c)
        for head in heads:
            at = columns(head)
            q, d = q_ref[:, at], jnp.concatenate([ref[:, at] for ref in d_refs], axis=0)
            probs = (dot(q, k_ref[:, at], NT) * weight_ref[...]).astype(BF)
            grad_probs = (dot(d, v_ref[:, at], NT) * weight_ref[...]).astype(BF)
            gk = dot(grad_probs, q, TN)
            gv = dot(probs, d, TN)
            for b in range(blocks):
                at_rows, here = rows_of(b), slice(b * BLOCK, (b + 1) * BLOCK)
                part_k, part_v = gk[here], gv[here]
                if peers:
                    state = mixed(w_refs, factors[b][1], head)
                    part_k = part_k + dot(v_ref[at_rows, at], state, NT) * factors[b][2]
                    part_v = part_v + dot(k_ref[at_rows, at], state, NN) * factors[b][2]
                gk_ref[at_rows, at] = part_k
                gv_ref[at_rows, at] = part_v
        leave(c)


def last_body(place_of, ins, outs, scratch, arrive, leave, chunks):
    k_ref, v_ref, gk_in, gv_in, gs_ref = ins
    gk_ref, gv_ref = outs
    place = place_of(k_ref.shape[0])
    factors = [place.after(b) for b in range(place.blocks)]
    reach = jnp.concatenate([reach * carried for carried, _, reach in factors], axis=0)
    for c, heads in enumerate(chunks):
        arrive(c)
        for head in heads:
            at = columns(head)
            gk = gk_in[:, at] + dot(v_ref[:, at], gs_ref[head], NT) * reach
            gv = gv_in[:, at] + dot(k_ref[:, at], gs_ref[head], NN) * reach
            gk_ref[:, at] = gk.astype(BF)
            gv_ref[:, at] = gv.astype(BF)
        leave(c)


class Part:
    def __init__(self, array, axis=None, block=None, near=False):
        self.array, self.axis, self.block, self.near = array, axis, block, near
        self.shape = array.shape if block is None else (BLOCK, *array.shape[1:])
        self.spec = pl.BlockSpec(memory_space=pltpu.VMEM if near else pltpu.HBM)

    def pieces(self, far, near, sems, count):
        far = far if self.block is None else far.at[rows_of(self.block)]
        if self.axis is None:
            return [(far, near, sems.at[0])]
        size = self.shape[self.axis] // count
        result = []
        for c in range(count):
            at = [slice(None)] * len(self.shape)
            at[self.axis] = pl.ds(c * size, size)
            result.append((far.at[tuple(at)], near.at[tuple(at)], sems.at[c]))
        return result


def call(body, name, scalars, ins, outs, heads, chunks, scratch=(), flops=0, after=(), limit=VMEM_BYTES):
    far = [p for p in (*ins, *outs) if not p.near]
    sizes = (len(scalars), len(ins), len(after), len(outs), len(far), 2, len(scratch))

    def kernel(*refs):
        split, at = [], 0
        for size in sizes:
            split.append(refs[at : at + size])
            at += size
        settings, in_refs, _, out_refs, buffers, (in_sems, out_sems), rest = split
        buffers = iter(buffers)

        def opened(parts, given, sems):
            refs, pieces = [], []
            for i, (part, ref) in enumerate(zip(parts, given, strict=True)):
                refs.append(ref if part.near else next(buffers))
                pieces.append([] if part.near else part.pieces(ref, refs[-1], sems.at[i], chunks))
            return refs, pieces

        near_in, coming = opened(ins, in_refs, in_sems)
        near_out, going = opened(outs, out_refs, out_sems)

        def copies(parts, c, which=None):
            for i, pieces in enumerate(parts):
                if c < len(pieces) and (which is None or i in which):
                    yield pieces[c]

        def arrive(c):
            for far, near, sem in copies(coming, c):
                pltpu.make_async_copy(far, near, sem).wait()

        def leave(c, which=None):
            for far, near, sem in copies(going, c, which):
                pltpu.make_async_copy(near, far, sem).start()

        for c in range(chunks):
            for far, near, sem in copies(coming, c):
                pltpu.make_async_copy(far, near, sem).start()
        each = heads // chunks
        turns = [range(c * each, (c + 1) * each) for c in range(chunks)]
        place_of = lambda rows: Place(settings[0], rows, *settings[1:])
        body(place_of, near_in, near_out, rest, arrive, leave, turns)
        for c in range(chunks):
            for far, near, sem in copies(going, c):
                pltpu.make_async_copy(near, far, sem).wait()

    anywhere = pl.BlockSpec(memory_space=pl.ANY)
    return pl.pallas_call(
        kernel,
        name=name,
        in_specs=[
            *[pl.BlockSpec(memory_space=pltpu.SMEM)] * len(scalars),
            *[p.spec for p in ins],
            *[anywhere] * len(after),
        ],
        out_specs=[p.spec for p in outs],
        out_shape=[p.array for p in outs],
        scratch_shapes=[
            *[pltpu.VMEM(p.shape, p.array.dtype) for p in far],
            pltpu.SemaphoreType.DMA((len(ins), chunks)),
            pltpu.SemaphoreType.DMA((len(outs), chunks)),
            *scratch,
        ],
        compiler_params=pltpu.CompilerParams(vmem_limit_bytes=limit),
        cost_estimate=pl.CostEstimate(
            flops=flops,
            bytes_accessed=sum(p.array.size * p.array.dtype.itemsize for p in (*ins, *outs)),
            transcendentals=0,
        ),
    )(*scalars, *[p.array for p in ins], *after)


def local(queries, keys, values, grad_out, gain, lengths, block_mask):
    rows, width = queries.shape
    heads = width // DH
    blocks = rows // BLOCK
    devices = GROUP // rows
    peers = devices - 1
    head_count = lax.axis_size("head")
    total = lax.axis_size("ctx") * head_count
    chunks = CHUNKS if heads % CHUNKS == 0 else 1
    shape = jax.ShapeDtypeStruct
    state = shape((heads, DH, DH), BF)
    tokens = shape((rows, width), BF)
    partial = shape((rows, width), F32)
    block_tokens = shape((BLOCK, width), BF)
    square = [pltpu.VMEM((rows, rows), F32)]
    unit = 2 * rows * width * DH
    inner = 2 * rows * rows * width
    scalars = [lengths, block_mask]
    token_part = Part(shape((8, DH), F32), near=True)

    def wide(array, block=None):
        return Part(array, 1, block)

    def states(array):
        return Part(array, 0)

    def to_peers(array, away, backward):
        pairs = [(z, z + away) for z in range(head_count - away) if z % devices + away < devices]
        if backward:
            pairs = [(b, a) for a, b in pairs]
        return lax.ppermute(array, "head", pairs)

    def exchanged(slices):
        return lax.all_to_all(slices, AXES, split_axis=0, concat_axis=0, tiled=True)

    def scanned(sums, backward, after=()):
        height = heads * DH // total
        slices = exchanged(sums.reshape(total, height, DH))
        slices, token = call(
            functools.partial(scan_body, rows=rows, backward=backward),
            "scan",
            [lengths],
            [Part(slices, near=True)],
            [Part(shape(slices.shape, BF), 1), token_part],
            heads,
            2 if height % 32 == 0 else 1,
            after=after,
            limit=SOME_BYTES,
        )
        return slices, token

    gain_row = Part(gain.reshape(1, width))
    sum_kv, *later = call(
        state_body,
        "states",
        scalars,
        [wide(keys), wide(values)],
        [states(state)] * (1 + blocks * peers),
        heads,
        chunks,
        flops=unit,
    )
    from_peers = [to_peers(x, 1 + at % peers, False) for at, x in enumerate(later)]
    slices, token = scanned(sum_kv, False)
    (raw_inner,) = call(
        functools.partial(inner_body, peers=peers),
        "inner",
        scalars,
        [wide(queries), wide(keys), wide(values), *[states(x) for x in from_peers]],
        [wide(partial)],
        heads,
        chunks,
        square,
        flops=LONG,
        after=[token],
    )
    kv_state = exchanged(slices).reshape(heads, DH, DH)

    scales, raws, grads, updates, back = [], [], [], [], []
    for b in range(blocks):
        ends = [states(state)] if b == blocks - 1 and blocks > 1 else []
        scale, raw, grad, update, *sums = call(
            functools.partial(norm_body, rows=rows, block=b),
            "norm",
            scalars,
            [
                gain_row,
                wide(queries, b),
                wide(raw_inner, b),
                wide(grad_out, b),
                states(kv_state),
                *[states(w) for w in (updates if ends else [])],
            ],
            [Part(shape((BLOCK, DH), F32)), wide(block_tokens), wide(block_tokens), states(state), *ends],
            heads,
            chunks,
            flops=LONG if b > 0 else 2 * unit // blocks,
        )
        scales.append(scale)
        raws.append(raw)
        grads.append(grad)
        updates.append(update)
        back += [to_peers(update, away, True) for away in range(1, devices)]
    output, grad_q, token = call(
        functools.partial(query_grads_body, peers=peers),
        "query_grads",
        scalars,
        [
            gain_row,
            wide(keys),
            wide(values),
            states(kv_state),
            *[wide(d) for d in grads],
            *[wide(r) for r in raws],
            *[Part(s) for s in scales],
            *[states(x) for x in from_peers],
        ],
        [wide(tokens), wide(tokens), token_part],
        heads,
        chunks,
        square,
        flops=LONG,
        after=back[:peers],
    )
    slices, token = scanned(sums[0] if sums else updates[0], True, [token])
    part_k, part_v = call(
        functools.partial(key_grads_body, peers=peers),
        "key_grads",
        scalars,
        [
            wide(queries),
            wide(keys),
            wide(values),
            *[wide(d) for d in grads],
            *[states(w) for w in back],
        ],
        [wide(partial), wide(partial)],
        heads,
        chunks,
        square,
        flops=LONG,
        after=[token],
    )
    grad_state = exchanged(slices).reshape(heads, DH, DH)
    grad_k, grad_v = call(
        last_body,
        "last",
        scalars,
        [wide(keys), wide(values), wide(part_k), wide(part_v), states(grad_state)],
        [wide(tokens), wide(tokens)],
        heads,
        chunks,
        flops=2 * unit,
    )
    return output, grad_q, grad_k, grad_v


def solution(mesh):
    tokens = P(AXES, None)
    return jax.shard_map(
        local,
        mesh=mesh,
        in_specs=(tokens, tokens, tokens, tokens, P(), P(), P("ctx", None)),
        out_specs=(tokens, tokens, tokens, tokens),
        check_vma=False,
    )
```

```python
import functools

import jax
import jax.numpy as jnp
from jax import lax
from jax.experimental import pallas as pl
from jax.experimental.pallas import tpu as pltpu
from jax.sharding import PartitionSpec as P

DH = 128
GROUP = 512
BLOCK = 128
CHUNKS = 4
LONG = 40_000_000_000
VMEM_BYTES = 60 * 1024 * 1024
SOME_BYTES = 24 * 1024 * 1024

eps_norm = 1e-06
BF = jnp.bfloat16
F32 = jnp.float32
AXES = ("ctx", "head")

NN = (((1,), (0,)), ((), ()))
NT = (((1,), (1,)), ((), ()))
TN = (((0,), (0,)), ((), ()))


def dot(a, b, dims):
    return lax.dot_general(a, b, dims, preferred_element_type=F32)


def bounds_of(len_ref):
    bounds, total = [], None
    for k in range(len_ref.shape[0] - 1):
        total = len_ref[k] if total is None else total + len_ref[k]
        bounds.append(total)
    return bounds


def segment(position, bounds):
    result = (position >= bounds[0]).astype(jnp.int32)
    for bound in bounds[1:]:
        result = result + (position >= bound).astype(jnp.int32)
    return result


def same(a, b):
    return (a == b).astype(F32)


class Place:
    def __init__(self, len_ref, rows, mask_ref=None):
        self.rows = rows
        self.blocks = rows // BLOCK
        self.devices = GROUP // rows
        self.bounds = bounds_of(len_ref)
        spot = lax.axis_index("head")
        index = lax.axis_index("ctx") * lax.axis_size("head") + spot
        self.first = index * rows
        self.part = lax.rem(spot, self.devices)
        self.group = lax.div(spot, self.devices)
        self.group_first = self.first - self.part * rows
        self.mask_ref = mask_ref

    def seg(self, position):
        return segment(position, self.bounds)

    def start(self, block):
        return self.first + block * BLOCK

    def row_segments(self, block):
        rows = lax.broadcasted_iota(jnp.int32, (BLOCK, 1), 0)
        return self.seg(rows + self.start(block))

    def pair(self, i, j):
        slot = jnp.clip(lax.div(i * (i - 1), 2) + j, 0, self.mask_ref.shape[1] - 1)
        return self.mask_ref[self.group, slot].astype(F32)

    def weights(self):
        rows = self.rows
        t = lax.broadcasted_iota(jnp.int32, (rows, rows), 0)
        s = lax.broadcasted_iota(jnp.int32, (rows, rows), 1)
        keep = (s <= t) & (self.seg(t + self.first) == self.seg(s + self.first))
        result = jnp.where(keep, 1.0, 0.0)
        for i in range(1, self.blocks):
            for j in range(i):
                bit = self.pair(self.part * self.blocks + i, self.part * self.blocks + j)
                inside = (
                    (t >= i * BLOCK)
                    & (t < (i + 1) * BLOCK)
                    & (s >= j * BLOCK)
                    & (s < (j + 1) * BLOCK)
                )
                result = jnp.where(inside, result * bit, result)
        return result

    def to_later(self, away, block):
        there = (self.part + away) * self.blocks + block
        edge = self.seg(self.start(block) + away * self.rows - 1)
        return [
            self.pair(there, self.part * self.blocks + j) * same(self.seg(self.start(j + 1) - 1), edge)
            for j in range(self.blocks)
        ]

    def before(self, block):
        edge = self.seg(self.start(block) - 1)
        carried = same(self.seg(self.group_first - 1), edge)
        peers = [(self.part >= away).astype(F32) for away in range(1, self.devices)]
        return carried, peers, (self.row_segments(block) == edge).astype(F32)

    def after(self, block):
        own = self.part * self.blocks + block
        edge = self.seg(self.start(block + 1))
        carried = same(self.seg(self.group_first + GROUP), edge)
        peers = []
        for i in range(self.blocks):
            for away in range(1, self.devices):
                there = (self.part + away < self.devices).astype(F32)
                other = (self.part + away) * self.blocks + i
                start = self.start(i) + away * self.rows
                peers.append(self.pair(other, own) * same(self.seg(start), edge) * there)
        return carried, peers, (self.row_segments(block) == edge).astype(F32)


def mixed(refs, factors, head):
    total = refs[0][head].astype(F32) * factors[0]
    for ref, factor in zip(refs[1:], factors[1:], strict=True):
        total = total + ref[head].astype(F32) * factor
    return total.astype(BF)


def columns(head):
    return pl.ds(head * DH, DH)


def rows_of(block):
    return pl.ds(block * BLOCK, BLOCK)


def state_body(place_of, ins, outs, scratch, arrive, leave, chunks):
    k_ref, v_ref = ins
    rows, width = k_ref.shape
    place = place_of(rows)
    last = place.seg(place.start(place.blocks) - 1)
    ends = [place.seg(place.start(b + 1) - 1) for b in range(place.blocks)]
    masks = [(place.row_segments(b) == ends[b]).astype(BF) for b in range(place.blocks)]
    wanted = [[same(e, last) for e in ends]]
    for b in range(place.blocks):
        for away in range(1, place.devices):
            wanted.append(place.to_later(away, b))
    for c, heads in enumerate(chunks):
        arrive(c)
        for head in heads:
            updates = []
            for b in range(place.blocks):
                k = k_ref[rows_of(b), columns(head)] * masks[b]
                updates.append(dot(k, v_ref[rows_of(b), columns(head)], TN))
            for ref, factors in zip(outs, wanted, strict=True):
                total = updates[0] * factors[0]
                for update, factor in zip(updates[1:], factors[1:], strict=True):
                    total = total + update * factor
                ref[head] = total.astype(BF)
        leave(c)


def inner_body(place_of, ins, outs, scratch, arrive, leave, chunks):
    q_ref, k_ref, v_ref = ins
    (raw_ref,), (weight_ref,) = outs, scratch
    weight_ref[...] = place_of(q_ref.shape[0]).weights()
    for c, heads in enumerate(chunks):
        arrive(c)
        for head in heads:
            at = columns(head)
            probs = (dot(q_ref[:, at], k_ref[:, at], NT) * weight_ref[...]).astype(BF)
            raw_ref[:, at] = dot(probs, v_ref[:, at], NN)
        leave(c)


def scan_body(place_of, ins, outs, scratch, arrive, leave, chunks, *, rows, backward):
    (t_ref,), (out_ref, token_ref) = ins, outs
    token_ref[...] = jnp.zeros_like(token_ref)
    count, height, _ = t_ref.shape
    devices = GROUP // rows
    bounds = place_of(rows).bounds
    part = height // len(chunks)
    for c in range(len(chunks)):
        arrive(c)
        at = pl.ds(c * part, part)

        def one(turn, acc):
            group = count // devices - 1 - turn if backward else turn
            for k in range(devices):
                out_ref[group * devices + k, at] = acc.astype(BF)
            for k in range(devices):
                index = group * devices + (devices - 1 - k if backward else k)
                first = index * rows
                if backward:
                    keep = same(segment(first, bounds), segment(first + rows, bounds))
                else:
                    keep = same(segment(first - 1, bounds), segment(first + rows - 1, bounds))
                acc = acc * keep + t_ref[index, at].astype(F32)
            return acc

        acc = jnp.zeros((part, DH), F32)
        if count <= 32:
            for turn in range(count // devices):
                acc = one(turn, acc)
        else:
            lax.fori_loop(0, count // devices, one, acc)
        leave(c)


def norm_body(place_of, ins, outs, scratch, arrive, leave, chunks, *, rows, block, peers):
    gain_ref, q_ref, raw_ref, grad_ref = ins[:4]
    state_refs, earlier_refs = ins[4 : 5 + peers], ins[5 + peers :]
    scale_ref, held_ref, d_ref, w_ref, *t_refs = outs
    width = q_ref.shape[1]
    place = place_of(rows)
    carried, there, reach = place.before(block)
    squares = cross = jnp.zeros((BLOCK, DH), F32)
    for c, heads in enumerate(chunks):
        arrive(c)
        for head in heads:
            at = columns(head)
            state = mixed(state_refs, [carried, *there], head)
            raw = raw_ref[:, at] + dot(q_ref[:, at], state, NN) * reach
            raw = raw.astype(BF)
            held_ref[:, at] = raw
            raw = raw.astype(F32)
            scaled = grad_ref[:, at].astype(F32) * gain_ref[:, at]
            squares = squares + raw * raw
            cross = cross + scaled * raw
        leave(c, [1])
    total = jnp.sum(squares, axis=1, keepdims=True)
    inverse = 1.0 / jnp.sqrt(total / width + eps_norm)
    mean = jnp.sum(cross, axis=1, keepdims=True) * inverse / width
    scale_ref[...] = jnp.broadcast_to(inverse, scale_ref.shape)
    leave(0, [0])
    own = place.seg(place.start(block))
    begin = (place.row_segments(block) == own).astype(BF)
    into = [same(place.seg(place.start(b)), place.seg(place.first)) for b in range(block + 1)]
    for c, heads in enumerate(chunks):
        for head in heads:
            at = columns(head)
            normed = held_ref[:, at].astype(F32) * inverse
            scaled = grad_ref[:, at].astype(F32) * gain_ref[:, at]
            grad = ((scaled - normed * mean) * inverse).astype(BF)
            d_ref[:, at] = grad
            update = dot(q_ref[:, at] * begin, grad, TN)
            w_ref[head] = update.astype(BF)
            for t_ref in t_refs:
                sums = update * into[block]
                for ref, factor in zip(earlier_refs, into[:block], strict=True):
                    sums = sums + ref[head].astype(F32) * factor
                t_ref[head] = sums.astype(BF)
        leave(c, range(2, len(outs)))


def query_grads_body(place_of, ins, outs, scratch, arrive, leave, chunks, *, peers):
    gain_ref, k_ref, v_ref, kv_ref = ins[:4]
    rows, width = k_ref.shape
    place = place_of(rows)
    blocks = place.blocks
    rest = ins[4:]
    d_refs, raw_refs, scale_refs = rest[:blocks], rest[blocks : 2 * blocks], rest[2 * blocks : 3 * blocks]
    peer_refs = rest[3 * blocks :]
    out_ref, gq_ref, token_ref = outs
    (weight_ref,) = scratch
    token_ref[...] = jnp.zeros_like(token_ref)
    weight_ref[...] = place.weights()
    factors = [place.before(b) for b in range(blocks)]
    for c, heads in enumerate(chunks):
        arrive(c)
        for head in heads:
            at = columns(head)
            d = jnp.concatenate([ref[:, at] for ref in d_refs], axis=0)
            grad_probs = (dot(d, v_ref[:, at], NT) * weight_ref[...]).astype(BF)
            inner = dot(grad_probs, k_ref[:, at], NN)
            for b in range(blocks):
                carried, there, _ = factors[b]
                state = mixed([kv_ref, *peer_refs[b * peers : (b + 1) * peers]], [carried, *there], head)
                outer = dot(d_refs[b][:, at], state, NT) * factors[b][2]
                part = inner[b * BLOCK : (b + 1) * BLOCK] + outer
                gq_ref[rows_of(b), at] = part.astype(BF)
                normed = raw_refs[b][:, at].astype(F32) * scale_refs[b][...]
                out_ref[rows_of(b), at] = (normed * gain_ref[:, at]).astype(BF)
        leave(c)


def key_grads_body(place_of, ins, outs, scratch, arrive, leave, chunks, *, peers):
    q_ref, k_ref, v_ref, *rest = ins
    place = place_of(q_ref.shape[0])
    blocks = place.blocks
    d_refs, w_refs = rest[:blocks], rest[blocks:]
    gk_ref, gv_ref = outs
    (weight_ref,) = scratch
    weight_ref[...] = place.weights()
    factors = [place.after(b) for b in range(blocks)]
    for c, heads in enumerate(chunks):
        arrive(c)
        for head in heads:
            at = columns(head)
            q, d = q_ref[:, at], jnp.concatenate([ref[:, at] for ref in d_refs], axis=0)
            probs = (dot(q, k_ref[:, at], NT) * weight_ref[...]).astype(BF)
            grad_probs = (dot(d, v_ref[:, at], NT) * weight_ref[...]).astype(BF)
            gk = dot(grad_probs, q, TN)
            gv = dot(probs, d, TN)
            for b in range(blocks):
                at_rows, here = rows_of(b), slice(b * BLOCK, (b + 1) * BLOCK)
                part_k, part_v = gk[here], gv[here]
                if peers:
                    state = mixed(w_refs, factors[b][1], head)
                    part_k = part_k + dot(v_ref[at_rows, at], state, NT) * factors[b][2]
                    part_v = part_v + dot(k_ref[at_rows, at], state, NN) * factors[b][2]
                gk_ref[at_rows, at] = part_k
                gv_ref[at_rows, at] = part_v
        leave(c)


def last_body(place_of, ins, outs, scratch, arrive, leave, chunks):
    k_ref, v_ref, gk_in, gv_in, gs_ref = ins
    gk_ref, gv_ref = outs
    place = place_of(k_ref.shape[0])
    factors = [place.after(b) for b in range(place.blocks)]
    reach = jnp.concatenate([reach * carried for carried, _, reach in factors], axis=0)
    for c, heads in enumerate(chunks):
        arrive(c)
        for head in heads:
            at = columns(head)
            gk = gk_in[:, at] + dot(v_ref[:, at], gs_ref[head], NT) * reach
            gv = gv_in[:, at] + dot(k_ref[:, at], gs_ref[head], NN) * reach
            gk_ref[:, at] = gk.astype(BF)
            gv_ref[:, at] = gv.astype(BF)
        leave(c)


class Part:
    def __init__(self, array, axis=None, block=None, near=False):
        self.array, self.axis, self.block, self.near = array, axis, block, near
        self.shape = array.shape if block is None else (BLOCK, *array.shape[1:])
        self.spec = pl.BlockSpec(memory_space=pltpu.VMEM if near else pltpu.HBM)

    def pieces(self, far, near, sems, count):
        far = far if self.block is None else far.at[rows_of(self.block)]
        if self.axis is None:
            return [(far, near, sems.at[0])]
        size = self.shape[self.axis] // count
        result = []
        for c in range(count):
            at = [slice(None)] * len(self.shape)
            at[self.axis] = pl.ds(c * size, size)
            result.append((far.at[tuple(at)], near.at[tuple(at)], sems.at[c]))
        return result


def call(body, name, scalars, ins, outs, heads, chunks, scratch=(), flops=0, after=(), limit=VMEM_BYTES):
    far = [p for p in (*ins, *outs) if not p.near]
    sizes = (len(scalars), len(ins), len(after), len(outs), len(far), 2, len(scratch))

    def kernel(*refs):
        split, at = [], 0
        for size in sizes:
            split.append(refs[at : at + size])
            at += size
        settings, in_refs, _, out_refs, buffers, (in_sems, out_sems), rest = split
        buffers = iter(buffers)

        def opened(parts, given, sems):
            refs, pieces = [], []
            for i, (part, ref) in enumerate(zip(parts, given, strict=True)):
                refs.append(ref if part.near else next(buffers))
                pieces.append([] if part.near else part.pieces(ref, refs[-1], sems.at[i], chunks))
            return refs, pieces

        near_in, coming = opened(ins, in_refs, in_sems)
        near_out, going = opened(outs, out_refs, out_sems)

        def copies(parts, c, which=None):
            for i, pieces in enumerate(parts):
                if c < len(pieces) and (which is None or i in which):
                    yield pieces[c]

        def arrive(c):
            for far, near, sem in copies(coming, c):
                pltpu.make_async_copy(far, near, sem).wait()

        def leave(c, which=None):
            for far, near, sem in copies(going, c, which):
                pltpu.make_async_copy(near, far, sem).start()

        for c in range(chunks):
            for far, near, sem in copies(coming, c):
                pltpu.make_async_copy(far, near, sem).start()
        each = heads // chunks
        turns = [range(c * each, (c + 1) * each) for c in range(chunks)]
        place_of = lambda rows: Place(settings[0], rows, *settings[1:])
        body(place_of, near_in, near_out, rest, arrive, leave, turns)
        for c in range(chunks):
            for far, near, sem in copies(going, c):
                pltpu.make_async_copy(near, far, sem).wait()

    anywhere = pl.BlockSpec(memory_space=pl.ANY)
    return pl.pallas_call(
        kernel,
        name=name,
        in_specs=[
            *[pl.BlockSpec(memory_space=pltpu.SMEM)] * len(scalars),
            *[p.spec for p in ins],
            *[anywhere] * len(after),
        ],
        out_specs=[p.spec for p in outs],
        out_shape=[p.array for p in outs],
        scratch_shapes=[
            *[pltpu.VMEM(p.shape, p.array.dtype) for p in far],
            pltpu.SemaphoreType.DMA((len(ins), chunks)),
            pltpu.SemaphoreType.DMA((len(outs), chunks)),
            *scratch,
        ],
        compiler_params=pltpu.CompilerParams(vmem_limit_bytes=limit),
        cost_estimate=pl.CostEstimate(
            flops=flops,
            bytes_accessed=sum(p.array.size * p.array.dtype.itemsize for p in (*ins, *outs)),
            transcendentals=0,
        ),
    )(*scalars, *[p.array for p in ins], *after)


def local(queries, keys, values, grad_out, gain, lengths, block_mask):
    rows, width = queries.shape
    heads = width // DH
    blocks = rows // BLOCK
    devices = GROUP // rows
    peers = devices - 1
    head_count = lax.axis_size("head")
    total = lax.axis_size("ctx") * head_count
    chunks = CHUNKS if heads % CHUNKS == 0 else 1
    shape = jax.ShapeDtypeStruct
    state = shape((heads, DH, DH), BF)
    tokens = shape((rows, width), BF)
    partial = shape((rows, width), F32)
    block_tokens = shape((BLOCK, width), BF)
    square = [pltpu.VMEM((rows, rows), F32)]
    unit = 2 * rows * width * DH
    inner = 2 * rows * rows * width
    scalars = [lengths, block_mask]
    token_part = Part(shape((8, DH), F32), near=True)

    def wide(array, block=None):
        return Part(array, 1, block)

    def states(array):
        return Part(array, 0)

    def to_peers(array, away, backward):
        pairs = [(z, z + away) for z in range(head_count - away) if z % devices + away < devices]
        if backward:
            pairs = [(b, a) for a, b in pairs]
        return lax.ppermute(array, "head", pairs)

    def exchanged(slices):
        return lax.all_to_all(slices, AXES, split_axis=0, concat_axis=0, tiled=True)

    def scanned(sums, backward, after=()):
        height = heads * DH // total
        slices = exchanged(sums.reshape(total, height, DH))
        slices, token = call(
            functools.partial(scan_body, rows=rows, backward=backward),
            "scan",
            [lengths],
            [Part(slices, near=True)],
            [Part(shape(slices.shape, BF), 1), token_part],
            heads,
            2 if height % 32 == 0 else 1,
            after=after,
            limit=SOME_BYTES,
        )
        return slices, token

    gain_row = Part(gain.reshape(1, width))
    sum_kv, *later = call(
        state_body,
        "states",
        scalars,
        [wide(keys), wide(values)],
        [states(state)] * (1 + blocks * peers),
        heads,
        chunks,
        flops=unit,
    )
    from_peers = [to_peers(x, 1 + at % peers, False) for at, x in enumerate(later)]
    slices, token = scanned(sum_kv, False)
    (raw_inner,) = call(
        inner_body,
        "inner",
        scalars,
        [wide(queries), wide(keys), wide(values)],
        [wide(partial)],
        heads,
        chunks,
        square,
        flops=LONG,
        after=[token, *from_peers[:peers]],
    )
    kv_state = exchanged(slices).reshape(heads, DH, DH)

    scales, raws, grads, updates, back = [], [], [], [], []
    for b in range(blocks):
        ends = [states(state)] if b == blocks - 1 and blocks > 1 else []
        scale, raw, grad, update, *sums = call(
            functools.partial(norm_body, rows=rows, block=b, peers=peers),
            "norm",
            scalars,
            [
                gain_row,
                wide(queries, b),
                wide(raw_inner, b),
                wide(grad_out, b),
                states(kv_state),
                *[states(x) for x in from_peers[b * peers : (b + 1) * peers]],
                *[states(w) for w in (updates if ends else [])],
            ],
            [Part(shape((BLOCK, DH), F32)), wide(block_tokens), wide(block_tokens), states(state), *ends],
            heads,
            chunks,
            flops=LONG if b > 0 else 2 * unit // blocks,
        )
        scales.append(scale)
        raws.append(raw)
        grads.append(grad)
        updates.append(update)
        back += [to_peers(update, away, True) for away in range(1, devices)]
    output, grad_q, token = call(
        functools.partial(query_grads_body, peers=peers),
        "query_grads",
        scalars,
        [
            gain_row,
            wide(keys),
            wide(values),
            states(kv_state),
            *[wide(d) for d in grads],
            *[wide(r) for r in raws],
            *[Part(s) for s in scales],
            *[states(x) for x in from_peers],
        ],
        [wide(tokens), wide(tokens), token_part],
        heads,
        chunks,
        square,
        flops=LONG,
        after=back[:peers],
    )
    slices, token = scanned(sums[0] if sums else updates[0], True, [token])
    part_k, part_v = call(
        functools.partial(key_grads_body, peers=peers),
        "key_grads",
        scalars,
        [
            wide(queries),
            wide(keys),
            wide(values),
            *[wide(d) for d in grads],
            *[states(w) for w in back],
        ],
        [wide(partial), wide(partial)],
        heads,
        chunks,
        square,
        flops=LONG,
        after=[token],
    )
    grad_state = exchanged(slices).reshape(heads, DH, DH)
    grad_k, grad_v = call(
        last_body,
        "last",
        scalars,
        [wide(keys), wide(values), wide(part_k), wide(part_v), states(grad_state)],
        [wide(tokens), wide(tokens)],
        heads,
        chunks,
        flops=2 * unit,
    )
    return output, grad_q, grad_k, grad_v


def solution(mesh):
    tokens = P(AXES, None)
    return jax.shard_map(
        local,
        mesh=mesh,
        in_specs=(tokens, tokens, tokens, tokens, P(), P(), P("ctx", None)),
        out_specs=(tokens, tokens, tokens, tokens),
        check_vma=False,
    )
```

```python
import functools

import jax
import jax.numpy as jnp
from jax import lax
from jax.experimental import pallas as pl
from jax.experimental.pallas import tpu as pltpu
from jax.sharding import PartitionSpec as P

DH = 128
GROUP = 512
BLOCK = 128
CHUNKS = 4
LONG = 400_000_000_000
VMEM_BYTES = 60 * 1024 * 1024
NARROW_BYTES = 53 * 1024 * 1024
SOME_BYTES = 24 * 1024 * 1024

eps_norm = 1e-06
BF = jnp.bfloat16
F32 = jnp.float32
AXES = ("ctx", "head")

NN = (((1,), (0,)), ((), ()))
NT = (((1,), (1,)), ((), ()))
TN = (((0,), (0,)), ((), ()))


def dot(a, b, dims):
    return lax.dot_general(a, b, dims, preferred_element_type=F32)


def bounds_of(len_ref):
    bounds, total = [], None
    for k in range(len_ref.shape[0] - 1):
        total = len_ref[k] if total is None else total + len_ref[k]
        bounds.append(total)
    return bounds


def segment(position, bounds):
    result = (position >= bounds[0]).astype(jnp.int32)
    for bound in bounds[1:]:
        result = result + (position >= bound).astype(jnp.int32)
    return result


def same(a, b):
    return (a == b).astype(F32)


class Place:
    def __init__(self, len_ref, rows, mask_ref=None):
        self.rows = rows
        self.blocks = rows // BLOCK
        self.devices = GROUP // rows
        self.bounds = bounds_of(len_ref)
        spot = lax.axis_index("head")
        index = lax.axis_index("ctx") * lax.axis_size("head") + spot
        self.first = index * rows
        self.part = lax.rem(spot, self.devices)
        self.group = lax.div(spot, self.devices)
        self.group_first = self.first - self.part * rows
        self.mask_ref = mask_ref

    def seg(self, position):
        return segment(position, self.bounds)

    def start(self, block):
        return self.first + block * BLOCK

    def row_segments(self, block):
        rows = lax.broadcasted_iota(jnp.int32, (BLOCK, 1), 0)
        return self.seg(rows + self.start(block))

    def pair(self, i, j):
        slot = jnp.clip(lax.div(i * (i - 1), 2) + j, 0, self.mask_ref.shape[1] - 1)
        return self.mask_ref[self.group, slot].astype(F32)

    def weights(self):
        rows = self.rows
        t = lax.broadcasted_iota(jnp.int32, (rows, rows), 0)
        s = lax.broadcasted_iota(jnp.int32, (rows, rows), 1)
        keep = (s <= t) & (self.seg(t + self.first) == self.seg(s + self.first))
        result = jnp.where(keep, 1.0, 0.0)
        for i in range(1, self.blocks):
            for j in range(i):
                bit = self.pair(self.part * self.blocks + i, self.part * self.blocks + j)
                inside = (
                    (t >= i * BLOCK)
                    & (t < (i + 1) * BLOCK)
                    & (s >= j * BLOCK)
                    & (s < (j + 1) * BLOCK)
                )
                result = jnp.where(inside, result * bit, result)
        return result

    def to_later(self, away, block):
        there = (self.part + away) * self.blocks + block
        edge = self.seg(self.start(block) + away * self.rows - 1)
        return [
            self.pair(there, self.part * self.blocks + j) * same(self.seg(self.start(j + 1) - 1), edge)
            for j in range(self.blocks)
        ]

    def before(self, block):
        edge = self.seg(self.start(block) - 1)
        carried = same(self.seg(self.group_first - 1), edge)
        peers = [(self.part >= away).astype(F32) for away in range(1, self.devices)]
        return carried, peers, (self.row_segments(block) == edge).astype(F32)

    def after(self, block):
        own = self.part * self.blocks + block
        edge = self.seg(self.start(block + 1))
        carried = same(self.seg(self.group_first + GROUP), edge)
        peers = []
        for i in range(self.blocks):
            for away in range(1, self.devices):
                there = (self.part + away < self.devices).astype(F32)
                other = (self.part + away) * self.blocks + i
                start = self.start(i) + away * self.rows
                peers.append(self.pair(other, own) * same(self.seg(start), edge) * there)
        return carried, peers, (self.row_segments(block) == edge).astype(F32)


def mixed(refs, factors, head):
    total = refs[0][head].astype(F32) * factors[0]
    for ref, factor in zip(refs[1:], factors[1:], strict=True):
        total = total + ref[head].astype(F32) * factor
    return total.astype(BF)


def columns(head):
    return pl.ds(head * DH, DH)


def rows_of(block):
    return pl.ds(block * BLOCK, BLOCK)


def state_body(place_of, ins, outs, scratch, arrive, leave, chunks):
    k_ref, v_ref = ins
    rows, width = k_ref.shape
    place = place_of(rows)
    last = place.seg(place.start(place.blocks) - 1)
    ends = [place.seg(place.start(b + 1) - 1) for b in range(place.blocks)]
    masks = [(place.row_segments(b) == ends[b]).astype(BF) for b in range(place.blocks)]
    wanted = [[same(e, last) for e in ends]]
    for b in range(place.blocks):
        for away in range(1, place.devices):
            wanted.append(place.to_later(away, b))
    for c, heads in enumerate(chunks):
        arrive(c)
        for head in heads:
            updates = []
            for b in range(place.blocks):
                k = k_ref[rows_of(b), columns(head)] * masks[b]
                updates.append(dot(k, v_ref[rows_of(b), columns(head)], TN))
            for ref, factors in zip(outs, wanted, strict=True):
                total = updates[0] * factors[0]
                for update, factor in zip(updates[1:], factors[1:], strict=True):
                    total = total + update * factor
                ref[head] = total.astype(BF)
        leave(c)


def inner_body(place_of, ins, outs, scratch, arrive, leave, chunks):
    q_ref, k_ref, v_ref = ins
    (raw_ref,), (weight_ref,) = outs, scratch
    weight_ref[...] = place_of(q_ref.shape[0]).weights()
    for c, heads in enumerate(chunks):
        arrive(c)
        for head in heads:
            at = columns(head)
            probs = (dot(q_ref[:, at], k_ref[:, at], NT) * weight_ref[...]).astype(BF)
            raw_ref[:, at] = dot(probs, v_ref[:, at], NN)
        leave(c)


def scan_body(place_of, ins, outs, scratch, arrive, leave, chunks, *, rows, backward):
    (t_ref,), (out_ref, token_ref) = ins, outs
    token_ref[...] = jnp.zeros_like(token_ref)
    count, height, _ = t_ref.shape
    devices = GROUP // rows
    bounds = place_of(rows).bounds
    part = height // len(chunks)
    for c in range(len(chunks)):
        arrive(c)
        at = pl.ds(c * part, part)

        def one(turn, acc):
            group = count // devices - 1 - turn if backward else turn
            for k in range(devices):
                out_ref[group * devices + k, at] = acc.astype(BF)
            for k in range(devices):
                index = group * devices + (devices - 1 - k if backward else k)
                first = index * rows
                if backward:
                    keep = same(segment(first, bounds), segment(first + rows, bounds))
                else:
                    keep = same(segment(first - 1, bounds), segment(first + rows - 1, bounds))
                acc = acc * keep + t_ref[index, at].astype(F32)
            return acc

        acc = jnp.zeros((part, DH), F32)
        if count <= 32:
            for turn in range(count // devices):
                acc = one(turn, acc)
        else:
            lax.fori_loop(0, count // devices, one, acc)
        leave(c)


def norm_body(place_of, ins, outs, scratch, arrive, leave, chunks, *, rows, block, peers):
    gain_ref, q_ref, raw_ref, grad_ref = ins[:4]
    state_refs, earlier_refs = ins[4 : 5 + peers], ins[5 + peers :]
    scale_ref, held_ref, d_ref, w_ref, *t_refs = outs
    width = q_ref.shape[1]
    place = place_of(rows)
    carried, there, reach = place.before(block)
    squares = cross = jnp.zeros((BLOCK, DH), F32)
    for c, heads in enumerate(chunks):
        arrive(c)
        for head in heads:
            at = columns(head)
            state = mixed(state_refs, [carried, *there], head)
            raw = raw_ref[:, at] + dot(q_ref[:, at], state, NN) * reach
            raw = raw.astype(BF)
            held_ref[:, at] = raw
            raw = raw.astype(F32)
            scaled = grad_ref[:, at].astype(F32) * gain_ref[:, at]
            squares = squares + raw * raw
            cross = cross + scaled * raw
        leave(c, [1])
    total = jnp.sum(squares, axis=1, keepdims=True)
    inverse = 1.0 / jnp.sqrt(total / width + eps_norm)
    mean = jnp.sum(cross, axis=1, keepdims=True) * inverse / width
    scale_ref[...] = jnp.broadcast_to(inverse, scale_ref.shape)
    leave(0, [0])
    own = place.seg(place.start(block))
    begin = (place.row_segments(block) == own).astype(BF)
    into = [same(place.seg(place.start(b)), place.seg(place.first)) for b in range(block + 1)]
    for c, heads in enumerate(chunks):
        for head in heads:
            at = columns(head)
            normed = held_ref[:, at].astype(F32) * inverse
            scaled = grad_ref[:, at].astype(F32) * gain_ref[:, at]
            grad = ((scaled - normed * mean) * inverse).astype(BF)
            d_ref[:, at] = grad
            update = dot(q_ref[:, at] * begin, grad, TN)
            w_ref[head] = update.astype(BF)
            for t_ref in t_refs:
                sums = update * into[block]
                for ref, factor in zip(earlier_refs, into[:block], strict=True):
                    sums = sums + ref[head].astype(F32) * factor
                t_ref[head] = sums.astype(BF)
        leave(c, range(2, len(outs)))


def query_grads_body(place_of, ins, outs, scratch, arrive, leave, chunks, *, peers):
    gain_ref, k_ref, v_ref, kv_ref = ins[:4]
    rows, width = k_ref.shape
    place = place_of(rows)
    blocks = place.blocks
    rest = ins[4:]
    d_refs, raw_refs, scale_refs = rest[:blocks], rest[blocks : 2 * blocks], rest[2 * blocks : 3 * blocks]
    peer_refs = rest[3 * blocks :]
    out_ref, gq_ref, token_ref = outs
    (weight_ref,) = scratch
    token_ref[...] = jnp.zeros_like(token_ref)
    weight_ref[...] = place.weights()
    factors = [place.before(b) for b in range(blocks)]
    for c, heads in enumerate(chunks):
        arrive(c)
        for head in heads:
            at = columns(head)
            d = jnp.concatenate([ref[:, at] for ref in d_refs], axis=0)
            grad_probs = (dot(d, v_ref[:, at], NT) * weight_ref[...]).astype(BF)
            inner = dot(grad_probs, k_ref[:, at], NN)
            for b in range(blocks):
                carried, there, _ = factors[b]
                state = mixed([kv_ref, *peer_refs[b * peers : (b + 1) * peers]], [carried, *there], head)
                outer = dot(d_refs[b][:, at], state, NT) * factors[b][2]
                part = inner[b * BLOCK : (b + 1) * BLOCK] + outer
                gq_ref[rows_of(b), at] = part.astype(BF)
                normed = raw_refs[b][:, at].astype(F32) * scale_refs[b][...]
                out_ref[rows_of(b), at] = (normed * gain_ref[:, at]).astype(BF)
        leave(c)


def key_grads_body(place_of, ins, outs, scratch, arrive, leave, chunks, *, peers):
    q_ref, k_ref, v_ref, *rest = ins
    place = place_of(q_ref.shape[0])
    blocks = place.blocks
    d_refs, w_refs = rest[:blocks], rest[blocks:]
    gk_ref, gv_ref = outs
    (weight_ref,) = scratch
    weight_ref[...] = place.weights()
    factors = [place.after(b) for b in range(blocks)]
    for c, heads in enumerate(chunks):
        arrive(c)
        for head in heads:
            at = columns(head)
            q, d = q_ref[:, at], jnp.concatenate([ref[:, at] for ref in d_refs], axis=0)
            probs = (dot(q, k_ref[:, at], NT) * weight_ref[...]).astype(BF)
            grad_probs = (dot(d, v_ref[:, at], NT) * weight_ref[...]).astype(BF)
            gk = dot(grad_probs, q, TN)
            gv = dot(probs, d, TN)
            for b in range(blocks):
                at_rows, here = rows_of(b), slice(b * BLOCK, (b + 1) * BLOCK)
                part_k, part_v = gk[here], gv[here]
                if peers:
                    state = mixed(w_refs, factors[b][1], head)
                    part_k = part_k + dot(v_ref[at_rows, at], state, NT) * factors[b][2]
                    part_v = part_v + dot(k_ref[at_rows, at], state, NN) * factors[b][2]
                gk_ref[at_rows, at] = part_k
                gv_ref[at_rows, at] = part_v
        leave(c)


def last_body(place_of, ins, outs, scratch, arrive, leave, chunks):
    k_ref, v_ref, gk_in, gv_in, gs_ref = ins
    gk_ref, gv_ref = outs
    place = place_of(k_ref.shape[0])
    factors = [place.after(b) for b in range(place.blocks)]
    reach = jnp.concatenate([reach * carried for carried, _, reach in factors], axis=0)
    for c, heads in enumerate(chunks):
        arrive(c)
        for head in heads:
            at = columns(head)
            gk = gk_in[:, at] + dot(v_ref[:, at], gs_ref[head], NT) * reach
            gv = gv_in[:, at] + dot(k_ref[:, at], gs_ref[head], NN) * reach
            gk_ref[:, at] = gk.astype(BF)
            gv_ref[:, at] = gv.astype(BF)
        leave(c)


class Part:
    def __init__(self, array, axis=None, block=None, near=False):
        self.array, self.axis, self.block, self.near = array, axis, block, near
        self.shape = array.shape if block is None else (BLOCK, *array.shape[1:])
        self.spec = pl.BlockSpec(memory_space=pltpu.VMEM if near else pltpu.HBM)

    def pieces(self, far, near, sems, count):
        far = far if self.block is None else far.at[rows_of(self.block)]
        if self.axis is None:
            return [(far, near, sems.at[0])]
        size = self.shape[self.axis] // count
        result = []
        for c in range(count):
            at = [slice(None)] * len(self.shape)
            at[self.axis] = pl.ds(c * size, size)
            result.append((far.at[tuple(at)], near.at[tuple(at)], sems.at[c]))
        return result


def call(body, name, scalars, ins, outs, heads, chunks, scratch=(), flops=0, after=(), limit=VMEM_BYTES):
    far = [p for p in (*ins, *outs) if not p.near]
    sizes = (len(scalars), len(ins), len(after), len(outs), len(far), 2, len(scratch))

    def kernel(*refs):
        split, at = [], 0
        for size in sizes:
            split.append(refs[at : at + size])
            at += size
        settings, in_refs, _, out_refs, buffers, (in_sems, out_sems), rest = split
        buffers = iter(buffers)

        def opened(parts, given, sems):
            refs, pieces = [], []
            for i, (part, ref) in enumerate(zip(parts, given, strict=True)):
                refs.append(ref if part.near else next(buffers))
                pieces.append([] if part.near else part.pieces(ref, refs[-1], sems.at[i], chunks))
            return refs, pieces

        near_in, coming = opened(ins, in_refs, in_sems)
        near_out, going = opened(outs, out_refs, out_sems)

        def copies(parts, c, which=None):
            for i, pieces in enumerate(parts):
                if c < len(pieces) and (which is None or i in which):
                    yield pieces[c]

        def arrive(c):
            for far, near, sem in copies(coming, c):
                pltpu.make_async_copy(far, near, sem).wait()

        def leave(c, which=None):
            for far, near, sem in copies(going, c, which):
                pltpu.make_async_copy(near, far, sem).start()

        for c in range(chunks):
            for far, near, sem in copies(coming, c):
                pltpu.make_async_copy(far, near, sem).start()
        each = heads // chunks
        turns = [range(c * each, (c + 1) * each) for c in range(chunks)]
        place_of = lambda rows: Place(settings[0], rows, *settings[1:])
        body(place_of, near_in, near_out, rest, arrive, leave, turns)
        for c in range(chunks):
            for far, near, sem in copies(going, c):
                pltpu.make_async_copy(near, far, sem).wait()

    anywhere = pl.BlockSpec(memory_space=pl.ANY)
    return pl.pallas_call(
        kernel,
        name=name,
        in_specs=[
            *[pl.BlockSpec(memory_space=pltpu.SMEM)] * len(scalars),
            *[p.spec for p in ins],
            *[anywhere] * len(after),
        ],
        out_specs=[p.spec for p in outs],
        out_shape=[p.array for p in outs],
        scratch_shapes=[
            *[pltpu.VMEM(p.shape, p.array.dtype) for p in far],
            pltpu.SemaphoreType.DMA((len(ins), chunks)),
            pltpu.SemaphoreType.DMA((len(outs), chunks)),
            *scratch,
        ],
        compiler_params=pltpu.CompilerParams(vmem_limit_bytes=limit),
        cost_estimate=pl.CostEstimate(
            flops=flops,
            bytes_accessed=sum(p.array.size * p.array.dtype.itemsize for p in (*ins, *outs)),
            transcendentals=0,
        ),
    )(*scalars, *[p.array for p in ins], *after)


def local(queries, keys, values, grad_out, gain, lengths, block_mask):
    rows, width = queries.shape
    heads = width // DH
    blocks = rows // BLOCK
    devices = GROUP // rows
    peers = devices - 1
    head_count = lax.axis_size("head")
    total = lax.axis_size("ctx") * head_count
    chunks = CHUNKS if heads % CHUNKS == 0 else 1
    shape = jax.ShapeDtypeStruct
    state = shape((heads, DH, DH), BF)
    tokens = shape((rows, width), BF)
    partial = shape((rows, width), F32)
    block_tokens = shape((BLOCK, width), BF)
    square = [pltpu.VMEM((rows, rows), F32)]
    unit = 2 * rows * width * DH
    inner = 2 * rows * rows * width
    scalars = [lengths, block_mask]
    token_part = Part(shape((8, DH), F32), near=True)

    def wide(array, block=None):
        return Part(array, 1, block)

    def states(array):
        return Part(array, 0)

    def to_peers(array, away, backward):
        pairs = [(z, z + away) for z in range(head_count - away) if z % devices + away < devices]
        if backward:
            pairs = [(b, a) for a, b in pairs]
        return lax.ppermute(array, "head", pairs)

    def exchanged(slices):
        return lax.all_to_all(slices, AXES, split_axis=0, concat_axis=0, tiled=True)

    def scanned(sums, backward, after=()):
        height = heads * DH // total
        slices = exchanged(sums.reshape(total, height, DH))
        slices, token = call(
            functools.partial(scan_body, rows=rows, backward=backward),
            "scan",
            [lengths],
            [Part(slices, near=True)],
            [Part(shape(slices.shape, BF), 1), token_part],
            heads,
            2 if height % 32 == 0 else 1,
            after=after,
            limit=SOME_BYTES,
        )
        return slices, token

    gain_row = Part(gain.reshape(1, width))
    sum_kv, *later = call(
        state_body,
        "states",
        scalars,
        [wide(keys), wide(values)],
        [states(state)] * (1 + blocks * peers),
        heads,
        chunks,
        flops=unit,
    )
    from_peers = [to_peers(x, 1 + at % peers, False) for at, x in enumerate(later)]
    slices, token = scanned(sum_kv, False)
    (raw_inner,) = call(
        inner_body,
        "inner",
        scalars,
        [wide(queries), wide(keys), wide(values)],
        [wide(partial)],
        heads,
        chunks,
        square,
        flops=LONG,
        after=[token, *from_peers[:peers]],
    )
    kv_state = exchanged(slices).reshape(heads, DH, DH)

    scales, raws, grads, updates, back = [], [], [], [], []
    for b in range(blocks):
        ends = [states(state)] if b == blocks - 1 and blocks > 1 else []
        scale, raw, grad, update, *sums = call(
            functools.partial(norm_body, rows=rows, block=b, peers=peers),
            "norm",
            scalars,
            [
                gain_row,
                wide(queries, b),
                wide(raw_inner, b),
                wide(grad_out, b),
                states(kv_state),
                *[states(x) for x in from_peers[b * peers : (b + 1) * peers]],
                *[states(w) for w in (updates if ends else [])],
            ],
            [Part(shape((BLOCK, DH), F32)), wide(block_tokens), wide(block_tokens), states(state), *ends],
            heads,
            chunks,
            flops=LONG if b > 0 else 2 * unit // blocks,
        )
        scales.append(scale)
        raws.append(raw)
        grads.append(grad)
        updates.append(update)
        back += [to_peers(update, away, True) for away in range(1, devices)]
    output, grad_q, token = call(
        functools.partial(query_grads_body, peers=peers),
        "query_grads",
        scalars,
        [
            gain_row,
            wide(keys),
            wide(values),
            states(kv_state),
            *[wide(d) for d in grads],
            *[wide(r) for r in raws],
            *[Part(s) for s in scales],
            *[states(x) for x in from_peers],
        ],
        [wide(tokens), wide(tokens), token_part],
        heads,
        chunks,
        square,
        flops=LONG,
        after=back[:peers],
    )
    slices, token = scanned(sums[0] if sums else updates[0], True, [token])
    part_k, part_v = call(
        functools.partial(key_grads_body, peers=peers),
        "key_grads",
        scalars,
        [
            wide(queries),
            wide(keys),
            wide(values),
            *[wide(d) for d in grads],
            *[states(w) for w in back],
        ],
        [wide(partial), wide(partial)],
        heads,
        chunks,
        square,
        flops=LONG,
        after=[token],
    )
    grad_state = exchanged(slices).reshape(heads, DH, DH)
    grad_k, grad_v = call(
        last_body,
        "last",
        scalars,
        [wide(keys), wide(values), wide(part_k), wide(part_v), states(grad_state)],
        [wide(tokens), wide(tokens)],
        heads,
        chunks,
        flops=2 * unit,
        limit=NARROW_BYTES,
    )
    return output, grad_q, grad_k, grad_v


def solution(mesh):
    tokens = P(AXES, None)
    return jax.shard_map(
        local,
        mesh=mesh,
        in_specs=(tokens, tokens, tokens, tokens, P(), P(), P("ctx", None)),
        out_specs=(tokens, tokens, tokens, tokens),
        check_vma=False,
    )
```

```python
import functools

import jax
import jax.numpy as jnp
from jax import lax
from jax.experimental import pallas as pl
from jax.experimental.pallas import tpu as pltpu
from jax.sharding import PartitionSpec as P

DH = 128
GROUP = 512
BLOCK = 128
CHUNKS = 4
LONG = 400_000_000_000
VMEM_BYTES = 60 * 1024 * 1024
NARROW_BYTES = 53 * 1024 * 1024
SOME_BYTES = 24 * 1024 * 1024

eps_norm = 1e-06
BF = jnp.bfloat16
F32 = jnp.float32
AXES = ("ctx", "head")

NN = (((1,), (0,)), ((), ()))
NT = (((1,), (1,)), ((), ()))
TN = (((0,), (0,)), ((), ()))


def dot(a, b, dims):
    return lax.dot_general(a, b, dims, preferred_element_type=F32)


def bounds_of(len_ref):
    bounds, total = [], None
    for k in range(len_ref.shape[0] - 1):
        total = len_ref[k] if total is None else total + len_ref[k]
        bounds.append(total)
    return bounds


def segment(position, bounds):
    result = (position >= bounds[0]).astype(jnp.int32)
    for bound in bounds[1:]:
        result = result + (position >= bound).astype(jnp.int32)
    return result


def same(a, b):
    return (a == b).astype(F32)


class Place:
    def __init__(self, len_ref, rows, mask_ref=None):
        self.rows = rows
        self.blocks = rows // BLOCK
        self.devices = GROUP // rows
        self.bounds = bounds_of(len_ref)
        spot = lax.axis_index("head")
        index = lax.axis_index("ctx") * lax.axis_size("head") + spot
        self.first = index * rows
        self.part = lax.rem(spot, self.devices)
        self.group = lax.div(spot, self.devices)
        self.group_first = self.first - self.part * rows
        self.mask_ref = mask_ref

    def seg(self, position):
        return segment(position, self.bounds)

    def start(self, block):
        return self.first + block * BLOCK

    def row_segments(self, block):
        rows = lax.broadcasted_iota(jnp.int32, (BLOCK, 1), 0)
        return self.seg(rows + self.start(block))

    def pair(self, i, j):
        slot = jnp.clip(lax.div(i * (i - 1), 2) + j, 0, self.mask_ref.shape[1] - 1)
        return self.mask_ref[self.group, slot].astype(F32)

    def weights(self):
        rows = self.rows
        t = lax.broadcasted_iota(jnp.int32, (rows, rows), 0)
        s = lax.broadcasted_iota(jnp.int32, (rows, rows), 1)
        keep = (s <= t) & (self.seg(t + self.first) == self.seg(s + self.first))
        result = jnp.where(keep, 1.0, 0.0)
        for i in range(1, self.blocks):
            for j in range(i):
                bit = self.pair(self.part * self.blocks + i, self.part * self.blocks + j)
                inside = (
                    (t >= i * BLOCK)
                    & (t < (i + 1) * BLOCK)
                    & (s >= j * BLOCK)
                    & (s < (j + 1) * BLOCK)
                )
                result = jnp.where(inside, result * bit, result)
        return result

    def to_later(self, away, block):
        there = (self.part + away) * self.blocks + block
        edge = self.seg(self.start(block) + away * self.rows - 1)
        return [
            self.pair(there, self.part * self.blocks + j) * same(self.seg(self.start(j + 1) - 1), edge)
            for j in range(self.blocks)
        ]

    def before(self, block):
        edge = self.seg(self.start(block) - 1)
        carried = same(self.seg(self.group_first - 1), edge)
        peers = [(self.part >= away).astype(F32) for away in range(1, self.devices)]
        return carried, peers, (self.row_segments(block) == edge).astype(F32)

    def after(self, block):
        own = self.part * self.blocks + block
        edge = self.seg(self.start(block + 1))
        carried = same(self.seg(self.group_first + GROUP), edge)
        peers = []
        for i in range(self.blocks):
            for away in range(1, self.devices):
                there = (self.part + away < self.devices).astype(F32)
                other = (self.part + away) * self.blocks + i
                start = self.start(i) + away * self.rows
                peers.append(self.pair(other, own) * same(self.seg(start), edge) * there)
        return carried, peers, (self.row_segments(block) == edge).astype(F32)


def mixed(refs, factors, head):
    total = refs[0][head].astype(F32) * factors[0]
    for ref, factor in zip(refs[1:], factors[1:], strict=True):
        total = total + ref[head].astype(F32) * factor
    return total.astype(BF)


class Joined:
    def __init__(self, refs):
        self.refs, self.each = refs, refs[0].shape[0]

    def __getitem__(self, head):
        return self.refs[head // self.each][head % self.each]

    def __setitem__(self, head, value):
        self.refs[head // self.each][head % self.each] = value


def joined(refs, counts):
    result, at = [], 0
    for count in counts:
        result.append(Joined(refs[at : at + count]))
        at += count
    return result


def columns(head):
    return pl.ds(head * DH, DH)


def rows_of(block):
    return pl.ds(block * BLOCK, BLOCK)


def state_body(place_of, ins, outs, scratch, arrive, leave, chunks, *, counts):
    k_ref, v_ref = ins
    outs = joined(outs, counts)
    rows, width = k_ref.shape
    place = place_of(rows)
    last = place.seg(place.start(place.blocks) - 1)
    ends = [place.seg(place.start(b + 1) - 1) for b in range(place.blocks)]
    masks = [(place.row_segments(b) == ends[b]).astype(BF) for b in range(place.blocks)]
    wanted = [[same(e, last) for e in ends]]
    for b in range(place.blocks):
        for away in range(1, place.devices):
            wanted.append(place.to_later(away, b))
    for c, heads in enumerate(chunks):
        arrive(c)
        for head in heads:
            updates = []
            for b in range(place.blocks):
                k = k_ref[rows_of(b), columns(head)] * masks[b]
                updates.append(dot(k, v_ref[rows_of(b), columns(head)], TN))
            for ref, factors in zip(outs, wanted, strict=True):
                total = updates[0] * factors[0]
                for update, factor in zip(updates[1:], factors[1:], strict=True):
                    total = total + update * factor
                ref[head] = total.astype(BF)
        leave(c)


def inner_body(place_of, ins, outs, scratch, arrive, leave, chunks):
    q_ref, k_ref, v_ref = ins
    (raw_ref,), (weight_ref,) = outs, scratch
    weight_ref[...] = place_of(q_ref.shape[0]).weights()
    for c, heads in enumerate(chunks):
        arrive(c)
        for head in heads:
            at = columns(head)
            probs = (dot(q_ref[:, at], k_ref[:, at], NT) * weight_ref[...]).astype(BF)
            raw_ref[:, at] = dot(probs, v_ref[:, at], NN)
        leave(c)


def scan_body(place_of, ins, outs, scratch, arrive, leave, chunks, *, rows, backward):
    (t_ref,), (out_ref, token_ref) = ins, outs
    token_ref[...] = jnp.zeros_like(token_ref)
    count, height, _ = t_ref.shape
    devices = GROUP // rows
    bounds = place_of(rows).bounds
    part = height // len(chunks)
    for c in range(len(chunks)):
        arrive(c)
        at = pl.ds(c * part, part)

        def one(turn, acc):
            group = count // devices - 1 - turn if backward else turn
            for k in range(devices):
                out_ref[group * devices + k, at] = acc.astype(BF)
            for k in range(devices):
                index = group * devices + (devices - 1 - k if backward else k)
                first = index * rows
                if backward:
                    keep = same(segment(first, bounds), segment(first + rows, bounds))
                else:
                    keep = same(segment(first - 1, bounds), segment(first + rows - 1, bounds))
                acc = acc * keep + t_ref[index, at].astype(F32)
            return acc

        acc = jnp.zeros((part, DH), F32)
        if count <= 32:
            for turn in range(count // devices):
                acc = one(turn, acc)
        else:
            lax.fori_loop(0, count // devices, one, acc)
        leave(c)


def norm_body(place_of, ins, outs, scratch, arrive, leave, chunks, *, rows, block, counts):
    gain_ref, q_ref, raw_ref, grad_ref = ins[:4]
    held = 4 + sum(counts)
    state_refs, earlier_refs = joined(ins[4:held], counts), ins[held:]
    scale_ref, held_ref, d_ref, w_ref, *t_refs = outs
    width = q_ref.shape[1]
    place = place_of(rows)
    carried, there, reach = place.before(block)
    squares = cross = jnp.zeros((BLOCK, DH), F32)
    for c, heads in enumerate(chunks):
        arrive(c)
        for head in heads:
            at = columns(head)
            state = mixed(state_refs, [carried, *there], head)
            raw = raw_ref[:, at] + dot(q_ref[:, at], state, NN) * reach
            raw = raw.astype(BF)
            held_ref[:, at] = raw
            raw = raw.astype(F32)
            scaled = grad_ref[:, at].astype(F32) * gain_ref[:, at]
            squares = squares + raw * raw
            cross = cross + scaled * raw
        leave(c, [1])
    total = jnp.sum(squares, axis=1, keepdims=True)
    inverse = 1.0 / jnp.sqrt(total / width + eps_norm)
    mean = jnp.sum(cross, axis=1, keepdims=True) * inverse / width
    scale_ref[...] = jnp.broadcast_to(inverse, scale_ref.shape)
    leave(0, [0])
    own = place.seg(place.start(block))
    begin = (place.row_segments(block) == own).astype(BF)
    into = [same(place.seg(place.start(b)), place.seg(place.first)) for b in range(block + 1)]
    for c, heads in enumerate(chunks):
        for head in heads:
            at = columns(head)
            normed = held_ref[:, at].astype(F32) * inverse
            scaled = grad_ref[:, at].astype(F32) * gain_ref[:, at]
            grad = ((scaled - normed * mean) * inverse).astype(BF)
            d_ref[:, at] = grad
            update = dot(q_ref[:, at] * begin, grad, TN)
            w_ref[head] = update.astype(BF)
            for t_ref in t_refs:
                sums = update * into[block]
                for ref, factor in zip(earlier_refs, into[:block], strict=True):
                    sums = sums + ref[head].astype(F32) * factor
                t_ref[head] = sums.astype(BF)
        leave(c, range(2, len(outs)))


def query_grads_body(place_of, ins, outs, scratch, arrive, leave, chunks, *, peers, counts):
    gain_ref, k_ref, v_ref, kv_ref = ins[:4]
    rows, width = k_ref.shape
    place = place_of(rows)
    blocks = place.blocks
    rest = ins[4:]
    d_refs, raw_refs, scale_refs = rest[:blocks], rest[blocks : 2 * blocks], rest[2 * blocks : 3 * blocks]
    peer_refs = joined(rest[3 * blocks :], counts)
    out_ref, gq_ref, token_ref = outs
    (weight_ref,) = scratch
    token_ref[...] = jnp.zeros_like(token_ref)
    weight_ref[...] = place.weights()
    factors = [place.before(b) for b in range(blocks)]
    for c, heads in enumerate(chunks):
        arrive(c)
        for head in heads:
            at = columns(head)
            d = jnp.concatenate([ref[:, at] for ref in d_refs], axis=0)
            grad_probs = (dot(d, v_ref[:, at], NT) * weight_ref[...]).astype(BF)
            inner = dot(grad_probs, k_ref[:, at], NN)
            for b in range(blocks):
                carried, there, _ = factors[b]
                state = mixed([kv_ref, *peer_refs[b * peers : (b + 1) * peers]], [carried, *there], head)
                outer = dot(d_refs[b][:, at], state, NT) * factors[b][2]
                part = inner[b * BLOCK : (b + 1) * BLOCK] + outer
                gq_ref[rows_of(b), at] = part.astype(BF)
                normed = raw_refs[b][:, at].astype(F32) * scale_refs[b][...]
                out_ref[rows_of(b), at] = (normed * gain_ref[:, at]).astype(BF)
        leave(c)


def key_grads_body(place_of, ins, outs, scratch, arrive, leave, chunks, *, peers):
    q_ref, k_ref, v_ref, *rest = ins
    place = place_of(q_ref.shape[0])
    blocks = place.blocks
    d_refs, w_refs = rest[:blocks], rest[blocks:]
    gk_ref, gv_ref = outs
    (weight_ref,) = scratch
    weight_ref[...] = place.weights()
    factors = [place.after(b) for b in range(blocks)]
    for c, heads in enumerate(chunks):
        arrive(c)
        for head in heads:
            at = columns(head)
            q, d = q_ref[:, at], jnp.concatenate([ref[:, at] for ref in d_refs], axis=0)
            probs = (dot(q, k_ref[:, at], NT) * weight_ref[...]).astype(BF)
            grad_probs = (dot(d, v_ref[:, at], NT) * weight_ref[...]).astype(BF)
            gk = dot(grad_probs, q, TN)
            gv = dot(probs, d, TN)
            for b in range(blocks):
                at_rows, here = rows_of(b), slice(b * BLOCK, (b + 1) * BLOCK)
                part_k, part_v = gk[here], gv[here]
                if peers:
                    state = mixed(w_refs, factors[b][1], head)
                    part_k = part_k + dot(v_ref[at_rows, at], state, NT) * factors[b][2]
                    part_v = part_v + dot(k_ref[at_rows, at], state, NN) * factors[b][2]
                gk_ref[at_rows, at] = part_k
                gv_ref[at_rows, at] = part_v
        leave(c)


def last_body(place_of, ins, outs, scratch, arrive, leave, chunks):
    k_ref, v_ref, gk_in, gv_in, gs_ref = ins
    gk_ref, gv_ref = outs
    place = place_of(k_ref.shape[0])
    factors = [place.after(b) for b in range(place.blocks)]
    reach = jnp.concatenate([reach * carried for carried, _, reach in factors], axis=0)
    for c, heads in enumerate(chunks):
        arrive(c)
        for head in heads:
            at = columns(head)
            gk = gk_in[:, at] + dot(v_ref[:, at], gs_ref[head], NT) * reach
            gv = gv_in[:, at] + dot(k_ref[:, at], gs_ref[head], NN) * reach
            gk_ref[:, at] = gk.astype(BF)
            gv_ref[:, at] = gv.astype(BF)
        leave(c)


class Part:
    def __init__(self, array, axis=None, block=None, near=False, lead=0, parts=None):
        self.array, self.axis, self.block, self.near = array, axis, block, near
        self.lead, self.parts = lead, parts
        self.shape = array.shape if block is None else (BLOCK, *array.shape[1:])
        self.spec = pl.BlockSpec(memory_space=pltpu.VMEM if near else pltpu.HBM)

    def pieces(self, far, near, sems, count):
        far = far if self.block is None else far.at[rows_of(self.block)]
        if self.axis is None:
            return [(far, near, sems.at[0])]
        count = self.parts or count
        size = self.shape[self.axis] // count
        result = [None] * self.lead
        for c in range(count):
            at = [slice(None)] * len(self.shape)
            at[self.axis] = pl.ds(c * size, size)
            result.append((far.at[tuple(at)], near.at[tuple(at)], sems.at[c]))
        return result


def call(body, name, scalars, ins, outs, heads, chunks, scratch=(), flops=0, after=(), limit=VMEM_BYTES):
    far = [p for p in (*ins, *outs) if not p.near]
    sizes = (len(scalars), len(ins), len(after), len(outs), len(far), 2, len(scratch))

    def kernel(*refs):
        split, at = [], 0
        for size in sizes:
            split.append(refs[at : at + size])
            at += size
        settings, in_refs, _, out_refs, buffers, (in_sems, out_sems), rest = split
        buffers = iter(buffers)

        def opened(parts, given, sems):
            refs, pieces = [], []
            for i, (part, ref) in enumerate(zip(parts, given, strict=True)):
                refs.append(ref if part.near else next(buffers))
                pieces.append([] if part.near else part.pieces(ref, refs[-1], sems.at[i], chunks))
            return refs, pieces

        near_in, coming = opened(ins, in_refs, in_sems)
        near_out, going = opened(outs, out_refs, out_sems)

        def copies(parts, c, which=None):
            for i, pieces in enumerate(parts):
                if c < len(pieces) and pieces[c] is not None and (which is None or i in which):
                    yield pieces[c]

        def arrive(c):
            for far, near, sem in copies(coming, c):
                pltpu.make_async_copy(far, near, sem).wait()

        def leave(c, which=None):
            for far, near, sem in copies(going, c, which):
                pltpu.make_async_copy(near, far, sem).start()

        for c in range(chunks):
            for far, near, sem in copies(coming, c):
                pltpu.make_async_copy(far, near, sem).start()
        each = heads // chunks
        turns = [range(c * each, (c + 1) * each) for c in range(chunks)]
        place_of = lambda rows: Place(settings[0], rows, *settings[1:])
        body(place_of, near_in, near_out, rest, arrive, leave, turns)
        for c in range(chunks):
            for far, near, sem in copies(going, c):
                pltpu.make_async_copy(near, far, sem).wait()

    anywhere = pl.BlockSpec(memory_space=pl.ANY)
    return pl.pallas_call(
        kernel,
        name=name,
        in_specs=[
            *[pl.BlockSpec(memory_space=pltpu.SMEM)] * len(scalars),
            *[p.spec for p in ins],
            *[anywhere] * len(after),
        ],
        out_specs=[p.spec for p in outs],
        out_shape=[p.array for p in outs],
        scratch_shapes=[
            *[pltpu.VMEM(p.shape, p.array.dtype) for p in far],
            pltpu.SemaphoreType.DMA((len(ins), chunks)),
            pltpu.SemaphoreType.DMA((len(outs), chunks)),
            *scratch,
        ],
        compiler_params=pltpu.CompilerParams(vmem_limit_bytes=limit),
        cost_estimate=pl.CostEstimate(
            flops=flops,
            bytes_accessed=sum(p.array.size * p.array.dtype.itemsize for p in (*ins, *outs)),
            transcendentals=0,
        ),
    )(*scalars, *[p.array for p in ins], *after)


def local(queries, keys, values, grad_out, gain, lengths, block_mask):
    rows, width = queries.shape
    heads = width // DH
    blocks = rows // BLOCK
    devices = GROUP // rows
    peers = devices - 1
    head_count = lax.axis_size("head")
    total = lax.axis_size("ctx") * head_count
    chunks = CHUNKS if heads % CHUNKS == 0 else 1
    shape = jax.ShapeDtypeStruct
    state = shape((heads, DH, DH), BF)
    tokens = shape((rows, width), BF)
    partial = shape((rows, width), F32)
    block_tokens = shape((BLOCK, width), BF)
    square = [pltpu.VMEM((rows, rows), F32)]
    unit = 2 * rows * width * DH
    inner = 2 * rows * rows * width
    scalars = [lengths, block_mask]
    token_part = Part(shape((8, DH), F32), near=True)

    def wide(array, block=None):
        return Part(array, 1, block)

    def states(array):
        return Part(array, 0)

    def split_states(arrays):
        count = chunks // len(arrays)
        return [Part(a, 0, lead=i * count, parts=count) for i, a in enumerate(arrays)]

    def to_peers(array, away, backward):
        pairs = [(z, z + away) for z in range(head_count - away) if z % devices + away < devices]
        if backward:
            pairs = [(b, a) for a, b in pairs]
        return lax.ppermute(array, "head", pairs)

    def exchanged(slices):
        return lax.all_to_all(slices, AXES, split_axis=0, concat_axis=0, tiled=True)

    def scanned(sums, backward, after=()):
        height = heads * DH // total
        slices = exchanged(sums.reshape(total, height, DH))
        slices, token = call(
            functools.partial(scan_body, rows=rows, backward=backward),
            "scan",
            [lengths],
            [Part(slices, near=True)],
            [Part(shape(slices.shape, BF), 1), token_part],
            heads,
            2 if height % 32 == 0 else 1,
            after=after,
            limit=SOME_BYTES,
        )
        return slices, token

    gain_row = Part(gain.reshape(1, width))
    halves = [2 if b > 0 and chunks % 2 == 0 else 1 for b in range(blocks) for _ in range(peers)]
    later = [[shape((heads // n, DH, DH), BF)] * n for n in halves]
    sum_kv, *later = call(
        functools.partial(state_body, counts=[1, *halves]),
        "states",
        scalars,
        [wide(keys), wide(values)],
        [states(state), *[part for arrays in later for part in split_states(arrays)]],
        heads,
        chunks,
        flops=unit,
    )
    later = iter(later)
    from_peers = [[next(later) for _ in range(n)] for n in halves]
    for at, arrays in enumerate(from_peers):
        arrays[0] = to_peers(arrays[0], 1 + at % peers, False)
    slices, token = scanned(sum_kv, False)
    (raw_inner,) = call(
        inner_body,
        "inner",
        scalars,
        [wide(queries), wide(keys), wide(values)],
        [wide(partial)],
        heads,
        chunks,
        square,
        flops=LONG,
        after=[token, *[x for arrays in from_peers[:peers] for x in arrays]],
    )
    kv_state = exchanged(slices).reshape(heads, DH, DH)
    for at, arrays in enumerate(from_peers):
        if len(arrays) > 1:
            later_half, kv_state = lax.optimization_barrier((arrays[1], kv_state))
            arrays[1] = to_peers(later_half, 1 + at % peers, False)

    scales, raws, grads, updates, back = [], [], [], [], []
    for b in range(blocks):
        ends = [states(state)] if b == blocks - 1 and blocks > 1 else []
        scale, raw, grad, update, *sums = call(
            functools.partial(norm_body, rows=rows, block=b, counts=[1, *halves[b * peers : (b + 1) * peers]]),
            "norm",
            scalars,
            [
                gain_row,
                wide(queries, b),
                wide(raw_inner, b),
                wide(grad_out, b),
                states(kv_state),
                *[p for arrays in from_peers[b * peers : (b + 1) * peers] for p in split_states(arrays)],
                *[states(w) for w in (updates if ends else [])],
            ],
            [Part(shape((BLOCK, DH), F32)), wide(block_tokens), wide(block_tokens), states(state), *ends],
            heads,
            chunks,
            flops=LONG if b > 0 else 2 * unit // blocks,
        )
        scales.append(scale)
        raws.append(raw)
        grads.append(grad)
        updates.append(update)
        back += [to_peers(update, away, True) for away in range(1, devices)]
    output, grad_q, token = call(
        functools.partial(query_grads_body, peers=peers, counts=halves),
        "query_grads",
        scalars,
        [
            gain_row,
            wide(keys),
            wide(values),
            states(kv_state),
            *[wide(d) for d in grads],
            *[wide(r) for r in raws],
            *[Part(s) for s in scales],
            *[part for arrays in from_peers for part in split_states(arrays)],
        ],
        [wide(tokens), wide(tokens), token_part],
        heads,
        chunks,
        square,
        flops=LONG,
        after=back[:peers],
    )
    slices, token = scanned(sums[0] if sums else updates[0], True, [token])
    part_k, part_v = call(
        functools.partial(key_grads_body, peers=peers),
        "key_grads",
        scalars,
        [
            wide(queries),
            wide(keys),
            wide(values),
            *[wide(d) for d in grads],
            *[states(w) for w in back],
        ],
        [wide(partial), wide(partial)],
        heads,
        chunks,
        square,
        flops=LONG,
        after=[token],
    )
    grad_state = exchanged(slices).reshape(heads, DH, DH)
    grad_k, grad_v = call(
        last_body,
        "last",
        scalars,
        [wide(keys), wide(values), wide(part_k), wide(part_v), states(grad_state)],
        [wide(tokens), wide(tokens)],
        heads,
        chunks,
        flops=2 * unit,
        limit=NARROW_BYTES,
    )
    return output, grad_q, grad_k, grad_v


def solution(mesh):
    tokens = P(AXES, None)
    return jax.shard_map(
        local,
        mesh=mesh,
        in_specs=(tokens, tokens, tokens, tokens, P(), P(), P("ctx", None)),
        out_specs=(tokens, tokens, tokens, tokens),
        check_vma=False,
    )
```

```python
import functools

import jax
import jax.numpy as jnp
from jax import lax
from jax.experimental import pallas as pl
from jax.experimental.pallas import tpu as pltpu
from jax.sharding import PartitionSpec as P

DH = 128
GROUP = 512
BLOCK = 128
CHUNKS = 4
LONG = 400_000_000_000
VMEM_BYTES = 60 * 1024 * 1024
NARROW_BYTES = 53 * 1024 * 1024
SOME_BYTES = 24 * 1024 * 1024

eps_norm = 1e-06
BF = jnp.bfloat16
F32 = jnp.float32
AXES = ("ctx", "head")

NN = (((1,), (0,)), ((), ()))
NT = (((1,), (1,)), ((), ()))
TN = (((0,), (0,)), ((), ()))


def dot(a, b, dims):
    return lax.dot_general(a, b, dims, preferred_element_type=F32)


def bounds_of(len_ref):
    bounds, total = [], None
    for k in range(len_ref.shape[0] - 1):
        total = len_ref[k] if total is None else total + len_ref[k]
        bounds.append(total)
    return bounds


def segment(position, bounds):
    result = (position >= bounds[0]).astype(jnp.int32)
    for bound in bounds[1:]:
        result = result + (position >= bound).astype(jnp.int32)
    return result


def same(a, b):
    return (a == b).astype(F32)


class Place:
    def __init__(self, len_ref, rows, mask_ref=None):
        self.rows = rows
        self.blocks = rows // BLOCK
        self.devices = GROUP // rows
        self.bounds = bounds_of(len_ref)
        spot = lax.axis_index("head")
        index = lax.axis_index("ctx") * lax.axis_size("head") + spot
        self.first = index * rows
        self.part = lax.rem(spot, self.devices)
        self.group = lax.div(spot, self.devices)
        self.group_first = self.first - self.part * rows
        self.mask_ref = mask_ref

    def seg(self, position):
        return segment(position, self.bounds)

    def start(self, block):
        return self.first + block * BLOCK

    def row_segments(self, block):
        rows = lax.broadcasted_iota(jnp.int32, (BLOCK, 1), 0)
        return self.seg(rows + self.start(block))

    def pair(self, i, j):
        slot = jnp.clip(lax.div(i * (i - 1), 2) + j, 0, self.mask_ref.shape[1] - 1)
        return self.mask_ref[self.group, slot].astype(F32)

    def weights(self):
        rows = self.rows
        t = lax.broadcasted_iota(jnp.int32, (rows, rows), 0)
        s = lax.broadcasted_iota(jnp.int32, (rows, rows), 1)
        keep = (s <= t) & (self.seg(t + self.first) == self.seg(s + self.first))
        result = jnp.where(keep, 1.0, 0.0)
        for i in range(1, self.blocks):
            for j in range(i):
                bit = self.pair(self.part * self.blocks + i, self.part * self.blocks + j)
                inside = (
                    (t >= i * BLOCK)
                    & (t < (i + 1) * BLOCK)
                    & (s >= j * BLOCK)
                    & (s < (j + 1) * BLOCK)
                )
                result = jnp.where(inside, result * bit, result)
        return result

    def to_later(self, away, block):
        there = (self.part + away) * self.blocks + block
        edge = self.seg(self.start(block) + away * self.rows - 1)
        return [
            self.pair(there, self.part * self.blocks + j) * same(self.seg(self.start(j + 1) - 1), edge)
            for j in range(self.blocks)
        ]

    def before(self, block):
        edge = self.seg(self.start(block) - 1)
        carried = same(self.seg(self.group_first - 1), edge)
        peers = [(self.part >= away).astype(F32) for away in range(1, self.devices)]
        return carried, peers, (self.row_segments(block) == edge).astype(F32)

    def after(self, block):
        own = self.part * self.blocks + block
        edge = self.seg(self.start(block + 1))
        carried = same(self.seg(self.group_first + GROUP), edge)
        peers = []
        for i in range(self.blocks):
            for away in range(1, self.devices):
                there = (self.part + away < self.devices).astype(F32)
                other = (self.part + away) * self.blocks + i
                start = self.start(i) + away * self.rows
                peers.append(self.pair(other, own) * same(self.seg(start), edge) * there)
        return carried, peers, (self.row_segments(block) == edge).astype(F32)


def mixed(refs, factors, head):
    total = refs[0][head].astype(F32) * factors[0]
    for ref, factor in zip(refs[1:], factors[1:], strict=True):
        total = total + ref[head].astype(F32) * factor
    return total.astype(BF)


class Joined:
    def __init__(self, refs):
        self.refs, self.each = refs, refs[0].shape[0]

    def __getitem__(self, head):
        return self.refs[head // self.each][head % self.each]

    def __setitem__(self, head, value):
        self.refs[head // self.each][head % self.each] = value


def joined(refs, counts):
    result, at = [], 0
    for count in counts:
        result.append(Joined(refs[at : at + count]))
        at += count
    return result


def columns(head):
    return pl.ds(head * DH, DH)


def rows_of(block):
    return pl.ds(block * BLOCK, BLOCK)


def state_body(place_of, ins, outs, scratch, arrive, leave, chunks, *, counts):
    k_ref, v_ref = ins
    outs = joined(outs, counts)
    rows, width = k_ref.shape
    place = place_of(rows)
    last = place.seg(place.start(place.blocks) - 1)
    ends = [place.seg(place.start(b + 1) - 1) for b in range(place.blocks)]
    masks = [(place.row_segments(b) == ends[b]).astype(BF) for b in range(place.blocks)]
    wanted = [[same(e, last) for e in ends]]
    for b in range(place.blocks):
        for away in range(1, place.devices):
            wanted.append(place.to_later(away, b))
    for c, heads in enumerate(chunks):
        arrive(c)
        for head in heads:
            updates = []
            for b in range(place.blocks):
                k = k_ref[rows_of(b), columns(head)] * masks[b]
                updates.append(dot(k, v_ref[rows_of(b), columns(head)], TN))
            for ref, factors in zip(outs, wanted, strict=True):
                total = updates[0] * factors[0]
                for update, factor in zip(updates[1:], factors[1:], strict=True):
                    total = total + update * factor
                ref[head] = total.astype(BF)
        leave(c)


def inner_body(place_of, ins, outs, scratch, arrive, leave, chunks):
    q_ref, k_ref, v_ref = ins
    (raw_ref,), (weight_ref,) = outs, scratch
    weight_ref[...] = place_of(q_ref.shape[0]).weights()
    for c, heads in enumerate(chunks):
        arrive(c)
        for head in heads:
            at = columns(head)
            probs = (dot(q_ref[:, at], k_ref[:, at], NT) * weight_ref[...]).astype(BF)
            raw_ref[:, at] = dot(probs, v_ref[:, at], NN)
        leave(c)


def scan_body(place_of, ins, outs, scratch, arrive, leave, chunks, *, rows, backward):
    (t_ref,), (out_ref, token_ref) = ins, outs
    token_ref[...] = jnp.zeros_like(token_ref)
    count, height, _ = t_ref.shape
    devices = GROUP // rows
    bounds = place_of(rows).bounds
    part = height // len(chunks)
    for c in range(len(chunks)):
        arrive(c)
        at = pl.ds(c * part, part)

        def one(turn, acc):
            group = count // devices - 1 - turn if backward else turn
            for k in range(devices):
                out_ref[group * devices + k, at] = acc.astype(BF)
            for k in range(devices):
                index = group * devices + (devices - 1 - k if backward else k)
                first = index * rows
                if backward:
                    keep = same(segment(first, bounds), segment(first + rows, bounds))
                else:
                    keep = same(segment(first - 1, bounds), segment(first + rows - 1, bounds))
                acc = acc * keep + t_ref[index, at].astype(F32)
            return acc

        acc = jnp.zeros((part, DH), F32)
        if count <= 32:
            for turn in range(count // devices):
                acc = one(turn, acc)
        else:
            lax.fori_loop(0, count // devices, one, acc)
        leave(c)


def norm_body(place_of, ins, outs, scratch, arrive, leave, chunks, *, rows, block, counts):
    gain_ref, q_ref, raw_ref, grad_ref = ins[:4]
    held = 4 + sum(counts)
    state_refs, earlier_refs = joined(ins[4:held], counts), ins[held:]
    scale_ref, held_ref, d_ref, w_ref, *t_refs = outs
    width = q_ref.shape[1]
    place = place_of(rows)
    carried, there, reach = place.before(block)
    squares = cross = jnp.zeros((BLOCK, DH), F32)
    for c, heads in enumerate(chunks):
        arrive(c)
        for head in heads:
            at = columns(head)
            state = mixed(state_refs, [carried, *there], head)
            raw = raw_ref[:, at] + dot(q_ref[:, at], state, NN) * reach
            raw = raw.astype(BF)
            held_ref[:, at] = raw
            raw = raw.astype(F32)
            scaled = grad_ref[:, at].astype(F32) * gain_ref[:, at]
            squares = squares + raw * raw
            cross = cross + scaled * raw
        leave(c, [1])
    total = jnp.sum(squares, axis=1, keepdims=True)
    inverse = 1.0 / jnp.sqrt(total / width + eps_norm)
    mean = jnp.sum(cross, axis=1, keepdims=True) * inverse / width
    scale_ref[...] = jnp.broadcast_to(inverse, scale_ref.shape)
    leave(0, [0])
    own = place.seg(place.start(block))
    begin = (place.row_segments(block) == own).astype(BF)
    into = [same(place.seg(place.start(b)), place.seg(place.first)) for b in range(block + 1)]
    for c, heads in enumerate(chunks):
        for head in heads:
            at = columns(head)
            normed = held_ref[:, at].astype(F32) * inverse
            scaled = grad_ref[:, at].astype(F32) * gain_ref[:, at]
            grad = ((scaled - normed * mean) * inverse).astype(BF)
            d_ref[:, at] = grad
            update = dot(q_ref[:, at] * begin, grad, TN)
            w_ref[head] = update.astype(BF)
            for t_ref in t_refs:
                sums = update * into[block]
                for ref, factor in zip(earlier_refs, into[:block], strict=True):
                    sums = sums + ref[head].astype(F32) * factor
                t_ref[head] = sums.astype(BF)
        leave(c, range(2, len(outs)))


def query_grads_body(place_of, ins, outs, scratch, arrive, leave, chunks, *, peers, counts):
    gain_ref, k_ref, v_ref, kv_ref = ins[:4]
    rows, width = k_ref.shape
    place = place_of(rows)
    blocks = place.blocks
    rest = ins[4:]
    d_refs, raw_refs, scale_refs = rest[:blocks], rest[blocks : 2 * blocks], rest[2 * blocks : 3 * blocks]
    peer_refs = joined(rest[3 * blocks :], counts)
    out_ref, gq_ref, token_ref = outs
    (weight_ref,) = scratch
    token_ref[...] = jnp.zeros_like(token_ref)
    weight_ref[...] = place.weights()
    factors = [place.before(b) for b in range(blocks)]
    for c, heads in enumerate(chunks):
        arrive(c)
        for head in heads:
            at = columns(head)
            d = jnp.concatenate([ref[:, at] for ref in d_refs], axis=0)
            grad_probs = (dot(d, v_ref[:, at], NT) * weight_ref[...]).astype(BF)
            inner = dot(grad_probs, k_ref[:, at], NN)
            for b in range(blocks):
                carried, there, _ = factors[b]
                state = mixed([kv_ref, *peer_refs[b * peers : (b + 1) * peers]], [carried, *there], head)
                outer = dot(d_refs[b][:, at], state, NT) * factors[b][2]
                part = inner[b * BLOCK : (b + 1) * BLOCK] + outer
                gq_ref[rows_of(b), at] = part.astype(BF)
                normed = raw_refs[b][:, at].astype(F32) * scale_refs[b][...]
                out_ref[rows_of(b), at] = (normed * gain_ref[:, at]).astype(BF)
        leave(c)


def key_grads_body(place_of, ins, outs, scratch, arrive, leave, chunks, *, peers):
    q_ref, k_ref, v_ref, *rest = ins
    place = place_of(q_ref.shape[0])
    blocks = place.blocks
    d_refs, w_refs = rest[:blocks], rest[blocks:]
    gk_ref, gv_ref = outs
    (weight_ref,) = scratch
    weight_ref[...] = place.weights()
    factors = [place.after(b) for b in range(blocks)]
    for c, heads in enumerate(chunks):
        arrive(c)
        for head in heads:
            at = columns(head)
            q, d = q_ref[:, at], jnp.concatenate([ref[:, at] for ref in d_refs], axis=0)
            probs = (dot(q, k_ref[:, at], NT) * weight_ref[...]).astype(BF)
            grad_probs = (dot(d, v_ref[:, at], NT) * weight_ref[...]).astype(BF)
            gk = dot(grad_probs, q, TN)
            gv = dot(probs, d, TN)
            for b in range(blocks):
                at_rows, here = rows_of(b), slice(b * BLOCK, (b + 1) * BLOCK)
                part_k, part_v = gk[here], gv[here]
                if peers:
                    state = mixed(w_refs, factors[b][1], head)
                    part_k = part_k + dot(v_ref[at_rows, at], state, NT) * factors[b][2]
                    part_v = part_v + dot(k_ref[at_rows, at], state, NN) * factors[b][2]
                gk_ref[at_rows, at] = part_k
                gv_ref[at_rows, at] = part_v
        leave(c)


def last_body(place_of, ins, outs, scratch, arrive, leave, chunks):
    k_ref, v_ref, gk_in, gv_in, gs_ref = ins
    gk_ref, gv_ref = outs
    place = place_of(k_ref.shape[0])
    factors = [place.after(b) for b in range(place.blocks)]
    reach = jnp.concatenate([reach * carried for carried, _, reach in factors], axis=0)
    for c, heads in enumerate(chunks):
        arrive(c)
        for head in heads:
            at = columns(head)
            gk = gk_in[:, at] + dot(v_ref[:, at], gs_ref[head], NT) * reach
            gv = gv_in[:, at] + dot(k_ref[:, at], gs_ref[head], NN) * reach
            gk_ref[:, at] = gk.astype(BF)
            gv_ref[:, at] = gv.astype(BF)
        leave(c)


class Part:
    def __init__(self, array, axis=None, block=None, near=False, lead=0, parts=None):
        self.array, self.axis, self.block, self.near = array, axis, block, near
        self.lead, self.parts = lead, parts
        self.shape = array.shape if block is None else (BLOCK, *array.shape[1:])
        self.spec = pl.BlockSpec(memory_space=pltpu.VMEM if near else pltpu.HBM)

    def pieces(self, far, near, sems, count):
        far = far if self.block is None else far.at[rows_of(self.block)]
        if self.axis is None:
            return [(far, near, sems.at[0])]
        count = self.parts or count
        size = self.shape[self.axis] // count
        result = [None] * self.lead
        for c in range(count):
            at = [slice(None)] * len(self.shape)
            at[self.axis] = pl.ds(c * size, size)
            result.append((far.at[tuple(at)], near.at[tuple(at)], sems.at[c]))
        return result


def call(body, name, scalars, ins, outs, heads, chunks, scratch=(), flops=0, after=(), limit=VMEM_BYTES):
    far = [p for p in (*ins, *outs) if not p.near]
    sizes = (len(scalars), len(ins), len(after), len(outs), len(far), 2, len(scratch))

    def kernel(*refs):
        split, at = [], 0
        for size in sizes:
            split.append(refs[at : at + size])
            at += size
        settings, in_refs, _, out_refs, buffers, (in_sems, out_sems), rest = split
        buffers = iter(buffers)

        def opened(parts, given, sems):
            refs, pieces = [], []
            for i, (part, ref) in enumerate(zip(parts, given, strict=True)):
                refs.append(ref if part.near else next(buffers))
                pieces.append([] if part.near else part.pieces(ref, refs[-1], sems.at[i], chunks))
            return refs, pieces

        near_in, coming = opened(ins, in_refs, in_sems)
        near_out, going = opened(outs, out_refs, out_sems)

        def copies(parts, c, which=None):
            for i, pieces in enumerate(parts):
                if c < len(pieces) and pieces[c] is not None and (which is None or i in which):
                    yield pieces[c]

        def arrive(c):
            for far, near, sem in copies(coming, c):
                pltpu.make_async_copy(far, near, sem).wait()

        def leave(c, which=None):
            for far, near, sem in copies(going, c, which):
                pltpu.make_async_copy(near, far, sem).start()

        for c in range(chunks):
            for far, near, sem in copies(coming, c):
                pltpu.make_async_copy(far, near, sem).start()
        each = heads // chunks
        turns = [range(c * each, (c + 1) * each) for c in range(chunks)]
        place_of = lambda rows: Place(settings[0], rows, *settings[1:])
        body(place_of, near_in, near_out, rest, arrive, leave, turns)
        for c in range(chunks):
            for far, near, sem in copies(going, c):
                pltpu.make_async_copy(near, far, sem).wait()

    anywhere = pl.BlockSpec(memory_space=pl.ANY)
    return pl.pallas_call(
        kernel,
        name=name,
        in_specs=[
            *[pl.BlockSpec(memory_space=pltpu.SMEM)] * len(scalars),
            *[p.spec for p in ins],
            *[anywhere] * len(after),
        ],
        out_specs=[p.spec for p in outs],
        out_shape=[p.array for p in outs],
        scratch_shapes=[
            *[pltpu.VMEM(p.shape, p.array.dtype) for p in far],
            pltpu.SemaphoreType.DMA((len(ins), chunks)),
            pltpu.SemaphoreType.DMA((len(outs), chunks)),
            *scratch,
        ],
        compiler_params=pltpu.CompilerParams(vmem_limit_bytes=limit),
        cost_estimate=pl.CostEstimate(
            flops=flops,
            bytes_accessed=sum(p.array.size * p.array.dtype.itemsize for p in (*ins, *outs)),
            transcendentals=0,
        ),
    )(*scalars, *[p.array for p in ins], *after)


def local(queries, keys, values, grad_out, gain, lengths, block_mask):
    rows, width = queries.shape
    heads = width // DH
    blocks = rows // BLOCK
    devices = GROUP // rows
    peers = devices - 1
    head_count = lax.axis_size("head")
    total = lax.axis_size("ctx") * head_count
    chunks = CHUNKS if heads % CHUNKS == 0 else 1
    shape = jax.ShapeDtypeStruct
    state = shape((heads, DH, DH), BF)
    tokens = shape((rows, width), BF)
    partial = shape((rows, width), F32)
    block_tokens = shape((BLOCK, width), BF)
    square = [pltpu.VMEM((rows, rows), F32)]
    unit = 2 * rows * width * DH
    inner = 2 * rows * rows * width
    scalars = [lengths, block_mask]
    token_part = Part(shape((8, DH), F32), near=True)

    def wide(array, block=None):
        return Part(array, 1, block)

    def states(array):
        return Part(array, 0)

    def split_states(arrays):
        count = chunks // len(arrays)
        return [Part(a, 0, lead=i * count, parts=count) for i, a in enumerate(arrays)]

    def to_peers(array, away, backward):
        pairs = [(z, z + away) for z in range(head_count - away) if z % devices + away < devices]
        if backward:
            pairs = [(b, a) for a, b in pairs]
        return lax.ppermute(array, "head", pairs)

    def exchanged(slices):
        return lax.all_to_all(slices, AXES, split_axis=0, concat_axis=0, tiled=True)

    def scanned(sums, backward, after=()):
        height = heads * DH // total
        slices = exchanged(sums.reshape(total, height, DH))
        slices, token = call(
            functools.partial(scan_body, rows=rows, backward=backward),
            "scan",
            [lengths],
            [Part(slices, near=True)],
            [Part(shape(slices.shape, BF), 1), token_part],
            heads,
            2 if height % 32 == 0 else 1,
            after=after,
            limit=SOME_BYTES,
        )
        return slices, token

    gain_row = Part(gain.reshape(1, width))
    halves = [2 if b > 0 and chunks % 2 == 0 else 1 for b in range(blocks) for _ in range(peers)]
    later = [[shape((heads // n, DH, DH), BF)] * n for n in halves]
    sum_kv, *later = call(
        functools.partial(state_body, counts=[1, *halves]),
        "states",
        scalars,
        [wide(keys), wide(values)],
        [states(state), *[part for arrays in later for part in split_states(arrays)]],
        heads,
        chunks,
        flops=unit,
    )
    later = iter(later)
    from_peers = [[next(later) for _ in range(n)] for n in halves]
    for at, arrays in enumerate(from_peers):
        arrays[0] = to_peers(arrays[0], 1 + at % peers, False)
    slices, token = scanned(sum_kv, False)
    (raw_inner,) = call(
        inner_body,
        "inner",
        scalars,
        [wide(queries), wide(keys), wide(values)],
        [wide(partial)],
        heads,
        chunks,
        square,
        flops=LONG,
        after=[token, *[x for arrays in from_peers[:peers] for x in arrays]],
    )
    kv_state = exchanged(slices).reshape(heads, DH, DH)
    for at, arrays in enumerate(from_peers):
        if len(arrays) > 1:
            held = lax.optimization_barrier((arrays[1], kv_state, raw_inner))
            later_half, kv_state, raw_inner = held
            arrays[1] = to_peers(later_half, 1 + at % peers, False)

    scales, raws, grads, updates, back = [], [], [], [], []
    for b in range(blocks):
        ends = [states(state)] if b == blocks - 1 and blocks > 1 else []
        scale, raw, grad, update, *sums = call(
            functools.partial(norm_body, rows=rows, block=b, counts=[1, *halves[b * peers : (b + 1) * peers]]),
            "norm",
            scalars,
            [
                gain_row,
                wide(queries, b),
                wide(raw_inner, b),
                wide(grad_out, b),
                states(kv_state),
                *[p for arrays in from_peers[b * peers : (b + 1) * peers] for p in split_states(arrays)],
                *[states(w) for w in (updates if ends else [])],
            ],
            [Part(shape((BLOCK, DH), F32)), wide(block_tokens), wide(block_tokens), states(state), *ends],
            heads,
            chunks,
            flops=LONG if b > 0 else 2 * unit // blocks,
        )
        scales.append(scale)
        raws.append(raw)
        grads.append(grad)
        updates.append(update)
        back += [to_peers(update, away, True) for away in range(1, devices)]
    output, grad_q, token = call(
        functools.partial(query_grads_body, peers=peers, counts=halves),
        "query_grads",
        scalars,
        [
            gain_row,
            wide(keys),
            wide(values),
            states(kv_state),
            *[wide(d) for d in grads],
            *[wide(r) for r in raws],
            *[Part(s) for s in scales],
            *[part for arrays in from_peers for part in split_states(arrays)],
        ],
        [wide(tokens), wide(tokens), token_part],
        heads,
        chunks,
        square,
        flops=LONG,
        after=back[:peers],
    )
    slices, token = scanned(sums[0] if sums else updates[0], True, [token])
    part_k, part_v = call(
        functools.partial(key_grads_body, peers=peers),
        "key_grads",
        scalars,
        [
            wide(queries),
            wide(keys),
            wide(values),
            *[wide(d) for d in grads],
            *[states(w) for w in back],
        ],
        [wide(partial), wide(partial)],
        heads,
        chunks,
        square,
        flops=LONG,
        after=[token],
    )
    grad_state = exchanged(slices).reshape(heads, DH, DH)
    grad_k, grad_v = call(
        last_body,
        "last",
        scalars,
        [wide(keys), wide(values), wide(part_k), wide(part_v), states(grad_state)],
        [wide(tokens), wide(tokens)],
        heads,
        chunks,
        flops=2 * unit,
        limit=NARROW_BYTES,
    )
    return output, grad_q, grad_k, grad_v


def solution(mesh):
    tokens = P(AXES, None)
    return jax.shard_map(
        local,
        mesh=mesh,
        in_specs=(tokens, tokens, tokens, tokens, P(), P(), P("ctx", None)),
        out_specs=(tokens, tokens, tokens, tokens),
        check_vma=False,
    )
```

```python
import functools

import jax
import jax.numpy as jnp
from jax import lax
from jax.experimental import pallas as pl
from jax.experimental.pallas import tpu as pltpu
from jax.sharding import PartitionSpec as P

DH = 128
GROUP = 512
BLOCK = 128
CHUNKS = 4
LONG = 400_000_000_000
VMEM_BYTES = 60 * 1024 * 1024
NARROW_BYTES = 53 * 1024 * 1024
SOME_BYTES = 24 * 1024 * 1024

eps_norm = 1e-06
BF = jnp.bfloat16
F32 = jnp.float32
AXES = ("ctx", "head")

NN = (((1,), (0,)), ((), ()))
NT = (((1,), (1,)), ((), ()))
TN = (((0,), (0,)), ((), ()))


def dot(a, b, dims):
    return lax.dot_general(a, b, dims, preferred_element_type=F32)


def bounds_of(len_ref):
    bounds, total = [], None
    for k in range(len_ref.shape[0] - 1):
        total = len_ref[k] if total is None else total + len_ref[k]
        bounds.append(total)
    return bounds


def segment(position, bounds):
    result = (position >= bounds[0]).astype(jnp.int32)
    for bound in bounds[1:]:
        result = result + (position >= bound).astype(jnp.int32)
    return result


def same(a, b):
    return (a == b).astype(F32)


class Place:
    def __init__(self, len_ref, rows, mask_ref=None):
        self.rows = rows
        self.blocks = rows // BLOCK
        self.devices = GROUP // rows
        self.bounds = bounds_of(len_ref)
        spot = lax.axis_index("head")
        index = lax.axis_index("ctx") * lax.axis_size("head") + spot
        self.first = index * rows
        self.part = lax.rem(spot, self.devices)
        self.group = lax.div(spot, self.devices)
        self.group_first = self.first - self.part * rows
        self.mask_ref = mask_ref

    def seg(self, position):
        return segment(position, self.bounds)

    def start(self, block):
        return self.first + block * BLOCK

    def row_segments(self, block):
        rows = lax.broadcasted_iota(jnp.int32, (BLOCK, 1), 0)
        return self.seg(rows + self.start(block))

    def pair(self, i, j):
        slot = jnp.clip(lax.div(i * (i - 1), 2) + j, 0, self.mask_ref.shape[1] - 1)
        return self.mask_ref[self.group, slot].astype(F32)

    def weights(self):
        rows = self.rows
        t = lax.broadcasted_iota(jnp.int32, (rows, rows), 0)
        s = lax.broadcasted_iota(jnp.int32, (rows, rows), 1)
        keep = (s <= t) & (self.seg(t + self.first) == self.seg(s + self.first))
        result = jnp.where(keep, 1.0, 0.0)
        for i in range(1, self.blocks):
            for j in range(i):
                bit = self.pair(self.part * self.blocks + i, self.part * self.blocks + j)
                inside = (
                    (t >= i * BLOCK)
                    & (t < (i + 1) * BLOCK)
                    & (s >= j * BLOCK)
                    & (s < (j + 1) * BLOCK)
                )
                result = jnp.where(inside, result * bit, result)
        return result

    def to_later(self, away, block):
        there = (self.part + away) * self.blocks + block
        edge = self.seg(self.start(block) + away * self.rows - 1)
        return [
            self.pair(there, self.part * self.blocks + j) * same(self.seg(self.start(j + 1) - 1), edge)
            for j in range(self.blocks)
        ]

    def before(self, block):
        edge = self.seg(self.start(block) - 1)
        carried = same(self.seg(self.group_first - 1), edge)
        peers = [(self.part >= away).astype(F32) for away in range(1, self.devices)]
        return carried, peers, (self.row_segments(block) == edge).astype(F32)

    def after(self, block):
        own = self.part * self.blocks + block
        edge = self.seg(self.start(block + 1))
        carried = same(self.seg(self.group_first + GROUP), edge)
        peers = []
        for i in range(self.blocks):
            for away in range(1, self.devices):
                there = (self.part + away < self.devices).astype(F32)
                other = (self.part + away) * self.blocks + i
                start = self.start(i) + away * self.rows
                peers.append(self.pair(other, own) * same(self.seg(start), edge) * there)
        return carried, peers, (self.row_segments(block) == edge).astype(F32)


def mixed(refs, factors, head):
    total = refs[0][head].astype(F32) * factors[0]
    for ref, factor in zip(refs[1:], factors[1:], strict=True):
        total = total + ref[head].astype(F32) * factor
    return total.astype(BF)


class Joined:
    def __init__(self, refs):
        self.refs, self.each = refs, refs[0].shape[0]

    def __getitem__(self, head):
        return self.refs[head // self.each][head % self.each]

    def __setitem__(self, head, value):
        self.refs[head // self.each][head % self.each] = value


def joined(refs, counts):
    result, at = [], 0
    for count in counts:
        result.append(Joined(refs[at : at + count]))
        at += count
    return result


def columns(head):
    return pl.ds(head * DH, DH)


def rows_of(block):
    return pl.ds(block * BLOCK, BLOCK)


def state_body(place_of, ins, outs, scratch, arrive, leave, chunks, *, counts):
    k_ref, v_ref = ins
    outs = joined(outs, counts)
    rows, width = k_ref.shape
    place = place_of(rows)
    last = place.seg(place.start(place.blocks) - 1)
    ends = [place.seg(place.start(b + 1) - 1) for b in range(place.blocks)]
    masks = [(place.row_segments(b) == ends[b]).astype(BF) for b in range(place.blocks)]
    wanted = [[same(e, last) for e in ends]]
    for b in range(place.blocks):
        for away in range(1, place.devices):
            wanted.append(place.to_later(away, b))
    for c, heads in enumerate(chunks):
        arrive(c)
        for head in heads:
            updates = []
            for b in range(place.blocks):
                k = k_ref[rows_of(b), columns(head)] * masks[b]
                updates.append(dot(k, v_ref[rows_of(b), columns(head)], TN))
            for ref, factors in zip(outs, wanted, strict=True):
                total = updates[0] * factors[0]
                for update, factor in zip(updates[1:], factors[1:], strict=True):
                    total = total + update * factor
                ref[head] = total.astype(BF)
        leave(c)


def inner_body(place_of, ins, outs, scratch, arrive, leave, chunks):
    q_ref, k_ref, v_ref = ins
    (raw_ref,), (weight_ref,) = outs, scratch
    weight_ref[...] = place_of(q_ref.shape[0]).weights()
    for c, heads in enumerate(chunks):
        arrive(c)
        for head in heads:
            at = columns(head)
            probs = (dot(q_ref[:, at], k_ref[:, at], NT) * weight_ref[...]).astype(BF)
            raw_ref[:, at] = dot(probs, v_ref[:, at], NN)
        leave(c)


def scan_body(place_of, ins, outs, scratch, arrive, leave, chunks, *, rows, backward):
    (t_ref,), (out_ref,) = ins, outs
    count, height, _ = t_ref.shape
    devices = GROUP // rows
    bounds = place_of(rows).bounds
    part = height // len(chunks)
    for c in range(len(chunks)):
        arrive(c)
        at = pl.ds(c * part, part)

        def one(turn, acc):
            group = count // devices - 1 - turn if backward else turn
            for k in range(devices):
                out_ref[group * devices + k, at] = acc.astype(BF)
            for k in range(devices):
                index = group * devices + (devices - 1 - k if backward else k)
                first = index * rows
                if backward:
                    keep = same(segment(first, bounds), segment(first + rows, bounds))
                else:
                    keep = same(segment(first - 1, bounds), segment(first + rows - 1, bounds))
                acc = acc * keep + t_ref[index, at].astype(F32)
            return acc

        acc = jnp.zeros((part, DH), F32)
        if count <= 32:
            for turn in range(count // devices):
                acc = one(turn, acc)
        else:
            lax.fori_loop(0, count // devices, one, acc)
        leave(c)


def norm_body(place_of, ins, outs, scratch, arrive, leave, chunks, *, rows, block, counts):
    gain_ref, q_ref, raw_ref, grad_ref = ins[:4]
    held = 4 + sum(counts)
    state_refs, earlier_refs = joined(ins[4:held], counts), ins[held:]
    scale_ref, held_ref, d_ref, w_ref, *t_refs = outs
    width = q_ref.shape[1]
    place = place_of(rows)
    carried, there, reach = place.before(block)
    squares = cross = jnp.zeros((BLOCK, DH), F32)
    for c, heads in enumerate(chunks):
        arrive(c)
        for head in heads:
            at = columns(head)
            state = mixed(state_refs, [carried, *there], head)
            raw = raw_ref[:, at] + dot(q_ref[:, at], state, NN) * reach
            raw = raw.astype(BF)
            held_ref[:, at] = raw
            raw = raw.astype(F32)
            scaled = grad_ref[:, at].astype(F32) * gain_ref[:, at]
            squares = squares + raw * raw
            cross = cross + scaled * raw
        leave(c, [1])
    total = jnp.sum(squares, axis=1, keepdims=True)
    inverse = 1.0 / jnp.sqrt(total / width + eps_norm)
    mean = jnp.sum(cross, axis=1, keepdims=True) * inverse / width
    scale_ref[...] = jnp.broadcast_to(inverse, scale_ref.shape)
    leave(0, [0])
    own = place.seg(place.start(block))
    begin = (place.row_segments(block) == own).astype(BF)
    into = [same(place.seg(place.start(b)), place.seg(place.first)) for b in range(block + 1)]
    for c, heads in enumerate(chunks):
        for head in heads:
            at = columns(head)
            normed = held_ref[:, at].astype(F32) * inverse
            scaled = grad_ref[:, at].astype(F32) * gain_ref[:, at]
            grad = ((scaled - normed * mean) * inverse).astype(BF)
            d_ref[:, at] = grad
            update = dot(q_ref[:, at] * begin, grad, TN)
            w_ref[head] = update.astype(BF)
            for t_ref in t_refs:
                sums = update * into[block]
                for ref, factor in zip(earlier_refs, into[:block], strict=True):
                    sums = sums + ref[head].astype(F32) * factor
                t_ref[head] = sums.astype(BF)
        leave(c, range(2, len(outs)))


def query_grads_body(place_of, ins, outs, scratch, arrive, leave, chunks, *, peers, counts):
    gain_ref, k_ref, v_ref, kv_ref = ins[:4]
    rows, width = k_ref.shape
    place = place_of(rows)
    blocks = place.blocks
    rest = ins[4:]
    d_refs, raw_refs, scale_refs = rest[:blocks], rest[blocks : 2 * blocks], rest[2 * blocks : 3 * blocks]
    peer_refs = joined(rest[3 * blocks :], counts)
    out_ref, gq_ref = outs
    (weight_ref,) = scratch
    weight_ref[...] = place.weights()
    factors = [place.before(b) for b in range(blocks)]
    for c, heads in enumerate(chunks):
        arrive(c)
        for head in heads:
            at = columns(head)
            d = jnp.concatenate([ref[:, at] for ref in d_refs], axis=0)
            grad_probs = (dot(d, v_ref[:, at], NT) * weight_ref[...]).astype(BF)
            inner = dot(grad_probs, k_ref[:, at], NN)
            for b in range(blocks):
                carried, there, _ = factors[b]
                state = mixed([kv_ref, *peer_refs[b * peers : (b + 1) * peers]], [carried, *there], head)
                outer = dot(d_refs[b][:, at], state, NT) * factors[b][2]
                part = inner[b * BLOCK : (b + 1) * BLOCK] + outer
                gq_ref[rows_of(b), at] = part.astype(BF)
                normed = raw_refs[b][:, at].astype(F32) * scale_refs[b][...]
                out_ref[rows_of(b), at] = (normed * gain_ref[:, at]).astype(BF)
        leave(c)


def key_grads_body(place_of, ins, outs, scratch, arrive, leave, chunks, *, peers):
    q_ref, k_ref, v_ref, *rest = ins
    place = place_of(q_ref.shape[0])
    blocks = place.blocks
    d_refs, w_refs = rest[:blocks], rest[blocks:]
    gk_ref, gv_ref = outs
    (weight_ref,) = scratch
    weight_ref[...] = place.weights()
    factors = [place.after(b) for b in range(blocks)]
    for c, heads in enumerate(chunks):
        arrive(c)
        for head in heads:
            at = columns(head)
            q, d = q_ref[:, at], jnp.concatenate([ref[:, at] for ref in d_refs], axis=0)
            probs = (dot(q, k_ref[:, at], NT) * weight_ref[...]).astype(BF)
            grad_probs = (dot(d, v_ref[:, at], NT) * weight_ref[...]).astype(BF)
            gk = dot(grad_probs, q, TN)
            gv = dot(probs, d, TN)
            for b in range(blocks):
                at_rows, here = rows_of(b), slice(b * BLOCK, (b + 1) * BLOCK)
                part_k, part_v = gk[here], gv[here]
                if peers:
                    state = mixed(w_refs, factors[b][1], head)
                    part_k = part_k + dot(v_ref[at_rows, at], state, NT) * factors[b][2]
                    part_v = part_v + dot(k_ref[at_rows, at], state, NN) * factors[b][2]
                gk_ref[at_rows, at] = part_k
                gv_ref[at_rows, at] = part_v
        leave(c)


def last_body(place_of, ins, outs, scratch, arrive, leave, chunks):
    k_ref, v_ref, gk_in, gv_in, gs_ref = ins
    gk_ref, gv_ref = outs
    place = place_of(k_ref.shape[0])
    factors = [place.after(b) for b in range(place.blocks)]
    reach = jnp.concatenate([reach * carried for carried, _, reach in factors], axis=0)
    for c, heads in enumerate(chunks):
        arrive(c)
        for head in heads:
            at = columns(head)
            gk = gk_in[:, at] + dot(v_ref[:, at], gs_ref[head], NT) * reach
            gv = gv_in[:, at] + dot(k_ref[:, at], gs_ref[head], NN) * reach
            gk_ref[:, at] = gk.astype(BF)
            gv_ref[:, at] = gv.astype(BF)
        leave(c)


class Part:
    def __init__(self, array, axis=None, block=None, near=False, lead=0, parts=None):
        self.array, self.axis, self.block, self.near = array, axis, block, near
        self.lead, self.parts = lead, parts
        self.shape = array.shape if block is None else (BLOCK, *array.shape[1:])
        self.spec = pl.BlockSpec(memory_space=pltpu.VMEM if near else pltpu.HBM)

    def pieces(self, far, near, sems, count):
        far = far if self.block is None else far.at[rows_of(self.block)]
        if self.axis is None:
            return [(far, near, sems.at[0])]
        count = self.parts or count
        size = self.shape[self.axis] // count
        result = [None] * self.lead
        for c in range(count):
            at = [slice(None)] * len(self.shape)
            at[self.axis] = pl.ds(c * size, size)
            result.append((far.at[tuple(at)], near.at[tuple(at)], sems.at[c]))
        return result


def call(body, name, scalars, ins, outs, heads, chunks, scratch=(), flops=0, after=(), limit=VMEM_BYTES):
    far = [p for p in (*ins, *outs) if not p.near]
    sizes = (len(scalars), len(ins), len(after), len(outs), len(far), 2, len(scratch))

    def kernel(*refs):
        split, at = [], 0
        for size in sizes:
            split.append(refs[at : at + size])
            at += size
        settings, in_refs, _, out_refs, buffers, (in_sems, out_sems), rest = split
        buffers = iter(buffers)

        def opened(parts, given, sems):
            refs, pieces = [], []
            for i, (part, ref) in enumerate(zip(parts, given, strict=True)):
                refs.append(ref if part.near else next(buffers))
                pieces.append([] if part.near else part.pieces(ref, refs[-1], sems.at[i], chunks))
            return refs, pieces

        near_in, coming = opened(ins, in_refs, in_sems)
        near_out, going = opened(outs, out_refs, out_sems)

        def copies(parts, c, which=None):
            for i, pieces in enumerate(parts):
                if c < len(pieces) and pieces[c] is not None and (which is None or i in which):
                    yield pieces[c]

        def arrive(c):
            for far, near, sem in copies(coming, c):
                pltpu.make_async_copy(far, near, sem).wait()

        def leave(c, which=None):
            for far, near, sem in copies(going, c, which):
                pltpu.make_async_copy(near, far, sem).start()

        for c in range(chunks):
            for far, near, sem in copies(coming, c):
                pltpu.make_async_copy(far, near, sem).start()
        each = heads // chunks
        turns = [range(c * each, (c + 1) * each) for c in range(chunks)]
        place_of = lambda rows: Place(settings[0], rows, *settings[1:])
        body(place_of, near_in, near_out, rest, arrive, leave, turns)
        for c in range(chunks):
            for far, near, sem in copies(going, c):
                pltpu.make_async_copy(near, far, sem).wait()

    anywhere = pl.BlockSpec(memory_space=pl.ANY)
    return pl.pallas_call(
        kernel,
        name=name,
        in_specs=[
            *[pl.BlockSpec(memory_space=pltpu.SMEM)] * len(scalars),
            *[p.spec for p in ins],
            *[anywhere] * len(after),
        ],
        out_specs=[p.spec for p in outs],
        out_shape=[p.array for p in outs],
        scratch_shapes=[
            *[pltpu.VMEM(p.shape, p.array.dtype) for p in far],
            pltpu.SemaphoreType.DMA((len(ins), chunks)),
            pltpu.SemaphoreType.DMA((len(outs), chunks)),
            *scratch,
        ],
        compiler_params=pltpu.CompilerParams(vmem_limit_bytes=limit),
        cost_estimate=pl.CostEstimate(
            flops=flops,
            bytes_accessed=sum(p.array.size * p.array.dtype.itemsize for p in (*ins, *outs)),
            transcendentals=0,
        ),
    )(*scalars, *[p.array for p in ins], *after)


def local(queries, keys, values, grad_out, gain, lengths, block_mask):
    rows, width = queries.shape
    heads = width // DH
    blocks = rows // BLOCK
    devices = GROUP // rows
    peers = devices - 1
    head_count = lax.axis_size("head")
    total = lax.axis_size("ctx") * head_count
    chunks = CHUNKS if heads % CHUNKS == 0 else 1
    few = min(chunks, 2)
    shape = jax.ShapeDtypeStruct
    state = shape((heads, DH, DH), BF)
    tokens = shape((rows, width), BF)
    partial = shape((rows, width), F32)
    block_tokens = shape((BLOCK, width), BF)
    square = [pltpu.VMEM((rows, rows), F32)]
    unit = 2 * rows * width * DH
    inner = 2 * rows * rows * width
    scalars = [lengths, block_mask]

    def wide(array, block=None):
        return Part(array, 1, block)

    def states(array):
        return Part(array, 0)

    def split_states(arrays, chunks):
        count = chunks // len(arrays)
        return [Part(a, 0, lead=i * count, parts=count) for i, a in enumerate(arrays)]

    def to_peers(array, away, backward):
        pairs = [(z, z + away) for z in range(head_count - away) if z % devices + away < devices]
        if backward:
            pairs = [(b, a) for a, b in pairs]
        return lax.ppermute(array, "head", pairs)

    def exchanged(slices):
        return lax.all_to_all(slices, AXES, split_axis=0, concat_axis=0, tiled=True)

    def scanned(slices, backward):
        (slices,) = call(
            functools.partial(scan_body, rows=rows, backward=backward),
            "scan",
            [lengths],
            [Part(slices, near=True)],
            [Part(shape(slices.shape, BF), 1)],
            heads,
            2 if slices.shape[1] % 32 == 0 else 1,
            limit=SOME_BYTES,
        )
        return slices

    gain_row = Part(gain.reshape(1, width))
    halves = [2 if b > 0 and chunks % 2 == 0 else 1 for b in range(blocks) for _ in range(peers)]
    later = [[shape((heads // n, DH, DH), BF)] * n for n in halves]
    sum_kv, *later = call(
        functools.partial(state_body, counts=[1, *halves]),
        "states",
        scalars,
        [wide(keys), wide(values)],
        [states(state), *[part for arrays in later for part in split_states(arrays, few)]],
        heads,
        few,
        flops=unit,
    )
    later = iter(later)
    from_peers = [[next(later) for _ in range(n)] for n in halves]
    for at, arrays in enumerate(from_peers):
        arrays[0] = to_peers(arrays[0], 1 + at % peers, False)
    slices = scanned(exchanged(sum_kv.reshape(total, -1, DH)), False)
    slices, late_queries = lax.optimization_barrier((slices, queries))
    (raw_inner,) = call(
        inner_body,
        "inner",
        scalars,
        [wide(late_queries), wide(keys), wide(values)],
        [wide(partial)],
        heads,
        chunks,
        square,
        flops=LONG,
        after=[x for arrays in from_peers[:peers] for x in arrays],
    )
    kv_state = exchanged(slices).reshape(heads, DH, DH)
    for at, arrays in enumerate(from_peers):
        if len(arrays) > 1:
            held = lax.optimization_barrier((arrays[1], kv_state, raw_inner))
            later_half, kv_state, raw_inner = held
            arrays[1] = to_peers(later_half, 1 + at % peers, False)

    scales, raws, grads, updates, back = [], [], [], [], []
    for b in range(blocks):
        ends = [states(state)] if b == blocks - 1 and blocks > 1 else []
        scale, raw, grad, update, *sums = call(
            functools.partial(norm_body, rows=rows, block=b, counts=[1, *halves[b * peers : (b + 1) * peers]]),
            "norm",
            scalars,
            [
                gain_row,
                wide(queries, b),
                wide(raw_inner, b),
                wide(grad_out, b),
                states(kv_state),
                *[p for arrays in from_peers[b * peers : (b + 1) * peers] for p in split_states(arrays, few)],
                *[states(w) for w in (updates if ends else [])],
            ],
            [Part(shape((BLOCK, DH), F32)), wide(block_tokens), wide(block_tokens), states(state), *ends],
            heads,
            few,
            flops=LONG if b > 0 else 2 * unit // blocks,
        )
        scales.append(scale)
        raws.append(raw)
        grads.append(grad)
        updates.append(update)
        back += [to_peers(update, away, True) for away in range(1, devices)]
    output, grad_q = call(
        functools.partial(query_grads_body, peers=peers, counts=halves),
        "query_grads",
        scalars,
        [
            gain_row,
            wide(keys),
            wide(values),
            states(kv_state),
            *[wide(d) for d in grads],
            *[wide(r) for r in raws],
            *[Part(s) for s in scales],
            *[part for arrays in from_peers for part in split_states(arrays, chunks)],
        ],
        [wide(tokens), wide(tokens)],
        heads,
        chunks,
        square,
        flops=LONG,
        after=back[:peers],
    )
    slices = exchanged((sums[0] if sums else updates[0]).reshape(total, -1, DH))
    slices, grad_q = lax.optimization_barrier((slices, grad_q))
    slices = scanned(slices, True)
    slices, late_queries = lax.optimization_barrier((slices, queries))
    part_k, part_v = call(
        functools.partial(key_grads_body, peers=peers),
        "key_grads",
        scalars,
        [
            wide(late_queries),
            wide(keys),
            wide(values),
            *[wide(d) for d in grads],
            *[states(w) for w in back],
        ],
        [wide(partial), wide(partial)],
        heads,
        chunks,
        square,
        flops=LONG,
    )
    grad_state = exchanged(slices).reshape(heads, DH, DH)
    grad_k, grad_v = call(
        last_body,
        "last",
        scalars,
        [wide(keys), wide(values), wide(part_k), wide(part_v), states(grad_state)],
        [wide(tokens), wide(tokens)],
        heads,
        chunks,
        flops=2 * unit,
        limit=NARROW_BYTES,
    )
    return output, grad_q, grad_k, grad_v


def solution(mesh):
    tokens = P(AXES, None)
    return jax.shard_map(
        local,
        mesh=mesh,
        in_specs=(tokens, tokens, tokens, tokens, P(), P(), P("ctx", None)),
        out_specs=(tokens, tokens, tokens, tokens),
        check_vma=False,
    )
```

```python
import functools

import jax
import jax.numpy as jnp
from jax import lax
from jax.experimental import pallas as pl
from jax.experimental.pallas import tpu as pltpu
from jax.sharding import PartitionSpec as P

DH = 128
GROUP = 512
BLOCK = 128
CHUNKS = 4
LONG = 400_000_000_000
VMEM_BYTES = 60 * 1024 * 1024
NARROW_BYTES = 53 * 1024 * 1024
SOME_BYTES = 24 * 1024 * 1024

eps_norm = 1e-06
BF = jnp.bfloat16
F32 = jnp.float32
AXES = ("ctx", "head")

NN = (((1,), (0,)), ((), ()))
NT = (((1,), (1,)), ((), ()))
TN = (((0,), (0,)), ((), ()))


def dot(a, b, dims):
    return lax.dot_general(a, b, dims, preferred_element_type=F32)


def bounds_of(len_ref):
    bounds, total = [], None
    for k in range(len_ref.shape[0] - 1):
        total = len_ref[k] if total is None else total + len_ref[k]
        bounds.append(total)
    return bounds


def segment(position, bounds):
    result = (position >= bounds[0]).astype(jnp.int32)
    for bound in bounds[1:]:
        result = result + (position >= bound).astype(jnp.int32)
    return result


def same(a, b):
    return (a == b).astype(F32)


class Place:
    def __init__(self, len_ref, rows, mask_ref=None):
        self.rows = rows
        self.blocks = rows // BLOCK
        self.devices = GROUP // rows
        self.bounds = bounds_of(len_ref)
        spot = lax.axis_index("head")
        index = lax.axis_index("ctx") * lax.axis_size("head") + spot
        self.first = index * rows
        self.part = lax.rem(spot, self.devices)
        self.group = lax.div(spot, self.devices)
        self.group_first = self.first - self.part * rows
        self.mask_ref = mask_ref

    def seg(self, position):
        return segment(position, self.bounds)

    def start(self, block):
        return self.first + block * BLOCK

    def row_segments(self, block):
        rows = lax.broadcasted_iota(jnp.int32, (BLOCK, 1), 0)
        return self.seg(rows + self.start(block))

    def pair(self, i, j):
        slot = jnp.clip(lax.div(i * (i - 1), 2) + j, 0, self.mask_ref.shape[1] - 1)
        return self.mask_ref[self.group, slot].astype(F32)

    def weights(self):
        rows = self.rows
        t = lax.broadcasted_iota(jnp.int32, (rows, rows), 0)
        s = lax.broadcasted_iota(jnp.int32, (rows, rows), 1)
        keep = (s <= t) & (self.seg(t + self.first) == self.seg(s + self.first))
        result = jnp.where(keep, 1.0, 0.0)
        for i in range(1, self.blocks):
            for j in range(i):
                bit = self.pair(self.part * self.blocks + i, self.part * self.blocks + j)
                inside = (
                    (t >= i * BLOCK)
                    & (t < (i + 1) * BLOCK)
                    & (s >= j * BLOCK)
                    & (s < (j + 1) * BLOCK)
                )
                result = jnp.where(inside, result * bit, result)
        return result

    def to_later(self, away, block):
        there = (self.part + away) * self.blocks + block
        edge = self.seg(self.start(block) + away * self.rows - 1)
        return [
            self.pair(there, self.part * self.blocks + j) * same(self.seg(self.start(j + 1) - 1), edge)
            for j in range(self.blocks)
        ]

    def before(self, block):
        edge = self.seg(self.start(block) - 1)
        carried = same(self.seg(self.group_first - 1), edge)
        peers = [(self.part >= away).astype(F32) for away in range(1, self.devices)]
        return carried, peers, (self.row_segments(block) == edge).astype(F32)

    def after(self, block):
        own = self.part * self.blocks + block
        edge = self.seg(self.start(block + 1))
        carried = same(self.seg(self.group_first + GROUP), edge)
        peers = []
        for i in range(self.blocks):
            for away in range(1, self.devices):
                there = (self.part + away < self.devices).astype(F32)
                other = (self.part + away) * self.blocks + i
                start = self.start(i) + away * self.rows
                peers.append(self.pair(other, own) * same(self.seg(start), edge) * there)
        return carried, peers, (self.row_segments(block) == edge).astype(F32)


def mixed(refs, factors, head):
    total = refs[0][head].astype(F32) * factors[0]
    for ref, factor in zip(refs[1:], factors[1:], strict=True):
        total = total + ref[head].astype(F32) * factor
    return total.astype(BF)


class Joined:
    def __init__(self, refs):
        self.refs, self.each = refs, refs[0].shape[0]

    def __getitem__(self, head):
        return self.refs[head // self.each][head % self.each]

    def __setitem__(self, head, value):
        self.refs[head // self.each][head % self.each] = value


def joined(refs, counts):
    result, at = [], 0
    for count in counts:
        result.append(Joined(refs[at : at + count]))
        at += count
    return result


def columns(head):
    return pl.ds(head * DH, DH)


def rows_of(block):
    return pl.ds(block * BLOCK, BLOCK)


def state_body(place_of, ins, outs, scratch, arrive, leave, chunks, *, counts, own):
    k_ref, v_ref = ins
    outs = joined(outs, counts)
    rows, width = k_ref.shape
    place = place_of(rows)
    last = place.seg(place.start(place.blocks) - 1)
    ends = [place.seg(place.start(b + 1) - 1) for b in range(place.blocks)]
    masks = [(place.row_segments(b) == ends[b]).astype(BF) for b in range(place.blocks)]
    if own:
        wanted = [[same(e, last) for e in ends]]
    else:
        wanted = [
            place.to_later(away, b) for b in range(place.blocks) for away in range(1, place.devices)
        ]
    for c, heads in enumerate(chunks):
        arrive(c)
        for head in heads:
            updates = []
            for b in range(place.blocks):
                k = k_ref[rows_of(b), columns(head)] * masks[b]
                updates.append(dot(k, v_ref[rows_of(b), columns(head)], TN))
            for ref, factors in zip(outs, wanted, strict=True):
                total = updates[0] * factors[0]
                for update, factor in zip(updates[1:], factors[1:], strict=True):
                    total = total + update * factor
                ref[head] = total.astype(BF)
        leave(c)


def inner_body(place_of, ins, outs, scratch, arrive, leave, chunks):
    q_ref, k_ref, v_ref = ins
    (raw_ref,), (weight_ref,) = outs, scratch
    weight_ref[...] = place_of(q_ref.shape[0]).weights()
    for c, heads in enumerate(chunks):
        arrive(c)
        for head in heads:
            at = columns(head)
            probs = (dot(q_ref[:, at], k_ref[:, at], NT) * weight_ref[...]).astype(BF)
            raw_ref[:, at] = dot(probs, v_ref[:, at], NN)
        leave(c)


def scan_body(place_of, ins, outs, scratch, arrive, leave, chunks, *, rows, backward):
    (t_ref,), (out_ref,) = ins, outs
    count, height, _ = t_ref.shape
    devices = GROUP // rows
    bounds = place_of(rows).bounds
    part = height // len(chunks)
    for c in range(len(chunks)):
        arrive(c)
        at = pl.ds(c * part, part)

        def one(turn, acc):
            group = count // devices - 1 - turn if backward else turn
            for k in range(devices):
                out_ref[group * devices + k, at] = acc.astype(BF)
            for k in range(devices):
                index = group * devices + (devices - 1 - k if backward else k)
                first = index * rows
                if backward:
                    keep = same(segment(first, bounds), segment(first + rows, bounds))
                else:
                    keep = same(segment(first - 1, bounds), segment(first + rows - 1, bounds))
                acc = acc * keep + t_ref[index, at].astype(F32)
            return acc

        acc = jnp.zeros((part, DH), F32)
        if count <= 32:
            for turn in range(count // devices):
                acc = one(turn, acc)
        else:
            lax.fori_loop(0, count // devices, one, acc)
        leave(c)


def norm_body(place_of, ins, outs, scratch, arrive, leave, chunks, *, rows, block, counts):
    gain_ref, q_ref, raw_ref, grad_ref = ins[:4]
    held = 4 + sum(counts)
    state_refs, earlier_refs = joined(ins[4:held], counts), ins[held:]
    scale_ref, held_ref, d_ref, w_ref, *t_refs = outs
    width = q_ref.shape[1]
    place = place_of(rows)
    carried, there, reach = place.before(block)
    squares = cross = jnp.zeros((BLOCK, DH), F32)
    for c, heads in enumerate(chunks):
        arrive(c)
        for head in heads:
            at = columns(head)
            state = mixed(state_refs, [carried, *there], head)
            raw = raw_ref[:, at] + dot(q_ref[:, at], state, NN) * reach
            raw = raw.astype(BF)
            held_ref[:, at] = raw
            raw = raw.astype(F32)
            scaled = grad_ref[:, at].astype(F32) * gain_ref[:, at]
            squares = squares + raw * raw
            cross = cross + scaled * raw
        leave(c, [1])
    total = jnp.sum(squares, axis=1, keepdims=True)
    inverse = 1.0 / jnp.sqrt(total / width + eps_norm)
    mean = jnp.sum(cross, axis=1, keepdims=True) * inverse / width
    scale_ref[...] = jnp.broadcast_to(inverse, scale_ref.shape)
    leave(0, [0])
    own = place.seg(place.start(block))
    begin = (place.row_segments(block) == own).astype(BF)
    into = [same(place.seg(place.start(b)), place.seg(place.first)) for b in range(block + 1)]
    for c, heads in enumerate(chunks):
        for head in heads:
            at = columns(head)
            normed = held_ref[:, at].astype(F32) * inverse
            scaled = grad_ref[:, at].astype(F32) * gain_ref[:, at]
            grad = ((scaled - normed * mean) * inverse).astype(BF)
            d_ref[:, at] = grad
            update = dot(q_ref[:, at] * begin, grad, TN)
            w_ref[head] = update.astype(BF)
            for t_ref in t_refs:
                sums = update * into[block]
                for ref, factor in zip(earlier_refs, into[:block], strict=True):
                    sums = sums + ref[head].astype(F32) * factor
                t_ref[head] = sums.astype(BF)
        leave(c, range(2, len(outs)))


def query_grads_body(place_of, ins, outs, scratch, arrive, leave, chunks, *, peers, counts):
    gain_ref, k_ref, v_ref, kv_ref = ins[:4]
    rows, width = k_ref.shape
    place = place_of(rows)
    blocks = place.blocks
    rest = ins[4:]
    d_refs, raw_refs, scale_refs = rest[:blocks], rest[blocks : 2 * blocks], rest[2 * blocks : 3 * blocks]
    peer_refs = joined(rest[3 * blocks :], counts)
    out_ref, gq_ref = outs
    (weight_ref,) = scratch
    weight_ref[...] = place.weights()
    factors = [place.before(b) for b in range(blocks)]
    for c, heads in enumerate(chunks):
        arrive(c)
        for head in heads:
            at = columns(head)
            d = jnp.concatenate([ref[:, at] for ref in d_refs], axis=0)
            grad_probs = (dot(d, v_ref[:, at], NT) * weight_ref[...]).astype(BF)
            inner = dot(grad_probs, k_ref[:, at], NN)
            for b in range(blocks):
                carried, there, _ = factors[b]
                state = mixed([kv_ref, *peer_refs[b * peers : (b + 1) * peers]], [carried, *there], head)
                outer = dot(d_refs[b][:, at], state, NT) * factors[b][2]
                part = inner[b * BLOCK : (b + 1) * BLOCK] + outer
                gq_ref[rows_of(b), at] = part.astype(BF)
                normed = raw_refs[b][:, at].astype(F32) * scale_refs[b][...]
                out_ref[rows_of(b), at] = (normed * gain_ref[:, at]).astype(BF)
        leave(c)


def key_grads_body(place_of, ins, outs, scratch, arrive, leave, chunks, *, peers):
    q_ref, k_ref, v_ref, *rest = ins
    place = place_of(q_ref.shape[0])
    blocks = place.blocks
    d_refs, w_refs = rest[:blocks], rest[blocks:]
    gk_ref, gv_ref = outs
    (weight_ref,) = scratch
    weight_ref[...] = place.weights()
    factors = [place.after(b) for b in range(blocks)]
    for c, heads in enumerate(chunks):
        arrive(c)
        for head in heads:
            at = columns(head)
            q, d = q_ref[:, at], jnp.concatenate([ref[:, at] for ref in d_refs], axis=0)
            probs = (dot(q, k_ref[:, at], NT) * weight_ref[...]).astype(BF)
            grad_probs = (dot(d, v_ref[:, at], NT) * weight_ref[...]).astype(BF)
            gk = dot(grad_probs, q, TN)
            gv = dot(probs, d, TN)
            for b in range(blocks):
                at_rows, here = rows_of(b), slice(b * BLOCK, (b + 1) * BLOCK)
                part_k, part_v = gk[here], gv[here]
                if peers:
                    state = mixed(w_refs, factors[b][1], head)
                    part_k = part_k + dot(v_ref[at_rows, at], state, NT) * factors[b][2]
                    part_v = part_v + dot(k_ref[at_rows, at], state, NN) * factors[b][2]
                gk_ref[at_rows, at] = part_k
                gv_ref[at_rows, at] = part_v
        leave(c)


def last_body(place_of, ins, outs, scratch, arrive, leave, chunks):
    k_ref, v_ref, gk_in, gv_in, gs_ref = ins
    gk_ref, gv_ref = outs
    place = place_of(k_ref.shape[0])
    factors = [place.after(b) for b in range(place.blocks)]
    reach = jnp.concatenate([reach * carried for carried, _, reach in factors], axis=0)
    for c, heads in enumerate(chunks):
        arrive(c)
        for head in heads:
            at = columns(head)
            gk = gk_in[:, at] + dot(v_ref[:, at], gs_ref[head], NT) * reach
            gv = gv_in[:, at] + dot(k_ref[:, at], gs_ref[head], NN) * reach
            gk_ref[:, at] = gk.astype(BF)
            gv_ref[:, at] = gv.astype(BF)
        leave(c)


class Part:
    def __init__(self, array, axis=None, block=None, near=False, lead=0, parts=None):
        self.array, self.axis, self.block, self.near = array, axis, block, near
        self.lead, self.parts = lead, parts
        self.shape = array.shape if block is None else (BLOCK, *array.shape[1:])
        self.spec = pl.BlockSpec(memory_space=pltpu.VMEM if near else pltpu.HBM)

    def pieces(self, far, near, sems, count):
        far = far if self.block is None else far.at[rows_of(self.block)]
        if self.axis is None:
            return [(far, near, sems.at[0])]
        count = self.parts or count
        size = self.shape[self.axis] // count
        result = [None] * self.lead
        for c in range(count):
            at = [slice(None)] * len(self.shape)
            at[self.axis] = pl.ds(c * size, size)
            result.append((far.at[tuple(at)], near.at[tuple(at)], sems.at[c]))
        return result


def call(body, name, scalars, ins, outs, heads, chunks, scratch=(), flops=0, after=(), limit=VMEM_BYTES):
    far = [p for p in (*ins, *outs) if not p.near]
    sizes = (len(scalars), len(ins), len(after), len(outs), len(far), 2, len(scratch))

    def kernel(*refs):
        split, at = [], 0
        for size in sizes:
            split.append(refs[at : at + size])
            at += size
        settings, in_refs, _, out_refs, buffers, (in_sems, out_sems), rest = split
        buffers = iter(buffers)

        def opened(parts, given, sems):
            refs, pieces = [], []
            for i, (part, ref) in enumerate(zip(parts, given, strict=True)):
                refs.append(ref if part.near else next(buffers))
                pieces.append([] if part.near else part.pieces(ref, refs[-1], sems.at[i], chunks))
            return refs, pieces

        near_in, coming = opened(ins, in_refs, in_sems)
        near_out, going = opened(outs, out_refs, out_sems)

        def copies(parts, c, which=None):
            for i, pieces in enumerate(parts):
                if c < len(pieces) and pieces[c] is not None and (which is None or i in which):
                    yield pieces[c]

        def arrive(c):
            for far, near, sem in copies(coming, c):
                pltpu.make_async_copy(far, near, sem).wait()

        def leave(c, which=None):
            for far, near, sem in copies(going, c, which):
                pltpu.make_async_copy(near, far, sem).start()

        for c in range(chunks):
            for far, near, sem in copies(coming, c):
                pltpu.make_async_copy(far, near, sem).start()
        each = heads // chunks
        turns = [range(c * each, (c + 1) * each) for c in range(chunks)]
        place_of = lambda rows: Place(settings[0], rows, *settings[1:])
        body(place_of, near_in, near_out, rest, arrive, leave, turns)
        for c in range(chunks):
            for far, near, sem in copies(going, c):
                pltpu.make_async_copy(near, far, sem).wait()

    anywhere = pl.BlockSpec(memory_space=pl.ANY)
    return pl.pallas_call(
        kernel,
        name=name,
        in_specs=[
            *[pl.BlockSpec(memory_space=pltpu.SMEM)] * len(scalars),
            *[p.spec for p in ins],
            *[anywhere] * len(after),
        ],
        out_specs=[p.spec for p in outs],
        out_shape=[p.array for p in outs],
        scratch_shapes=[
            *[pltpu.VMEM(p.shape, p.array.dtype) for p in far],
            pltpu.SemaphoreType.DMA((len(ins), chunks)),
            pltpu.SemaphoreType.DMA((len(outs), chunks)),
            *scratch,
        ],
        compiler_params=pltpu.CompilerParams(vmem_limit_bytes=limit),
        cost_estimate=pl.CostEstimate(
            flops=flops,
            bytes_accessed=sum(p.array.size * p.array.dtype.itemsize for p in (*ins, *outs)),
            transcendentals=0,
        ),
    )(*scalars, *[p.array for p in ins], *after)


def local(queries, keys, values, grad_out, gain, lengths, block_mask):
    rows, width = queries.shape
    heads = width // DH
    blocks = rows // BLOCK
    devices = GROUP // rows
    peers = devices - 1
    head_count = lax.axis_size("head")
    total = lax.axis_size("ctx") * head_count
    chunks = CHUNKS if heads % CHUNKS == 0 else 1
    few = min(chunks, 2)
    shape = jax.ShapeDtypeStruct
    state = shape((heads, DH, DH), BF)
    tokens = shape((rows, width), BF)
    partial = shape((rows, width), F32)
    block_tokens = shape((BLOCK, width), BF)
    square = [pltpu.VMEM((rows, rows), F32)]
    unit = 2 * rows * width * DH
    inner = 2 * rows * rows * width
    scalars = [lengths, block_mask]

    def wide(array, block=None):
        return Part(array, 1, block)

    def states(array):
        return Part(array, 0)

    def split_states(arrays, chunks):
        count = chunks // len(arrays)
        return [Part(a, 0, lead=i * count, parts=count) for i, a in enumerate(arrays)]

    def to_peers(array, away, backward):
        pairs = [(z, z + away) for z in range(head_count - away) if z % devices + away < devices]
        if backward:
            pairs = [(b, a) for a, b in pairs]
        return lax.ppermute(array, "head", pairs)

    def exchanged(slices):
        return lax.all_to_all(slices, AXES, split_axis=0, concat_axis=0, tiled=True)

    def scanned(slices, backward):
        (slices,) = call(
            functools.partial(scan_body, rows=rows, backward=backward),
            "scan",
            [lengths],
            [Part(slices, near=True)],
            [Part(shape(slices.shape, BF), 1)],
            heads,
            2 if slices.shape[1] % 32 == 0 else 1,
            limit=SOME_BYTES,
        )
        return slices

    gain_row = Part(gain.reshape(1, width))
    halves = [2 if b > 0 and chunks % 2 == 0 else 1 for b in range(blocks) for _ in range(peers)]
    later = [[shape((heads // n, DH, DH), BF)] * n for n in halves]
    (sum_kv,) = call(
        functools.partial(state_body, counts=[1], own=True),
        "total",
        scalars,
        [wide(keys), wide(values)],
        [states(state)],
        heads,
        few,
        flops=unit,
    )
    slices = sum_kv.reshape(total, -1, DH)
    slices, late_keys = lax.optimization_barrier((slices, keys))
    slices = exchanged(slices)
    if later:
        later = call(
            functools.partial(state_body, counts=halves, own=False),
            "states",
            scalars,
            [wide(late_keys), wide(values)],
            [part for arrays in later for part in split_states(arrays, few)],
            heads,
            few,
            flops=LONG,
        )
    later = iter(later)
    from_peers = [[next(later) for _ in range(n)] for n in halves]
    for at, arrays in enumerate(from_peers):
        arrays[0] = to_peers(arrays[0], 1 + at % peers, False)
    slices = scanned(slices, False)
    slices, late_queries = lax.optimization_barrier((slices, queries))
    (raw_inner,) = call(
        inner_body,
        "inner",
        scalars,
        [wide(late_queries), wide(keys), wide(values)],
        [wide(partial)],
        heads,
        chunks,
        square,
        flops=LONG,
        after=[x for arrays in from_peers[:peers] for x in arrays],
    )
    kv_state = exchanged(slices).reshape(heads, DH, DH)
    for at, arrays in enumerate(from_peers):
        if len(arrays) > 1:
            held = lax.optimization_barrier((arrays[1], kv_state, raw_inner))
            later_half, kv_state, raw_inner = held
            arrays[1] = to_peers(later_half, 1 + at % peers, False)

    scales, raws, grads, updates, back = [], [], [], [], []
    for b in range(blocks):
        ends = [states(state)] if b == blocks - 1 and blocks > 1 else []
        scale, raw, grad, update, *sums = call(
            functools.partial(norm_body, rows=rows, block=b, counts=[1, *halves[b * peers : (b + 1) * peers]]),
            "norm",
            scalars,
            [
                gain_row,
                wide(queries, b),
                wide(raw_inner, b),
                wide(grad_out, b),
                states(kv_state),
                *[p for arrays in from_peers[b * peers : (b + 1) * peers] for p in split_states(arrays, few)],
                *[states(w) for w in (updates if ends else [])],
            ],
            [Part(shape((BLOCK, DH), F32)), wide(block_tokens), wide(block_tokens), states(state), *ends],
            heads,
            few,
            flops=LONG if b > 0 else 2 * unit // blocks,
        )
        scales.append(scale)
        raws.append(raw)
        grads.append(grad)
        updates.append(update)
        back += [to_peers(update, away, True) for away in range(1, devices)]
    output, grad_q = call(
        functools.partial(query_grads_body, peers=peers, counts=halves),
        "query_grads",
        scalars,
        [
            gain_row,
            wide(keys),
            wide(values),
            states(kv_state),
            *[wide(d) for d in grads],
            *[wide(r) for r in raws],
            *[Part(s) for s in scales],
            *[part for arrays in from_peers for part in split_states(arrays, chunks)],
        ],
        [wide(tokens), wide(tokens)],
        heads,
        chunks,
        square,
        flops=LONG,
        after=back[:peers],
    )
    slices = exchanged((sums[0] if sums else updates[0]).reshape(total, -1, DH))
    slices, grad_q = lax.optimization_barrier((slices, grad_q))
    slices = scanned(slices, True)
    slices, late_queries = lax.optimization_barrier((slices, queries))
    part_k, part_v = call(
        functools.partial(key_grads_body, peers=peers),
        "key_grads",
        scalars,
        [
            wide(late_queries),
            wide(keys),
            wide(values),
            *[wide(d) for d in grads],
            *[states(w) for w in back],
        ],
        [wide(partial), wide(partial)],
        heads,
        chunks,
        square,
        flops=LONG,
    )
    grad_state = exchanged(slices).reshape(heads, DH, DH)
    grad_k, grad_v = call(
        last_body,
        "last",
        scalars,
        [wide(keys), wide(values), wide(part_k), wide(part_v), states(grad_state)],
        [wide(tokens), wide(tokens)],
        heads,
        few,
        flops=2 * unit,
        limit=NARROW_BYTES,
    )
    return output, grad_q, grad_k, grad_v


def solution(mesh):
    tokens = P(AXES, None)
    return jax.shard_map(
        local,
        mesh=mesh,
        in_specs=(tokens, tokens, tokens, tokens, P(), P(), P("ctx", None)),
        out_specs=(tokens, tokens, tokens, tokens),
        check_vma=False,
    )
```

```python
import functools

import jax
import jax.numpy as jnp
from jax import lax
from jax.experimental import pallas as pl
from jax.experimental.pallas import tpu as pltpu
from jax.sharding import PartitionSpec as P

DH = 128
GROUP = 512
BLOCK = 128
CHUNKS = 4
LONG = 400_000_000_000
VMEM_BYTES = 60 * 1024 * 1024
NARROW_BYTES = 53 * 1024 * 1024
SOME_BYTES = 24 * 1024 * 1024

eps_norm = 1e-06
BF = jnp.bfloat16
F32 = jnp.float32
AXES = ("ctx", "head")

NN = (((1,), (0,)), ((), ()))
NT = (((1,), (1,)), ((), ()))
TN = (((0,), (0,)), ((), ()))


def dot(a, b, dims):
    return lax.dot_general(a, b, dims, preferred_element_type=F32)


def bounds_of(len_ref):
    bounds, total = [], None
    for k in range(len_ref.shape[0] - 1):
        total = len_ref[k] if total is None else total + len_ref[k]
        bounds.append(total)
    return bounds


def segment(position, bounds):
    result = (position >= bounds[0]).astype(jnp.int32)
    for bound in bounds[1:]:
        result = result + (position >= bound).astype(jnp.int32)
    return result


def same(a, b):
    return (a == b).astype(F32)


class Place:
    def __init__(self, len_ref, rows, mask_ref=None):
        self.rows = rows
        self.blocks = rows // BLOCK
        self.devices = GROUP // rows
        self.bounds = bounds_of(len_ref)
        spot = lax.axis_index("head")
        index = lax.axis_index("ctx") * lax.axis_size("head") + spot
        self.first = index * rows
        self.part = lax.rem(spot, self.devices)
        self.group = lax.div(spot, self.devices)
        self.group_first = self.first - self.part * rows
        self.mask_ref = mask_ref

    def seg(self, position):
        return segment(position, self.bounds)

    def start(self, block):
        return self.first + block * BLOCK

    def row_segments(self, block):
        rows = lax.broadcasted_iota(jnp.int32, (BLOCK, 1), 0)
        return self.seg(rows + self.start(block))

    def pair(self, i, j):
        slot = jnp.clip(lax.div(i * (i - 1), 2) + j, 0, self.mask_ref.shape[1] - 1)
        return self.mask_ref[self.group, slot].astype(F32)

    def weights(self):
        rows = self.rows
        t = lax.broadcasted_iota(jnp.int32, (rows, rows), 0)
        s = lax.broadcasted_iota(jnp.int32, (rows, rows), 1)
        keep = (s <= t) & (self.seg(t + self.first) == self.seg(s + self.first))
        result = jnp.where(keep, 1.0, 0.0)
        for i in range(1, self.blocks):
            for j in range(i):
                bit = self.pair(self.part * self.blocks + i, self.part * self.blocks + j)
                inside = (
                    (t >= i * BLOCK)
                    & (t < (i + 1) * BLOCK)
                    & (s >= j * BLOCK)
                    & (s < (j + 1) * BLOCK)
                )
                result = jnp.where(inside, result * bit, result)
        return result

    def to_later(self, away, block):
        there = (self.part + away) * self.blocks + block
        edge = self.seg(self.start(block) + away * self.rows - 1)
        return [
            self.pair(there, self.part * self.blocks + j) * same(self.seg(self.start(j + 1) - 1), edge)
            for j in range(self.blocks)
        ]

    def before(self, block):
        edge = self.seg(self.start(block) - 1)
        carried = same(self.seg(self.group_first - 1), edge)
        peers = [(self.part >= away).astype(F32) for away in range(1, self.devices)]
        return carried, peers, (self.row_segments(block) == edge).astype(F32)

    def after(self, block):
        own = self.part * self.blocks + block
        edge = self.seg(self.start(block + 1))
        carried = same(self.seg(self.group_first + GROUP), edge)
        peers = []
        for i in range(self.blocks):
            for away in range(1, self.devices):
                there = (self.part + away < self.devices).astype(F32)
                other = (self.part + away) * self.blocks + i
                start = self.start(i) + away * self.rows
                peers.append(self.pair(other, own) * same(self.seg(start), edge) * there)
        return carried, peers, (self.row_segments(block) == edge).astype(F32)


def mixed(refs, factors, head):
    total = refs[0][head].astype(F32) * factors[0]
    for ref, factor in zip(refs[1:], factors[1:], strict=True):
        total = total + ref[head].astype(F32) * factor
    return total.astype(BF)


class Joined:
    def __init__(self, refs):
        self.refs, self.each = refs, refs[0].shape[0]

    def __getitem__(self, head):
        return self.refs[head // self.each][head % self.each]

    def __setitem__(self, head, value):
        self.refs[head // self.each][head % self.each] = value


def joined(refs, counts):
    result, at = [], 0
    for count in counts:
        result.append(Joined(refs[at : at + count]))
        at += count
    return result


def columns(head):
    return pl.ds(head * DH, DH)


def rows_of(block):
    return pl.ds(block * BLOCK, BLOCK)


def total_body(place_of, ins, outs, scratch, arrive, leave, chunks):
    k_ref, v_ref = ins
    (t_ref,) = outs
    place = place_of(k_ref.shape[0])
    last = place.seg(place.start(place.blocks) - 1)
    segments = [place.row_segments(b) for b in range(place.blocks)]
    mask = (jnp.concatenate(segments, axis=0) == last).astype(BF)
    for c, heads in enumerate(chunks):
        arrive(c)
        for head in heads:
            at = columns(head)
            t_ref[head] = dot(k_ref[:, at] * mask, v_ref[:, at], TN).astype(BF)
        leave(c)


def state_body(place_of, ins, outs, scratch, arrive, leave, chunks, *, counts):
    k_ref, v_ref = ins
    outs = joined(outs, counts)
    rows, width = k_ref.shape
    place = place_of(rows)
    ends = [place.seg(place.start(b + 1) - 1) for b in range(place.blocks)]
    masks = [(place.row_segments(b) == ends[b]).astype(BF) for b in range(place.blocks)]
    wanted = [
        place.to_later(away, b) for b in range(place.blocks) for away in range(1, place.devices)
    ]
    for c, heads in enumerate(chunks):
        arrive(c)
        for head in heads:
            updates = []
            for b in range(place.blocks):
                k = k_ref[rows_of(b), columns(head)] * masks[b]
                updates.append(dot(k, v_ref[rows_of(b), columns(head)], TN))
            for ref, factors in zip(outs, wanted, strict=True):
                total = updates[0] * factors[0]
                for update, factor in zip(updates[1:], factors[1:], strict=True):
                    total = total + update * factor
                ref[head] = total.astype(BF)
        leave(c)


def inner_body(place_of, ins, outs, scratch, arrive, leave, chunks):
    q_ref, k_ref, v_ref = ins
    (raw_ref,), (weight_ref,) = outs, scratch
    weight_ref[...] = place_of(q_ref.shape[0]).weights()
    for c, heads in enumerate(chunks):
        arrive(c)
        for head in heads:
            at = columns(head)
            probs = (dot(q_ref[:, at], k_ref[:, at], NT) * weight_ref[...]).astype(BF)
            raw_ref[:, at] = dot(probs, v_ref[:, at], NN)
        leave(c)


def scan_body(place_of, ins, outs, scratch, arrive, leave, chunks, *, rows, backward):
    (t_ref,), (out_ref,) = ins, outs
    count, height, _ = t_ref.shape
    devices = GROUP // rows
    bounds = place_of(rows).bounds
    part = height // len(chunks)
    for c in range(len(chunks)):
        arrive(c)
        at = pl.ds(c * part, part)

        def one(turn, acc):
            group = count // devices - 1 - turn if backward else turn
            for k in range(devices):
                out_ref[group * devices + k, at] = acc.astype(BF)
            for k in range(devices):
                index = group * devices + (devices - 1 - k if backward else k)
                first = index * rows
                if backward:
                    keep = same(segment(first, bounds), segment(first + rows, bounds))
                else:
                    keep = same(segment(first - 1, bounds), segment(first + rows - 1, bounds))
                acc = acc * keep + t_ref[index, at].astype(F32)
            return acc

        acc = jnp.zeros((part, DH), F32)
        if count <= 32:
            for turn in range(count // devices):
                acc = one(turn, acc)
        else:
            lax.fori_loop(0, count // devices, one, acc)
        leave(c)


def norm_body(place_of, ins, outs, scratch, arrive, leave, chunks, *, rows, block, counts):
    gain_ref, q_ref, raw_ref, grad_ref = ins[:4]
    held = 4 + sum(counts)
    state_refs, earlier_refs = joined(ins[4:held], counts), ins[held:]
    scale_ref, held_ref, d_ref, w_ref, *t_refs = outs
    width = q_ref.shape[1]
    place = place_of(rows)
    carried, there, reach = place.before(block)
    squares = cross = jnp.zeros((BLOCK, DH), F32)
    for c, heads in enumerate(chunks):
        arrive(c)
        for head in heads:
            at = columns(head)
            state = mixed(state_refs, [carried, *there], head)
            raw = raw_ref[:, at] + dot(q_ref[:, at], state, NN) * reach
            raw = raw.astype(BF)
            held_ref[:, at] = raw
            raw = raw.astype(F32)
            scaled = grad_ref[:, at].astype(F32) * gain_ref[:, at]
            squares = squares + raw * raw
            cross = cross + scaled * raw
        leave(c, [1])
    total = jnp.sum(squares, axis=1, keepdims=True)
    inverse = 1.0 / jnp.sqrt(total / width + eps_norm)
    mean = jnp.sum(cross, axis=1, keepdims=True) * inverse / width
    scale_ref[...] = jnp.broadcast_to(inverse, scale_ref.shape)
    leave(0, [0])
    own = place.seg(place.start(block))
    begin = (place.row_segments(block) == own).astype(BF)
    into = [same(place.seg(place.start(b)), place.seg(place.first)) for b in range(block + 1)]
    for c, heads in enumerate(chunks):
        for head in heads:
            at = columns(head)
            normed = held_ref[:, at].astype(F32) * inverse
            scaled = grad_ref[:, at].astype(F32) * gain_ref[:, at]
            grad = ((scaled - normed * mean) * inverse).astype(BF)
            d_ref[:, at] = grad
            update = dot(q_ref[:, at] * begin, grad, TN)
            w_ref[head] = update.astype(BF)
            for t_ref in t_refs:
                sums = update * into[block]
                for ref, factor in zip(earlier_refs, into[:block], strict=True):
                    sums = sums + ref[head].astype(F32) * factor
                t_ref[head] = sums.astype(BF)
        leave(c, range(2, len(outs)))


def query_grads_body(place_of, ins, outs, scratch, arrive, leave, chunks, *, peers, counts):
    gain_ref, k_ref, v_ref, kv_ref = ins[:4]
    rows, width = k_ref.shape
    place = place_of(rows)
    blocks = place.blocks
    rest = ins[4:]
    d_refs, raw_refs, scale_refs = rest[:blocks], rest[blocks : 2 * blocks], rest[2 * blocks : 3 * blocks]
    peer_refs = joined(rest[3 * blocks :], counts)
    out_ref, gq_ref = outs
    (weight_ref,) = scratch
    weight_ref[...] = place.weights()
    factors = [place.before(b) for b in range(blocks)]
    for c, heads in enumerate(chunks):
        arrive(c)
        for head in heads:
            at = columns(head)
            d = jnp.concatenate([ref[:, at] for ref in d_refs], axis=0)
            grad_probs = (dot(d, v_ref[:, at], NT) * weight_ref[...]).astype(BF)
            inner = dot(grad_probs, k_ref[:, at], NN)
            for b in range(blocks):
                carried, there, _ = factors[b]
                state = mixed([kv_ref, *peer_refs[b * peers : (b + 1) * peers]], [carried, *there], head)
                outer = dot(d_refs[b][:, at], state, NT) * factors[b][2]
                part = inner[b * BLOCK : (b + 1) * BLOCK] + outer
                gq_ref[rows_of(b), at] = part.astype(BF)
                normed = raw_refs[b][:, at].astype(F32) * scale_refs[b][...]
                out_ref[rows_of(b), at] = (normed * gain_ref[:, at]).astype(BF)
        leave(c)


def key_grads_body(place_of, ins, outs, scratch, arrive, leave, chunks, *, peers):
    q_ref, k_ref, v_ref, *rest = ins
    place = place_of(q_ref.shape[0])
    blocks = place.blocks
    d_refs, w_refs = rest[:blocks], rest[blocks:]
    gk_ref, gv_ref = outs
    (weight_ref,) = scratch
    weight_ref[...] = place.weights()
    factors = [place.after(b) for b in range(blocks)]
    for c, heads in enumerate(chunks):
        arrive(c)
        for head in heads:
            at = columns(head)
            q, d = q_ref[:, at], jnp.concatenate([ref[:, at] for ref in d_refs], axis=0)
            probs = (dot(q, k_ref[:, at], NT) * weight_ref[...]).astype(BF)
            grad_probs = (dot(d, v_ref[:, at], NT) * weight_ref[...]).astype(BF)
            gk = dot(grad_probs, q, TN)
            gv = dot(probs, d, TN)
            for b in range(blocks):
                at_rows, here = rows_of(b), slice(b * BLOCK, (b + 1) * BLOCK)
                part_k, part_v = gk[here], gv[here]
                if peers:
                    state = mixed(w_refs, factors[b][1], head)
                    part_k = part_k + dot(v_ref[at_rows, at], state, NT) * factors[b][2]
                    part_v = part_v + dot(k_ref[at_rows, at], state, NN) * factors[b][2]
                gk_ref[at_rows, at] = part_k
                gv_ref[at_rows, at] = part_v
        leave(c)


def last_body(place_of, ins, outs, scratch, arrive, leave, chunks):
    k_ref, v_ref, gk_in, gv_in, gs_ref = ins
    gk_ref, gv_ref = outs
    place = place_of(k_ref.shape[0])
    factors = [place.after(b) for b in range(place.blocks)]
    reach = jnp.concatenate([reach * carried for carried, _, reach in factors], axis=0)
    for c, heads in enumerate(chunks):
        arrive(c)
        for head in heads:
            at = columns(head)
            gk = gk_in[:, at] + dot(v_ref[:, at], gs_ref[head], NT) * reach
            gv = gv_in[:, at] + dot(k_ref[:, at], gs_ref[head], NN) * reach
            gk_ref[:, at] = gk.astype(BF)
            gv_ref[:, at] = gv.astype(BF)
        leave(c)


class Part:
    def __init__(self, array, axis=None, block=None, near=False, lead=0, parts=None):
        self.array, self.axis, self.block, self.near = array, axis, block, near
        self.lead, self.parts = lead, parts
        self.shape = array.shape if block is None else (BLOCK, *array.shape[1:])
        self.spec = pl.BlockSpec(memory_space=pltpu.VMEM if near else pltpu.HBM)

    def pieces(self, far, near, sems, count):
        far = far if self.block is None else far.at[rows_of(self.block)]
        if self.axis is None:
            return [(far, near, sems.at[0])]
        count = self.parts or count
        size = self.shape[self.axis] // count
        result = [None] * self.lead
        for c in range(count):
            at = [slice(None)] * len(self.shape)
            at[self.axis] = pl.ds(c * size, size)
            result.append((far.at[tuple(at)], near.at[tuple(at)], sems.at[c]))
        return result


def call(body, name, scalars, ins, outs, heads, chunks, scratch=(), flops=0, after=(), limit=VMEM_BYTES):
    far = [p for p in (*ins, *outs) if not p.near]
    sizes = (len(scalars), len(ins), len(after), len(outs), len(far), 2, len(scratch))

    def kernel(*refs):
        split, at = [], 0
        for size in sizes:
            split.append(refs[at : at + size])
            at += size
        settings, in_refs, _, out_refs, buffers, (in_sems, out_sems), rest = split
        buffers = iter(buffers)

        def opened(parts, given, sems):
            refs, pieces = [], []
            for i, (part, ref) in enumerate(zip(parts, given, strict=True)):
                refs.append(ref if part.near else next(buffers))
                pieces.append([] if part.near else part.pieces(ref, refs[-1], sems.at[i], chunks))
            return refs, pieces

        near_in, coming = opened(ins, in_refs, in_sems)
        near_out, going = opened(outs, out_refs, out_sems)

        def copies(parts, c, which=None):
            for i, pieces in enumerate(parts):
                if c < len(pieces) and pieces[c] is not None and (which is None or i in which):
                    yield pieces[c]

        def arrive(c):
            for far, near, sem in copies(coming, c):
                pltpu.make_async_copy(far, near, sem).wait()

        def leave(c, which=None):
            for far, near, sem in copies(going, c, which):
                pltpu.make_async_copy(near, far, sem).start()

        for c in range(chunks):
            for far, near, sem in copies(coming, c):
                pltpu.make_async_copy(far, near, sem).start()
        each = heads // chunks
        turns = [range(c * each, (c + 1) * each) for c in range(chunks)]
        place_of = lambda rows: Place(settings[0], rows, *settings[1:])
        body(place_of, near_in, near_out, rest, arrive, leave, turns)
        for c in range(chunks):
            for far, near, sem in copies(going, c):
                pltpu.make_async_copy(near, far, sem).wait()

    anywhere = pl.BlockSpec(memory_space=pl.ANY)
    return pl.pallas_call(
        kernel,
        name=name,
        in_specs=[
            *[pl.BlockSpec(memory_space=pltpu.SMEM)] * len(scalars),
            *[p.spec for p in ins],
            *[anywhere] * len(after),
        ],
        out_specs=[p.spec for p in outs],
        out_shape=[p.array for p in outs],
        scratch_shapes=[
            *[pltpu.VMEM(p.shape, p.array.dtype) for p in far],
            pltpu.SemaphoreType.DMA((len(ins), chunks)),
            pltpu.SemaphoreType.DMA((len(outs), chunks)),
            *scratch,
        ],
        compiler_params=pltpu.CompilerParams(vmem_limit_bytes=limit),
        cost_estimate=pl.CostEstimate(
            flops=flops,
            bytes_accessed=sum(p.array.size * p.array.dtype.itemsize for p in (*ins, *outs)),
            transcendentals=0,
        ),
    )(*scalars, *[p.array for p in ins], *after)


def local(queries, keys, values, grad_out, gain, lengths, block_mask):
    rows, width = queries.shape
    heads = width // DH
    blocks = rows // BLOCK
    devices = GROUP // rows
    peers = devices - 1
    head_count = lax.axis_size("head")
    total = lax.axis_size("ctx") * head_count
    chunks = CHUNKS if heads % CHUNKS == 0 else 1
    few = min(chunks, 2)
    shape = jax.ShapeDtypeStruct
    state = shape((heads, DH, DH), BF)
    tokens = shape((rows, width), BF)
    partial = shape((rows, width), F32)
    block_tokens = shape((BLOCK, width), BF)
    square = [pltpu.VMEM((rows, rows), F32)]
    unit = 2 * rows * width * DH
    inner = 2 * rows * rows * width
    scalars = [lengths, block_mask]

    def wide(array, block=None):
        return Part(array, 1, block)

    def states(array):
        return Part(array, 0)

    def split_states(arrays, chunks):
        count = chunks // len(arrays)
        return [Part(a, 0, lead=i * count, parts=count) for i, a in enumerate(arrays)]

    def to_peers(array, away, backward):
        pairs = [(z, z + away) for z in range(head_count - away) if z % devices + away < devices]
        if backward:
            pairs = [(b, a) for a, b in pairs]
        return lax.ppermute(array, "head", pairs)

    def exchanged(slices):
        return lax.all_to_all(slices, AXES, split_axis=0, concat_axis=0, tiled=True)

    def scanned(slices, backward):
        (slices,) = call(
            functools.partial(scan_body, rows=rows, backward=backward),
            "scan",
            [lengths],
            [Part(slices, near=True)],
            [Part(shape(slices.shape, BF), 1)],
            heads,
            2 if slices.shape[1] % 32 == 0 else 1,
            limit=SOME_BYTES,
        )
        return slices

    gain_row = Part(gain.reshape(1, width))
    halves = [2 if b > 0 and chunks % 2 == 0 else 1 for b in range(blocks) for _ in range(peers)]
    later = [[shape((heads // n, DH, DH), BF)] * n for n in halves]
    (sum_kv,) = call(
        total_body,
        "total",
        scalars,
        [wide(keys), wide(values)],
        [states(state)],
        heads,
        chunks,
        flops=unit,
    )
    slices = sum_kv.reshape(total, -1, DH)
    slices, late_keys = lax.optimization_barrier((slices, keys))
    slices = exchanged(slices)
    if later:
        later = call(
            functools.partial(state_body, counts=halves),
            "states",
            scalars,
            [wide(late_keys), wide(values)],
            [part for arrays in later for part in split_states(arrays, few)],
            heads,
            few,
            flops=LONG,
        )
    later = iter(later)
    from_peers = [[next(later) for _ in range(n)] for n in halves]
    for at, arrays in enumerate(from_peers):
        arrays[0] = to_peers(arrays[0], 1 + at % peers, False)
    slices = scanned(slices, False)
    slices, late_queries = lax.optimization_barrier((slices, queries))
    (raw_inner,) = call(
        inner_body,
        "inner",
        scalars,
        [wide(late_queries), wide(keys), wide(values)],
        [wide(partial)],
        heads,
        chunks,
        square,
        flops=LONG,
        after=[x for arrays in from_peers[:peers] for x in arrays],
    )
    kv_state = exchanged(slices).reshape(heads, DH, DH)
    for at, arrays in enumerate(from_peers):
        if len(arrays) > 1:
            later_half, raw_inner = lax.optimization_barrier((arrays[1], raw_inner))
            arrays[1] = to_peers(later_half, 1 + at % peers, False)

    scales, raws, grads, updates, back = [], [], [], [], []
    for b in range(blocks):
        ends = [states(state)] if b == blocks - 1 and blocks > 1 else []
        scale, raw, grad, update, *sums = call(
            functools.partial(norm_body, rows=rows, block=b, counts=[1, *halves[b * peers : (b + 1) * peers]]),
            "norm",
            scalars,
            [
                gain_row,
                wide(queries, b),
                wide(raw_inner, b),
                wide(grad_out, b),
                states(kv_state),
                *[p for arrays in from_peers[b * peers : (b + 1) * peers] for p in split_states(arrays, few)],
                *[states(w) for w in (updates if ends else [])],
            ],
            [Part(shape((BLOCK, DH), F32)), wide(block_tokens), wide(block_tokens), states(state), *ends],
            heads,
            few,
            flops=LONG if b > 0 else 2 * unit // blocks,
        )
        scales.append(scale)
        raws.append(raw)
        grads.append(grad)
        updates.append(update)
        back += [to_peers(update, away, True) for away in range(1, devices)]
    output, grad_q = call(
        functools.partial(query_grads_body, peers=peers, counts=halves),
        "query_grads",
        scalars,
        [
            gain_row,
            wide(keys),
            wide(values),
            states(kv_state),
            *[wide(d) for d in grads],
            *[wide(r) for r in raws],
            *[Part(s) for s in scales],
            *[part for arrays in from_peers for part in split_states(arrays, chunks)],
        ],
        [wide(tokens), wide(tokens)],
        heads,
        chunks,
        square,
        flops=LONG,
        after=back[:peers],
    )
    slices = exchanged((sums[0] if sums else updates[0]).reshape(total, -1, DH))
    slices, grad_q = lax.optimization_barrier((slices, grad_q))
    slices = scanned(slices, True)
    slices, late_queries = lax.optimization_barrier((slices, queries))
    part_k, part_v = call(
        functools.partial(key_grads_body, peers=peers),
        "key_grads",
        scalars,
        [
            wide(late_queries),
            wide(keys),
            wide(values),
            *[wide(d) for d in grads],
            *[states(w) for w in back],
        ],
        [wide(partial), wide(partial)],
        heads,
        chunks,
        square,
        flops=LONG,
    )
    grad_state = exchanged(slices).reshape(heads, DH, DH)
    grad_k, grad_v = call(
        last_body,
        "last",
        scalars,
        [wide(keys), wide(values), wide(part_k), wide(part_v), states(grad_state)],
        [wide(tokens), wide(tokens)],
        heads,
        few,
        flops=2 * unit,
        limit=NARROW_BYTES,
    )
    return output, grad_q, grad_k, grad_v


def solution(mesh):
    tokens = P(AXES, None)
    return jax.shard_map(
        local,
        mesh=mesh,
        in_specs=(tokens, tokens, tokens, tokens, P(), P(), P("ctx", None)),
        out_specs=(tokens, tokens, tokens, tokens),
        check_vma=False,
    )
```

```python
import functools

import jax
import jax.numpy as jnp
from jax import lax
from jax.experimental import pallas as pl
from jax.experimental.pallas import tpu as pltpu
from jax.sharding import PartitionSpec as P

DH = 128
GROUP = 512
BLOCK = 128
CHUNKS = 4
LONG = 400_000_000_000
VMEM_BYTES = 60 * 1024 * 1024
NARROW_BYTES = 53 * 1024 * 1024
SOME_BYTES = 24 * 1024 * 1024

eps_norm = 1e-06
BF = jnp.bfloat16
F32 = jnp.float32
AXES = ("ctx", "head")

NN = (((1,), (0,)), ((), ()))
NT = (((1,), (1,)), ((), ()))
TN = (((0,), (0,)), ((), ()))


def dot(a, b, dims):
    return lax.dot_general(a, b, dims, preferred_element_type=F32)


def bounds_of(len_ref):
    bounds, total = [], None
    for k in range(len_ref.shape[0] - 1):
        total = len_ref[k] if total is None else total + len_ref[k]
        bounds.append(total)
    return bounds


def segment(position, bounds):
    result = (position >= bounds[0]).astype(jnp.int32)
    for bound in bounds[1:]:
        result = result + (position >= bound).astype(jnp.int32)
    return result


def same(a, b):
    return (a == b).astype(F32)


class Place:
    def __init__(self, len_ref, rows, mask_ref=None):
        self.rows = rows
        self.blocks = rows // BLOCK
        self.devices = GROUP // rows
        self.bounds = bounds_of(len_ref)
        spot = lax.axis_index("head")
        index = lax.axis_index("ctx") * lax.axis_size("head") + spot
        self.first = index * rows
        self.part = lax.rem(spot, self.devices)
        self.group = lax.div(spot, self.devices)
        self.group_first = self.first - self.part * rows
        self.mask_ref = mask_ref

    def seg(self, position):
        return segment(position, self.bounds)

    def start(self, block):
        return self.first + block * BLOCK

    def row_segments(self, block):
        rows = lax.broadcasted_iota(jnp.int32, (BLOCK, 1), 0)
        return self.seg(rows + self.start(block))

    def pair(self, i, j):
        slot = jnp.clip(lax.div(i * (i - 1), 2) + j, 0, self.mask_ref.shape[1] - 1)
        return self.mask_ref[self.group, slot].astype(F32)

    def weights(self):
        rows = self.rows
        t = lax.broadcasted_iota(jnp.int32, (rows, rows), 0)
        s = lax.broadcasted_iota(jnp.int32, (rows, rows), 1)
        keep = (s <= t) & (self.seg(t + self.first) == self.seg(s + self.first))
        result = jnp.where(keep, 1.0, 0.0)
        for i in range(1, self.blocks):
            for j in range(i):
                bit = self.pair(self.part * self.blocks + i, self.part * self.blocks + j)
                inside = (
                    (t >= i * BLOCK)
                    & (t < (i + 1) * BLOCK)
                    & (s >= j * BLOCK)
                    & (s < (j + 1) * BLOCK)
                )
                result = jnp.where(inside, result * bit, result)
        return result

    def to_later(self, away, block):
        there = (self.part + away) * self.blocks + block
        edge = self.seg(self.start(block) + away * self.rows - 1)
        return [
            self.pair(there, self.part * self.blocks + j) * same(self.seg(self.start(j + 1) - 1), edge)
            for j in range(self.blocks)
        ]

    def before(self, block):
        edge = self.seg(self.start(block) - 1)
        carried = same(self.seg(self.group_first - 1), edge)
        peers = [(self.part >= away).astype(F32) for away in range(1, self.devices)]
        return carried, peers, (self.row_segments(block) == edge).astype(F32)

    def after(self, block):
        own = self.part * self.blocks + block
        edge = self.seg(self.start(block + 1))
        carried = same(self.seg(self.group_first + GROUP), edge)
        peers = []
        for i in range(self.blocks):
            for away in range(1, self.devices):
                there = (self.part + away < self.devices).astype(F32)
                other = (self.part + away) * self.blocks + i
                start = self.start(i) + away * self.rows
                peers.append(self.pair(other, own) * same(self.seg(start), edge) * there)
        return carried, peers, (self.row_segments(block) == edge).astype(F32)


def mixed(refs, factors, head):
    total = refs[0][head].astype(F32) * factors[0]
    for ref, factor in zip(refs[1:], factors[1:], strict=True):
        total = total + ref[head].astype(F32) * factor
    return total.astype(BF)


class Joined:
    def __init__(self, refs):
        self.refs, self.each = refs, refs[0].shape[0]

    def __getitem__(self, head):
        return self.refs[head // self.each][head % self.each]

    def __setitem__(self, head, value):
        self.refs[head // self.each][head % self.each] = value


def joined(refs, counts):
    result, at = [], 0
    for count in counts:
        result.append(Joined(refs[at : at + count]))
        at += count
    return result


def columns(head):
    return pl.ds(head * DH, DH)


def rows_of(block):
    return pl.ds(block * BLOCK, BLOCK)


def total_body(place_of, ins, outs, scratch, arrive, leave, chunks):
    k_ref, v_ref = ins
    (t_ref,) = outs
    place = place_of(k_ref.shape[0])
    last = place.seg(place.start(place.blocks) - 1)
    segments = [place.row_segments(b) for b in range(place.blocks)]
    mask = (jnp.concatenate(segments, axis=0) == last).astype(BF)
    for c, heads in enumerate(chunks):
        arrive(c)
        for head in heads:
            at = columns(head)
            t_ref[head] = dot(k_ref[:, at] * mask, v_ref[:, at], TN).astype(BF)
        leave(c)


def state_body(place_of, ins, outs, scratch, arrive, leave, chunks, *, counts):
    k_ref, v_ref = ins
    outs = joined(outs, counts)
    rows, width = k_ref.shape
    place = place_of(rows)
    ends = [place.seg(place.start(b + 1) - 1) for b in range(place.blocks)]
    masks = [(place.row_segments(b) == ends[b]).astype(BF) for b in range(place.blocks)]
    wanted = [
        place.to_later(away, b) for b in range(place.blocks) for away in range(1, place.devices)
    ]
    for c, heads in enumerate(chunks):
        arrive(c)
        for head in heads:
            updates = []
            for b in range(place.blocks):
                k = k_ref[rows_of(b), columns(head)] * masks[b]
                updates.append(dot(k, v_ref[rows_of(b), columns(head)], TN))
            for ref, factors in zip(outs, wanted, strict=True):
                total = updates[0] * factors[0]
                for update, factor in zip(updates[1:], factors[1:], strict=True):
                    total = total + update * factor
                ref[head] = total.astype(BF)
        leave(c)


def inner_body(place_of, ins, outs, scratch, arrive, leave, chunks):
    q_ref, k_ref, v_ref = ins
    (raw_ref,), (weight_ref,) = outs, scratch
    weight_ref[...] = place_of(q_ref.shape[0]).weights()
    for c, heads in enumerate(chunks):
        arrive(c)
        for head in heads:
            at = columns(head)
            probs = (dot(q_ref[:, at], k_ref[:, at], NT) * weight_ref[...]).astype(BF)
            raw_ref[:, at] = dot(probs, v_ref[:, at], NN)
        leave(c)


def scan_body(place_of, ins, outs, scratch, arrive, leave, chunks, *, rows, backward):
    (t_ref,), (out_ref,) = ins, outs
    count, height, _ = t_ref.shape
    devices = GROUP // rows
    bounds = place_of(rows).bounds
    part = height // len(chunks)
    for c in range(len(chunks)):
        arrive(c)
        at = pl.ds(c * part, part)

        def one(turn, acc):
            group = count // devices - 1 - turn if backward else turn
            for k in range(devices):
                out_ref[group * devices + k, at] = acc.astype(BF)
            for k in range(devices):
                index = group * devices + (devices - 1 - k if backward else k)
                first = index * rows
                if backward:
                    keep = same(segment(first, bounds), segment(first + rows, bounds))
                else:
                    keep = same(segment(first - 1, bounds), segment(first + rows - 1, bounds))
                acc = acc * keep + t_ref[index, at].astype(F32)
            return acc

        acc = jnp.zeros((part, DH), F32)
        if count <= 32:
            for turn in range(count // devices):
                acc = one(turn, acc)
        else:
            lax.fori_loop(0, count // devices, one, acc)
        leave(c)


def norm_body(place_of, ins, outs, scratch, arrive, leave, chunks, *, rows, block, counts):
    gain_ref, q_ref, raw_ref, grad_ref = ins[:4]
    held = 4 + sum(counts)
    state_refs, earlier_refs = joined(ins[4:held], counts), ins[held:]
    scale_ref, held_ref, d_ref, w_ref, *t_refs = outs
    width = q_ref.shape[1]
    place = place_of(rows)
    carried, there, reach = place.before(block)
    squares = cross = jnp.zeros((BLOCK, DH), F32)
    for c, heads in enumerate(chunks):
        arrive(c)
        for head in heads:
            at = columns(head)
            state = mixed(state_refs, [carried, *there], head)
            raw = raw_ref[:, at] + dot(q_ref[:, at], state, NN) * reach
            raw = raw.astype(BF)
            held_ref[:, at] = raw
            raw = raw.astype(F32)
            scaled = grad_ref[:, at].astype(F32) * gain_ref[:, at]
            squares = squares + raw * raw
            cross = cross + scaled * raw
        leave(c, [1])
    total = jnp.sum(squares, axis=1, keepdims=True)
    inverse = 1.0 / jnp.sqrt(total / width + eps_norm)
    mean = jnp.sum(cross, axis=1, keepdims=True) * inverse / width
    scale_ref[...] = jnp.broadcast_to(inverse, scale_ref.shape)
    leave(0, [0])
    own = place.seg(place.start(block))
    begin = (place.row_segments(block) == own).astype(BF)
    into = [same(place.seg(place.start(b)), place.seg(place.first)) for b in range(block + 1)]
    for c, heads in enumerate(chunks):
        for head in heads:
            at = columns(head)
            normed = held_ref[:, at].astype(F32) * inverse
            scaled = grad_ref[:, at].astype(F32) * gain_ref[:, at]
            grad = ((scaled - normed * mean) * inverse).astype(BF)
            d_ref[:, at] = grad
            update = dot(q_ref[:, at] * begin, grad, TN)
            w_ref[head] = update.astype(BF)
            for t_ref in t_refs:
                sums = update * into[block]
                for ref, factor in zip(earlier_refs, into[:block], strict=True):
                    sums = sums + ref[head].astype(F32) * factor
                t_ref[head] = sums.astype(BF)
        leave(c, range(2, len(outs)))


def query_grads_body(place_of, ins, outs, scratch, arrive, leave, chunks, *, peers, counts):
    gain_ref, k_ref, v_ref, kv_ref = ins[:4]
    rows, width = k_ref.shape
    place = place_of(rows)
    blocks = place.blocks
    rest = ins[4:]
    d_refs, raw_refs, scale_refs = rest[:blocks], rest[blocks : 2 * blocks], rest[2 * blocks : 3 * blocks]
    peer_refs = joined(rest[3 * blocks :], counts)
    out_ref, gq_ref = outs
    (weight_ref,) = scratch
    weight_ref[...] = place.weights()
    factors = [place.before(b) for b in range(blocks)]
    for c, heads in enumerate(chunks):
        arrive(c)
        for head in heads:
            at = columns(head)
            d = jnp.concatenate([ref[:, at] for ref in d_refs], axis=0)
            grad_probs = (dot(d, v_ref[:, at], NT) * weight_ref[...]).astype(BF)
            inner = dot(grad_probs, k_ref[:, at], NN)
            for b in range(blocks):
                carried, there, _ = factors[b]
                state = mixed([kv_ref, *peer_refs[b * peers : (b + 1) * peers]], [carried, *there], head)
                outer = dot(d_refs[b][:, at], state, NT) * factors[b][2]
                part = inner[b * BLOCK : (b + 1) * BLOCK] + outer
                gq_ref[rows_of(b), at] = part.astype(BF)
                normed = raw_refs[b][:, at].astype(F32) * scale_refs[b][...]
                out_ref[rows_of(b), at] = (normed * gain_ref[:, at]).astype(BF)
        leave(c)


def key_grads_body(place_of, ins, outs, scratch, arrive, leave, chunks, *, peers):
    q_ref, k_ref, v_ref, *rest = ins
    place = place_of(q_ref.shape[0])
    blocks = place.blocks
    d_refs, w_refs = rest[:blocks], rest[blocks:]
    gk_ref, gv_ref = outs
    (weight_ref,) = scratch
    weight_ref[...] = place.weights()
    factors = [place.after(b) for b in range(blocks)]
    for c, heads in enumerate(chunks):
        arrive(c)
        for head in heads:
            at = columns(head)
            q, d = q_ref[:, at], jnp.concatenate([ref[:, at] for ref in d_refs], axis=0)
            probs = (dot(q, k_ref[:, at], NT) * weight_ref[...]).astype(BF)
            grad_probs = (dot(d, v_ref[:, at], NT) * weight_ref[...]).astype(BF)
            gk = dot(grad_probs, q, TN)
            gv = dot(probs, d, TN)
            for b in range(blocks):
                at_rows, here = rows_of(b), slice(b * BLOCK, (b + 1) * BLOCK)
                part_k, part_v = gk[here], gv[here]
                if peers:
                    state = mixed(w_refs, factors[b][1], head)
                    part_k = part_k + dot(v_ref[at_rows, at], state, NT) * factors[b][2]
                    part_v = part_v + dot(k_ref[at_rows, at], state, NN) * factors[b][2]
                gk_ref[at_rows, at] = part_k
                gv_ref[at_rows, at] = part_v
        leave(c)


def last_body(place_of, ins, outs, scratch, arrive, leave, chunks):
    k_ref, v_ref, gk_in, gv_in, gs_ref = ins
    gk_ref, gv_ref = outs
    place = place_of(k_ref.shape[0])
    factors = [place.after(b) for b in range(place.blocks)]
    reach = jnp.concatenate([reach * carried for carried, _, reach in factors], axis=0)
    for c, heads in enumerate(chunks):
        arrive(c)
        for head in heads:
            at = columns(head)
            gk = gk_in[:, at] + dot(v_ref[:, at], gs_ref[head], NT) * reach
            gv = gv_in[:, at] + dot(k_ref[:, at], gs_ref[head], NN) * reach
            gk_ref[:, at] = gk.astype(BF)
            gv_ref[:, at] = gv.astype(BF)
        leave(c)


class Part:
    def __init__(self, array, axis=None, block=None, near=False, lead=0, parts=None):
        self.array, self.axis, self.block, self.near = array, axis, block, near
        self.lead, self.parts = lead, parts
        self.shape = array.shape if block is None else (BLOCK, *array.shape[1:])
        self.spec = pl.BlockSpec(memory_space=pltpu.VMEM if near else pltpu.HBM)

    def pieces(self, far, near, sems, count):
        far = far if self.block is None else far.at[rows_of(self.block)]
        if self.axis is None:
            return [(far, near, sems.at[0])]
        count = self.parts or count
        size = self.shape[self.axis] // count
        result = [None] * self.lead
        for c in range(count):
            at = [slice(None)] * len(self.shape)
            at[self.axis] = pl.ds(c * size, size)
            result.append((far.at[tuple(at)], near.at[tuple(at)], sems.at[c]))
        return result


def call(body, name, scalars, ins, outs, heads, chunks, scratch=(), flops=0, after=(), limit=VMEM_BYTES):
    far = [p for p in (*ins, *outs) if not p.near]
    sizes = (len(scalars), len(ins), len(after), len(outs), len(far), 2, len(scratch))

    def kernel(*refs):
        split, at = [], 0
        for size in sizes:
            split.append(refs[at : at + size])
            at += size
        settings, in_refs, _, out_refs, buffers, (in_sems, out_sems), rest = split
        buffers = iter(buffers)

        def opened(parts, given, sems):
            refs, pieces = [], []
            for i, (part, ref) in enumerate(zip(parts, given, strict=True)):
                refs.append(ref if part.near else next(buffers))
                pieces.append([] if part.near else part.pieces(ref, refs[-1], sems.at[i], chunks))
            return refs, pieces

        near_in, coming = opened(ins, in_refs, in_sems)
        near_out, going = opened(outs, out_refs, out_sems)

        def copies(parts, c, which=None):
            for i, pieces in enumerate(parts):
                if c < len(pieces) and pieces[c] is not None and (which is None or i in which):
                    yield pieces[c]

        def arrive(c):
            for far, near, sem in copies(coming, c):
                pltpu.make_async_copy(far, near, sem).wait()

        def leave(c, which=None):
            for far, near, sem in copies(going, c, which):
                pltpu.make_async_copy(near, far, sem).start()

        for c in range(chunks):
            for far, near, sem in copies(coming, c):
                pltpu.make_async_copy(far, near, sem).start()
        each = heads // chunks
        turns = [range(c * each, (c + 1) * each) for c in range(chunks)]
        place_of = lambda rows: Place(settings[0], rows, *settings[1:])
        body(place_of, near_in, near_out, rest, arrive, leave, turns)
        for c in range(chunks):
            for far, near, sem in copies(going, c):
                pltpu.make_async_copy(near, far, sem).wait()

    anywhere = pl.BlockSpec(memory_space=pl.ANY)
    return pl.pallas_call(
        kernel,
        name=name,
        in_specs=[
            *[pl.BlockSpec(memory_space=pltpu.SMEM)] * len(scalars),
            *[p.spec for p in ins],
            *[anywhere] * len(after),
        ],
        out_specs=[p.spec for p in outs],
        out_shape=[p.array for p in outs],
        scratch_shapes=[
            *[pltpu.VMEM(p.shape, p.array.dtype) for p in far],
            pltpu.SemaphoreType.DMA((len(ins), chunks)),
            pltpu.SemaphoreType.DMA((len(outs), chunks)),
            *scratch,
        ],
        compiler_params=pltpu.CompilerParams(vmem_limit_bytes=limit),
        cost_estimate=pl.CostEstimate(
            flops=flops,
            bytes_accessed=sum(p.array.size * p.array.dtype.itemsize for p in (*ins, *outs)),
            transcendentals=0,
        ),
    )(*scalars, *[p.array for p in ins], *after)


def local(queries, keys, values, grad_out, gain, lengths, block_mask):
    rows, width = queries.shape
    heads = width // DH
    blocks = rows // BLOCK
    devices = GROUP // rows
    peers = devices - 1
    head_count = lax.axis_size("head")
    total = lax.axis_size("ctx") * head_count
    chunks = CHUNKS if heads % CHUNKS == 0 else 1
    few = min(chunks, 2)
    shape = jax.ShapeDtypeStruct
    state = shape((heads, DH, DH), BF)
    tokens = shape((rows, width), BF)
    partial = shape((rows, width), F32)
    block_tokens = shape((BLOCK, width), BF)
    square = [pltpu.VMEM((rows, rows), F32)]
    unit = 2 * rows * width * DH
    inner = 2 * rows * rows * width
    scalars = [lengths, block_mask]

    def wide(array, block=None):
        return Part(array, 1, block)

    def states(array):
        return Part(array, 0)

    def split_states(arrays, chunks):
        count = chunks // len(arrays)
        return [Part(a, 0, lead=i * count, parts=count) for i, a in enumerate(arrays)]

    def to_peers(array, away, backward):
        pairs = [(z, z + away) for z in range(head_count - away) if z % devices + away < devices]
        if backward:
            pairs = [(b, a) for a, b in pairs]
        return lax.ppermute(array, "head", pairs)

    def exchanged(slices):
        return lax.all_to_all(slices, AXES, split_axis=0, concat_axis=0, tiled=True)

    def scanned(slices, backward):
        (slices,) = call(
            functools.partial(scan_body, rows=rows, backward=backward),
            "scan",
            [lengths],
            [Part(slices, near=True)],
            [Part(shape(slices.shape, BF), 1)],
            heads,
            2 if slices.shape[1] % 32 == 0 else 1,
            limit=SOME_BYTES,
        )
        return slices

    gain_row = Part(gain.reshape(1, width))
    halves = [1] * (blocks * peers)
    later = [[shape((heads // n, DH, DH), BF)] * n for n in halves]
    (sum_kv,) = call(
        total_body,
        "total",
        scalars,
        [wide(keys), wide(values)],
        [states(state)],
        heads,
        few,
        flops=unit,
    )
    slices = sum_kv.reshape(total, -1, DH)
    slices, late_keys = lax.optimization_barrier((slices, keys))
    slices = exchanged(slices)
    if later:
        later = call(
            functools.partial(state_body, counts=halves),
            "states",
            scalars,
            [wide(late_keys), wide(values)],
            [part for arrays in later for part in split_states(arrays, few)],
            heads,
            few,
            flops=LONG,
        )
    later = iter(later)
    from_peers = [[next(later) for _ in range(n)] for n in halves]
    for away, arrays in enumerate(from_peers[:peers], 1):
        arrays[0] = to_peers(arrays[0], away, False)
    slices = scanned(slices, False)
    slices, late_queries = lax.optimization_barrier((slices, queries))
    (raw_inner,) = call(
        inner_body,
        "inner",
        scalars,
        [wide(late_queries), wide(keys), wide(values)],
        [wide(partial)],
        heads,
        chunks,
        square,
        flops=LONG,
        after=[x for arrays in from_peers[:peers] for x in arrays],
    )
    kv_state = exchanged(slices).reshape(heads, DH, DH)
    for at, arrays in enumerate(from_peers[peers:]):
        delayed, raw_inner = lax.optimization_barrier((arrays[0], raw_inner))
        arrays[0] = to_peers(delayed, 1 + at % peers, False)

    scales, raws, grads, updates, back = [], [], [], [], []
    for b in range(blocks):
        ends = [states(state)] if b == blocks - 1 and blocks > 1 else []
        scale, raw, grad, update, *sums = call(
            functools.partial(norm_body, rows=rows, block=b, counts=[1, *halves[b * peers : (b + 1) * peers]]),
            "norm",
            scalars,
            [
                gain_row,
                wide(queries, b),
                wide(raw_inner, b),
                wide(grad_out, b),
                states(kv_state),
                *[p for arrays in from_peers[b * peers : (b + 1) * peers] for p in split_states(arrays, few)],
                *[states(w) for w in (updates if ends else [])],
            ],
            [Part(shape((BLOCK, DH), F32)), wide(block_tokens), wide(block_tokens), states(state), *ends],
            heads,
            few,
            flops=LONG if b > 0 else 2 * unit // blocks,
        )
        scales.append(scale)
        raws.append(raw)
        grads.append(grad)
        updates.append(update)
        back += [to_peers(update, away, True) for away in range(1, devices)]
    output, grad_q = call(
        functools.partial(query_grads_body, peers=peers, counts=halves),
        "query_grads",
        scalars,
        [
            gain_row,
            wide(keys),
            wide(values),
            states(kv_state),
            *[wide(d) for d in grads],
            *[wide(r) for r in raws],
            *[Part(s) for s in scales],
            *[part for arrays in from_peers for part in split_states(arrays, chunks)],
        ],
        [wide(tokens), wide(tokens)],
        heads,
        chunks,
        square,
        flops=LONG,
        after=back[:peers],
    )
    slices = exchanged((sums[0] if sums else updates[0]).reshape(total, -1, DH))
    slices, grad_q = lax.optimization_barrier((slices, grad_q))
    slices = scanned(slices, True)
    slices, late_queries = lax.optimization_barrier((slices, queries))
    part_k, part_v = call(
        functools.partial(key_grads_body, peers=peers),
        "key_grads",
        scalars,
        [
            wide(late_queries),
            wide(keys),
            wide(values),
            *[wide(d) for d in grads],
            *[states(w) for w in back],
        ],
        [wide(partial), wide(partial)],
        heads,
        chunks,
        square,
        flops=LONG,
    )
    grad_state = exchanged(slices).reshape(heads, DH, DH)
    grad_k, grad_v = call(
        last_body,
        "last",
        scalars,
        [wide(keys), wide(values), wide(part_k), wide(part_v), states(grad_state)],
        [wide(tokens), wide(tokens)],
        heads,
        few,
        flops=2 * unit,
        limit=NARROW_BYTES,
    )
    return output, grad_q, grad_k, grad_v


def solution(mesh):
    tokens = P(AXES, None)
    return jax.shard_map(
        local,
        mesh=mesh,
        in_specs=(tokens, tokens, tokens, tokens, P(), P(), P("ctx", None)),
        out_specs=(tokens, tokens, tokens, tokens),
        check_vma=False,
    )
```

```python
import functools

import jax
import jax.numpy as jnp
from jax import lax
from jax.experimental import pallas as pl
from jax.experimental.pallas import tpu as pltpu
from jax.sharding import PartitionSpec as P

DH = 128
GROUP = 512
BLOCK = 128
CHUNKS = 4
LONG = 400_000_000_000
VMEM_BYTES = 60 * 1024 * 1024
NARROW_BYTES = 53 * 1024 * 1024
SOME_BYTES = 24 * 1024 * 1024

eps_norm = 1e-06
BF = jnp.bfloat16
F32 = jnp.float32
AXES = ("ctx", "head")

NN = (((1,), (0,)), ((), ()))
NT = (((1,), (1,)), ((), ()))
TN = (((0,), (0,)), ((), ()))


def dot(a, b, dims):
    return lax.dot_general(a, b, dims, preferred_element_type=F32)


def bounds_of(len_ref):
    bounds, total = [], None
    for k in range(len_ref.shape[0] - 1):
        total = len_ref[k] if total is None else total + len_ref[k]
        bounds.append(total)
    return bounds


def segment(position, bounds):
    result = (position >= bounds[0]).astype(jnp.int32)
    for bound in bounds[1:]:
        result = result + (position >= bound).astype(jnp.int32)
    return result


def same(a, b):
    return (a == b).astype(F32)


class Place:
    def __init__(self, len_ref, rows, mask_ref=None):
        self.rows = rows
        self.blocks = rows // BLOCK
        self.devices = GROUP // rows
        self.bounds = bounds_of(len_ref)
        spot = lax.axis_index("head")
        index = lax.axis_index("ctx") * lax.axis_size("head") + spot
        self.first = index * rows
        self.part = lax.rem(spot, self.devices)
        self.group = lax.div(spot, self.devices)
        self.group_first = self.first - self.part * rows
        self.mask_ref = mask_ref

    def seg(self, position):
        return segment(position, self.bounds)

    def start(self, block):
        return self.first + block * BLOCK

    def row_segments(self, block):
        rows = lax.broadcasted_iota(jnp.int32, (BLOCK, 1), 0)
        return self.seg(rows + self.start(block))

    def pair(self, i, j):
        slot = jnp.clip(lax.div(i * (i - 1), 2) + j, 0, self.mask_ref.shape[1] - 1)
        return self.mask_ref[self.group, slot].astype(F32)

    def weights(self):
        rows = self.rows
        t = lax.broadcasted_iota(jnp.int32, (rows, rows), 0)
        s = lax.broadcasted_iota(jnp.int32, (rows, rows), 1)
        keep = (s <= t) & (self.seg(t + self.first) == self.seg(s + self.first))
        result = jnp.where(keep, 1.0, 0.0)
        for i in range(1, self.blocks):
            for j in range(i):
                bit = self.pair(self.part * self.blocks + i, self.part * self.blocks + j)
                inside = (
                    (t >= i * BLOCK)
                    & (t < (i + 1) * BLOCK)
                    & (s >= j * BLOCK)
                    & (s < (j + 1) * BLOCK)
                )
                result = jnp.where(inside, result * bit, result)
        return result

    def to_later(self, away, block):
        there = (self.part + away) * self.blocks + block
        edge = self.seg(self.start(block) + away * self.rows - 1)
        return [
            self.pair(there, self.part * self.blocks + j) * same(self.seg(self.start(j + 1) - 1), edge)
            for j in range(self.blocks)
        ]

    def before(self, block):
        edge = self.seg(self.start(block) - 1)
        carried = same(self.seg(self.group_first - 1), edge)
        peers = [(self.part >= away).astype(F32) for away in range(1, self.devices)]
        return carried, peers, (self.row_segments(block) == edge).astype(F32)

    def after(self, block):
        own = self.part * self.blocks + block
        edge = self.seg(self.start(block + 1))
        carried = same(self.seg(self.group_first + GROUP), edge)
        peers = []
        for i in range(self.blocks):
            for away in range(1, self.devices):
                there = (self.part + away < self.devices).astype(F32)
                other = (self.part + away) * self.blocks + i
                start = self.start(i) + away * self.rows
                peers.append(self.pair(other, own) * same(self.seg(start), edge) * there)
        return carried, peers, (self.row_segments(block) == edge).astype(F32)


def mixed(refs, factors, head):
    total = refs[0][head].astype(F32) * factors[0]
    for ref, factor in zip(refs[1:], factors[1:], strict=True):
        total = total + ref[head].astype(F32) * factor
    return total.astype(BF)


class Joined:
    def __init__(self, refs):
        self.spots = [(ref, k) for ref in refs for k in range(ref.shape[0])]

    def __getitem__(self, head):
        ref, at = self.spots[head]
        return ref[at]

    def __setitem__(self, head, value):
        ref, at = self.spots[head]
        ref[at] = value


def joined(refs, counts):
    result, at = [], 0
    for count in counts:
        result.append(Joined(refs[at : at + count]))
        at += count
    return result


def columns(head):
    return pl.ds(head * DH, DH)


def rows_of(block):
    return pl.ds(block * BLOCK, BLOCK)


def total_body(place_of, ins, outs, scratch, arrive, leave, chunks):
    k_ref, v_ref = ins
    (t_ref,) = outs
    place = place_of(k_ref.shape[0])
    last = place.seg(place.start(place.blocks) - 1)
    segments = [place.row_segments(b) for b in range(place.blocks)]
    mask = (jnp.concatenate(segments, axis=0) == last).astype(BF)
    for c, heads in enumerate(chunks):
        arrive(c)
        for head in heads:
            at = columns(head)
            t_ref[head] = dot(k_ref[:, at] * mask, v_ref[:, at], TN).astype(BF)
        leave(c)


def state_body(place_of, ins, outs, scratch, arrive, leave, chunks, *, counts):
    k_ref, v_ref = ins
    outs = joined(outs, counts)
    rows, width = k_ref.shape
    place = place_of(rows)
    ends = [place.seg(place.start(b + 1) - 1) for b in range(place.blocks)]
    masks = [(place.row_segments(b) == ends[b]).astype(BF) for b in range(place.blocks)]
    wanted = [
        place.to_later(away, b) for b in range(place.blocks) for away in range(1, place.devices)
    ]
    for c, heads in enumerate(chunks):
        arrive(c)
        for head in heads:
            updates = []
            for b in range(place.blocks):
                k = k_ref[rows_of(b), columns(head)] * masks[b]
                updates.append(dot(k, v_ref[rows_of(b), columns(head)], TN))
            for ref, factors in zip(outs, wanted, strict=True):
                total = updates[0] * factors[0]
                for update, factor in zip(updates[1:], factors[1:], strict=True):
                    total = total + update * factor
                ref[head] = total.astype(BF)
        leave(c)


def inner_body(place_of, ins, outs, scratch, arrive, leave, chunks):
    q_ref, k_ref, v_ref = ins
    (raw_ref,), (weight_ref,) = outs, scratch
    weight_ref[...] = place_of(q_ref.shape[0]).weights()
    for c, heads in enumerate(chunks):
        arrive(c)
        for head in heads:
            at = columns(head)
            probs = (dot(q_ref[:, at], k_ref[:, at], NT) * weight_ref[...]).astype(BF)
            raw_ref[:, at] = dot(probs, v_ref[:, at], NN)
        leave(c)


def scan_body(place_of, ins, outs, scratch, arrive, leave, chunks, *, rows, backward):
    (t_ref,), (out_ref,) = ins, outs
    count, height, _ = t_ref.shape
    devices = GROUP // rows
    bounds = place_of(rows).bounds
    part = height // len(chunks)
    for c in range(len(chunks)):
        arrive(c)
        at = pl.ds(c * part, part)

        def one(turn, acc):
            group = count // devices - 1 - turn if backward else turn
            for k in range(devices):
                out_ref[group * devices + k, at] = acc.astype(BF)
            for k in range(devices):
                index = group * devices + (devices - 1 - k if backward else k)
                first = index * rows
                if backward:
                    keep = same(segment(first, bounds), segment(first + rows, bounds))
                else:
                    keep = same(segment(first - 1, bounds), segment(first + rows - 1, bounds))
                acc = acc * keep + t_ref[index, at].astype(F32)
            return acc

        acc = jnp.zeros((part, DH), F32)
        if count <= 32:
            for turn in range(count // devices):
                acc = one(turn, acc)
        else:
            lax.fori_loop(0, count // devices, one, acc)
        leave(c)


def norm_body(place_of, ins, outs, scratch, arrive, leave, chunks, *, rows, block, counts):
    gain_ref, q_ref, raw_ref, grad_ref = ins[:4]
    held = 4 + sum(counts)
    state_refs, earlier_refs = joined(ins[4:held], counts), ins[held:]
    scale_ref, held_ref, d_ref, w_ref, *t_refs = outs
    width = q_ref.shape[1]
    place = place_of(rows)
    carried, there, reach = place.before(block)
    squares = cross = jnp.zeros((BLOCK, DH), F32)
    for c, heads in enumerate(chunks):
        arrive(c)
        for head in heads:
            at = columns(head)
            state = mixed(state_refs, [carried, *there], head)
            raw = raw_ref[:, at] + dot(q_ref[:, at], state, NN) * reach
            raw = raw.astype(BF)
            held_ref[:, at] = raw
            raw = raw.astype(F32)
            scaled = grad_ref[:, at].astype(F32) * gain_ref[:, at]
            squares = squares + raw * raw
            cross = cross + scaled * raw
        leave(c, [1])
    total = jnp.sum(squares, axis=1, keepdims=True)
    inverse = 1.0 / jnp.sqrt(total / width + eps_norm)
    mean = jnp.sum(cross, axis=1, keepdims=True) * inverse / width
    scale_ref[...] = jnp.broadcast_to(inverse, scale_ref.shape)
    leave(0, [0])
    own = place.seg(place.start(block))
    begin = (place.row_segments(block) == own).astype(BF)
    into = [same(place.seg(place.start(b)), place.seg(place.first)) for b in range(block + 1)]
    for c, heads in enumerate(chunks):
        for head in heads:
            at = columns(head)
            normed = held_ref[:, at].astype(F32) * inverse
            scaled = grad_ref[:, at].astype(F32) * gain_ref[:, at]
            grad = ((scaled - normed * mean) * inverse).astype(BF)
            d_ref[:, at] = grad
            update = dot(q_ref[:, at] * begin, grad, TN)
            w_ref[head] = update.astype(BF)
            for t_ref in t_refs:
                sums = update * into[block]
                for ref, factor in zip(earlier_refs, into[:block], strict=True):
                    sums = sums + ref[head].astype(F32) * factor
                t_ref[head] = sums.astype(BF)
        leave(c, range(2, len(outs)))


def query_grads_body(place_of, ins, outs, scratch, arrive, leave, chunks, *, peers, counts):
    gain_ref, k_ref, v_ref, kv_ref = ins[:4]
    rows, width = k_ref.shape
    place = place_of(rows)
    blocks = place.blocks
    rest = ins[4:]
    d_refs, raw_refs, scale_refs = rest[:blocks], rest[blocks : 2 * blocks], rest[2 * blocks : 3 * blocks]
    peer_refs = joined(rest[3 * blocks :], counts)
    out_ref, gq_ref = outs
    (weight_ref,) = scratch
    weight_ref[...] = place.weights()
    factors = [place.before(b) for b in range(blocks)]
    for c, heads in enumerate(chunks):
        arrive(c)
        for head in heads:
            at = columns(head)
            d = jnp.concatenate([ref[:, at] for ref in d_refs], axis=0)
            grad_probs = (dot(d, v_ref[:, at], NT) * weight_ref[...]).astype(BF)
            inner = dot(grad_probs, k_ref[:, at], NN)
            for b in range(blocks):
                carried, there, _ = factors[b]
                state = mixed([kv_ref, *peer_refs[b * peers : (b + 1) * peers]], [carried, *there], head)
                outer = dot(d_refs[b][:, at], state, NT) * factors[b][2]
                part = inner[b * BLOCK : (b + 1) * BLOCK] + outer
                gq_ref[rows_of(b), at] = part.astype(BF)
                normed = raw_refs[b][:, at].astype(F32) * scale_refs[b][...]
                out_ref[rows_of(b), at] = (normed * gain_ref[:, at]).astype(BF)
        leave(c)


def key_grads_body(place_of, ins, outs, scratch, arrive, leave, chunks, *, peers):
    q_ref, k_ref, v_ref, *rest = ins
    place = place_of(q_ref.shape[0])
    blocks = place.blocks
    d_refs, w_refs = rest[:blocks], rest[blocks:]
    gk_ref, gv_ref = outs
    (weight_ref,) = scratch
    weight_ref[...] = place.weights()
    factors = [place.after(b) for b in range(blocks)]
    for c, heads in enumerate(chunks):
        arrive(c)
        for head in heads:
            at = columns(head)
            q, d = q_ref[:, at], jnp.concatenate([ref[:, at] for ref in d_refs], axis=0)
            probs = (dot(q, k_ref[:, at], NT) * weight_ref[...]).astype(BF)
            grad_probs = (dot(d, v_ref[:, at], NT) * weight_ref[...]).astype(BF)
            gk = dot(grad_probs, q, TN)
            gv = dot(probs, d, TN)
            for b in range(blocks):
                at_rows, here = rows_of(b), slice(b * BLOCK, (b + 1) * BLOCK)
                part_k, part_v = gk[here], gv[here]
                if peers:
                    state = mixed(w_refs, factors[b][1], head)
                    part_k = part_k + dot(v_ref[at_rows, at], state, NT) * factors[b][2]
                    part_v = part_v + dot(k_ref[at_rows, at], state, NN) * factors[b][2]
                gk_ref[at_rows, at] = part_k
                gv_ref[at_rows, at] = part_v
        leave(c)


def last_body(place_of, ins, outs, scratch, arrive, leave, chunks):
    k_ref, v_ref, gk_in, gv_in, gs_ref = ins
    gk_ref, gv_ref = outs
    place = place_of(k_ref.shape[0])
    factors = [place.after(b) for b in range(place.blocks)]
    reach = jnp.concatenate([reach * carried for carried, _, reach in factors], axis=0)
    for c, heads in enumerate(chunks):
        arrive(c)
        for head in heads:
            at = columns(head)
            gk = gk_in[:, at] + dot(v_ref[:, at], gs_ref[head], NT) * reach
            gv = gv_in[:, at] + dot(k_ref[:, at], gs_ref[head], NN) * reach
            gk_ref[:, at] = gk.astype(BF)
            gv_ref[:, at] = gv.astype(BF)
        leave(c)


class Part:
    def __init__(self, array, axis=None, block=None, near=False, lead=0, parts=None):
        self.array, self.axis, self.block, self.near = array, axis, block, near
        self.lead, self.parts = lead, parts
        self.shape = array.shape if block is None else (BLOCK, *array.shape[1:])
        self.spec = pl.BlockSpec(memory_space=pltpu.VMEM if near else pltpu.HBM)

    def pieces(self, far, near, sems, count):
        far = far if self.block is None else far.at[rows_of(self.block)]
        if self.axis is None:
            return [(far, near, sems.at[0])]
        count = self.parts or count
        size = self.shape[self.axis] // count
        result = [None] * self.lead
        for c in range(count):
            at = [slice(None)] * len(self.shape)
            at[self.axis] = pl.ds(c * size, size)
            result.append((far.at[tuple(at)], near.at[tuple(at)], sems.at[c]))
        return result


def call(body, name, scalars, ins, outs, heads, chunks, scratch=(), flops=0, after=(), limit=VMEM_BYTES):
    far = [p for p in (*ins, *outs) if not p.near]
    sizes = (len(scalars), len(ins), len(after), len(outs), len(far), 2, len(scratch))

    def kernel(*refs):
        split, at = [], 0
        for size in sizes:
            split.append(refs[at : at + size])
            at += size
        settings, in_refs, _, out_refs, buffers, (in_sems, out_sems), rest = split
        buffers = iter(buffers)

        def opened(parts, given, sems):
            refs, pieces = [], []
            for i, (part, ref) in enumerate(zip(parts, given, strict=True)):
                refs.append(ref if part.near else next(buffers))
                pieces.append([] if part.near else part.pieces(ref, refs[-1], sems.at[i], chunks))
            return refs, pieces

        near_in, coming = opened(ins, in_refs, in_sems)
        near_out, going = opened(outs, out_refs, out_sems)

        def copies(parts, c, which=None):
            for i, pieces in enumerate(parts):
                if c < len(pieces) and pieces[c] is not None and (which is None or i in which):
                    yield pieces[c]

        def arrive(c):
            for far, near, sem in copies(coming, c):
                pltpu.make_async_copy(far, near, sem).wait()

        def leave(c, which=None):
            for far, near, sem in copies(going, c, which):
                pltpu.make_async_copy(near, far, sem).start()

        for c in range(chunks):
            for far, near, sem in copies(coming, c):
                pltpu.make_async_copy(far, near, sem).start()
        each = heads // chunks
        turns = [range(c * each, (c + 1) * each) for c in range(chunks)]
        place_of = lambda rows: Place(settings[0], rows, *settings[1:])
        body(place_of, near_in, near_out, rest, arrive, leave, turns)
        for c in range(chunks):
            for far, near, sem in copies(going, c):
                pltpu.make_async_copy(near, far, sem).wait()

    anywhere = pl.BlockSpec(memory_space=pl.ANY)
    return pl.pallas_call(
        kernel,
        name=name,
        in_specs=[
            *[pl.BlockSpec(memory_space=pltpu.SMEM)] * len(scalars),
            *[p.spec for p in ins],
            *[anywhere] * len(after),
        ],
        out_specs=[p.spec for p in outs],
        out_shape=[p.array for p in outs],
        scratch_shapes=[
            *[pltpu.VMEM(p.shape, p.array.dtype) for p in far],
            pltpu.SemaphoreType.DMA((len(ins), chunks)),
            pltpu.SemaphoreType.DMA((len(outs), chunks)),
            *scratch,
        ],
        compiler_params=pltpu.CompilerParams(vmem_limit_bytes=limit),
        cost_estimate=pl.CostEstimate(
            flops=flops,
            bytes_accessed=sum(p.array.size * p.array.dtype.itemsize for p in (*ins, *outs)),
            transcendentals=0,
        ),
    )(*scalars, *[p.array for p in ins], *after)


def local(queries, keys, values, grad_out, gain, lengths, block_mask):
    rows, width = queries.shape
    heads = width // DH
    blocks = rows // BLOCK
    devices = GROUP // rows
    peers = devices - 1
    head_count = lax.axis_size("head")
    total = lax.axis_size("ctx") * head_count
    chunks = CHUNKS if heads % CHUNKS == 0 else 1
    few = min(chunks, 2)
    shape = jax.ShapeDtypeStruct
    state = shape((heads, DH, DH), BF)
    tokens = shape((rows, width), BF)
    partial = shape((rows, width), F32)
    block_tokens = shape((BLOCK, width), BF)
    square = [pltpu.VMEM((rows, rows), F32)]
    unit = 2 * rows * width * DH
    inner = 2 * rows * rows * width
    scalars = [lengths, block_mask]

    def wide(array, block=None):
        return Part(array, 1, block)

    def states(array):
        return Part(array, 0)

    def split_states(arrays):
        result, lead = [], 0
        for a in arrays:
            count = a.shape[0] * chunks // heads
            result.append(Part(a, 0, lead=lead, parts=count))
            lead += count
        return result

    def to_peers(array, away, backward):
        pairs = [(z, z + away) for z in range(head_count - away) if z % devices + away < devices]
        if backward:
            pairs = [(b, a) for a, b in pairs]
        return lax.ppermute(array, "head", pairs)

    def exchanged(slices):
        return lax.all_to_all(slices, AXES, split_axis=0, concat_axis=0, tiled=True)

    def scanned(slices, backward):
        (slices,) = call(
            functools.partial(scan_body, rows=rows, backward=backward),
            "scan",
            [lengths],
            [Part(slices, near=True)],
            [Part(shape(slices.shape, BF), 1)],
            heads,
            2 if slices.shape[1] % 32 == 0 else 1,
            limit=SOME_BYTES,
        )
        return slices

    gain_row = Part(gain.reshape(1, width))
    early = heads // chunks
    sizes = [heads], [early, heads - early] if chunks > 1 else [heads]
    sizes = [sizes[b > 0] for b in range(blocks) for _ in range(peers)]
    halves = [len(n) for n in sizes]
    later = [[shape((k, DH, DH), BF) for k in n] for n in sizes]
    (sum_kv,) = call(
        total_body,
        "total",
        scalars,
        [wide(keys), wide(values)],
        [states(state)],
        heads,
        few,
        flops=unit,
    )
    slices = sum_kv.reshape(total, -1, DH)
    slices, late_keys = lax.optimization_barrier((slices, keys))
    slices = exchanged(slices)
    if later:
        later = call(
            functools.partial(state_body, counts=halves),
            "states",
            scalars,
            [wide(late_keys), wide(values)],
            [part for arrays in later for part in split_states(arrays)],
            heads,
            chunks,
            flops=LONG,
        )
    later = iter(later)
    from_peers = [[next(later) for _ in range(n)] for n in halves]
    for at, arrays in enumerate(from_peers):
        arrays[0] = to_peers(arrays[0], 1 + at % peers, False)
    slices = scanned(slices, False)
    slices, late_queries = lax.optimization_barrier((slices, queries))
    (raw_inner,) = call(
        inner_body,
        "inner",
        scalars,
        [wide(late_queries), wide(keys), wide(values)],
        [wide(partial)],
        heads,
        chunks,
        square,
        flops=LONG,
        after=[x for arrays in from_peers[:peers] for x in arrays],
    )
    kv_state = exchanged(slices).reshape(heads, DH, DH)
    for at, arrays in enumerate(from_peers):
        if len(arrays) > 1:
            later_half, raw_inner = lax.optimization_barrier((arrays[1], raw_inner))
            arrays[1] = to_peers(later_half, 1 + at % peers, False)

    scales, raws, grads, updates, back = [], [], [], [], []
    for b in range(blocks):
        ends = [states(state)] if b == blocks - 1 and blocks > 1 else []
        scale, raw, grad, update, *sums = call(
            functools.partial(norm_body, rows=rows, block=b, counts=[1, *halves[b * peers : (b + 1) * peers]]),
            "norm",
            scalars,
            [
                gain_row,
                wide(queries, b),
                wide(raw_inner, b),
                wide(grad_out, b),
                states(kv_state),
                *[Part(x) for arrays in from_peers[b * peers : (b + 1) * peers] for x in arrays],
                *[states(w) for w in (updates if ends else [])],
            ],
            [Part(shape((BLOCK, DH), F32)), wide(block_tokens), wide(block_tokens), states(state), *ends],
            heads,
            few,
            flops=LONG if b > 0 else 2 * unit // blocks,
        )
        scales.append(scale)
        raws.append(raw)
        grads.append(grad)
        updates.append(update)
        back += [to_peers(update, away, True) for away in range(1, devices)]
    output, grad_q = call(
        functools.partial(query_grads_body, peers=peers, counts=halves),
        "query_grads",
        scalars,
        [
            gain_row,
            wide(keys),
            wide(values),
            states(kv_state),
            *[wide(d) for d in grads],
            *[wide(r) for r in raws],
            *[Part(s) for s in scales],
            *[part for arrays in from_peers for part in split_states(arrays)],
        ],
        [wide(tokens), wide(tokens)],
        heads,
        chunks,
        square,
        flops=LONG,
        after=back[:peers],
    )
    slices = exchanged((sums[0] if sums else updates[0]).reshape(total, -1, DH))
    slices, grad_q = lax.optimization_barrier((slices, grad_q))
    slices = scanned(slices, True)
    slices, late_queries = lax.optimization_barrier((slices, queries))
    part_k, part_v = call(
        functools.partial(key_grads_body, peers=peers),
        "key_grads",
        scalars,
        [
            wide(late_queries),
            wide(keys),
            wide(values),
            *[wide(d) for d in grads],
            *[states(w) for w in back],
        ],
        [wide(partial), wide(partial)],
        heads,
        chunks,
        square,
        flops=LONG,
    )
    grad_state = exchanged(slices).reshape(heads, DH, DH)
    grad_k, grad_v = call(
        last_body,
        "last",
        scalars,
        [wide(keys), wide(values), wide(part_k), wide(part_v), states(grad_state)],
        [wide(tokens), wide(tokens)],
        heads,
        few,
        flops=2 * unit,
        limit=NARROW_BYTES,
    )
    return output, grad_q, grad_k, grad_v


def solution(mesh):
    tokens = P(AXES, None)
    return jax.shard_map(
        local,
        mesh=mesh,
        in_specs=(tokens, tokens, tokens, tokens, P(), P(), P("ctx", None)),
        out_specs=(tokens, tokens, tokens, tokens),
        check_vma=False,
    )
```

```python
import functools

import jax
import jax.numpy as jnp
from jax import lax
from jax.experimental import pallas as pl
from jax.experimental.pallas import tpu as pltpu
from jax.sharding import PartitionSpec as P

DH = 128
GROUP = 512
BLOCK = 128
CHUNKS = 4
LONG = 400_000_000_000
VMEM_BYTES = 60 * 1024 * 1024
NARROW_BYTES = 53 * 1024 * 1024
SOME_BYTES = 24 * 1024 * 1024

eps_norm = 1e-06
BF = jnp.bfloat16
F32 = jnp.float32
AXES = ("ctx", "head")

NN = (((1,), (0,)), ((), ()))
NT = (((1,), (1,)), ((), ()))
TN = (((0,), (0,)), ((), ()))


def dot(a, b, dims):
    return lax.dot_general(a, b, dims, preferred_element_type=F32)


def bounds_of(len_ref):
    bounds, total = [], None
    for k in range(len_ref.shape[0] - 1):
        total = len_ref[k] if total is None else total + len_ref[k]
        bounds.append(total)
    return bounds


def segment(position, bounds):
    result = (position >= bounds[0]).astype(jnp.int32)
    for bound in bounds[1:]:
        result = result + (position >= bound).astype(jnp.int32)
    return result


def same(a, b):
    return (a == b).astype(F32)


class Place:
    def __init__(self, len_ref, rows, mask_ref=None):
        self.rows = rows
        self.blocks = rows // BLOCK
        self.devices = GROUP // rows
        self.bounds = bounds_of(len_ref)
        spot = lax.axis_index("head")
        index = lax.axis_index("ctx") * lax.axis_size("head") + spot
        self.first = index * rows
        self.part = lax.rem(spot, self.devices)
        self.group = lax.div(spot, self.devices)
        self.group_first = self.first - self.part * rows
        self.mask_ref = mask_ref

    def seg(self, position):
        return segment(position, self.bounds)

    def start(self, block):
        return self.first + block * BLOCK

    def row_segments(self, block):
        rows = lax.broadcasted_iota(jnp.int32, (BLOCK, 1), 0)
        return self.seg(rows + self.start(block))

    def pair(self, i, j):
        slot = jnp.clip(lax.div(i * (i - 1), 2) + j, 0, self.mask_ref.shape[1] - 1)
        return self.mask_ref[self.group, slot].astype(F32)

    def weights(self):
        rows = self.rows
        t = lax.broadcasted_iota(jnp.int32, (rows, rows), 0)
        s = lax.broadcasted_iota(jnp.int32, (rows, rows), 1)
        keep = (s <= t) & (self.seg(t + self.first) == self.seg(s + self.first))
        result = jnp.where(keep, 1.0, 0.0)
        for i in range(1, self.blocks):
            for j in range(i):
                bit = self.pair(self.part * self.blocks + i, self.part * self.blocks + j)
                inside = (
                    (t >= i * BLOCK)
                    & (t < (i + 1) * BLOCK)
                    & (s >= j * BLOCK)
                    & (s < (j + 1) * BLOCK)
                )
                result = jnp.where(inside, result * bit, result)
        return result

    def to_later(self, away, block):
        there = (self.part + away) * self.blocks + block
        edge = self.seg(self.start(block) + away * self.rows - 1)
        return [
            self.pair(there, self.part * self.blocks + j) * same(self.seg(self.start(j + 1) - 1), edge)
            for j in range(self.blocks)
        ]

    def before(self, block):
        edge = self.seg(self.start(block) - 1)
        carried = same(self.seg(self.group_first - 1), edge)
        peers = [(self.part >= away).astype(F32) for away in range(1, self.devices)]
        return carried, peers, (self.row_segments(block) == edge).astype(F32)

    def after(self, block):
        own = self.part * self.blocks + block
        edge = self.seg(self.start(block + 1))
        carried = same(self.seg(self.group_first + GROUP), edge)
        peers = []
        for i in range(self.blocks):
            for away in range(1, self.devices):
                there = (self.part + away < self.devices).astype(F32)
                other = (self.part + away) * self.blocks + i
                start = self.start(i) + away * self.rows
                peers.append(self.pair(other, own) * same(self.seg(start), edge) * there)
        return carried, peers, (self.row_segments(block) == edge).astype(F32)


def mixed(refs, factors, head):
    total = refs[0][head].astype(F32) * factors[0]
    for ref, factor in zip(refs[1:], factors[1:], strict=True):
        total = total + ref[head].astype(F32) * factor
    return total.astype(BF)


class Joined:
    def __init__(self, refs):
        self.refs, self.each = refs, refs[0].shape[0]

    def __getitem__(self, head):
        return self.refs[head // self.each][head % self.each]

    def __setitem__(self, head, value):
        self.refs[head // self.each][head % self.each] = value


def joined(refs, counts):
    result, at = [], 0
    for count in counts:
        result.append(Joined(refs[at : at + count]))
        at += count
    return result


def columns(head):
    return pl.ds(head * DH, DH)


def rows_of(block):
    return pl.ds(block * BLOCK, BLOCK)


def total_body(place_of, ins, outs, scratch, arrive, leave, chunks):
    k_ref, v_ref = ins
    (t_ref,) = outs
    place = place_of(k_ref.shape[0])
    last = place.seg(place.start(place.blocks) - 1)
    segments = [place.row_segments(b) for b in range(place.blocks)]
    mask = (jnp.concatenate(segments, axis=0) == last).astype(BF)
    for c, heads in enumerate(chunks):
        arrive(c)
        for head in heads:
            at = columns(head)
            t_ref[head] = dot(k_ref[:, at] * mask, v_ref[:, at], TN).astype(BF)
        leave(c)


def state_body(place_of, ins, outs, scratch, arrive, leave, chunks, *, counts):
    k_ref, v_ref = ins
    outs = joined(outs, counts)
    rows, width = k_ref.shape
    place = place_of(rows)
    ends = [place.seg(place.start(b + 1) - 1) for b in range(place.blocks)]
    masks = [(place.row_segments(b) == ends[b]).astype(BF) for b in range(place.blocks)]
    wanted = [
        place.to_later(away, b) for b in range(place.blocks) for away in range(1, place.devices)
    ]
    for c, heads in enumerate(chunks):
        arrive(c)
        for head in heads:
            updates = []
            for b in range(place.blocks):
                k = k_ref[rows_of(b), columns(head)] * masks[b]
                updates.append(dot(k, v_ref[rows_of(b), columns(head)], TN))
            for ref, factors in zip(outs, wanted, strict=True):
                total = updates[0] * factors[0]
                for update, factor in zip(updates[1:], factors[1:], strict=True):
                    total = total + update * factor
                ref[head] = total.astype(BF)
        leave(c)


def inner_body(place_of, ins, outs, scratch, arrive, leave, chunks):
    q_ref, k_ref, v_ref = ins
    (raw_ref,), (weight_ref,) = outs, scratch
    weight_ref[...] = place_of(q_ref.shape[0]).weights()
    for c, heads in enumerate(chunks):
        arrive(c)
        for head in heads:
            at = columns(head)
            probs = (dot(q_ref[:, at], k_ref[:, at], NT) * weight_ref[...]).astype(BF)
            raw_ref[:, at] = dot(probs, v_ref[:, at], NN)
        leave(c)


def scan_body(place_of, ins, outs, scratch, arrive, leave, chunks, *, rows, backward):
    (t_ref,), (out_ref,) = ins, outs
    count, height, _ = t_ref.shape
    devices = GROUP // rows
    bounds = place_of(rows).bounds
    part = height // len(chunks)
    for c in range(len(chunks)):
        arrive(c)
        at = pl.ds(c * part, part)

        def one(turn, acc):
            group = count // devices - 1 - turn if backward else turn
            for k in range(devices):
                out_ref[group * devices + k, at] = acc.astype(BF)
            for k in range(devices):
                index = group * devices + (devices - 1 - k if backward else k)
                first = index * rows
                if backward:
                    keep = same(segment(first, bounds), segment(first + rows, bounds))
                else:
                    keep = same(segment(first - 1, bounds), segment(first + rows - 1, bounds))
                acc = acc * keep + t_ref[index, at].astype(F32)
            return acc

        acc = jnp.zeros((part, DH), F32)
        if count <= 32:
            for turn in range(count // devices):
                acc = one(turn, acc)
        else:
            lax.fori_loop(0, count // devices, one, acc)
        leave(c)


def norm_body(place_of, ins, outs, scratch, arrive, leave, chunks, *, rows, block, counts):
    gain_ref, q_ref, raw_ref, grad_ref = ins[:4]
    held = 4 + sum(counts)
    state_refs, earlier_refs = joined(ins[4:held], counts), ins[held:]
    scale_ref, held_ref, d_ref, w_ref, *t_refs = outs
    width = q_ref.shape[1]
    place = place_of(rows)
    carried, there, reach = place.before(block)
    squares = cross = jnp.zeros((BLOCK, DH), F32)
    for c, heads in enumerate(chunks):
        arrive(c)
        for head in heads:
            at = columns(head)
            state = mixed(state_refs, [carried, *there], head)
            raw = raw_ref[:, at] + dot(q_ref[:, at], state, NN) * reach
            raw = raw.astype(BF)
            held_ref[:, at] = raw
            raw = raw.astype(F32)
            scaled = grad_ref[:, at].astype(F32) * gain_ref[:, at]
            squares = squares + raw * raw
            cross = cross + scaled * raw
        leave(c, [1])
    total = jnp.sum(squares, axis=1, keepdims=True)
    inverse = 1.0 / jnp.sqrt(total / width + eps_norm)
    mean = jnp.sum(cross, axis=1, keepdims=True) * inverse / width
    scale_ref[...] = jnp.broadcast_to(inverse, scale_ref.shape)
    leave(0, [0])
    own = place.seg(place.start(block))
    begin = (place.row_segments(block) == own).astype(BF)
    into = [same(place.seg(place.start(b)), place.seg(place.first)) for b in range(block + 1)]
    for c, heads in enumerate(chunks):
        for head in heads:
            at = columns(head)
            normed = held_ref[:, at].astype(F32) * inverse
            scaled = grad_ref[:, at].astype(F32) * gain_ref[:, at]
            grad = ((scaled - normed * mean) * inverse).astype(BF)
            d_ref[:, at] = grad
            update = dot(q_ref[:, at] * begin, grad, TN)
            w_ref[head] = update.astype(BF)
            for t_ref in t_refs:
                sums = update * into[block]
                for ref, factor in zip(earlier_refs, into[:block], strict=True):
                    sums = sums + ref[head].astype(F32) * factor
                t_ref[head] = sums.astype(BF)
        leave(c, range(2, len(outs)))


def query_grads_body(place_of, ins, outs, scratch, arrive, leave, chunks, *, peers, counts):
    gain_ref, k_ref, v_ref, kv_ref = ins[:4]
    rows, width = k_ref.shape
    place = place_of(rows)
    blocks = place.blocks
    rest = ins[4:]
    d_refs, raw_refs, scale_refs = rest[:blocks], rest[blocks : 2 * blocks], rest[2 * blocks : 3 * blocks]
    peer_refs = joined(rest[3 * blocks :], counts)
    out_ref, gq_ref = outs
    (weight_ref,) = scratch
    weight_ref[...] = place.weights()
    factors = [place.before(b) for b in range(blocks)]
    for c, heads in enumerate(chunks):
        arrive(c)
        for head in heads:
            at = columns(head)
            d = jnp.concatenate([ref[:, at] for ref in d_refs], axis=0)
            grad_probs = (dot(d, v_ref[:, at], NT) * weight_ref[...]).astype(BF)
            inner = dot(grad_probs, k_ref[:, at], NN)
            for b in range(blocks):
                carried, there, _ = factors[b]
                state = mixed([kv_ref, *peer_refs[b * peers : (b + 1) * peers]], [carried, *there], head)
                outer = dot(d_refs[b][:, at], state, NT) * factors[b][2]
                part = inner[b * BLOCK : (b + 1) * BLOCK] + outer
                gq_ref[rows_of(b), at] = part.astype(BF)
                normed = raw_refs[b][:, at].astype(F32) * scale_refs[b][...]
                out_ref[rows_of(b), at] = (normed * gain_ref[:, at]).astype(BF)
        leave(c)


def key_grads_body(place_of, ins, outs, scratch, arrive, leave, chunks, *, peers):
    q_ref, k_ref, v_ref, *rest = ins
    place = place_of(q_ref.shape[0])
    blocks = place.blocks
    d_refs, w_refs = rest[:blocks], rest[blocks:]
    gk_ref, gv_ref = outs
    (weight_ref,) = scratch
    weight_ref[...] = place.weights()
    factors = [place.after(b) for b in range(blocks)]
    for c, heads in enumerate(chunks):
        arrive(c)
        for head in heads:
            at = columns(head)
            q, d = q_ref[:, at], jnp.concatenate([ref[:, at] for ref in d_refs], axis=0)
            probs = (dot(q, k_ref[:, at], NT) * weight_ref[...]).astype(BF)
            grad_probs = (dot(d, v_ref[:, at], NT) * weight_ref[...]).astype(BF)
            gk = dot(grad_probs, q, TN)
            gv = dot(probs, d, TN)
            for b in range(blocks):
                at_rows, here = rows_of(b), slice(b * BLOCK, (b + 1) * BLOCK)
                part_k, part_v = gk[here], gv[here]
                if peers:
                    state = mixed(w_refs, factors[b][1], head)
                    part_k = part_k + dot(v_ref[at_rows, at], state, NT) * factors[b][2]
                    part_v = part_v + dot(k_ref[at_rows, at], state, NN) * factors[b][2]
                gk_ref[at_rows, at] = part_k
                gv_ref[at_rows, at] = part_v
        leave(c)


def last_body(place_of, ins, outs, scratch, arrive, leave, chunks):
    k_ref, v_ref, gk_in, gv_in, gs_ref = ins
    gk_ref, gv_ref = outs
    place = place_of(k_ref.shape[0])
    factors = [place.after(b) for b in range(place.blocks)]
    reach = jnp.concatenate([reach * carried for carried, _, reach in factors], axis=0)
    for c, heads in enumerate(chunks):
        arrive(c)
        for head in heads:
            at = columns(head)
            gk = gk_in[:, at] + dot(v_ref[:, at], gs_ref[head], NT) * reach
            gv = gv_in[:, at] + dot(k_ref[:, at], gs_ref[head], NN) * reach
            gk_ref[:, at] = gk.astype(BF)
            gv_ref[:, at] = gv.astype(BF)
        leave(c)


class Part:
    def __init__(self, array, axis=None, block=None, near=False, lead=0, parts=None):
        self.array, self.axis, self.block, self.near = array, axis, block, near
        self.lead, self.parts = lead, parts
        self.shape = array.shape if block is None else (BLOCK, *array.shape[1:])
        self.spec = pl.BlockSpec(memory_space=pltpu.VMEM if near else pltpu.HBM)

    def pieces(self, far, near, sems, count):
        far = far if self.block is None else far.at[rows_of(self.block)]
        if self.axis is None:
            return [(far, near, sems.at[0])]
        count = self.parts or count
        size = self.shape[self.axis] // count
        result = [None] * self.lead
        for c in range(count):
            at = [slice(None)] * len(self.shape)
            at[self.axis] = pl.ds(c * size, size)
            result.append((far.at[tuple(at)], near.at[tuple(at)], sems.at[c]))
        return result


def call(body, name, scalars, ins, outs, heads, chunks, scratch=(), flops=0, after=(), limit=VMEM_BYTES):
    far = [p for p in (*ins, *outs) if not p.near]
    sizes = (len(scalars), len(ins), len(after), len(outs), len(far), 2, len(scratch))

    def kernel(*refs):
        split, at = [], 0
        for size in sizes:
            split.append(refs[at : at + size])
            at += size
        settings, in_refs, _, out_refs, buffers, (in_sems, out_sems), rest = split
        buffers = iter(buffers)

        def opened(parts, given, sems):
            refs, pieces = [], []
            for i, (part, ref) in enumerate(zip(parts, given, strict=True)):
                refs.append(ref if part.near else next(buffers))
                pieces.append([] if part.near else part.pieces(ref, refs[-1], sems.at[i], chunks))
            return refs, pieces

        near_in, coming = opened(ins, in_refs, in_sems)
        near_out, going = opened(outs, out_refs, out_sems)

        def copies(parts, c, which=None):
            for i, pieces in enumerate(parts):
                if c < len(pieces) and pieces[c] is not None and (which is None or i in which):
                    yield pieces[c]

        def arrive(c):
            for far, near, sem in copies(coming, c):
                pltpu.make_async_copy(far, near, sem).wait()

        def leave(c, which=None):
            for far, near, sem in copies(going, c, which):
                pltpu.make_async_copy(near, far, sem).start()

        for c in range(chunks):
            for far, near, sem in copies(coming, c):
                pltpu.make_async_copy(far, near, sem).start()
        each = heads // chunks
        turns = [range(c * each, (c + 1) * each) for c in range(chunks)]
        place_of = lambda rows: Place(settings[0], rows, *settings[1:])
        body(place_of, near_in, near_out, rest, arrive, leave, turns)
        for c in range(chunks):
            for far, near, sem in copies(going, c):
                pltpu.make_async_copy(near, far, sem).wait()

    anywhere = pl.BlockSpec(memory_space=pl.ANY)
    return pl.pallas_call(
        kernel,
        name=name,
        in_specs=[
            *[pl.BlockSpec(memory_space=pltpu.SMEM)] * len(scalars),
            *[p.spec for p in ins],
            *[anywhere] * len(after),
        ],
        out_specs=[p.spec for p in outs],
        out_shape=[p.array for p in outs],
        scratch_shapes=[
            *[pltpu.VMEM(p.shape, p.array.dtype) for p in far],
            pltpu.SemaphoreType.DMA((len(ins), chunks)),
            pltpu.SemaphoreType.DMA((len(outs), chunks)),
            *scratch,
        ],
        compiler_params=pltpu.CompilerParams(vmem_limit_bytes=limit),
        cost_estimate=pl.CostEstimate(
            flops=flops,
            bytes_accessed=sum(p.array.size * p.array.dtype.itemsize for p in (*ins, *outs)),
            transcendentals=0,
        ),
    )(*scalars, *[p.array for p in ins], *after)


def local(queries, keys, values, grad_out, gain, lengths, block_mask):
    rows, width = queries.shape
    heads = width // DH
    blocks = rows // BLOCK
    devices = GROUP // rows
    peers = devices - 1
    head_count = lax.axis_size("head")
    total = lax.axis_size("ctx") * head_count
    chunks = CHUNKS if heads % CHUNKS == 0 else 1
    few = min(chunks, 2)
    shape = jax.ShapeDtypeStruct
    state = shape((heads, DH, DH), BF)
    tokens = shape((rows, width), BF)
    partial = shape((rows, width), F32)
    block_tokens = shape((BLOCK, width), BF)
    square = [pltpu.VMEM((rows, rows), F32)]
    unit = 2 * rows * width * DH
    inner = 2 * rows * rows * width
    scalars = [lengths, block_mask]

    def wide(array, block=None):
        return Part(array, 1, block)

    def states(array):
        return Part(array, 0)

    def split_states(arrays, chunks):
        count = chunks // len(arrays)
        return [Part(a, 0, lead=i * count, parts=count) for i, a in enumerate(arrays)]

    def to_peers(array, away, backward):
        pairs = [(z, z + away) for z in range(head_count - away) if z % devices + away < devices]
        if backward:
            pairs = [(b, a) for a, b in pairs]
        return lax.ppermute(array, "head", pairs)

    def exchanged(slices):
        return lax.all_to_all(slices, AXES, split_axis=0, concat_axis=0, tiled=True)

    def scanned(slices, backward):
        (slices,) = call(
            functools.partial(scan_body, rows=rows, backward=backward),
            "scan",
            [lengths],
            [Part(slices, near=True)],
            [Part(shape(slices.shape, BF), 1)],
            heads,
            2 if slices.shape[1] % 32 == 0 else 1,
            limit=SOME_BYTES,
        )
        return slices

    gain_row = Part(gain.reshape(1, width))
    halves = [2 if b > 0 and chunks % 2 == 0 else 1 for b in range(blocks) for _ in range(peers)]
    later = [[shape((heads // n, DH, DH), BF)] * n for n in halves]
    (sum_kv,) = call(
        total_body,
        "total",
        scalars,
        [wide(keys), wide(values)],
        [states(state)],
        heads,
        few,
        flops=unit,
    )
    slices = sum_kv.reshape(total, -1, DH)
    slices, late_keys = lax.optimization_barrier((slices, keys))
    slices = exchanged(slices)
    if later:
        later = call(
            functools.partial(state_body, counts=halves),
            "states",
            scalars,
            [wide(late_keys), wide(values)],
            [part for arrays in later for part in split_states(arrays, few)],
            heads,
            few,
            flops=LONG,
        )
    later = iter(later)
    from_peers = [[next(later) for _ in range(n)] for n in halves]
    for at, arrays in enumerate(from_peers):
        arrays[0] = to_peers(arrays[0], 1 + at % peers, False)
    slices = scanned(slices, False)
    slices, late_queries = lax.optimization_barrier((slices, queries))
    (raw_inner,) = call(
        inner_body,
        "inner",
        scalars,
        [wide(late_queries), wide(keys), wide(values)],
        [wide(partial)],
        heads,
        chunks,
        square,
        flops=LONG,
        after=[x for arrays in from_peers[:peers] for x in arrays],
    )
    kv_state = exchanged(slices).reshape(heads, DH, DH)
    for at, arrays in enumerate(from_peers):
        if len(arrays) > 1:
            later_half, raw_inner = lax.optimization_barrier((arrays[1], raw_inner))
            arrays[1] = to_peers(later_half, 1 + at % peers, False)

    scales, raws, grads, updates, back = [], [], [], [], []
    for b in range(blocks):
        ends = [states(state)] if b == blocks - 1 and blocks > 1 else []
        scale, raw, grad, update, *sums = call(
            functools.partial(norm_body, rows=rows, block=b, counts=[1, *halves[b * peers : (b + 1) * peers]]),
            "norm",
            scalars,
            [
                gain_row,
                wide(queries, b),
                wide(raw_inner, b),
                wide(grad_out, b),
                states(kv_state),
                *[p for arrays in from_peers[b * peers : (b + 1) * peers] for p in split_states(arrays, few)],
                *[states(w) for w in (updates if ends else [])],
            ],
            [Part(shape((BLOCK, DH), F32)), wide(block_tokens), wide(block_tokens), states(state), *ends],
            heads,
            few,
            flops=LONG if b > 0 else 2 * unit // blocks,
        )
        scales.append(scale)
        raws.append(raw)
        grads.append(grad)
        updates.append(update)
        back += [to_peers(update, away, True) for away in range(1, devices)]
    output, grad_q = call(
        functools.partial(query_grads_body, peers=peers, counts=halves),
        "query_grads",
        scalars,
        [
            gain_row,
            wide(keys),
            wide(values),
            states(kv_state),
            *[wide(d) for d in grads],
            *[wide(r) for r in raws],
            *[Part(s) for s in scales],
            *[part for arrays in from_peers for part in split_states(arrays, chunks)],
        ],
        [wide(tokens), wide(tokens)],
        heads,
        chunks,
        square,
        flops=LONG,
        after=back[:peers],
    )
    slices = exchanged((sums[0] if sums else updates[0]).reshape(total, -1, DH))
    slices, grad_q = lax.optimization_barrier((slices, grad_q))
    slices = scanned(slices, True)
    slices, late_queries = lax.optimization_barrier((slices, queries))
    part_k, part_v = call(
        functools.partial(key_grads_body, peers=peers),
        "key_grads",
        scalars,
        [
            wide(late_queries),
            wide(keys),
            wide(values),
            *[wide(d) for d in grads],
            *[states(w) for w in back],
        ],
        [wide(partial), wide(partial)],
        heads,
        chunks,
        square,
        flops=LONG,
    )
    grad_state = exchanged(slices).reshape(heads, DH, DH)
    grad_k, grad_v = call(
        last_body,
        "last",
        scalars,
        [wide(keys), wide(values), wide(part_k), wide(part_v), states(grad_state)],
        [wide(tokens), wide(tokens)],
        heads,
        few,
        flops=2 * unit,
        limit=NARROW_BYTES,
    )
    return output, grad_q, grad_k, grad_v


def solution(mesh):
    tokens = P(AXES, None)
    return jax.shard_map(
        local,
        mesh=mesh,
        in_specs=(tokens, tokens, tokens, tokens, P(), P(), P("ctx", None)),
        out_specs=(tokens, tokens, tokens, tokens),
        check_vma=False,
    )
```

```python
import functools

import jax
import jax.numpy as jnp
from jax import lax
from jax.experimental import pallas as pl
from jax.experimental.pallas import tpu as pltpu
from jax.sharding import PartitionSpec as P

DH = 128
GROUP = 512
BLOCK = 128
CHUNKS = 4
LONG = 400_000_000_000
VMEM_BYTES = 60 * 1024 * 1024
NARROW_BYTES = 53 * 1024 * 1024
SOME_BYTES = 24 * 1024 * 1024

eps_norm = 1e-06
BF = jnp.bfloat16
F32 = jnp.float32
AXES = ("ctx", "head")

NN = (((1,), (0,)), ((), ()))
NT = (((1,), (1,)), ((), ()))
TN = (((0,), (0,)), ((), ()))


def dot(a, b, dims):
    return lax.dot_general(a, b, dims, preferred_element_type=F32)


def bounds_of(len_ref):
    bounds, total = [], None
    for k in range(len_ref.shape[0] - 1):
        total = len_ref[k] if total is None else total + len_ref[k]
        bounds.append(total)
    return bounds


def segment(position, bounds):
    result = (position >= bounds[0]).astype(jnp.int32)
    for bound in bounds[1:]:
        result = result + (position >= bound).astype(jnp.int32)
    return result


def same(a, b):
    return (a == b).astype(F32)


class Place:
    def __init__(self, len_ref, rows, mask_ref=None):
        self.rows = rows
        self.blocks = rows // BLOCK
        self.devices = GROUP // rows
        self.bounds = bounds_of(len_ref)
        spot = lax.axis_index("head")
        index = lax.axis_index("ctx") * lax.axis_size("head") + spot
        self.first = index * rows
        self.part = lax.rem(spot, self.devices)
        self.group = lax.div(spot, self.devices)
        self.group_first = self.first - self.part * rows
        self.mask_ref = mask_ref

    def seg(self, position):
        return segment(position, self.bounds)

    def start(self, block):
        return self.first + block * BLOCK

    def row_segments(self, block):
        rows = lax.broadcasted_iota(jnp.int32, (BLOCK, 1), 0)
        return self.seg(rows + self.start(block))

    def pair(self, i, j):
        slot = jnp.clip(lax.div(i * (i - 1), 2) + j, 0, self.mask_ref.shape[1] - 1)
        return self.mask_ref[self.group, slot].astype(F32)

    def weights(self):
        rows = self.rows
        t = lax.broadcasted_iota(jnp.int32, (rows, rows), 0)
        s = lax.broadcasted_iota(jnp.int32, (rows, rows), 1)
        keep = (s <= t) & (self.seg(t + self.first) == self.seg(s + self.first))
        result = jnp.where(keep, 1.0, 0.0)
        for i in range(1, self.blocks):
            for j in range(i):
                bit = self.pair(self.part * self.blocks + i, self.part * self.blocks + j)
                inside = (
                    (t >= i * BLOCK)
                    & (t < (i + 1) * BLOCK)
                    & (s >= j * BLOCK)
                    & (s < (j + 1) * BLOCK)
                )
                result = jnp.where(inside, result * bit, result)
        return result

    def to_later(self, away, block):
        there = (self.part + away) * self.blocks + block
        edge = self.seg(self.start(block) + away * self.rows - 1)
        return [
            self.pair(there, self.part * self.blocks + j) * same(self.seg(self.start(j + 1) - 1), edge)
            for j in range(self.blocks)
        ]

    def before(self, block):
        edge = self.seg(self.start(block) - 1)
        carried = same(self.seg(self.group_first - 1), edge)
        peers = [(self.part >= away).astype(F32) for away in range(1, self.devices)]
        return carried, peers, (self.row_segments(block) == edge).astype(F32)

    def after(self, block):
        own = self.part * self.blocks + block
        edge = self.seg(self.start(block + 1))
        carried = same(self.seg(self.group_first + GROUP), edge)
        peers = []
        for i in range(self.blocks):
            for away in range(1, self.devices):
                there = (self.part + away < self.devices).astype(F32)
                other = (self.part + away) * self.blocks + i
                start = self.start(i) + away * self.rows
                peers.append(self.pair(other, own) * same(self.seg(start), edge) * there)
        return carried, peers, (self.row_segments(block) == edge).astype(F32)


def mixed(refs, factors, head):
    total = refs[0][head].astype(F32) * factors[0]
    for ref, factor in zip(refs[1:], factors[1:], strict=True):
        total = total + ref[head].astype(F32) * factor
    return total.astype(BF)


class Joined:
    def __init__(self, refs):
        self.refs, self.each = refs, refs[0].shape[0]

    def __getitem__(self, head):
        return self.refs[head // self.each][head % self.each]

    def __setitem__(self, head, value):
        self.refs[head // self.each][head % self.each] = value


def joined(refs, counts):
    result, at = [], 0
    for count in counts:
        result.append(Joined(refs[at : at + count]))
        at += count
    return result


def columns(head):
    return pl.ds(head * DH, DH)


def rows_of(block):
    return pl.ds(block * BLOCK, BLOCK)


def total_body(place_of, ins, outs, scratch, arrive, leave, chunks):
    k_ref, v_ref = ins
    (t_ref,) = outs
    place = place_of(k_ref.shape[0])
    last = place.seg(place.start(place.blocks) - 1)
    segments = [place.row_segments(b) for b in range(place.blocks)]
    mask = (jnp.concatenate(segments, axis=0) == last).astype(BF)
    for c, heads in enumerate(chunks):
        arrive(c)
        for head in heads:
            at = columns(head)
            t_ref[head] = dot(k_ref[:, at] * mask, v_ref[:, at], TN).astype(BF)
        leave(c)


def state_body(place_of, ins, outs, scratch, arrive, leave, chunks, *, counts):
    k_ref, v_ref = ins
    outs = joined(outs, counts)
    rows, width = k_ref.shape
    place = place_of(rows)
    ends = [place.seg(place.start(b + 1) - 1) for b in range(place.blocks)]
    masks = [(place.row_segments(b) == ends[b]).astype(BF) for b in range(place.blocks)]
    wanted = [
        place.to_later(away, b) for b in range(place.blocks) for away in range(1, place.devices)
    ]
    for c, heads in enumerate(chunks):
        arrive(c)
        for head in heads:
            updates = []
            for b in range(place.blocks):
                k = k_ref[rows_of(b), columns(head)] * masks[b]
                updates.append(dot(k, v_ref[rows_of(b), columns(head)], TN))
            for ref, factors in zip(outs, wanted, strict=True):
                total = updates[0] * factors[0]
                for update, factor in zip(updates[1:], factors[1:], strict=True):
                    total = total + update * factor
                ref[head] = total.astype(BF)
        leave(c)


def inner_body(place_of, ins, outs, scratch, arrive, leave, chunks):
    q_ref, k_ref, v_ref = ins
    (raw_ref,), (weight_ref,) = outs, scratch
    weight_ref[...] = place_of(q_ref.shape[0]).weights()
    for c, heads in enumerate(chunks):
        arrive(c)
        for head in heads:
            at = columns(head)
            probs = (dot(q_ref[:, at], k_ref[:, at], NT) * weight_ref[...]).astype(BF)
            raw_ref[:, at] = dot(probs, v_ref[:, at], NN)
        leave(c)


def scan_body(place_of, ins, outs, scratch, arrive, leave, chunks, *, rows, backward):
    (t_ref,), (out_ref,) = ins, outs
    count, height, _ = t_ref.shape
    devices = GROUP // rows
    bounds = place_of(rows).bounds
    part = height // len(chunks)
    for c in range(len(chunks)):
        arrive(c)
        at = pl.ds(c * part, part)

        def one(turn, acc):
            group = count // devices - 1 - turn if backward else turn
            for k in range(devices):
                out_ref[group * devices + k, at] = acc.astype(BF)
            for k in range(devices):
                index = group * devices + (devices - 1 - k if backward else k)
                first = index * rows
                if backward:
                    keep = same(segment(first, bounds), segment(first + rows, bounds))
                else:
                    keep = same(segment(first - 1, bounds), segment(first + rows - 1, bounds))
                acc = acc * keep + t_ref[index, at].astype(F32)
            return acc

        acc = jnp.zeros((part, DH), F32)
        if count <= 32:
            for turn in range(count // devices):
                acc = one(turn, acc)
        else:
            lax.fori_loop(0, count // devices, one, acc)
        leave(c)


def norm_body(place_of, ins, outs, scratch, arrive, leave, chunks, *, rows, block, counts):
    gain_ref, q_ref, raw_ref, grad_ref = ins[:4]
    held = 4 + sum(counts)
    state_refs, earlier_refs = joined(ins[4:held], counts), ins[held:]
    scale_ref, held_ref, d_ref, w_ref, *t_refs = outs
    width = q_ref.shape[1]
    place = place_of(rows)
    carried, there, reach = place.before(block)
    squares = cross = jnp.zeros((BLOCK, DH), F32)
    for c, heads in enumerate(chunks):
        arrive(c)
        for head in heads:
            at = columns(head)
            state = mixed(state_refs, [carried, *there], head)
            raw = raw_ref[:, at] + dot(q_ref[:, at], state, NN) * reach
            raw = raw.astype(BF)
            held_ref[:, at] = raw
            raw = raw.astype(F32)
            scaled = grad_ref[:, at].astype(F32) * gain_ref[:, at]
            squares = squares + raw * raw
            cross = cross + scaled * raw
        leave(c, [1])
    total = jnp.sum(squares, axis=1, keepdims=True)
    inverse = 1.0 / jnp.sqrt(total / width + eps_norm)
    mean = jnp.sum(cross, axis=1, keepdims=True) * inverse / width
    scale_ref[...] = jnp.broadcast_to(inverse, scale_ref.shape)
    leave(0, [0])
    own = place.seg(place.start(block))
    begin = (place.row_segments(block) == own).astype(BF)
    into = [same(place.seg(place.start(b)), place.seg(place.first)) for b in range(block + 1)]
    for c, heads in enumerate(chunks):
        for head in heads:
            at = columns(head)
            normed = held_ref[:, at].astype(F32) * inverse
            scaled = grad_ref[:, at].astype(F32) * gain_ref[:, at]
            grad = ((scaled - normed * mean) * inverse).astype(BF)
            d_ref[:, at] = grad
            update = dot(q_ref[:, at] * begin, grad, TN)
            w_ref[head] = update.astype(BF)
            for t_ref in t_refs:
                sums = update * into[block]
                for ref, factor in zip(earlier_refs, into[:block], strict=True):
                    sums = sums + ref[head].astype(F32) * factor
                t_ref[head] = sums.astype(BF)
        leave(c, range(2, len(outs)))


def query_grads_body(place_of, ins, outs, scratch, arrive, leave, chunks, *, peers, counts):
    gain_ref, k_ref, v_ref, kv_ref = ins[:4]
    rows, width = k_ref.shape
    place = place_of(rows)
    blocks = place.blocks
    rest = ins[4:]
    d_refs, raw_refs, scale_refs = rest[:blocks], rest[blocks : 2 * blocks], rest[2 * blocks : 3 * blocks]
    peer_refs = joined(rest[3 * blocks :], counts)
    out_ref, gq_ref = outs
    (weight_ref,) = scratch
    weight_ref[...] = place.weights()
    factors = [place.before(b) for b in range(blocks)]
    for c, heads in enumerate(chunks):
        arrive(c)
        for head in heads:
            at = columns(head)
            d = jnp.concatenate([ref[:, at] for ref in d_refs], axis=0)
            grad_probs = (dot(d, v_ref[:, at], NT) * weight_ref[...]).astype(BF)
            inner = dot(grad_probs, k_ref[:, at], NN)
            for b in range(blocks):
                carried, there, _ = factors[b]
                state = mixed([kv_ref, *peer_refs[b * peers : (b + 1) * peers]], [carried, *there], head)
                outer = dot(d_refs[b][:, at], state, NT) * factors[b][2]
                part = inner[b * BLOCK : (b + 1) * BLOCK] + outer
                gq_ref[rows_of(b), at] = part.astype(BF)
                normed = raw_refs[b][:, at].astype(F32) * scale_refs[b][...]
                out_ref[rows_of(b), at] = (normed * gain_ref[:, at]).astype(BF)
        leave(c)


def key_grads_body(place_of, ins, outs, scratch, arrive, leave, chunks, *, peers):
    q_ref, k_ref, v_ref, *rest = ins
    place = place_of(q_ref.shape[0])
    blocks = place.blocks
    d_refs, w_refs = rest[:blocks], rest[blocks:]
    gk_ref, gv_ref = outs
    (weight_ref,) = scratch
    weight_ref[...] = place.weights()
    factors = [place.after(b) for b in range(blocks)]
    for c, heads in enumerate(chunks):
        arrive(c)
        for head in heads:
            at = columns(head)
            q, d = q_ref[:, at], jnp.concatenate([ref[:, at] for ref in d_refs], axis=0)
            probs = (dot(q, k_ref[:, at], NT) * weight_ref[...]).astype(BF)
            grad_probs = (dot(d, v_ref[:, at], NT) * weight_ref[...]).astype(BF)
            gk = dot(grad_probs, q, TN)
            gv = dot(probs, d, TN)
            for b in range(blocks):
                at_rows, here = rows_of(b), slice(b * BLOCK, (b + 1) * BLOCK)
                part_k, part_v = gk[here], gv[here]
                if peers:
                    state = mixed(w_refs, factors[b][1], head)
                    part_k = part_k + dot(v_ref[at_rows, at], state, NT) * factors[b][2]
                    part_v = part_v + dot(k_ref[at_rows, at], state, NN) * factors[b][2]
                gk_ref[at_rows, at] = part_k
                gv_ref[at_rows, at] = part_v
        leave(c)


def last_body(place_of, ins, outs, scratch, arrive, leave, chunks):
    k_ref, v_ref, gk_in, gv_in, gs_ref = ins
    gk_ref, gv_ref = outs
    place = place_of(k_ref.shape[0])
    factors = [place.after(b) for b in range(place.blocks)]
    reach = jnp.concatenate([reach * carried for carried, _, reach in factors], axis=0)
    for c, heads in enumerate(chunks):
        arrive(c)
        for head in heads:
            at = columns(head)
            gk = gk_in[:, at] + dot(v_ref[:, at], gs_ref[head], NT) * reach
            gv = gv_in[:, at] + dot(k_ref[:, at], gs_ref[head], NN) * reach
            gk_ref[:, at] = gk.astype(BF)
            gv_ref[:, at] = gv.astype(BF)
        leave(c)


class Part:
    def __init__(self, array, axis=None, block=None, near=False, lead=0, parts=None):
        self.array, self.axis, self.block, self.near = array, axis, block, near
        self.lead, self.parts = lead, parts
        self.shape = array.shape if block is None else (BLOCK, *array.shape[1:])
        self.spec = pl.BlockSpec(memory_space=pltpu.VMEM if near else pltpu.HBM)

    def pieces(self, far, near, sems, count):
        far = far if self.block is None else far.at[rows_of(self.block)]
        if self.axis is None:
            return [(far, near, sems.at[0])]
        count = self.parts or count
        size = self.shape[self.axis] // count
        result = [None] * self.lead
        for c in range(count):
            at = [slice(None)] * len(self.shape)
            at[self.axis] = pl.ds(c * size, size)
            result.append((far.at[tuple(at)], near.at[tuple(at)], sems.at[c]))
        return result


def call(body, name, scalars, ins, outs, heads, chunks, scratch=(), flops=0, after=(), limit=VMEM_BYTES):
    far = [p for p in (*ins, *outs) if not p.near]
    sizes = (len(scalars), len(ins), len(after), len(outs), len(far), 2, len(scratch))

    def kernel(*refs):
        split, at = [], 0
        for size in sizes:
            split.append(refs[at : at + size])
            at += size
        settings, in_refs, _, out_refs, buffers, (in_sems, out_sems), rest = split
        buffers = iter(buffers)

        def opened(parts, given, sems):
            refs, pieces = [], []
            for i, (part, ref) in enumerate(zip(parts, given, strict=True)):
                refs.append(ref if part.near else next(buffers))
                pieces.append([] if part.near else part.pieces(ref, refs[-1], sems.at[i], chunks))
            return refs, pieces

        near_in, coming = opened(ins, in_refs, in_sems)
        near_out, going = opened(outs, out_refs, out_sems)

        def copies(parts, c, which=None):
            for i, pieces in enumerate(parts):
                if c < len(pieces) and pieces[c] is not None and (which is None or i in which):
                    yield pieces[c]

        def arrive(c):
            for far, near, sem in copies(coming, c):
                pltpu.make_async_copy(far, near, sem).wait()

        def leave(c, which=None):
            for far, near, sem in copies(going, c, which):
                pltpu.make_async_copy(near, far, sem).start()

        for c in range(chunks):
            for far, near, sem in copies(coming, c):
                pltpu.make_async_copy(far, near, sem).start()
        each = heads // chunks
        turns = [range(c * each, (c + 1) * each) for c in range(chunks)]
        place_of = lambda rows: Place(settings[0], rows, *settings[1:])
        body(place_of, near_in, near_out, rest, arrive, leave, turns)
        for c in range(chunks):
            for far, near, sem in copies(going, c):
                pltpu.make_async_copy(near, far, sem).wait()

    anywhere = pl.BlockSpec(memory_space=pl.ANY)
    return pl.pallas_call(
        kernel,
        name=name,
        in_specs=[
            *[pl.BlockSpec(memory_space=pltpu.SMEM)] * len(scalars),
            *[p.spec for p in ins],
            *[anywhere] * len(after),
        ],
        out_specs=[p.spec for p in outs],
        out_shape=[p.array for p in outs],
        scratch_shapes=[
            *[pltpu.VMEM(p.shape, p.array.dtype) for p in far],
            pltpu.SemaphoreType.DMA((len(ins), chunks)),
            pltpu.SemaphoreType.DMA((len(outs), chunks)),
            *scratch,
        ],
        compiler_params=pltpu.CompilerParams(vmem_limit_bytes=limit),
        cost_estimate=pl.CostEstimate(
            flops=flops,
            bytes_accessed=sum(p.array.size * p.array.dtype.itemsize for p in (*ins, *outs)),
            transcendentals=0,
        ),
    )(*scalars, *[p.array for p in ins], *after)


def local(queries, keys, values, grad_out, gain, lengths, block_mask):
    rows, width = queries.shape
    heads = width // DH
    blocks = rows // BLOCK
    devices = GROUP // rows
    peers = devices - 1
    head_count = lax.axis_size("head")
    total = lax.axis_size("ctx") * head_count
    chunks = CHUNKS if heads % CHUNKS == 0 else 1
    few = min(chunks, 2)
    shape = jax.ShapeDtypeStruct
    state = shape((heads, DH, DH), BF)
    tokens = shape((rows, width), BF)
    partial = shape((rows, width), F32)
    block_tokens = shape((BLOCK, width), BF)
    square = [pltpu.VMEM((rows, rows), F32)]
    unit = 2 * rows * width * DH
    inner = 2 * rows * rows * width
    scalars = [lengths, block_mask]

    def wide(array, block=None):
        return Part(array, 1, block)

    def states(array):
        return Part(array, 0)

    def split_states(arrays, chunks):
        count = chunks // len(arrays)
        return [Part(a, 0, lead=i * count, parts=count) for i, a in enumerate(arrays)]

    def to_peers(array, away, backward):
        pairs = [(z, z + away) for z in range(head_count - away) if z % devices + away < devices]
        if backward:
            pairs = [(b, a) for a, b in pairs]
        return lax.ppermute(array, "head", pairs)

    def exchanged(slices):
        return lax.all_to_all(slices, AXES, split_axis=0, concat_axis=0, tiled=True)

    def scanned(slices, backward):
        (slices,) = call(
            functools.partial(scan_body, rows=rows, backward=backward),
            "scan",
            [lengths],
            [Part(slices, near=True)],
            [Part(shape(slices.shape, BF), 1)],
            heads,
            1,
            limit=SOME_BYTES,
        )
        return slices

    gain_row = Part(gain.reshape(1, width))
    halves = [2 if b > 0 and chunks % 2 == 0 else 1 for b in range(blocks) for _ in range(peers)]
    later = [[shape((heads // n, DH, DH), BF)] * n for n in halves]
    (sum_kv,) = call(
        total_body,
        "total",
        scalars,
        [wide(keys), wide(values)],
        [states(state)],
        heads,
        1,
        flops=unit,
    )
    slices = sum_kv.reshape(total, -1, DH)
    slices, late_keys = lax.optimization_barrier((slices, keys))
    slices = exchanged(slices)
    if later:
        later = call(
            functools.partial(state_body, counts=halves),
            "states",
            scalars,
            [wide(late_keys), wide(values)],
            [part for arrays in later for part in split_states(arrays, few)],
            heads,
            few,
            flops=LONG,
        )
    later = iter(later)
    from_peers = [[next(later) for _ in range(n)] for n in halves]
    for at, arrays in enumerate(from_peers):
        arrays[0] = to_peers(arrays[0], 1 + at % peers, False)
    slices = scanned(slices, False)
    slices, late_queries = lax.optimization_barrier((slices, queries))
    (raw_inner,) = call(
        inner_body,
        "inner",
        scalars,
        [wide(late_queries), wide(keys), wide(values)],
        [wide(partial)],
        heads,
        chunks,
        square,
        flops=LONG,
        after=[x for arrays in from_peers[:peers] for x in arrays],
    )
    kv_state = exchanged(slices).reshape(heads, DH, DH)
    for at, arrays in enumerate(from_peers):
        if len(arrays) > 1:
            later_half, raw_inner = lax.optimization_barrier((arrays[1], raw_inner))
            arrays[1] = to_peers(later_half, 1 + at % peers, False)

    scales, raws, grads, updates, back = [], [], [], [], []
    for b in range(blocks):
        ends = [states(state)] if b == blocks - 1 and blocks > 1 else []
        scale, raw, grad, update, *sums = call(
            functools.partial(norm_body, rows=rows, block=b, counts=[1, *halves[b * peers : (b + 1) * peers]]),
            "norm",
            scalars,
            [
                gain_row,
                wide(queries, b),
                wide(raw_inner, b),
                wide(grad_out, b),
                states(kv_state),
                *[p for arrays in from_peers[b * peers : (b + 1) * peers] for p in split_states(arrays, few)],
                *[states(w) for w in (updates if ends else [])],
            ],
            [Part(shape((BLOCK, DH), F32)), wide(block_tokens), wide(block_tokens), states(state), *ends],
            heads,
            few,
            flops=LONG if b > 0 else 2 * unit // blocks,
        )
        scales.append(scale)
        raws.append(raw)
        grads.append(grad)
        updates.append(update)
        back += [to_peers(update, away, True) for away in range(1, devices)]
    output, grad_q = call(
        functools.partial(query_grads_body, peers=peers, counts=halves),
        "query_grads",
        scalars,
        [
            gain_row,
            wide(keys),
            wide(values),
            states(kv_state),
            *[wide(d) for d in grads],
            *[wide(r) for r in raws],
            *[Part(s) for s in scales],
            *[part for arrays in from_peers for part in split_states(arrays, chunks)],
        ],
        [wide(tokens), wide(tokens)],
        heads,
        chunks,
        square,
        flops=LONG,
        after=back[:peers],
    )
    slices = exchanged((sums[0] if sums else updates[0]).reshape(total, -1, DH))
    slices, grad_q = lax.optimization_barrier((slices, grad_q))
    slices = scanned(slices, True)
    slices, late_queries = lax.optimization_barrier((slices, queries))
    part_k, part_v = call(
        functools.partial(key_grads_body, peers=peers),
        "key_grads",
        scalars,
        [
            wide(late_queries),
            wide(keys),
            wide(values),
            *[wide(d) for d in grads],
            *[states(w) for w in back],
        ],
        [wide(partial), wide(partial)],
        heads,
        chunks,
        square,
        flops=LONG,
    )
    grad_state = exchanged(slices).reshape(heads, DH, DH)
    grad_k, grad_v = call(
        last_body,
        "last",
        scalars,
        [wide(keys), wide(values), wide(part_k), wide(part_v), states(grad_state)],
        [wide(tokens), wide(tokens)],
        heads,
        few,
        flops=2 * unit,
        limit=NARROW_BYTES,
    )
    return output, grad_q, grad_k, grad_v


def solution(mesh):
    tokens = P(AXES, None)
    return jax.shard_map(
        local,
        mesh=mesh,
        in_specs=(tokens, tokens, tokens, tokens, P(), P(), P("ctx", None)),
        out_specs=(tokens, tokens, tokens, tokens),
        check_vma=False,
    )
```

```python
import functools

import jax
import jax.numpy as jnp
from jax import lax
from jax.experimental import pallas as pl
from jax.experimental.pallas import tpu as pltpu
from jax.sharding import PartitionSpec as P

DH = 128
GROUP = 512
BLOCK = 128
CHUNKS = 4
LONG = 400_000_000_000
VMEM_BYTES = 60 * 1024 * 1024
NARROW_BYTES = 53 * 1024 * 1024
SOME_BYTES = 24 * 1024 * 1024

eps_norm = 1e-06
BF = jnp.bfloat16
F32 = jnp.float32
AXES = ("ctx", "head")

NN = (((1,), (0,)), ((), ()))
NT = (((1,), (1,)), ((), ()))
TN = (((0,), (0,)), ((), ()))


def dot(a, b, dims):
    return lax.dot_general(a, b, dims, preferred_element_type=F32)


def bounds_of(len_ref):
    bounds, total = [], None
    for k in range(len_ref.shape[0] - 1):
        total = len_ref[k] if total is None else total + len_ref[k]
        bounds.append(total)
    return bounds


def segment(position, bounds):
    result = (position >= bounds[0]).astype(jnp.int32)
    for bound in bounds[1:]:
        result = result + (position >= bound).astype(jnp.int32)
    return result


def same(a, b):
    return (a == b).astype(F32)


class Place:
    def __init__(self, len_ref, rows, mask_ref=None):
        self.rows = rows
        self.blocks = rows // BLOCK
        self.devices = GROUP // rows
        self.bounds = bounds_of(len_ref)
        spot = lax.axis_index("head")
        index = lax.axis_index("ctx") * lax.axis_size("head") + spot
        self.first = index * rows
        self.part = lax.rem(spot, self.devices)
        self.group = lax.div(spot, self.devices)
        self.group_first = self.first - self.part * rows
        self.mask_ref = mask_ref

    def seg(self, position):
        return segment(position, self.bounds)

    def start(self, block):
        return self.first + block * BLOCK

    def row_segments(self, block):
        rows = lax.broadcasted_iota(jnp.int32, (BLOCK, 1), 0)
        return self.seg(rows + self.start(block))

    def pair(self, i, j):
        slot = jnp.clip(lax.div(i * (i - 1), 2) + j, 0, self.mask_ref.shape[1] - 1)
        return self.mask_ref[self.group, slot].astype(F32)

    def weights(self):
        rows = self.rows
        t = lax.broadcasted_iota(jnp.int32, (rows, rows), 0)
        s = lax.broadcasted_iota(jnp.int32, (rows, rows), 1)
        keep = (s <= t) & (self.seg(t + self.first) == self.seg(s + self.first))
        result = jnp.where(keep, 1.0, 0.0)
        for i in range(1, self.blocks):
            for j in range(i):
                bit = self.pair(self.part * self.blocks + i, self.part * self.blocks + j)
                inside = (
                    (t >= i * BLOCK)
                    & (t < (i + 1) * BLOCK)
                    & (s >= j * BLOCK)
                    & (s < (j + 1) * BLOCK)
                )
                result = jnp.where(inside, result * bit, result)
        return result

    def to_later(self, away, block):
        there = (self.part + away) * self.blocks + block
        edge = self.seg(self.start(block) + away * self.rows - 1)
        return [
            self.pair(there, self.part * self.blocks + j) * same(self.seg(self.start(j + 1) - 1), edge)
            for j in range(self.blocks)
        ]

    def before(self, block):
        edge = self.seg(self.start(block) - 1)
        carried = same(self.seg(self.group_first - 1), edge)
        peers = [(self.part >= away).astype(F32) for away in range(1, self.devices)]
        return carried, peers, (self.row_segments(block) == edge).astype(F32)

    def after(self, block):
        own = self.part * self.blocks + block
        edge = self.seg(self.start(block + 1))
        carried = same(self.seg(self.group_first + GROUP), edge)
        peers = []
        for i in range(self.blocks):
            for away in range(1, self.devices):
                there = (self.part + away < self.devices).astype(F32)
                other = (self.part + away) * self.blocks + i
                start = self.start(i) + away * self.rows
                peers.append(self.pair(other, own) * same(self.seg(start), edge) * there)
        return carried, peers, (self.row_segments(block) == edge).astype(F32)


def mixed(refs, factors, head):
    total = refs[0][head].astype(F32) * factors[0]
    for ref, factor in zip(refs[1:], factors[1:], strict=True):
        total = total + ref[head].astype(F32) * factor
    return total.astype(BF)


class Joined:
    def __init__(self, refs):
        self.refs, self.each = refs, refs[0].shape[0]

    def __getitem__(self, head):
        return self.refs[head // self.each][head % self.each]

    def __setitem__(self, head, value):
        self.refs[head // self.each][head % self.each] = value


def joined(refs, counts):
    result, at = [], 0
    for count in counts:
        result.append(Joined(refs[at : at + count]))
        at += count
    return result


def columns(head):
    return pl.ds(head * DH, DH)


def rows_of(block):
    return pl.ds(block * BLOCK, BLOCK)


def total_body(place_of, ins, outs, scratch, arrive, leave, chunks):
    k_ref, v_ref = ins
    (t_ref,) = outs
    place = place_of(k_ref.shape[0])
    last = place.seg(place.start(place.blocks) - 1)
    segments = [place.row_segments(b) for b in range(place.blocks)]
    mask = (jnp.concatenate(segments, axis=0) == last).astype(BF)
    for c, heads in enumerate(chunks):
        arrive(c)
        for head in heads:
            at = columns(head)
            t_ref[head] = dot(k_ref[:, at] * mask, v_ref[:, at], TN).astype(BF)
        leave(c)


def state_body(place_of, ins, outs, scratch, arrive, leave, chunks, *, counts):
    k_ref, v_ref = ins
    outs = joined(outs, counts)
    rows, width = k_ref.shape
    place = place_of(rows)
    ends = [place.seg(place.start(b + 1) - 1) for b in range(place.blocks)]
    masks = [(place.row_segments(b) == ends[b]).astype(BF) for b in range(place.blocks)]
    wanted = [
        place.to_later(away, b) for b in range(place.blocks) for away in range(1, place.devices)
    ]
    for c, heads in enumerate(chunks):
        arrive(c)
        for head in heads:
            updates = []
            for b in range(place.blocks):
                k = k_ref[rows_of(b), columns(head)] * masks[b]
                updates.append(dot(k, v_ref[rows_of(b), columns(head)], TN))
            for ref, factors in zip(outs, wanted, strict=True):
                total = updates[0] * factors[0]
                for update, factor in zip(updates[1:], factors[1:], strict=True):
                    total = total + update * factor
                ref[head] = total.astype(BF)
        leave(c)


def inner_body(place_of, ins, outs, scratch, arrive, leave, chunks):
    q_ref, k_ref, v_ref = ins
    (raw_ref,), (weight_ref,) = outs, scratch
    weight_ref[...] = place_of(q_ref.shape[0]).weights()
    for c, heads in enumerate(chunks):
        arrive(c)
        for head in heads:
            at = columns(head)
            probs = (dot(q_ref[:, at], k_ref[:, at], NT) * weight_ref[...]).astype(BF)
            raw_ref[:, at] = dot(probs, v_ref[:, at], NN)
        leave(c)


def scan_body(place_of, ins, outs, scratch, arrive, leave, chunks, *, rows, backward):
    (t_ref,), (out_ref,) = ins, outs
    count, height, _ = t_ref.shape
    devices = GROUP // rows
    bounds = place_of(rows).bounds
    part = height // len(chunks)
    for c in range(len(chunks)):
        arrive(c)
        at = pl.ds(c * part, part)

        def one(turn, acc):
            group = count // devices - 1 - turn if backward else turn
            for k in range(devices):
                out_ref[group * devices + k, at] = acc.astype(BF)
            for k in range(devices):
                index = group * devices + (devices - 1 - k if backward else k)
                first = index * rows
                if backward:
                    keep = same(segment(first, bounds), segment(first + rows, bounds))
                else:
                    keep = same(segment(first - 1, bounds), segment(first + rows - 1, bounds))
                acc = acc * keep + t_ref[index, at].astype(F32)
            return acc

        acc = jnp.zeros((part, DH), F32)
        if count <= 32:
            for turn in range(count // devices):
                acc = one(turn, acc)
        else:
            lax.fori_loop(0, count // devices, one, acc)
        leave(c)


def norm_body(place_of, ins, outs, scratch, arrive, leave, chunks, *, rows, block, counts):
    gain_ref, q_ref, raw_ref, grad_ref = ins[:4]
    held = 4 + sum(counts)
    state_refs, earlier_refs = joined(ins[4:held], counts), ins[held:]
    scale_ref, held_ref, d_ref, w_ref, *t_refs = outs
    width = q_ref.shape[1]
    place = place_of(rows)
    carried, there, reach = place.before(block)
    squares = cross = jnp.zeros((BLOCK, DH), F32)
    for c, heads in enumerate(chunks):
        arrive(c)
        for head in heads:
            at = columns(head)
            state = mixed(state_refs, [carried, *there], head)
            raw = raw_ref[:, at] + dot(q_ref[:, at], state, NN) * reach
            raw = raw.astype(BF)
            held_ref[:, at] = raw
            raw = raw.astype(F32)
            scaled = grad_ref[:, at].astype(F32) * gain_ref[:, at]
            squares = squares + raw * raw
            cross = cross + scaled * raw
        leave(c, [1])
    total = jnp.sum(squares, axis=1, keepdims=True)
    inverse = 1.0 / jnp.sqrt(total / width + eps_norm)
    mean = jnp.sum(cross, axis=1, keepdims=True) * inverse / width
    scale_ref[...] = jnp.broadcast_to(inverse, scale_ref.shape)
    leave(0, [0])
    own = place.seg(place.start(block))
    begin = (place.row_segments(block) == own).astype(BF)
    into = [same(place.seg(place.start(b)), place.seg(place.first)) for b in range(block + 1)]
    for c, heads in enumerate(chunks):
        for head in heads:
            at = columns(head)
            normed = held_ref[:, at].astype(F32) * inverse
            scaled = grad_ref[:, at].astype(F32) * gain_ref[:, at]
            grad = ((scaled - normed * mean) * inverse).astype(BF)
            d_ref[:, at] = grad
            update = dot(q_ref[:, at] * begin, grad, TN)
            w_ref[head] = update.astype(BF)
            for t_ref in t_refs:
                sums = update * into[block]
                for ref, factor in zip(earlier_refs, into[:block], strict=True):
                    sums = sums + ref[head].astype(F32) * factor
                t_ref[head] = sums.astype(BF)
        leave(c, range(2, len(outs)))


def query_grads_body(place_of, ins, outs, scratch, arrive, leave, chunks, *, peers, counts):
    gain_ref, k_ref, v_ref, kv_ref = ins[:4]
    rows, width = k_ref.shape
    place = place_of(rows)
    blocks = place.blocks
    rest = ins[4:]
    d_refs, raw_refs, scale_refs = rest[:blocks], rest[blocks : 2 * blocks], rest[2 * blocks : 3 * blocks]
    peer_refs = joined(rest[3 * blocks :], counts)
    out_ref, gq_ref = outs
    (weight_ref,) = scratch
    weight_ref[...] = place.weights()
    factors = [place.before(b) for b in range(blocks)]
    for c, heads in enumerate(chunks):
        arrive(c)
        for head in heads:
            at = columns(head)
            d = jnp.concatenate([ref[:, at] for ref in d_refs], axis=0)
            grad_probs = (dot(d, v_ref[:, at], NT) * weight_ref[...]).astype(BF)
            inner = dot(grad_probs, k_ref[:, at], NN)
            for b in range(blocks):
                carried, there, _ = factors[b]
                state = mixed([kv_ref, *peer_refs[b * peers : (b + 1) * peers]], [carried, *there], head)
                outer = dot(d_refs[b][:, at], state, NT) * factors[b][2]
                part = inner[b * BLOCK : (b + 1) * BLOCK] + outer
                gq_ref[rows_of(b), at] = part.astype(BF)
                normed = raw_refs[b][:, at].astype(F32) * scale_refs[b][...]
                out_ref[rows_of(b), at] = (normed * gain_ref[:, at]).astype(BF)
        leave(c)


def key_grads_body(place_of, ins, outs, scratch, arrive, leave, chunks, *, peers):
    q_ref, k_ref, v_ref, *rest = ins
    place = place_of(q_ref.shape[0])
    blocks = place.blocks
    d_refs, w_refs = rest[:blocks], rest[blocks:]
    gk_ref, gv_ref = outs
    (weight_ref,) = scratch
    weight_ref[...] = place.weights()
    factors = [place.after(b) for b in range(blocks)]
    for c, heads in enumerate(chunks):
        arrive(c)
        for head in heads:
            at = columns(head)
            q, d = q_ref[:, at], jnp.concatenate([ref[:, at] for ref in d_refs], axis=0)
            probs = (dot(q, k_ref[:, at], NT) * weight_ref[...]).astype(BF)
            grad_probs = (dot(d, v_ref[:, at], NT) * weight_ref[...]).astype(BF)
            gk = dot(grad_probs, q, TN)
            gv = dot(probs, d, TN)
            for b in range(blocks):
                at_rows, here = rows_of(b), slice(b * BLOCK, (b + 1) * BLOCK)
                part_k, part_v = gk[here], gv[here]
                if peers:
                    state = mixed(w_refs, factors[b][1], head)
                    part_k = part_k + dot(v_ref[at_rows, at], state, NT) * factors[b][2]
                    part_v = part_v + dot(k_ref[at_rows, at], state, NN) * factors[b][2]
                gk_ref[at_rows, at] = part_k
                gv_ref[at_rows, at] = part_v
        leave(c)


def last_body(place_of, ins, outs, scratch, arrive, leave, chunks):
    k_ref, v_ref, gk_in, gv_in, gs_ref = ins
    gk_ref, gv_ref = outs
    place = place_of(k_ref.shape[0])
    factors = [place.after(b) for b in range(place.blocks)]
    reach = jnp.concatenate([reach * carried for carried, _, reach in factors], axis=0)
    for c, heads in enumerate(chunks):
        arrive(c)
        for head in heads:
            at = columns(head)
            gk = gk_in[:, at] + dot(v_ref[:, at], gs_ref[head], NT) * reach
            gv = gv_in[:, at] + dot(k_ref[:, at], gs_ref[head], NN) * reach
            gk_ref[:, at] = gk.astype(BF)
            gv_ref[:, at] = gv.astype(BF)
        leave(c)


class Part:
    def __init__(self, array, axis=None, block=None, near=False, lead=0, parts=None):
        self.array, self.axis, self.block, self.near = array, axis, block, near
        self.lead, self.parts = lead, parts
        self.shape = array.shape if block is None else (BLOCK, *array.shape[1:])
        self.spec = pl.BlockSpec(memory_space=pltpu.VMEM if near else pltpu.HBM)

    def pieces(self, far, near, sems, count):
        far = far if self.block is None else far.at[rows_of(self.block)]
        if self.axis is None:
            return [(far, near, sems.at[0])]
        count = self.parts or count
        size = self.shape[self.axis] // count
        result = [None] * self.lead
        for c in range(count):
            at = [slice(None)] * len(self.shape)
            at[self.axis] = pl.ds(c * size, size)
            result.append((far.at[tuple(at)], near.at[tuple(at)], sems.at[c]))
        return result


def call(body, name, scalars, ins, outs, heads, chunks, scratch=(), flops=0, after=(), limit=VMEM_BYTES):
    far = [p for p in (*ins, *outs) if not p.near]
    sizes = (len(scalars), len(ins), len(after), len(outs), len(far), 2, len(scratch))

    def kernel(*refs):
        split, at = [], 0
        for size in sizes:
            split.append(refs[at : at + size])
            at += size
        settings, in_refs, _, out_refs, buffers, (in_sems, out_sems), rest = split
        buffers = iter(buffers)

        def opened(parts, given, sems):
            refs, pieces = [], []
            for i, (part, ref) in enumerate(zip(parts, given, strict=True)):
                refs.append(ref if part.near else next(buffers))
                pieces.append([] if part.near else part.pieces(ref, refs[-1], sems.at[i], chunks))
            return refs, pieces

        near_in, coming = opened(ins, in_refs, in_sems)
        near_out, going = opened(outs, out_refs, out_sems)

        def copies(parts, c, which=None):
            for i, pieces in enumerate(parts):
                if c < len(pieces) and pieces[c] is not None and (which is None or i in which):
                    yield pieces[c]

        def arrive(c):
            for far, near, sem in copies(coming, c):
                pltpu.make_async_copy(far, near, sem).wait()

        def leave(c, which=None):
            for far, near, sem in copies(going, c, which):
                pltpu.make_async_copy(near, far, sem).start()

        for c in range(chunks):
            for far, near, sem in copies(coming, c):
                pltpu.make_async_copy(far, near, sem).start()
        each = heads // chunks
        turns = [range(c * each, (c + 1) * each) for c in range(chunks)]
        place_of = lambda rows: Place(settings[0], rows, *settings[1:])
        body(place_of, near_in, near_out, rest, arrive, leave, turns)
        for c in range(chunks):
            for far, near, sem in copies(going, c):
                pltpu.make_async_copy(near, far, sem).wait()

    anywhere = pl.BlockSpec(memory_space=pl.ANY)
    return pl.pallas_call(
        kernel,
        name=name,
        in_specs=[
            *[pl.BlockSpec(memory_space=pltpu.SMEM)] * len(scalars),
            *[p.spec for p in ins],
            *[anywhere] * len(after),
        ],
        out_specs=[p.spec for p in outs],
        out_shape=[p.array for p in outs],
        scratch_shapes=[
            *[pltpu.VMEM(p.shape, p.array.dtype) for p in far],
            pltpu.SemaphoreType.DMA((len(ins), chunks)),
            pltpu.SemaphoreType.DMA((len(outs), chunks)),
            *scratch,
        ],
        compiler_params=pltpu.CompilerParams(vmem_limit_bytes=limit),
        cost_estimate=pl.CostEstimate(
            flops=flops,
            bytes_accessed=sum(p.array.size * p.array.dtype.itemsize for p in (*ins, *outs)),
            transcendentals=0,
        ),
    )(*scalars, *[p.array for p in ins], *after)


def local(queries, keys, values, grad_out, gain, lengths, block_mask):
    rows, width = queries.shape
    heads = width // DH
    blocks = rows // BLOCK
    devices = GROUP // rows
    peers = devices - 1
    head_count = lax.axis_size("head")
    total = lax.axis_size("ctx") * head_count
    chunks = CHUNKS if heads % CHUNKS == 0 else 1
    few = min(chunks, 2)
    shape = jax.ShapeDtypeStruct
    state = shape((heads, DH, DH), BF)
    tokens = shape((rows, width), BF)
    partial = shape((rows, width), F32)
    block_tokens = shape((BLOCK, width), BF)
    square = [pltpu.VMEM((rows, rows), F32)]
    unit = 2 * rows * width * DH
    inner = 2 * rows * rows * width
    scalars = [lengths, block_mask]

    def wide(array, block=None):
        return Part(array, 1, block)

    def states(array):
        return Part(array, 0)

    def split_states(arrays, chunks):
        count = chunks // len(arrays)
        return [Part(a, 0, lead=i * count, parts=count) for i, a in enumerate(arrays)]

    def to_peers(array, away, backward):
        pairs = [(z, z + away) for z in range(head_count - away) if z % devices + away < devices]
        if backward:
            pairs = [(b, a) for a, b in pairs]
        return lax.ppermute(array, "head", pairs)

    def exchanged(slices):
        return lax.all_to_all(slices, AXES, split_axis=0, concat_axis=0, tiled=True)

    def scanned(slices, backward):
        (slices,) = call(
            functools.partial(scan_body, rows=rows, backward=backward),
            "scan",
            [lengths],
            [Part(slices, near=True)],
            [Part(shape(slices.shape, BF), 1)],
            heads,
            2 if slices.shape[1] % 32 == 0 else 1,
            limit=SOME_BYTES,
        )
        return slices

    gain_row = Part(gain.reshape(1, width))
    halves = [2 if b > 0 and chunks % 2 == 0 else 1 for b in range(blocks) for _ in range(peers)]
    later = [[shape((heads // n, DH, DH), BF)] * n for n in halves]
    (sum_kv,) = call(
        total_body,
        "total",
        scalars,
        [wide(keys), wide(values)],
        [states(state)],
        heads,
        few,
        flops=unit,
    )
    slices = sum_kv.reshape(total, -1, DH)
    slices, late_keys = lax.optimization_barrier((slices, keys))
    slices = exchanged(slices)
    if later:
        later = call(
            functools.partial(state_body, counts=halves),
            "states",
            scalars,
            [wide(late_keys), wide(values)],
            [part for arrays in later for part in split_states(arrays, few)],
            heads,
            few,
            flops=LONG,
        )
    later = iter(later)
    from_peers = [[next(later) for _ in range(n)] for n in halves]
    for at, arrays in enumerate(from_peers):
        arrays[0] = to_peers(arrays[0], 1 + at % peers, False)
    slices = scanned(slices, False)
    slices, late_queries = lax.optimization_barrier((slices, queries))
    (raw_inner,) = call(
        inner_body,
        "inner",
        scalars,
        [wide(late_queries), wide(keys), wide(values)],
        [wide(partial)],
        heads,
        chunks,
        square,
        flops=LONG,
        after=[x for arrays in from_peers[:peers] for x in arrays],
    )
    kv_state = exchanged(slices).reshape(heads, DH, DH)
    for at, arrays in enumerate(from_peers):
        if len(arrays) > 1:
            later_half, raw_inner = lax.optimization_barrier((arrays[1], raw_inner))
            arrays[1] = to_peers(later_half, 1 + at % peers, False)

    scales, raws, grads, updates, back = [], [], [], [], []
    for b in range(blocks):
        ends = [states(state)] if b == blocks - 1 and blocks > 1 else []
        scale, raw, grad, update, *sums = call(
            functools.partial(norm_body, rows=rows, block=b, counts=[1, *halves[b * peers : (b + 1) * peers]]),
            "norm",
            scalars,
            [
                gain_row,
                wide(queries, b),
                wide(raw_inner, b),
                wide(grad_out, b),
                Part(kv_state),
                *[Part(x) for arrays in from_peers[b * peers : (b + 1) * peers] for x in arrays],
                *[states(w) for w in (updates if ends else [])],
            ],
            [Part(shape((BLOCK, DH), F32)), wide(block_tokens), wide(block_tokens), states(state), *ends],
            heads,
            few,
            flops=LONG if b > 0 else 2 * unit // blocks,
        )
        scales.append(scale)
        raws.append(raw)
        grads.append(grad)
        updates.append(update)
        back += [to_peers(update, away, True) for away in range(1, devices)]
    output, grad_q = call(
        functools.partial(query_grads_body, peers=peers, counts=halves),
        "query_grads",
        scalars,
        [
            gain_row,
            wide(keys),
            wide(values),
            states(kv_state),
            *[wide(d) for d in grads],
            *[wide(r) for r in raws],
            *[Part(s) for s in scales],
            *[part for arrays in from_peers for part in split_states(arrays, chunks)],
        ],
        [wide(tokens), wide(tokens)],
        heads,
        chunks,
        square,
        flops=LONG,
        after=back[:peers],
    )
    slices = exchanged((sums[0] if sums else updates[0]).reshape(total, -1, DH))
    slices, grad_q = lax.optimization_barrier((slices, grad_q))
    slices = scanned(slices, True)
    slices, late_queries = lax.optimization_barrier((slices, queries))
    part_k, part_v = call(
        functools.partial(key_grads_body, peers=peers),
        "key_grads",
        scalars,
        [
            wide(late_queries),
            wide(keys),
            wide(values),
            *[wide(d) for d in grads],
            *[states(w) for w in back],
        ],
        [wide(partial), wide(partial)],
        heads,
        chunks,
        square,
        flops=LONG,
    )
    grad_state = exchanged(slices).reshape(heads, DH, DH)
    grad_k, grad_v = call(
        last_body,
        "last",
        scalars,
        [wide(keys), wide(values), wide(part_k), wide(part_v), states(grad_state)],
        [wide(tokens), wide(tokens)],
        heads,
        few,
        flops=2 * unit,
        limit=NARROW_BYTES,
    )
    return output, grad_q, grad_k, grad_v


def solution(mesh):
    tokens = P(AXES, None)
    return jax.shard_map(
        local,
        mesh=mesh,
        in_specs=(tokens, tokens, tokens, tokens, P(), P(), P("ctx", None)),
        out_specs=(tokens, tokens, tokens, tokens),
        check_vma=False,
    )
```
